128 devices in a mesh: dp: 16 (over x, y_lo, core), tensor: 8 (over y_hi, z).
Axes of the slice: x: 4, y: 4 (y_hi: 2, y_lo: 2; y = y_hi * 2 + y_lo), z: 4, core: 2. Of those that a mesh axis runs over, the one named last changes fastest.
Arguments:
- hidden_in: bfloat16 [16, 1024, 1536], P('dp', 'tensor'), may hold values from -6 to 6
- grad_out: bfloat16 [16, 1024, 1536], P('dp', 'tensor'), may hold values from -6 to 6
- norm_in: float32 [2, 1536], replicated, may hold values from 0.5 to 1.5
- w_z: bfloat16 [2, 1536, 3072], P(None, None, 'tensor'), may hold values from -0.15625 to 0.15625
- w_x: bfloat16 [2, 1536, 3072], P(None, None, 'tensor'), may hold values from -1.7350552 to 1.7350552
- w_bc: bfloat16 [2, 1536, 256], P(None, None, 'tensor'), may hold values from -0.15625 to 0.15625
- w_dt: bfloat16 [2, 1536, 48], P(None, None, 'tensor'), may hold values from -0.15625 to 0.15625
- conv_x: float32 [2, 4, 3072], P(None, None, 'tensor'), may hold values from -3 to 3
- conv_x_bias: float32 [2, 3072], P(None, 'tensor'), may hold values from -3 to 3
- conv_bc: float32 [2, 4, 256], replicated, may hold values from -3 to 3
- conv_bc_bias: float32 [2, 256], replicated, may hold values from -3 to 3
- dt_bias: float32 [2, 48], P(None, 'tensor'), may hold values from -7 to -2.3
- a_log: float32 [2, 48], P(None, 'tensor'), may hold values from 0 to 2.77
- skip: float32 [2, 48], P(None, 'tensor'), may hold values from 0.5 to 2
- norm_gate: float32 [2, 3072], P(None, 'tensor'), may hold values from 0.5 to 1.5
- w_out: bfloat16 [2, 3072, 1536], P(None, 'tensor'), may hold values from -0.109375 to 0.109375
Outputs:
- hidden_out: float32 [16, 1024, 1536], P('dp', 'tensor')
- grad_in: float32 [16, 1024, 1536], P('dp', 'tensor')
- grad_norm_in: float32 [2, 1536], replicated
- grad_w_z: float32 [2, 1536, 3072], P(None, None, 'tensor')
- grad_w_x: float32 [2, 1536, 3072], P(None, None, 'tensor')
- grad_w_bc: float32 [2, 1536, 256], P(None, None, 'tensor')
- grad_w_dt: float32 [2, 1536, 48], P(None, None, 'tensor')
- grad_conv_x: float32 [2, 4, 3072], P(None, None, 'tensor')
- grad_conv_x_bias: float32 [2, 3072], P(None, 'tensor')
- grad_conv_bc: float32 [2, 4, 256], replicated
- grad_conv_bc_bias: float32 [2, 256], replicated
- grad_dt_bias: float32 [2, 48], P(None, 'tensor')
- grad_a_log: float32 [2, 48], P(None, 'tensor')
- grad_skip: float32 [2, 48], P(None, 'tensor')
- grad_norm_gate: float32 [2, 3072], P(None, 'tensor')
- grad_w_out: float32 [2, 3072, 1536], P(None, 'tensor')
The draws below stay inside these ranges and needn't reach their ends.
All inputs are finite; a program needn't handle non-finite values.
Results may differ from the reference program's by a relative error of at most 0.025.
Values may be sent and summed in bfloat16 or wider, within the bound.
No kernel may reach another device: no remote copies, remote signals or barrier semaphores. Data moves between devices by JAX's collectives and lax.ppermute only.
A program may use at most 192 MiB of HBM per device.

```python
import jax
import jax.numpy as jnp
from jax import lax

D = 1536
HEADS = 48
STATE = 128
CONV = 4
SPAN = 256
LAYERS = 2
LENGTH = 1024
INNER = 3072
BATCH = 16


def draw_w_x(key, part):
    key = jax.random.fold_in(key, 11)
    key_normal, key_jitter = jax.random.split(key)
    normal_vals = jnp.clip(jax.random.normal(key_normal, (LAYERS, D, INNER), jnp.float32), -6.0, 6.0)
    column = lax.broadcasted_iota(jnp.float32, (1, 1, INNER), 2) / (INNER - 1)
    jitter = jax.random.uniform(key_jitter, (LAYERS, 1, INNER), jnp.float32, 0.8, 1.25)
    spread = 3.0
    scaled = normal_vals * jitter * jnp.power(spread, column) * D ** (-0.5)
    return scaled.astype(jnp.bfloat16)


def block_levels(key, extent, shards, smallest, top_value):
    def one(dim, shards_of):
        draws = jax.random.uniform(jax.random.fold_in(jax.random.fold_in(key, 6), dim), (shards_of,), jnp.float32, smallest / len(shards), top_value / len(shards))
        return jnp.repeat(jnp.exp(draws), extent[dim] // shards_of).reshape((-1,) + (1,) * (len(extent) - dim - 1))

    loudness = one(*shards[0])
    for cut in shards[1:]:
        loudness = loudness * one(*cut)
    return loudness


def normal_values(rng, extent, scale, reach, cuts=(), dtype=jnp.bfloat16):
    array = jax.random.normal(rng, extent, jnp.float32) * scale
    if len(cuts) > 0:
        array = block_levels(rng, extent, cuts, -0.22, 0.18) * array
    return jnp.clip(array, min=-reach, max=reach).astype(dtype)


def setup_inputs(seed: int = 0) -> dict:
    seeds = jax.random.split(jax.random.key(seed), 17)
    hidden_in = normal_values(seeds[0], (BATCH, LENGTH, D), 1.0, 6.0, ((0, 16), (1, 8)))
    grad_out = normal_values(seeds[1], (BATCH, LENGTH, D), 1.0, 6.0, ((0, 16), (1, 8)))
    norm_in = jnp.clip(1.0 + 0.1 * jax.random.normal(seeds[2], (LAYERS, D), jnp.float32), 0.5, 1.5)
    w_z = normal_values(seeds[3], (LAYERS, D, INNER), D ** -0.5, 0.15625, ((2, 8),))
    w_x = draw_w_x(jax.random.fold_in(seeds[16], 71), 0)
    w_bc = normal_values(seeds[5], (LAYERS, D, 2 * STATE), D ** -0.5, 0.15625, ((2, 8),))
    w_dt = normal_values(seeds[6], (LAYERS, D, HEADS), D ** -0.5, 0.15625, ((2, 8),))
    conv_x = normal_values(seeds[7], (LAYERS, CONV, INNER), CONV ** -0.5, 3.0, ((2, 8),), jnp.float32)
    conv_x_bias = normal_values(seeds[8], (LAYERS, INNER), 0.5, 3.0, ((1, 8),), jnp.float32)
    conv_bc = normal_values(seeds[9], (LAYERS, CONV, 2 * STATE), CONV ** -0.5, 3.0, (), jnp.float32)
    conv_bc_bias = normal_values(seeds[10], (LAYERS, 2 * STATE), 0.5, 3.0, (), jnp.float32)
    dt_bias = jnp.clip(-7.0 + 4.7 * jax.random.uniform(seeds[11], (LAYERS, HEADS), jnp.float32) ** block_levels(seeds[11], (LAYERS, HEADS), ((1, 8),), -0.2, 0.2), -7.0, -2.3)
    a_log = jnp.clip(2.77 * jax.random.uniform(seeds[12], (LAYERS, HEADS), jnp.float32) ** block_levels(seeds[12], (LAYERS, HEADS), ((1, 8),), -0.2, 0.2), 0.0, 2.77)
    skip = jnp.clip(0.5 + 1.5 * jax.random.uniform(seeds[13], (LAYERS, HEADS), jnp.float32) ** block_levels(seeds[13], (LAYERS, HEADS), ((1, 8),), -0.2, 0.2), 0.5, 2.0)
    norm_gate = jnp.clip(1.0 + 0.1 * jax.random.normal(seeds[14], (LAYERS, INNER), jnp.float32), 0.5, 1.5)
    w_out = normal_values(seeds[15], (LAYERS, INNER, D), INNER ** -0.5, 0.109375, ((1, 8),))
    return dict(hidden_in=hidden_in, grad_out=grad_out, norm_in=norm_in, w_z=w_z, w_x=w_x, w_bc=w_bc, w_dt=w_dt, conv_x=conv_x, conv_x_bias=conv_x_bias, conv_bc=conv_bc, conv_bc_bias=conv_bc_bias, dt_bias=dt_bias, a_log=a_log, skip=skip, norm_gate=norm_gate, w_out=w_out)


epsilon = 1e-05
highest = lax.Precision.HIGHEST

@jax.custom_vjp
def low(v):
    return lax.optimization_barrier(v.astype(jnp.bfloat16)).astype(jnp.float32)

@jax.custom_vjp
def low_back(v):
    return v

def low_keep(v):
    return (low(v), None)

def low_pass(kept, grad):
    return (grad,)

def back_keep(v):
    return (v, None)

def back_low(kept, grad):
    return (low(grad),)
low.defvjp(low_keep, low_pass)
low_back.defvjp(back_keep, back_low)

def matmul(left_mat, right_mat):
    return jnp.dot(left_mat, right_mat, precision=highest, preferred_element_type=jnp.float32)

def causal_conv(values, kernel, offset):
    width = kernel.shape[0]
    padded = jnp.pad(values, ((width - 1, 0), (0, 0)))
    summed = offset[None, :] + jnp.zeros_like(values)
    for kernel_tap in range(width):
        summed = summed + kernel[kernel_tap][None, :] * padded[kernel_tap:kernel_tap + values.shape[0]]
    return summed

def span_scan(carried, block_data):
    x_block, b_block, c_block, step_block, rate_block = block_data
    length = rate_block.shape[0]
    row_ids = lax.broadcasted_iota(jnp.int32, (length, length), 0)
    col_ids = lax.broadcasted_iota(jnp.int32, (length, length), 1)
    tri_mask = row_ids >= col_ids
    cumulative = jnp.dot(tri_mask.astype(jnp.float32), rate_block, precision=highest)
    segment = cumulative[:, None, :] - cumulative[None, :, :]
    mask_three = tri_mask[:, :, None]
    decay_mat = jnp.where(mask_three, jnp.exp(jnp.where(mask_three, segment, 0.0)), 0.0)
    scores = jnp.dot(c_block, b_block.T, precision=highest)
    weights = scores[:, :, None] * decay_mat * step_block[None, :, :]
    y_within = jnp.einsum('tsh,shp->thp', weights, x_block, precision=highest)
    y_carried = jnp.einsum('tn,hpn->thp', c_block, carried, precision=highest) * jnp.exp(cumulative)[:, :, None]
    tail_weight = jnp.exp(cumulative[-1][None, :] - cumulative) * step_block
    weighted = tail_weight[:, :, None] * x_block
    new_state = jnp.exp(cumulative[-1])[:, None, None] * carried + jnp.einsum('shp,sn->hpn', weighted, b_block, precision=highest)
    return (new_state, y_within + y_carried)

def state_scan(x_heads, b_mat, c_mat, step_size, log_decay):
    seq_len, head_count, head_dim = x_heads.shape
    state_dim = b_mat.shape[1]
    block_count = seq_len // SPAN
    blocks = (x_heads.reshape(block_count, SPAN, head_count, head_dim), b_mat.reshape(block_count, SPAN, state_dim), c_mat.reshape(block_count, SPAN, state_dim), step_size.reshape(block_count, SPAN, head_count), log_decay.reshape(block_count, SPAN, head_count))
    start_state = jnp.zeros((head_count, head_dim, state_dim), jnp.float32)
    last_state, outputs = lax.scan(jax.checkpoint(span_scan), start_state, blocks)
    return outputs.reshape(seq_len, head_count, head_dim)

def mixer_core(x_proj, bc_proj, dt_proj, z_proj, conv_kernel, conv_offset, bc_kernel, bc_offset, dt_offset, decay_log, skip_gain):
    seq_len = x_proj.shape[0]
    head_count = dt_proj.shape[1]
    x_conv = jax.nn.silu(causal_conv(x_proj, conv_kernel, conv_offset))
    bc_conv = jax.nn.silu(causal_conv(bc_proj, bc_kernel, bc_offset))
    state_width = bc_conv.shape[1] // 2
    b_mat = bc_conv[:, :state_width]
    c_mat = bc_conv[:, state_width:]
    step_size = jax.nn.softplus(dt_proj + dt_offset[None, :])
    log_decay = -jnp.exp(decay_log)[None, :] * step_size
    x_heads = x_conv.reshape(seq_len, head_count, -1)
    y_heads = state_scan(x_heads, b_mat, c_mat, step_size, log_decay) + skip_gain[None, :, None] * x_heads
    return y_heads.reshape(seq_len, -1) * jax.nn.silu(z_proj)

def rms_norm(values, gain_vec):
    return values * lax.rsqrt(lax.optimization_barrier(jnp.mean(values * values, axis=-1, keepdims=True)) + epsilon) * gain_vec[None, :]

def one_layer(residual, params):
    norm_w, wz_mat, wx_mat, wbc_mat, wdt_mat, cx_kernel, cx_offset, cbc_kernel, cbc_offset, dt_offset, decay_log, skip_gain, gate_gain, wout_mat = params
    normed = low(rms_norm(residual, norm_w))
    z_proj = low_back(matmul(normed, wz_mat))
    x_proj = low_back(matmul(normed, wx_mat))
    bc_proj = low(low_back(matmul(normed, wbc_mat)))
    dt_proj = low_back(matmul(normed, wdt_mat))
    gated_vals = mixer_core(x_proj, bc_proj, dt_proj, z_proj, cx_kernel, cx_offset, cbc_kernel, cbc_offset, dt_offset, decay_log, skip_gain)
    gate_out = low(rms_norm(gated_vals, gate_gain))
    mixed_part = low_back(matmul(gate_out, wout_mat))
    return residual + mixed_part

def reference(hidden_in, grad_out, norm_in, w_z, w_x, w_bc, w_dt, conv_x, conv_x_bias, conv_bc, conv_bc_bias, dt_bias, a_log, skip, norm_gate, w_out):
    params = tuple((stacked.astype(jnp.float32) for stacked in (norm_in, w_z, w_x, w_bc, w_dt, conv_x, conv_x_bias, conv_bc, conv_bc_bias, dt_bias, a_log, skip, norm_gate, w_out)))

    def forward_pass(sequence, weights_all):
        for layer_id in range(LAYERS):
            sequence = one_layer(sequence, tuple((stacked[layer_id] for stacked in weights_all)))
        return sequence

    def per_sequence(totals, inputs):
        seq_in, seq_grad = inputs
        result, pullback = jax.vjp(forward_pass, seq_in.astype(jnp.float32), params)
        grad_seq, grad_params = pullback(seq_grad.astype(jnp.float32))
        totals = tuple((left_sum + right_sum for left_sum, right_sum in zip(totals, grad_params)))
        return (totals, (result, grad_seq))
    zero_grads = tuple((jnp.zeros_like(stacked) for stacked in params))
    totals, (outputs, grads_in) = lax.scan(per_sequence, zero_grads, (hidden_in, grad_out))
    return (outputs, grads_in, totals[0], totals[1], totals[2], totals[3], totals[4], totals[5], totals[6], totals[7], totals[8], totals[9], totals[10], totals[11], totals[12], totals[13])
```

```python
import functools

import jax
import jax.numpy as jnp
from jax import lax
from jax.experimental import pallas as pl
from jax.experimental.pallas import tpu as pltpu
from jax.sharding import PartitionSpec as P

SPAN = 256
EPS = 1e-05
LANES = 128
VMEM_BYTES = 56 * 1024 * 1024

f32 = jnp.float32
bf16 = jnp.bfloat16
highest = lax.Precision.HIGHEST

ROWS = ((0,), (0,))
COLS = ((1,), (1,))
PLAIN = ((1,), (0,))


def dot(left, right, dims=PLAIN, precision=None):
    return lax.dot_general(
        left, right, (dims, ((), ())), preferred_element_type=f32, precision=precision
    )


def sigmoid(v):
    return 1.0 / (1.0 + jnp.exp(-v))


def softplus(v):
    return jnp.maximum(v, 0.0) + jnp.log1p(jnp.exp(-jnp.abs(v)))


def spread_heads(per_head, channels, head_dim):
    rows = per_head.shape[0]
    per_tile = LANES // head_dim
    lane = lax.broadcasted_iota(jnp.int32, (rows, LANES), 1)
    tiles = []
    for tile in range(channels // LANES):
        out = jnp.broadcast_to(
            per_head[:, tile * per_tile : tile * per_tile + 1], (rows, LANES)
        )
        for sub in range(1, per_tile):
            head = tile * per_tile + sub
            out = jnp.where(
                lane >= sub * head_dim,
                jnp.broadcast_to(per_head[:, head : head + 1], (rows, LANES)),
                out,
            )
        tiles.append(out)
    return jnp.concatenate(tiles, axis=1)


def conv_taps(buf, taps, offset, width):
    out = offset
    for j in range(4):
        out = out + taps[j : j + 1] * buf[pl.ds(5 + j, width), :]
    return out


def decay_matrix(mask, cum_col, cum_row):
    return jnp.exp(jnp.where(mask, cum_col - cum_row, -1e30))


def span_values(dt, head_ref):
    length = dt.shape[0]
    rows = lax.broadcasted_iota(jnp.int32, (length, length), 0)
    cols = lax.broadcasted_iota(jnp.int32, (length, length), 1)
    mask = rows >= cols
    pre = dt + head_ref[0:1, :]
    step = softplus(pre)
    rate = head_ref[1:2, :] * step
    cum = dot(mask.astype(f32), rate, PLAIN, highest)
    return mask, pre, step, rate, cum


def forward_kernel(
    last_layer,
    head_dim,
    *refs,
):
    if last_layer:
        (xn_ref, wz_ref, wx_ref, wbc_ref, wdt_ref, wo_ref, cx_ref, cbc_ref, head_ref, h0_ref, xt0_ref, bt0_ref, g_ref,
         z_ref, xp_ref, bc_ref, dt_ref, y_ref, hin_ref, mixed_ref, sums_ref, gg_ref, xbuf, bbuf, hst) = refs
    else:
        (xn_ref, wz_ref, wx_ref, wbc_ref, wdt_ref, wo_ref, cx_ref, cbc_ref, head_ref, h0_ref, xt0_ref, bt0_ref,
         z_ref, xp_ref, bc_ref, dt_ref, y_ref, hin_ref, mixed_ref, xbuf, bbuf, hst) = refs
    length = xn_ref.shape[0]
    channels = wz_ref.shape[1]
    state = hst.shape[0]
    width = wo_ref.shape[1]

    @pl.when(pl.program_id(0) == 0)
    def _():
        xbuf[0:8, :] = xt0_ref[...]
        bbuf[0:8, :] = bt0_ref[...]
        hst[...] = h0_ref[...]

    xn = xn_ref[...]
    z = dot(xn, wz_ref[...])
    z_ref[...] = z
    xp = dot(xn, wx_ref[...])
    xp_ref[...] = xp
    xbuf[8:, :] = xp
    bc = dot(xn, wbc_ref[...], COLS).astype(bf16)
    bc_ref[...] = bc
    bbuf[8:, :] = bc.astype(f32)
    dt = dot(xn, wdt_ref[...])
    dt_ref[...] = dt

    pre_x = conv_taps(xbuf, cx_ref[0:4, :], cx_ref[4:5, :], length)
    xc = pre_x * sigmoid(pre_x)
    pre_bc = conv_taps(bbuf, cbc_ref[0:4, :], cbc_ref[4:5, :], length)
    bcc = (pre_bc * sigmoid(pre_bc)).astype(bf16)
    xbuf[0:8, :] = xbuf[length : length + 8, :]
    bbuf[0:8, :] = bbuf[length : length + 8, :]
    b_mat = bcc[:, :state]
    c_mat = bcc[:, state:]

    mask, _, step, _, cum = span_values(dt, head_ref)
    cum_t = jnp.transpose(cum)
    scores = dot(c_mat, b_mat, COLS)
    xs = xc * spread_heads(step, channels, head_dim)
    xs_b = xs.astype(bf16)
    lane = lax.broadcasted_iota(jnp.int32, (length, LANES), 1)
    per_tile = LANES // head_dim
    tiles = []
    for tile in range(channels // LANES):
        xs_tile = xs_b[:, tile * LANES : (tile + 1) * LANES]
        out = None
        for sub in range(per_tile):
            head = tile * per_tile + sub
            decay = decay_matrix(mask, cum[:, head : head + 1], cum_t[head : head + 1, :])
            part = dot((scores * decay).astype(bf16), xs_tile)
            out = part if out is None else jnp.where(lane >= sub * head_dim, part, out)
        tiles.append(out)
    hin = hst[...]
    hin_ref[0] = hin
    last = cum[length - 1 : length, :]
    y = jnp.concatenate(tiles, axis=1)
    y = y + dot(c_mat, hin.astype(bf16)) * spread_heads(jnp.exp(cum), channels, head_dim)
    y = y + cx_ref[6:7, :] * xc
    y_ref[...] = y
    tail = spread_heads(jnp.exp(last - cum), channels, head_dim)
    keep = spread_heads(jnp.exp(last), channels, head_dim)
    hst[...] = keep * hin + dot(b_mat, (tail * xs).astype(bf16), ROWS)

    gated = y * (z * sigmoid(z))
    scaled = gated * cx_ref[5:6, :]
    mixed_ref[:, :width] = dot(scaled.astype(bf16), wo_ref[...]).astype(bf16)
    squares = jnp.sum(gated * gated, axis=1, keepdims=True)
    high = squares.astype(bf16)
    low = (squares - high.astype(f32)).astype(bf16)
    mixed_ref[:, width:] = jnp.where(
        lane == 0, high.astype(f32), jnp.where(lane == 1, low.astype(f32), 0.0)
    ).astype(bf16)
    if last_layer:
        gg = dot(g_ref[...], wo_ref[...], COLS)
        gg_ref[...] = gg
        products = jnp.sum(gg * scaled, axis=1, keepdims=True)
        both = jnp.where(lane == 0, squares, jnp.where(lane == 1, products, 0.0))
        sums_ref[...] = jnp.transpose(both)[0:8, :]


def backward_kernel(last_layer, head_dim, inner_all, *refs):
    (first_ref, tok_ref, z_ref, xp_ref, xhalo_ref, bc_ref, bchalo_ref, dt_ref, y_ref, hin_ref,
     wz_ref, wx_ref, wbc_ref, wdt_ref, wo_ref, cx_ref, cbc_ref, head_ref, pick_ref,
     dh0_ref, du0_ref, dub0_ref, xt0_ref, bt0_ref,
     go_ref, dz_ref, dx_ref, dbc_ref, ddt_ref, gn_ref, acc_ref, accbc_ref, acch_ref,
     xbuf, bbuf, dubuf, dubbuf, dhst) = refs
    length = z_ref.shape[0]
    channels = wz_ref.shape[1]
    state = dhst.shape[0]
    width = wo_ref.shape[1]
    step_id = pl.program_id(0)
    first_span = step_id == pl.num_programs(0) - 1

    @pl.when(step_id == 0)
    def _():
        dubuf[length:, :] = du0_ref[...]
        dubbuf[length:, :] = dub0_ref[...]
        dhst[...] = dh0_ref[...]
        acc_ref[...] = jnp.zeros_like(acc_ref)
        accbc_ref[...] = jnp.zeros_like(accbc_ref)
        acch_ref[...] = jnp.zeros_like(acch_ref)

    @pl.when(first_span)
    def _():
        xbuf[0:8, :] = xt0_ref[...]
        bbuf[0:8, :] = bt0_ref[...]

    @pl.when(jnp.logical_not(first_span))
    def _():
        xbuf[0:8, :] = xhalo_ref[...]
        bbuf[0:8, :] = bchalo_ref[...].astype(f32)[8:16, :]

    xbuf[8:, :] = xp_ref[...]
    bbuf[8:, :] = bc_ref[...].astype(f32)

    if last_layer:
        gg = first_ref[...]
        tok = jnp.transpose(tok_ref[...])
        rms = lax.rsqrt(tok[:, 0:1] / inner_all + EPS)
        coef = rms * rms * rms * tok[:, 1:2] / inner_all
    else:
        gg = dot(first_ref[:, :width], wo_ref[...], COLS)
        tok = first_ref[:, width:].astype(f32)
        rms = tok[:, 0:1] + tok[:, 1:2]
        coef = tok[:, 2:3] + tok[:, 3:4]
    norm_gate = cx_ref[5:6, :]
    skip = cx_ref[6:7, :]
    z = z_ref[...]
    y = y_ref[...]
    sz = sigmoid(z)
    silu_z = z * sz
    gated = y * silu_z
    rg = rms * gg
    gated_rms = gated * rms
    go_ref[...] = (gated_rms * norm_gate).astype(bf16)
    d_gated = rg * norm_gate - gated * coef
    acc_norm = jnp.sum(rg * gated, axis=0, keepdims=True)
    dz_b = (d_gated * y * (sz * (1.0 + z * (1.0 - sz)))).astype(bf16)
    dz_ref[...] = dz_b
    dy = d_gated * silu_z

    pre_x = conv_taps(xbuf, cx_ref[0:4, :], cx_ref[4:5, :], length)
    sx = sigmoid(pre_x)
    xc = pre_x * sx
    pre_bc = conv_taps(bbuf, cbc_ref[0:4, :], cbc_ref[4:5, :], length)
    sbc = sigmoid(pre_bc)
    bcc = (pre_bc * sbc).astype(bf16)
    b_mat = bcc[:, :state]
    c_mat = bcc[:, state:]
    mask, pre_dt, step, rate, cum = span_values(dt_ref[...], head_ref)
    cum_t = jnp.transpose(cum)
    last = cum[length - 1 : length, :]
    scores = dot(c_mat, b_mat, COLS)
    step_all = spread_heads(step, channels, head_dim)
    xs = xc * step_all
    xs_b = xs.astype(bf16)
    tail = spread_heads(jnp.exp(last - cum), channels, head_dim)
    keep = spread_heads(jnp.exp(last), channels, head_dim)

    hin = hin_ref[0]
    hin_b = hin.astype(bf16)
    dh = dhst[...]
    dh_b = dh.astype(bf16)
    dye = dy * spread_heads(jnp.exp(cum), channels, head_dim)
    dye_b = dye.astype(bf16)
    txs = tail * xs
    txs_b = txs.astype(bf16)
    carried = dot(c_mat, hin_b)
    pulled = dot(b_mat, dh_b)
    d_c = dot(dye_b, hin_b, COLS)
    d_b = dot(txs_b, dh_b, COLS)
    dhst[...] = keep * dh + dot(c_mat, dye_b, ROWS)
    into = txs * pulled
    across = dye * carried - into
    at_last = jnp.sum(into, axis=0, keepdims=True) + keep * jnp.sum(hin * dh, axis=0, keepdims=True)

    dy_b = dy.astype(bf16)
    dy_t = jnp.transpose(dy).astype(bf16)
    lane = lax.broadcasted_iota(jnp.int32, (length, LANES), 1)
    per_tile = LANES // head_dim
    d_scores = jnp.zeros((length, length), f32)
    row_sums = jnp.zeros((length, LANES), f32)
    col_sums = []
    dxs_parts = []
    for head in range(channels // head_dim):
        tile, sub = divmod(head, per_tile)
        dy_tile = dy_b[:, tile * LANES : (tile + 1) * LANES]
        own = (lane >= sub * head_dim) & (lane < (sub + 1) * head_dim)
        dy_head = jnp.where(own, dy_tile, jnp.zeros_like(dy_tile))
        d_m = dot(dy_head, xs_b[:, tile * LANES : (tile + 1) * LANES], COLS)
        decay = decay_matrix(mask, cum[:, head : head + 1], cum_t[head : head + 1, :])
        dxs_parts.append(
            dot(dy_t[head * head_dim : (head + 1) * head_dim, :], (scores * decay).astype(bf16))
        )
        d_m = d_m * decay
        d_scores = d_scores + d_m
        pairs = d_m * scores
        row_sums = jnp.where(lane == head, jnp.sum(pairs, axis=1, keepdims=True), row_sums)
        col_sums.append(jnp.sum(pairs, axis=0, keepdims=True))
    heads = len(col_sums)
    col_sums = jnp.concatenate(col_sums + [jnp.zeros((LANES - heads, length), f32)], axis=0)
    dxs = jnp.transpose(jnp.concatenate(dxs_parts, axis=0)) + tail * pulled
    pick = pick_ref[...]
    d_cum = row_sums - jnp.transpose(col_sums) + dot(across, pick, PLAIN, highest)
    at_last = dot(jnp.broadcast_to(at_last, (8, channels)), pick, PLAIN, highest)[0:1, :]
    d_rate = dot(mask.astype(f32), d_cum, ROWS, highest) + at_last
    d_step = d_rate * head_ref[1:2, :] + dot(dxs * xc, pick, PLAIN, highest)
    d_dt = d_step * sigmoid(pre_dt)
    acch_ref[0:1, :] += jnp.sum(d_dt, axis=0, keepdims=True)
    acch_ref[1:2, :] += jnp.sum(d_rate * rate, axis=0, keepdims=True)
    dt_b = d_dt.astype(bf16)
    ddt_ref[...] = dt_b
    ds_b = d_scores.astype(bf16)
    d_c = d_c + dot(ds_b, b_mat)
    d_b = d_b + dot(ds_b, c_mat, ROWS)
    d_xc = dxs * step_all + skip * dy
    acc_skip = jnp.sum(dy * xc, axis=0, keepdims=True)

    d_u = d_xc * (sx * (1.0 + pre_x * (1.0 - sx)))
    d_ub = jnp.concatenate([d_b, d_c], axis=1) * (sbc * (1.0 + pre_bc * (1.0 - sbc)))
    dubuf[0:length, :] = d_u
    dubbuf[0:length, :] = d_ub
    d_x = jnp.zeros_like(d_u)
    d_bc = jnp.zeros_like(d_ub)
    acc_rows = []
    accbc_rows = []
    for j in range(4):
        d_x = d_x + cx_ref[j : j + 1, :] * dubuf[pl.ds(3 - j, length), :]
        d_bc = d_bc + cbc_ref[j : j + 1, :] * dubbuf[pl.ds(3 - j, length), :]
        acc_rows.append(jnp.sum(d_u * xbuf[pl.ds(5 + j, length), :], axis=0, keepdims=True))
        accbc_rows.append(jnp.sum(d_ub * bbuf[pl.ds(5 + j, length), :], axis=0, keepdims=True))
    dubuf[length:, :] = d_u[0:8, :]
    dubbuf[length:, :] = d_ub[0:8, :]
    zero = jnp.zeros((1, channels), f32)
    acc_ref[...] += jnp.concatenate(
        acc_rows + [jnp.sum(d_u, axis=0, keepdims=True), acc_norm, acc_skip, zero], axis=0
    )
    zero = jnp.zeros((3, d_ub.shape[1]), f32)
    accbc_ref[...] += jnp.concatenate(
        accbc_rows + [jnp.sum(d_ub, axis=0, keepdims=True), zero], axis=0
    )
    dx_b = d_x.astype(bf16)
    dbc_b = d_bc.astype(bf16)
    dx_ref[...] = dx_b
    dbc_ref[...] = dbc_b
    total = dot(dz_b, wz_ref[...], COLS) + dot(dx_b, wx_ref[...], COLS)
    total = total + dot(dbc_b, wbc_ref[...]) + dot(dt_b, wdt_ref[...], COLS)
    gn_ref[...] = total.astype(bf16)


def whole(shape):
    zeros = (0,) * len(shape)
    return pl.BlockSpec(shape, lambda i: zeros)


def span_rows(columns, rows=SPAN):
    return pl.BlockSpec((rows, columns), lambda i: (i, 0))


def run_forward(xn, weights, small, carry, head_dim, grad_rows=None):
    tokens, width = xn.shape
    channels = weights[0].shape[1]
    state = carry[0].shape[0]
    spans = tokens // SPAN
    last_layer = grad_rows is not None
    operands = [xn, *weights, *small, *carry]
    in_specs = [span_rows(width)] + [whole(v.shape) for v in operands[1:]]
    shapes = [
        jax.ShapeDtypeStruct((tokens, channels), f32),
        jax.ShapeDtypeStruct((tokens, channels), f32),
        jax.ShapeDtypeStruct((tokens, 2 * state), bf16),
        jax.ShapeDtypeStruct((tokens, LANES), f32),
        jax.ShapeDtypeStruct((tokens, channels), f32),
        jax.ShapeDtypeStruct((spans, state, channels), f32),
        jax.ShapeDtypeStruct((tokens, width + LANES), bf16),
    ]
    out_specs = [
        span_rows(channels),
        span_rows(channels),
        span_rows(2 * state),
        span_rows(LANES),
        span_rows(channels),
        pl.BlockSpec((1, state, channels), lambda i: (i, 0, 0)),
        span_rows(width + LANES),
    ]
    if last_layer:
        operands.append(grad_rows)
        in_specs.append(span_rows(width))
        shapes += [
            jax.ShapeDtypeStruct((8, tokens), f32),
            jax.ShapeDtypeStruct((tokens, channels), f32),
        ]
        out_specs += [pl.BlockSpec((8, SPAN), lambda i: (0, i)), span_rows(channels)]
    return pl.pallas_call(
        functools.partial(forward_kernel, last_layer, head_dim),
        grid=(spans,),
        in_specs=in_specs,
        out_specs=out_specs,
        out_shape=shapes,
        scratch_shapes=[
            pltpu.VMEM((SPAN + 8, channels), f32),
            pltpu.VMEM((SPAN + 8, 2 * state), f32),
            pltpu.VMEM((state, channels), f32),
        ],
        compiler_params=pltpu.CompilerParams(
            dimension_semantics=("arbitrary",), vmem_limit_bytes=VMEM_BYTES
        ),
        name="layer_forward",
    )(*operands)


def run_backward(first, sums, kept, weights, small, pick, carry, head_dim, inner_all):
    z, xp, bc, dt, y, hin = kept
    tokens, channels = z.shape
    state = hin.shape[1]
    width = weights[4].shape[1]
    spans = tokens // SPAN
    last_layer = sums is not None
    if sums is None:
        sums = jnp.zeros((8, tokens), f32)

    def rev(columns, rows=SPAN):
        return pl.BlockSpec((rows, columns), lambda i: (spans - 1 - i, 0))

    def halo(columns, rows):
        per = SPAN // rows
        return pl.BlockSpec(
            (rows, columns), lambda i: (jnp.maximum((spans - 1 - i) * per - 1, 0), 0)
        )

    operands = [first, sums, z, xp, xp, bc, bc, dt, y, hin, *weights, *small, pick, *carry]
    in_specs = [
        rev(first.shape[1]),
        pl.BlockSpec((8, SPAN), lambda i: (0, spans - 1 - i)),
        rev(channels),
        rev(channels),
        halo(channels, 8),
        rev(2 * state),
        halo(2 * state, 16),
        rev(LANES),
        rev(channels),
        pl.BlockSpec((1, state, channels), lambda i: (spans - 1 - i, 0, 0)),
    ]
    in_specs += [whole(v.shape) for v in operands[len(in_specs) :]]
    shapes = [
        jax.ShapeDtypeStruct((tokens, channels), bf16),
        jax.ShapeDtypeStruct((tokens, channels), bf16),
        jax.ShapeDtypeStruct((tokens, channels), bf16),
        jax.ShapeDtypeStruct((tokens, 2 * state), bf16),
        jax.ShapeDtypeStruct((tokens, LANES), bf16),
        jax.ShapeDtypeStruct((tokens, width), bf16),
        jax.ShapeDtypeStruct((8, channels), f32),
        jax.ShapeDtypeStruct((8, 2 * state), f32),
        jax.ShapeDtypeStruct((8, LANES), f32),
    ]
    out_specs = [rev(s.shape[1]) for s in shapes[:6]] + [whole(s.shape) for s in shapes[6:]]
    return pl.pallas_call(
        functools.partial(backward_kernel, last_layer, head_dim, inner_all),
        grid=(spans,),
        in_specs=in_specs,
        out_specs=out_specs,
        out_shape=shapes,
        scratch_shapes=[
            pltpu.VMEM((SPAN + 8, channels), f32),
            pltpu.VMEM((SPAN + 8, 2 * state), f32),
            pltpu.VMEM((SPAN + 8, channels), f32),
            pltpu.VMEM((SPAN + 8, 2 * state), f32),
            pltpu.VMEM((state, channels), f32),
        ],
        compiler_params=pltpu.CompilerParams(
            dimension_semantics=("arbitrary",), vmem_limit_bytes=VMEM_BYTES
        ),
        name="layer_backward",
    )(*operands)


HIGH, DEEP = 2, 4
TENSOR_MOVES = [(dy, dz) for dy in range(HIGH) for dz in range(DEEP) if (dy, dz) != (0, 0)]


def tensor_index(y, z):
    return (y % HIGH) * DEEP + z % DEEP


def tensor_send(v, dy, dz):
    pairs = [
        (tensor_index(y, z), tensor_index(y + dy, z + dz))
        for y in range(HIGH)
        for z in range(DEEP)
    ]
    return lax.ppermute(v, "tensor", pairs)


def place():
    me = lax.axis_index("tensor")
    return me, me // DEEP, me % DEEP


def gather_tensor(v):
    me, y, z = place()
    out = jnp.zeros((HIGH * DEEP,) + v.shape, v.dtype)
    out = lax.dynamic_update_index_in_dim(out, v, me, 0)
    for dy, dz in TENSOR_MOVES:
        source = ((y - dy) % HIGH) * DEEP + (z - dz) % DEEP
        out = lax.dynamic_update_index_in_dim(out, tensor_send(v, dy, dz), source, 0)
    return out


def scatter_tensor(v):
    me, y, z = place()
    blocks = v.reshape((HIGH * DEEP, v.shape[0] // (HIGH * DEEP)) + v.shape[1:])
    total = lax.dynamic_index_in_dim(blocks, me, 0, False).astype(f32)
    for dy, dz in TENSOR_MOVES:
        target = ((y + dy) % HIGH) * DEEP + (z + dz) % DEEP
        block = lax.dynamic_index_in_dim(blocks, target, 0, False)
        total = total + tensor_send(block, dy, dz).astype(f32)
    return total


def sum_tensor(v):
    total = v
    for dy, dz in TENSOR_MOVES:
        total = total + tensor_send(v, dy, dz)
    return total


def pad_lanes(v, lanes=LANES):
    return jnp.pad(v, [(0, 0)] * (v.ndim - 1) + [(0, lanes - v.shape[-1])])


def split_two(v):
    high = v.astype(bf16)
    return high, (v - high.astype(f32)).astype(bf16)


def local(
    hidden_in,
    grad_out,
    norm_in,
    w_z,
    w_x,
    w_bc,
    w_dt,
    conv_x,
    conv_x_bias,
    conv_bc,
    conv_bc_bias,
    dt_bias,
    a_log,
    skip,
    norm_gate,
    w_out,
):
    layers, width, channels = w_z.shape
    heads = w_dt.shape[2]
    head_dim = channels // heads
    both = conv_bc.shape[2]
    state = both // 2
    inner_all = channels * lax.axis_size("tensor")
    rows = hidden_in.shape[1]
    tokens = rows * lax.axis_size("tensor")

    residual = hidden_in[0].astype(f32)
    grad_res = grad_out[0].astype(f32)

    def normalize(v, gain):
        inv = lax.rsqrt(jnp.mean(v * v, axis=-1, keepdims=True) + EPS)
        return inv, (v * inv * gain[None, :]).astype(bf16)

    inv_rms, normed = normalize(residual, norm_in[0])
    gathered = gather_tensor(normed).reshape(tokens, width)

    bc_rows = jnp.swapaxes(w_bc, 1, 2)
    bc_rows = gather_tensor(bc_rows)
    bc_rows = jnp.swapaxes(bc_rows, 0, 1).reshape(layers, both, width)
    grad_rows = gather_tensor(grad_out[0]).reshape(tokens, width)

    channel_head = jnp.arange(channels) // head_dim
    pick = (channel_head[:, None] == jnp.arange(LANES)[None, :]).astype(f32)
    zero_row = jnp.zeros((1, channels), f32)
    weights, smalls = [], []
    for layer in range(layers):
        weights.append((w_z[layer], w_x[layer], bc_rows[layer], pad_lanes(w_dt[layer]), w_out[layer]))
        skip_all = jnp.repeat(skip[layer], head_dim)
        cx = jnp.concatenate(
            [conv_x[layer], conv_x_bias[layer][None], norm_gate[layer][None], skip_all[None], zero_row],
            axis=0,
        )
        cbc = jnp.concatenate(
            [conv_bc[layer], conv_bc_bias[layer][None], jnp.zeros((3, both), f32)], axis=0
        )
        head = jnp.concatenate(
            [
                pad_lanes(dt_bias[layer][None]),
                pad_lanes(-jnp.exp(a_log[layer])[None]),
                jnp.zeros((6, LANES), f32),
            ],
            axis=0,
        )
        smalls.append((cx, cbc, head))
    zero_state = jnp.zeros((state, channels), f32)
    zero_x = jnp.zeros((8, channels), f32)
    zero_bc = jnp.zeros((8, both), f32)
    carry = (zero_state, zero_x, zero_bc)

    kept = []
    for layer in range(layers):
        last = layer == layers - 1
        out = run_forward(
            gathered, weights[layer], smalls[layer], carry, head_dim, grad_rows if last else None
        )
        mixed = scatter_tensor(out[6])
        squares = mixed[:, width : width + 1] + mixed[:, width + 1 : width + 2]
        gate_rms = lax.rsqrt(squares / inner_all + EPS)
        mixed = mixed[:, :width] * gate_rms
        kept.append((residual, inv_rms, gathered, out, gate_rms, mixed))
        residual = residual + mixed
        if not last:
            inv_rms, normed = normalize(residual, norm_in[layer + 1])
            gathered = gather_tensor(normed).reshape(tokens, width)

    head_parts = [None] * layers
    shared_parts = [None] * layers
    for layer in reversed(range(layers)):
        res_in, inv_rms, gathered, out, gate_rms, mixed = kept[layer]
        if layer == layers - 1:
            sums = sum_tensor(out[7])
            first = out[8]
        else:
            sums = None
            g_mixed = grad_res.astype(bf16)
            products = jnp.sum(g_mixed.astype(f32) * mixed, axis=-1, keepdims=True)
            coef = gate_rms * gate_rms * products / inner_all
            extra = jnp.concatenate([*split_two(gate_rms), *split_two(coef)], axis=1)
            sent = jnp.concatenate([g_mixed, pad_lanes(extra)], axis=1)
            first = gather_tensor(sent).reshape(tokens, width + LANES)
            grad_rows = first[:, :width]
        back = run_backward(
            first, sums, out[:6], weights[layer], smalls[layer], pick,
            (zero_state, zero_x, zero_bc, zero_x, zero_bc), head_dim, inner_all,
        )
        gate_out, dz, dx, dbc, ddt, gn, acc, accbc, acch = back
        grad_normed = scatter_tensor(gn)
        scaled = grad_normed * norm_in[layer][None, :]
        g_norm_in = jnp.sum(grad_normed * res_in * inv_rms, axis=0)
        grad_res = (
            grad_res
            + inv_rms * scaled
            - res_in
            * inv_rms**3
            * (jnp.sum(scaled * res_in, axis=-1, keepdims=True) / width)
        )
        bc_sum = scatter_tensor(jnp.transpose(dbc)).astype(bf16)
        head_parts[layer] = (
            dot(gathered, dz, ROWS),
            dot(gathered, dx, ROWS),
            dot(bc_sum, gathered),
            dot(gathered, ddt, ROWS)[:, :heads],
            acc[0:4],
            acc[4],
            acch[0, :heads],
            acch[1, :heads],
            jnp.sum(acc[6].reshape(heads, head_dim), axis=1),
            acc[5],
            dot(gate_out, grad_rows, ROWS),
        )
        shared_parts[layer] = (g_norm_in, accbc[0:4], accbc[4])

    big = (0, 1, 2, 10)
    head_sums = [None] * layers
    for layer in reversed(range(layers)):
        sums_big = lax.psum(tuple(head_parts[layer][i].astype(bf16) for i in big), "dp")
        head_sums[layer] = {i: v.astype(f32) for i, v in zip(big, sums_big)}
    little = tuple(
        jnp.stack([head_parts[layer][i] for layer in range(layers)])
        for i in range(11)
        if i not in big
    )
    little = lax.psum(little, "dp")
    shared = tuple(
        jnp.stack([shared_parts[layer][i] for layer in range(layers)]) for i in range(3)
    )
    shared = lax.psum(shared, ("dp", "tensor"))
    g_wz, g_wx, g_wbc, g_wo = (
        jnp.stack([head_sums[layer][i] for layer in range(layers)]) for i in big
    )
    g_wdt, g_cx, g_cxb, g_dtb, g_alog, g_skip, g_ng = little
    return (
        residual[None],
        grad_res[None],
        shared[0],
        g_wz,
        g_wx,
        jnp.swapaxes(g_wbc, 1, 2),
        g_wdt,
        g_cx,
        g_cxb,
        shared[1],
        shared[2],
        g_dtb,
        g_alog,
        g_skip,
        g_ng,
        g_wo,
    )


def solution(mesh):
    specs_in = (
        P("dp", "tensor", None),
        P("dp", "tensor", None),
        P(),
        P(None, None, "tensor"),
        P(None, None, "tensor"),
        P(None, None, "tensor"),
        P(None, None, "tensor"),
        P(None, None, "tensor"),
        P(None, "tensor"),
        P(),
        P(),
        P(None, "tensor"),
        P(None, "tensor"),
        P(None, "tensor"),
        P(None, "tensor"),
        P(None, "tensor", None),
    )
    specs_out = (
        P("dp", "tensor", None),
        P("dp", "tensor", None),
        P(),
        P(None, None, "tensor"),
        P(None, None, "tensor"),
        P(None, None, "tensor"),
        P(None, None, "tensor"),
        P(None, None, "tensor"),
        P(None, "tensor"),
        P(),
        P(),
        P(None, "tensor"),
        P(None, "tensor"),
        P(None, "tensor"),
        P(None, "tensor"),
        P(None, "tensor", None),
    )
    return jax.shard_map(
        local, mesh=mesh, in_specs=specs_in, out_specs=specs_out, check_vma=False
    )
```

```python
import functools

import jax
import jax.numpy as jnp
from jax import lax
from jax.experimental import pallas as pl
from jax.experimental.pallas import tpu as pltpu
from jax.sharding import PartitionSpec as P

SPAN = 256
EPS = 1e-05
LANES = 128
VMEM_BYTES = 56 * 1024 * 1024

f32 = jnp.float32
bf16 = jnp.bfloat16
highest = lax.Precision.HIGHEST

ROWS = ((0,), (0,))
COLS = ((1,), (1,))
PLAIN = ((1,), (0,))


def dot(left, right, dims=PLAIN, precision=None):
    return lax.dot_general(
        left, right, (dims, ((), ())), preferred_element_type=f32, precision=precision
    )


def sigmoid(v):
    return 1.0 / (1.0 + jnp.exp(-v))


def softplus(v):
    return jnp.maximum(v, 0.0) + jnp.log1p(jnp.exp(-jnp.abs(v)))


def spread_heads(per_head, channels, head_dim):
    rows = per_head.shape[0]
    per_tile = LANES // head_dim
    lane = lax.broadcasted_iota(jnp.int32, (rows, LANES), 1)
    tiles = []
    for tile in range(channels // LANES):
        out = jnp.broadcast_to(
            per_head[:, tile * per_tile : tile * per_tile + 1], (rows, LANES)
        )
        for sub in range(1, per_tile):
            head = tile * per_tile + sub
            out = jnp.where(
                lane >= sub * head_dim,
                jnp.broadcast_to(per_head[:, head : head + 1], (rows, LANES)),
                out,
            )
        tiles.append(out)
    return jnp.concatenate(tiles, axis=1)


def conv_taps(buf, taps, offset, width):
    out = offset
    for j in range(4):
        out = out + taps[j : j + 1] * buf[pl.ds(5 + j, width), :]
    return out


def decay_matrix(mask, cum_col, cum_row):
    return jnp.exp(jnp.where(mask, cum_col - cum_row, -1e30))


def span_values(dt, head_ref):
    length = dt.shape[0]
    rows = lax.broadcasted_iota(jnp.int32, (length, length), 0)
    cols = lax.broadcasted_iota(jnp.int32, (length, length), 1)
    mask = rows >= cols
    pre = dt + head_ref[0:1, :]
    step = softplus(pre)
    rate = head_ref[1:2, :] * step
    cum = dot(mask.astype(f32), rate, PLAIN, highest)
    return mask, pre, step, rate, cum


def put_half(place_ref, span, half, mine_ref, other_ref, value):
    own = span // half == place_ref[0]

    @pl.when(own)
    def _():
        mine_ref[...] = value

    @pl.when(jnp.logical_not(own))
    def _():
        other_ref[...] = value


def forward_kernel(last_layer, head_dim, place_ref, *refs):
    if last_layer:
        (xn_ref, wz_ref, wx_ref, wbc_ref, wdt_ref, wo_ref, cx_ref, cbc_ref, head_ref, g_ref,
         z_ref, xp_ref, bc_ref, dt_ref, y_ref, hin_ref, mine_ref, other_ref, sums_ref, gg_ref, xbuf, bbuf, hst) = refs
    else:
        (xn_ref, wz_ref, wx_ref, wbc_ref, wdt_ref, wo_ref, cx_ref, cbc_ref, head_ref,
         z_ref, xp_ref, bc_ref, dt_ref, y_ref, hin_ref, mine_ref, other_ref, xbuf, bbuf, hst) = refs
    length = xn_ref.shape[0]
    channels = wz_ref.shape[1]
    state = hst.shape[0]

    @pl.when(pl.program_id(0) == 0)
    def _():
        xbuf[0:8, :] = jnp.zeros((8, channels), f32)
        bbuf[0:8, :] = jnp.zeros((8, 2 * state), f32)
        hst[...] = jnp.zeros_like(hst)

    xn = xn_ref[...]
    z = dot(xn, wz_ref[...])
    z_ref[...] = z
    xp = dot(xn, wx_ref[...])
    xp_ref[...] = xp
    xbuf[8:, :] = xp
    bc = dot(xn, wbc_ref[...], COLS).astype(bf16)
    bc_ref[...] = bc
    bbuf[8:, :] = bc.astype(f32)
    dt = dot(xn, wdt_ref[...], COLS)
    dt_ref[...] = dt

    pre_x = conv_taps(xbuf, cx_ref[0:4, :], cx_ref[4:5, :], length)
    xc = pre_x * sigmoid(pre_x)
    pre_bc = conv_taps(bbuf, cbc_ref[0:4, :], cbc_ref[4:5, :], length)
    bcc = (pre_bc * sigmoid(pre_bc)).astype(bf16)
    xbuf[0:8, :] = xbuf[length : length + 8, :]
    bbuf[0:8, :] = bbuf[length : length + 8, :]
    b_mat = bcc[:, :state]
    c_mat = bcc[:, state:]

    mask, _, step, _, cum = span_values(dt, head_ref)
    cum_t = jnp.transpose(cum)
    scores = dot(c_mat, b_mat, COLS)
    xs = xc * spread_heads(step, channels, head_dim)
    xs_b = xs.astype(bf16)
    lane = lax.broadcasted_iota(jnp.int32, (length, LANES), 1)
    per_tile = LANES // head_dim
    tiles = []
    for tile in range(channels // LANES):
        xs_tile = xs_b[:, tile * LANES : (tile + 1) * LANES]
        out = None
        for sub in range(per_tile):
            head = tile * per_tile + sub
            decay = decay_matrix(mask, cum[:, head : head + 1], cum_t[head : head + 1, :])
            part = dot((scores * decay).astype(bf16), xs_tile)
            out = part if out is None else jnp.where(lane >= sub * head_dim, part, out)
        tiles.append(out)
    hin = hst[...]
    hin_ref[0] = hin
    last = cum[length - 1 : length, :]
    y = jnp.concatenate(tiles, axis=1)
    y = y + dot(c_mat, hin.astype(bf16)) * spread_heads(jnp.exp(cum), channels, head_dim)
    y = y + cx_ref[6:7, :] * xc
    y_ref[...] = y
    tail = spread_heads(jnp.exp(last - cum), channels, head_dim)
    keep = spread_heads(jnp.exp(last), channels, head_dim)
    hst[...] = keep * hin + dot(b_mat, (tail * xs).astype(bf16), ROWS)

    gated = y * (z * sigmoid(z))
    scaled = gated * cx_ref[5:6, :]
    squares = jnp.sum(gated * gated, axis=1, keepdims=True)
    high = squares.astype(bf16).astype(f32)
    extra = jnp.where(lane == 0, high, jnp.where(lane == 1, squares - high, 0.0)).astype(bf16)
    mixed = dot(scaled.astype(bf16), wo_ref[...]).astype(bf16)
    put_half(
        place_ref,
        pl.program_id(0),
        pl.num_programs(0) // 2,
        mine_ref,
        other_ref,
        jnp.concatenate([mixed, extra], axis=1),
    )
    if last_layer:
        gg = dot(g_ref[...], wo_ref[...], COLS)
        gg_ref[...] = gg
        products = jnp.sum(gg * scaled, axis=1, keepdims=True)
        both = jnp.where(lane == 0, squares, jnp.where(lane == 1, products, 0.0))
        sums_ref[...] = jnp.transpose(both)[0:8, :]


def backward_kernel(last_layer, head_dim, inner_all, place_ref, *refs):
    (first_ref, xn_ref, tok_ref, z_ref, xp_ref, xhalo_ref, bc_ref, bchalo_ref, dt_ref, y_ref, hin_ref,
     wz_ref, wx_ref, wbc_ref, wdt_ref, wo_ref, cx_ref, cbc_ref, head_ref, pick_ref,
     go_ref, dz_ref, dx_ref, dbc_ref, ddt_ref, mine_ref, other_ref, acc_ref, accbc_ref, acch_ref, accn_ref,
     xbuf, bbuf, dubuf, dubbuf, dhst) = refs
    length = z_ref.shape[0]
    channels = wz_ref.shape[1]
    state = dhst.shape[0]
    width = wo_ref.shape[1]
    step_id = pl.program_id(0)
    first_span = step_id == pl.num_programs(0) - 1

    @pl.when(step_id == 0)
    def _():
        dubuf[length:, :] = jnp.zeros((8, channels), f32)
        dubbuf[length:, :] = jnp.zeros((8, 2 * state), f32)
        dhst[...] = jnp.zeros_like(dhst)
        accn_ref[...] = jnp.zeros_like(accn_ref)
        acc_ref[...] = jnp.zeros_like(acc_ref)
        accbc_ref[...] = jnp.zeros_like(accbc_ref)
        acch_ref[...] = jnp.zeros_like(acch_ref)

    @pl.when(first_span)
    def _():
        xbuf[0:8, :] = jnp.zeros((8, channels), f32)
        bbuf[0:8, :] = jnp.zeros((8, 2 * state), f32)

    @pl.when(jnp.logical_not(first_span))
    def _():
        xbuf[0:8, :] = xhalo_ref[...]
        bbuf[0:8, :] = bchalo_ref[...].astype(f32)[8:16, :]

    xbuf[8:, :] = xp_ref[...]
    bbuf[8:, :] = bc_ref[...].astype(f32)

    if last_layer:
        gg = first_ref[...]
        tok = jnp.transpose(tok_ref[...])
        rms = lax.rsqrt(tok[:, 0:1] / inner_all + EPS)
        coef = rms * rms * rms * tok[:, 1:2] / inner_all
    else:
        gg = dot(first_ref[:, :width], wo_ref[...], COLS)
        tok = first_ref[:, width:].astype(f32)
        rms = tok[:, 0:1] + tok[:, 1:2]
        coef = tok[:, 2:3] + tok[:, 3:4]
    norm_gate = cx_ref[5:6, :]
    skip = cx_ref[6:7, :]
    z = z_ref[...]
    y = y_ref[...]
    sz = sigmoid(z)
    silu_z = z * sz
    gated = y * silu_z
    rg = rms * gg
    gated_rms = gated * rms
    go_ref[...] = (gated_rms * norm_gate).astype(bf16)
    d_gated = rg * norm_gate - gated * coef
    acc_norm = jnp.sum(rg * gated, axis=0, keepdims=True)
    dz_b = (d_gated * y * (sz * (1.0 + z * (1.0 - sz)))).astype(bf16)
    dz_ref[...] = dz_b
    dy = d_gated * silu_z

    pre_x = conv_taps(xbuf, cx_ref[0:4, :], cx_ref[4:5, :], length)
    sx = sigmoid(pre_x)
    xc = pre_x * sx
    pre_bc = conv_taps(bbuf, cbc_ref[0:4, :], cbc_ref[4:5, :], length)
    sbc = sigmoid(pre_bc)
    bcc = (pre_bc * sbc).astype(bf16)
    b_mat = bcc[:, :state]
    c_mat = bcc[:, state:]
    mask, pre_dt, step, rate, cum = span_values(dt_ref[...], head_ref)
    cum_t = jnp.transpose(cum)
    last = cum[length - 1 : length, :]
    scores = dot(c_mat, b_mat, COLS)
    step_all = spread_heads(step, channels, head_dim)
    xs = xc * step_all
    xs_b = xs.astype(bf16)
    tail = spread_heads(jnp.exp(last - cum), channels, head_dim)
    keep = spread_heads(jnp.exp(last), channels, head_dim)

    hin = hin_ref[0]
    hin_b = hin.astype(bf16)
    dh = dhst[...]
    dh_b = dh.astype(bf16)
    dye = dy * spread_heads(jnp.exp(cum), channels, head_dim)
    dye_b = dye.astype(bf16)
    txs = tail * xs
    txs_b = txs.astype(bf16)
    carried = dot(c_mat, hin_b)
    pulled = dot(b_mat, dh_b)
    d_c = dot(dye_b, hin_b, COLS)
    d_b = dot(txs_b, dh_b, COLS)
    dhst[...] = keep * dh + dot(c_mat, dye_b, ROWS)
    into = txs * pulled
    across = dye * carried - into
    at_last = jnp.sum(into, axis=0, keepdims=True) + keep * jnp.sum(hin * dh, axis=0, keepdims=True)

    dy_b = dy.astype(bf16)
    dy_t = jnp.transpose(dy).astype(bf16)
    lane = lax.broadcasted_iota(jnp.int32, (length, LANES), 1)
    per_tile = LANES // head_dim
    d_scores = jnp.zeros((length, length), f32)
    row_sums = jnp.zeros((length, LANES), f32)
    col_sums = []
    dxs_parts = []
    for head in range(channels // head_dim):
        tile, sub = divmod(head, per_tile)
        dy_tile = dy_b[:, tile * LANES : (tile + 1) * LANES]
        own = (lane >= sub * head_dim) & (lane < (sub + 1) * head_dim)
        dy_head = jnp.where(own, dy_tile, jnp.zeros_like(dy_tile))
        d_m = dot(dy_head, xs_b[:, tile * LANES : (tile + 1) * LANES], COLS)
        decay = decay_matrix(mask, cum[:, head : head + 1], cum_t[head : head + 1, :])
        dxs_parts.append(
            dot(dy_t[head * head_dim : (head + 1) * head_dim, :], (scores * decay).astype(bf16))
        )
        d_m = d_m * decay
        d_scores = d_scores + d_m
        pairs = d_m * scores
        row_sums = jnp.where(lane == head, jnp.sum(pairs, axis=1, keepdims=True), row_sums)
        col_sums.append(jnp.sum(pairs, axis=0, keepdims=True))
    heads = len(col_sums)
    col_sums = jnp.concatenate(col_sums + [jnp.zeros((LANES - heads, length), f32)], axis=0)
    dxs = jnp.transpose(jnp.concatenate(dxs_parts, axis=0)) + tail * pulled
    pick = pick_ref[...]
    d_cum = row_sums - jnp.transpose(col_sums) + dot(across, pick, PLAIN, highest)
    at_last = dot(jnp.broadcast_to(at_last, (8, channels)), pick, PLAIN, highest)[0:1, :]
    d_rate = dot(mask.astype(f32), d_cum, ROWS, highest) + at_last
    d_step = d_rate * head_ref[1:2, :] + dot(dxs * xc, pick, PLAIN, highest)
    d_dt = d_step * sigmoid(pre_dt)
    acch_ref[0:1, :] += jnp.sum(d_dt, axis=0, keepdims=True)
    acch_ref[1:2, :] += jnp.sum(d_rate * rate, axis=0, keepdims=True)
    dt_b = d_dt.astype(bf16)
    ddt_ref[...] = dt_b
    ds_b = d_scores.astype(bf16)
    d_c = d_c + dot(ds_b, b_mat)
    d_b = d_b + dot(ds_b, c_mat, ROWS)
    d_xc = dxs * step_all + skip * dy
    acc_skip = jnp.sum(dy * xc, axis=0, keepdims=True)

    d_u = d_xc * (sx * (1.0 + pre_x * (1.0 - sx)))
    d_ub = jnp.concatenate([d_b, d_c], axis=1) * (sbc * (1.0 + pre_bc * (1.0 - sbc)))
    dubuf[0:length, :] = d_u
    dubbuf[0:length, :] = d_ub
    d_x = jnp.zeros_like(d_u)
    d_bc = jnp.zeros_like(d_ub)
    acc_rows = []
    accbc_rows = []
    for j in range(4):
        d_x = d_x + cx_ref[j : j + 1, :] * dubuf[pl.ds(3 - j, length), :]
        d_bc = d_bc + cbc_ref[j : j + 1, :] * dubbuf[pl.ds(3 - j, length), :]
        acc_rows.append(jnp.sum(d_u * xbuf[pl.ds(5 + j, length), :], axis=0, keepdims=True))
        accbc_rows.append(jnp.sum(d_ub * bbuf[pl.ds(5 + j, length), :], axis=0, keepdims=True))
    dubuf[length:, :] = d_u[0:8, :]
    dubbuf[length:, :] = d_ub[0:8, :]
    zero = jnp.zeros((1, channels), f32)
    acc_ref[...] += jnp.concatenate(
        acc_rows + [jnp.sum(d_u, axis=0, keepdims=True), acc_norm, acc_skip, zero], axis=0
    )
    zero = jnp.zeros((3, d_ub.shape[1]), f32)
    accbc_ref[...] += jnp.concatenate(
        accbc_rows + [jnp.sum(d_ub, axis=0, keepdims=True), zero], axis=0
    )
    dx_b = d_x.astype(bf16)
    dbc_b = d_bc.astype(bf16)
    dx_ref[...] = dx_b
    dbc_ref[...] = jnp.transpose(d_bc).astype(bf16)
    total = dot(dz_b, wz_ref[...], COLS) + dot(dx_b, wx_ref[...], COLS)
    total = total + dot(dbc_b, wbc_ref[...]) + dot(dt_b, wdt_ref[...])
    accn_ref[0:1, :] += jnp.sum(total * xn_ref[...].astype(f32), axis=0, keepdims=True)
    put_half(
        place_ref,
        pl.num_programs(0) - 1 - step_id,
        pl.num_programs(0) // 2,
        mine_ref,
        other_ref,
        total.astype(bf16),
    )


def whole(shape):
    zeros = (0,) * len(shape)
    return pl.BlockSpec(shape, lambda i, p: zeros)


def span_rows(columns):
    return pl.BlockSpec((SPAN, columns), lambda i, p: (i, 0))


def half_rows(columns, spans, reverse):
    half = spans // 2

    def block(i, core):
        span = spans - 1 - i if reverse else i
        return jnp.clip(span - half * core, 0, half - 1), 0

    return [
        pl.BlockSpec((SPAN, columns), lambda i, p: block(i, p[0])),
        pl.BlockSpec((SPAN, columns), lambda i, p: block(i, 1 - p[0])),
    ]


def span_call(kernel, name, spans, place, operands, in_specs, shapes, out_specs, scratch):
    return pl.pallas_call(
        kernel,
        grid_spec=pltpu.PrefetchScalarGridSpec(
            num_scalar_prefetch=1,
            grid=(spans,),
            in_specs=in_specs,
            out_specs=out_specs,
            scratch_shapes=scratch,
        ),
        out_shape=shapes,
        compiler_params=pltpu.CompilerParams(
            dimension_semantics=("arbitrary",), vmem_limit_bytes=VMEM_BYTES
        ),
        name=name,
    )(place, *operands)


def run_forward(place, xn, weights, small, state, head_dim, grad_rows=None):
    tokens, width = xn.shape
    channels = weights[0].shape[1]
    spans = tokens // SPAN
    last_layer = grad_rows is not None
    operands = [xn, *weights, *small]
    in_specs = [span_rows(width)] + [whole(v.shape) for v in operands[1:]]
    shapes = [
        jax.ShapeDtypeStruct((tokens, channels), f32),
        jax.ShapeDtypeStruct((tokens, channels), f32),
        jax.ShapeDtypeStruct((tokens, 2 * state), bf16),
        jax.ShapeDtypeStruct((tokens, LANES), f32),
        jax.ShapeDtypeStruct((tokens, channels), f32),
        jax.ShapeDtypeStruct((spans, state, channels), f32),
        jax.ShapeDtypeStruct((tokens // 2, width + LANES), bf16),
        jax.ShapeDtypeStruct((tokens // 2, width + LANES), bf16),
    ]
    out_specs = [span_rows(s.shape[1]) for s in shapes[:5]]
    out_specs.append(pl.BlockSpec((1, state, channels), lambda i, p: (i, 0, 0)))
    out_specs += half_rows(width + LANES, spans, False)
    if last_layer:
        operands.append(grad_rows)
        in_specs.append(span_rows(width))
        shapes += [
            jax.ShapeDtypeStruct((8, tokens), f32),
            jax.ShapeDtypeStruct((tokens, channels), f32),
        ]
        out_specs += [pl.BlockSpec((8, SPAN), lambda i, p: (0, i)), span_rows(channels)]
    scratch = [
        pltpu.VMEM((SPAN + 8, channels), f32),
        pltpu.VMEM((SPAN + 8, 2 * state), f32),
        pltpu.VMEM((state, channels), f32),
    ]
    kernel = functools.partial(forward_kernel, last_layer, head_dim)
    return span_call(
        kernel, "layer_forward", spans, place, operands, in_specs, shapes, out_specs, scratch
    )


def run_backward(place, first, sums, xn, kept, weights, small, pick, head_dim, inner_all):
    z, xp, bc, dt, y, hin = kept
    tokens, channels = z.shape
    state = hin.shape[1]
    width = weights[4].shape[1]
    spans = tokens // SPAN
    last_layer = sums is not None
    if sums is None:
        sums = jnp.zeros((8, tokens), f32)

    def rev(columns):
        return pl.BlockSpec((SPAN, columns), lambda i, p: (spans - 1 - i, 0))

    def rev_cols(rows):
        return pl.BlockSpec((rows, SPAN), lambda i, p: (0, spans - 1 - i))

    def halo(columns, rows):
        per = SPAN // rows
        return pl.BlockSpec(
            (rows, columns), lambda i, p: (jnp.maximum((spans - 1 - i) * per - 1, 0), 0)
        )

    operands = [first, xn, sums, z, xp, xp, bc, bc, dt, y, hin, *weights, *small, pick]
    in_specs = [
        rev(first.shape[1]),
        rev(width),
        rev_cols(8),
        rev(channels),
        rev(channels),
        halo(channels, 8),
        rev(2 * state),
        halo(2 * state, 16),
        rev(LANES),
        rev(channels),
        pl.BlockSpec((1, state, channels), lambda i, p: (spans - 1 - i, 0, 0)),
    ]
    in_specs += [whole(v.shape) for v in operands[len(in_specs) :]]
    shapes = [
        jax.ShapeDtypeStruct((tokens, channels), bf16),
        jax.ShapeDtypeStruct((tokens, channels), bf16),
        jax.ShapeDtypeStruct((tokens, channels), bf16),
        jax.ShapeDtypeStruct((2 * state, tokens), bf16),
        jax.ShapeDtypeStruct((tokens, LANES), bf16),
        jax.ShapeDtypeStruct((tokens // 2, width), bf16),
        jax.ShapeDtypeStruct((tokens // 2, width), bf16),
        jax.ShapeDtypeStruct((8, channels), f32),
        jax.ShapeDtypeStruct((8, 2 * state), f32),
        jax.ShapeDtypeStruct((8, LANES), f32),
        jax.ShapeDtypeStruct((8, width), f32),
    ]
    out_specs = [rev(channels), rev(channels), rev(channels), rev_cols(2 * state), rev(LANES)]
    out_specs += half_rows(width, spans, True)
    out_specs += [whole(s.shape) for s in shapes[7:]]
    scratch = [
        pltpu.VMEM((SPAN + 8, channels), f32),
        pltpu.VMEM((SPAN + 8, 2 * state), f32),
        pltpu.VMEM((SPAN + 8, channels), f32),
        pltpu.VMEM((SPAN + 8, 2 * state), f32),
        pltpu.VMEM((state, channels), f32),
    ]
    kernel = functools.partial(backward_kernel, last_layer, head_dim, inner_all)
    return span_call(
        kernel, "layer_backward", spans, place, operands, in_specs, shapes, out_specs, scratch
    )


SIZES = (4, 2, 2, 2, 4)
NX, NYL, NC, NYH, NZ = SIZES
EVERY = [
    (x, yl, c, yh, z)
    for x in range(NX)
    for yl in range(NYL)
    for c in range(NC)
    for yh in range(NYH)
    for z in range(NZ)
]


def linear(x, yl, c, yh, z):
    return ((((x % NX) * NYL + yl % NYL) * NC + c % NC) * NYH + yh % NYH) * NZ + z % NZ


def send(v, step, only=None):
    pairs = [(linear(*d), linear(*step(*d))) for d in EVERY if only is None or only(*d)]
    return lax.ppermute(v, ("dp", "tensor"), pairs)


def send_z(v, k):
    return send(v, lambda x, yl, c, yh, z: (x, yl, c, yh, z + k))


def send_core(v):
    return send(v, lambda x, yl, c, yh, z: (x, yl, c + 1, yh, z))


def trade(v, k=0):
    return send(v, lambda x, yl, c, yh, z: (x, yl, yh, c, z + k))


def position():
    dp, tensor = lax.axis_index("dp"), lax.axis_index("tensor")
    return dp // (NYL * NC), dp // NC % NYL, dp % NC, tensor // NZ, tensor % NZ


def assemble_kernel(plan, n_pieces, n_out, place_ref, *refs):
    pieces, outs = refs[:n_pieces], refs[n_pieces : n_pieces + n_out]
    core, z = place_ref[0], place_ref[1]
    for piece, other, dz, start, out, per, offset, rows in plan:
        member = (1 - core if other else core) * NZ + lax.rem(z + dz, NZ)
        row = pl.multiple_of(member * per + offset, 16)
        outs[out][pl.ds(row, rows), :] = pieces[piece][start : start + rows, :]


def gather(place, v, parts):
    rows, columns = v.shape
    half = rows // 2
    from_left = send_z(v, 1)
    from_right = send_z(v, -1)
    low = send_z(from_left[:half], 1)
    high = send_z(from_right[half:], -1)
    pieces, plan = [], []
    for piece, dz, first in (
        (v, 0, 0),
        (from_left, NZ - 1, 0),
        (from_right, 1, 0),
        (low, 2, 0),
        (high, 2, half),
    ):
        for other, held in ((False, piece), (True, send_core(piece))):
            base = 0
            for out, per in enumerate(parts):
                begin, end = max(first, base), min(first + held.shape[0], base + per)
                if begin < end:
                    plan.append(
                        (len(pieces), other, dz, begin - first, out, per, begin - base, end - begin)
                    )
                base += per
            pieces.append(held)
    shapes = [jax.ShapeDtypeStruct((NC * NZ * per, columns), v.dtype) for per in parts]
    return pl.pallas_call(
        functools.partial(assemble_kernel, plan, len(pieces), len(parts)),
        grid_spec=pltpu.PrefetchScalarGridSpec(
            num_scalar_prefetch=1,
            grid=(1,),
            in_specs=[whole(p.shape) for p in pieces],
            out_specs=[whole(s.shape) for s in shapes],
        ),
        out_shape=shapes,
        compiler_params=pltpu.CompilerParams(vmem_limit_bytes=VMEM_BYTES),
        name="assemble",
    )(place, *pieces)


def fold_kernel(place_ref, mine_ref, other_ref, *out_refs):
    rows = out_refs[0].shape[0]
    for k, out_ref in enumerate(out_refs):
        at = pl.ds(pl.multiple_of(lax.rem(place_ref[1] + k, NZ) * rows, 16), rows)
        out_ref[...] = (mine_ref[at, :].astype(f32) + other_ref[at, :].astype(f32)).astype(
            out_ref.dtype
        )


def fold(place, mine, other, own_type):
    rows, columns = mine.shape[0] // NZ, mine.shape[1]
    whole_in = pl.BlockSpec(mine.shape, lambda i, p: (0, 0))
    whole_out = pl.BlockSpec((rows, columns), lambda i, p: (0, 0))
    return pl.pallas_call(
        fold_kernel,
        grid_spec=pltpu.PrefetchScalarGridSpec(
            num_scalar_prefetch=1,
            grid=(1,),
            in_specs=[whole_in] * 2,
            out_specs=[whole_out] * NZ,
        ),
        out_shape=[
            jax.ShapeDtypeStruct((rows, columns), own_type if k == 0 else bf16) for k in range(NZ)
        ],
        compiler_params=pltpu.CompilerParams(vmem_limit_bytes=VMEM_BYTES),
        name="fold",
    )(place, mine, other)


def scatter(place, mine, other):
    own, one, two, three = fold(place, mine, send_core(other), f32)
    return own, send_z(one, 1), send_z(two, 2), send_z(three, 3)


def scatter_home(place, mine, other):
    blocks = fold(place, mine, send_core(other), bf16)
    return tuple(trade(block, k) for k, block in enumerate(blocks))


def scatter_rows(v):
    _, _, core, _, z = position()
    cut = v.reshape((NC, NZ, v.shape[0] // (NC * NZ)) + v.shape[1:])
    mine = lax.dynamic_index_in_dim(cut, core, 0, False).astype(f32)
    other = lax.dynamic_index_in_dim(cut, 1 - core, 0, False)
    both = mine + send_core(other).astype(f32)
    total = lax.dynamic_index_in_dim(both, z, 0, False)
    both = both.astype(bf16)
    for k in range(1, NZ):
        block = lax.dynamic_index_in_dim(both, (z + k) % NZ, 0, False)
        total = total + send_z(block, k).astype(f32)
    return total


def sum_members(v):
    both = v + send_core(v)
    total = both
    for k in range(1, NZ):
        total = total + send_z(both, k)
    return total


def reduce_front(v):
    _, _, core, yh, _ = position()
    half = v.shape[0] // 2
    low, high = v[:half], v[half:]

    def away(x, yl, c, yh, z):
        return c != yh

    def home(x, yl, c, yh, z):
        return c == yh

    low_far = send(low, lambda x, yl, c, yh, z: (x, yl, c, yh + 1, z), away)
    high_far = send(high, lambda x, yl, c, yh, z: (x, yl, c + 1, yh + 1, z), away)
    high_near = send(high, lambda x, yl, c, yh, z: (x, yl, c + 1, yh, z), home)
    stays = core == yh
    near = jnp.where(stays, low, high_near).astype(f32)
    far = jnp.where(stays, low_far, high_far).astype(f32)
    return (near + far).astype(bf16)


def reduce_back(half):
    _, _, core, yh, _ = position()
    other = send_core(half)
    stays = core == yh
    return jnp.concatenate([jnp.where(stays, half, other), jnp.where(stays, other, half)], axis=0)


def sum_chips(v):
    x, yl, _, _, _ = position()
    cut = v.reshape((NX, v.shape[0] // NX) + v.shape[1:])
    total = lax.dynamic_index_in_dim(cut, x, 0, False).astype(f32)
    for k in range(1, NX):
        block = lax.dynamic_index_in_dim(cut, (x + k) % NX, 0, False)
        total = total + send(block, lambda x, yl, c, yh, z, k=k: (x + k, yl, c, yh, z)).astype(f32)

    def beside(v):
        return send(v, lambda x, yl, c, yh, z: (x, yl + 1, c, yh, z))

    total = total.astype(bf16)
    total = (total.astype(f32) + beside(total).astype(f32)).astype(bf16)
    out = jnp.zeros(cut.shape, bf16)
    out = lax.dynamic_update_index_in_dim(out, total, x, 0)
    for k in range(1, NX):
        block = send(total, lambda x, yl, c, yh, z, k=k: (x + k, yl, c, yh, z))
        out = lax.dynamic_update_index_in_dim(out, block, (x - k) % NX, 0)
    return out.reshape(v.shape)


def sum_chips_beside(v):
    groups = [[2 * k + c for k in range(NX * NYL)] for c in range(NC)]
    return lax.psum(v, "dp", axis_index_groups=groups)


def row_call(kernel, name, operands, shapes):
    return pl.pallas_call(
        kernel,
        grid=(1,),
        in_specs=[pl.BlockSpec((rows, v.shape[1]), lambda i: (0, 0)) for v, rows in operands],
        out_specs=[pl.BlockSpec(s.shape, lambda i: (0, 0)) for s in shapes],
        out_shape=shapes,
        compiler_params=pltpu.CompilerParams(vmem_limit_bytes=VMEM_BYTES),
        name=name,
    )(*[v for v, _ in operands])


def inverse_rms(v):
    return lax.rsqrt(jnp.mean(v * v, axis=-1, keepdims=True) + EPS)


def first_kernel(packed_ref, gain_ref, out_ref):
    rows = 128
    v = packed_ref[0:rows, :].astype(f32)
    out_ref[0:rows, :] = (v * inverse_rms(v) * gain_ref[...]).astype(bf16)
    out_ref[rows:, :] = packed_ref[rows : out_ref.shape[0], :]


def add_terms(own_ref, a_ref, b_ref, c_ref):
    total = own_ref[...].astype(f32) + a_ref[...].astype(f32)
    return total + (b_ref[...].astype(f32) + c_ref[...].astype(f32))


def unscaled_output(inner_all, terms, width):
    total = add_terms(*terms)
    squares = total[:, width : width + 1] + total[:, width + 1 : width + 2]
    gate_rms = lax.rsqrt(squares / inner_all + EPS)
    return gate_rms, total[:, :width] * gate_rms


def middle_kernel(inner_all, own_ref, a_ref, b_ref, c_ref, res_ref, gain_ref, res1_ref, mixed_ref, rms_ref, normed_ref):
    width = res_ref.shape[1]
    gate_rms, mixed = unscaled_output(inner_all, (own_ref, a_ref, b_ref, c_ref), width)
    res = res_ref[...].astype(f32) + mixed
    res1_ref[...] = res
    mixed_ref[...] = mixed
    rms_ref[...] = jnp.broadcast_to(gate_rms, rms_ref.shape)
    normed_ref[...] = (res * inverse_rms(res) * gain_ref[...]).astype(bf16)


def last_kernel(inner_all, own_ref, a_ref, b_ref, c_ref, res_ref, out_ref):
    _, mixed = unscaled_output(inner_all, (own_ref, a_ref, b_ref, c_ref), res_ref.shape[1])
    out_ref[...] = res_ref[...] + mixed


def input_gradient(grad_normed, res, d_res, gain):
    inv = inverse_rms(res)
    scaled = grad_normed * gain
    dots = jnp.sum(scaled * res, axis=-1, keepdims=True) / res.shape[1]
    return d_res + inv * scaled - res * (inv * inv * inv) * dots


def between_kernel(inner_all, own_ref, a_ref, b_ref, c_ref, res_ref, dres_ref, gain_ref, mixed_ref, rms_ref, out_ref, sent_ref):
    width = res_ref.shape[1]
    grad_normed = add_terms(own_ref, a_ref, b_ref, c_ref)
    d_res = input_gradient(grad_normed, res_ref[...], dres_ref[...].astype(f32), gain_ref[...])
    out_ref[...] = d_res
    g_mixed = d_res.astype(bf16)
    sent_ref[:, :width] = g_mixed
    gate_rms = rms_ref[:, 0:1]
    products = jnp.sum(g_mixed.astype(f32) * mixed_ref[...], axis=-1, keepdims=True)
    coef = gate_rms * gate_rms * products / inner_all
    lane = lax.broadcasted_iota(jnp.int32, rms_ref.shape, 1)
    rms_high = gate_rms.astype(bf16).astype(f32)
    coef_high = coef.astype(bf16).astype(f32)
    extra = jnp.where(lane == 0, rms_high, jnp.where(lane == 1, gate_rms - rms_high, 0.0))
    extra = jnp.where(lane == 2, coef_high, jnp.where(lane == 3, coef - coef_high, extra))
    sent_ref[:, width:] = extra.astype(bf16)


def end_kernel(own_ref, a_ref, b_ref, c_ref, res_ref, dres_ref, gain_ref, out_ref):
    grad_normed = add_terms(own_ref, a_ref, b_ref, c_ref)
    out_ref[...] = input_gradient(
        grad_normed, res_ref[...].astype(f32), dres_ref[...], gain_ref[...]
    )


def after(v, *others):
    return lax.optimization_barrier((v, *others))[0]


def pad_to(v, rows, lanes):
    return jnp.pad(v, ((0, rows - v.shape[0]), (0, lanes - v.shape[1])))


def local(
    hidden_in,
    grad_out,
    norm_in,
    w_z,
    w_x,
    w_bc,
    w_dt,
    conv_x,
    conv_x_bias,
    conv_bc,
    conv_bc_bias,
    dt_bias,
    a_log,
    skip,
    norm_gate,
    w_out,
):
    layers, width, channels = w_z.shape
    heads = w_dt.shape[2]
    head_dim = channels // heads
    both = conv_bc.shape[2]
    state = both // 2
    members = NC * NZ
    inner_all = channels * members
    rows = hidden_in.shape[1]
    bc_rows = both // members
    _, _, core, _, z = position()
    place = jnp.stack([core, z]).astype(jnp.int32)

    bc_t = jnp.swapaxes(w_bc, 1, 2)
    dt_t = jnp.pad(jnp.swapaxes(w_dt, 1, 2), ((0, 0), (0, 8 - heads), (0, 0)))
    packed = jnp.concatenate([hidden_in[0], bc_t[0], dt_t.reshape(layers * 8, width)], axis=0)
    packed = trade(packed)
    per_channel = jnp.concatenate(
        [conv_x, conv_x_bias[:, None], norm_gate[:, None], jnp.repeat(skip, head_dim, axis=1)[:, None]],
        axis=1,
    )
    per_channel = jnp.pad(per_channel, ((0, 0), (0, 1), (0, 0)))
    per_head = jnp.stack([dt_bias, -jnp.exp(a_log)], axis=1)
    per_head = jnp.pad(per_head, ((0, 0), (0, 6), (0, LANES - heads)))
    little = jnp.concatenate([per_channel, per_head], axis=2).reshape(layers * 8, channels + LANES)
    little = trade(little).reshape(layers, 8, channels + LANES)
    wz0 = trade(after(w_z[0], packed))
    wx0 = trade(after(w_x[0], packed))
    grads = trade(after(jnp.concatenate([grad_out[0], bc_t[1]], axis=0), wz0, wx0))
    wo0 = trade(after(w_out[0], wz0, wx0))
    wz1 = trade(after(w_z[1], wo0))
    wx1 = trade(after(w_x[1], wo0))
    wo1 = trade(after(w_out[1], wz1, wx1))

    [sent] = row_call(
        first_kernel,
        "first_norm",
        [(packed, packed.shape[0]), (norm_in[0:1], 1)],
        [jax.ShapeDtypeStruct((rows + bc_rows, width), bf16)],
    )
    xn0, wbc0 = gather(place, sent, (rows, bc_rows))
    wdt = [pad_to(packed[rows + bc_rows + 8 * l : rows + bc_rows + 8 * (l + 1)], LANES, width) for l in range(layers)]
    smalls = []
    for layer in range(layers):
        cbc = jnp.concatenate([conv_bc[layer], conv_bc_bias[layer][None], jnp.zeros((3, both), f32)], axis=0)
        smalls.append((little[layer, :, :channels], cbc, little[layer, :, channels:]))
    channel_head = jnp.arange(channels) // head_dim
    pick = (channel_head[:, None] == jnp.arange(LANES)[None, :]).astype(f32)
    weights0 = (wz0, wx0, wbc0, wdt[0], wo0)

    out0 = run_forward(place, xn0, weights0, smalls[0], state, head_dim)
    grad_rows1, wbc1 = gather(place, grads, (rows, bc_rows))
    weights1 = (wz1, wx1, wbc1, wdt[1], wo1)
    terms = scatter(place, out0[6], out0[7])
    full = jax.ShapeDtypeStruct((rows, width), f32)
    res1, mixed0, rms0, normed1 = row_call(
        functools.partial(middle_kernel, inner_all),
        "middle_norm",
        [(v, rows) for v in terms] + [(packed, rows), (norm_in[1:2], 1)],
        [full, full, jax.ShapeDtypeStruct((rows, LANES), f32), jax.ShapeDtypeStruct((rows, width), bf16)],
    )
    [xn1] = gather(place, normed1, (rows,))
    out1 = run_forward(place, xn1, weights1, smalls[1], state, head_dim, grad_rows1)
    sums = sum_members(out1[8])

    back1 = run_backward(
        place, out1[9], sums, xn1, out1[:6], weights1, smalls[1], pick, head_dim, inner_all
    )
    terms = scatter(place, back1[5], back1[6])
    d_res1, sent = row_call(
        functools.partial(between_kernel, inner_all),
        "between_layers",
        [(v, rows) for v in terms]
        + [(res1, rows), (grads, rows), (norm_in[1:2], 1), (mixed0, rows), (rms0, rows)],
        [full, jax.ShapeDtypeStruct((rows, width + LANES), bf16)],
    )
    [first0] = gather(place, sent, (rows,))

    terms = scatter(place, out1[6], out1[7])
    [hidden_out] = row_call(
        functools.partial(last_kernel, inner_all),
        "last_output",
        [(v, rows) for v in terms] + [(res1, rows)],
        [full],
    )
    hidden_out = trade(hidden_out)

    def weight_grads(back, xn, grad_rows):
        gate_out, dz, dx, dbc, ddt = back[:5]
        wide = jnp.concatenate([dot(xn, dz, ROWS).astype(bf16), dot(xn, dx, ROWS).astype(bf16)], axis=0)
        bc_sum = scatter_rows(dbc).astype(bf16)
        narrow = jnp.concatenate([dot(bc_sum, xn), dot(ddt, xn, ROWS)[:8]], axis=0)
        return wide, narrow, dot(gate_out, grad_rows, ROWS).astype(bf16)

    wide1, narrow1, tall1 = weight_grads(back1, xn1, grad_rows1)
    wide1 = reduce_front(wide1)
    tall1 = reduce_front(tall1)
    wide1, tall1 = sum_chips_beside((wide1, tall1))
    wide1, tall1 = reduce_back(wide1), reduce_back(tall1)

    d_res1 = trade(d_res1)
    back0 = run_backward(
        place, first0, None, xn0, out0[:6], weights0, smalls[0], pick, head_dim, inner_all
    )
    terms = scatter_home(place, back0[5], back0[6])
    [grad_in] = row_call(
        end_kernel,
        "input_gradient",
        [(v, rows) for v in terms] + [(hidden_in[0], rows), (d_res1, rows), (norm_in[0:1], 1)],
        [full],
    )
    wide0, narrow0, tall0 = weight_grads(back0, xn0, first0[:, :width])
    wide0 = reduce_back(sum_chips(reduce_front(wide0)))
    tall0 = reduce_back(sum_chips(reduce_front(tall0)))

    shared = jnp.concatenate(
        [back0[10][0:1], back1[10][0:1]]
        + [pad_to(v[8][0:5].reshape(1, 5 * both), 1, width) for v in (back0, back1)],
        axis=0,
    )
    shared = sum_members(shared)
    per_shard = [back0[7].reshape(-1, width), back1[7].reshape(-1, width)]
    per_shard += [pad_to(v[9][0:2].reshape(1, 2 * LANES), 1, width) for v in (back0, back1)]
    misc = jnp.concatenate([narrow0, narrow1, shared] + per_shard, axis=0)
    misc_rows = misc.shape[0]
    misc = pad_to(misc, 128, width).astype(bf16)
    misc = reduce_back(sum_chips(reduce_front(misc))).astype(f32)[:misc_rows]

    at = 0
    parts = []
    for count in (bc_rows, 8, bc_rows, 8, 1, 1, 1, 1, 2, 2, 1, 1):
        parts.append(misc[at : at + count])
        at += count
    g_wbc = jnp.stack([parts[0].T, parts[2].T])
    g_wdt = jnp.stack([parts[1][:heads].T, parts[3][:heads].T])
    g_norm_in = jnp.concatenate([parts[4], parts[5]], axis=0) / norm_in
    g_bc = jnp.concatenate([parts[6], parts[7]], axis=0)[:, : 5 * both].reshape(layers, 5, both)
    g_x = jnp.stack([parts[8].reshape(8, channels), parts[9].reshape(8, channels)])
    g_head = jnp.concatenate([parts[10], parts[11]], axis=0)[:, : 2 * LANES].reshape(layers, 2, LANES)[:, :, :heads]
    wide = jnp.stack([wide0, wide1]).astype(f32)
    return (
        hidden_out[None],
        grad_in[None],
        g_norm_in,
        wide[:, :width],
        wide[:, width:],
        g_wbc,
        g_wdt,
        g_x[:, 0:4],
        g_x[:, 4],
        g_bc[:, 0:4],
        g_bc[:, 4],
        g_head[:, 0],
        g_head[:, 1],
        jnp.sum(g_x[:, 6].reshape(layers, heads, head_dim), axis=2),
        g_x[:, 5],
        jnp.stack([tall0, tall1]).astype(f32),
    )


def solution(mesh):
    specs_in = (
        P("dp", "tensor", None),
        P("dp", "tensor", None),
        P(),
        P(None, None, "tensor"),
        P(None, None, "tensor"),
        P(None, None, "tensor"),
        P(None, None, "tensor"),
        P(None, None, "tensor"),
        P(None, "tensor"),
        P(),
        P(),
        P(None, "tensor"),
        P(None, "tensor"),
        P(None, "tensor"),
        P(None, "tensor"),
        P(None, "tensor", None),
    )
    specs_out = (
        P("dp", "tensor", None),
        P("dp", "tensor", None),
        P(),
        P(None, None, "tensor"),
        P(None, None, "tensor"),
        P(None, None, "tensor"),
        P(None, None, "tensor"),
        P(None, None, "tensor"),
        P(None, "tensor"),
        P(),
        P(),
        P(None, "tensor"),
        P(None, "tensor"),
        P(None, "tensor"),
        P(None, "tensor"),
        P(None, "tensor", None),
    )
    return jax.shard_map(
        local, mesh=mesh, in_specs=specs_in, out_specs=specs_out, check_vma=False
    )
```

```python
import functools

import jax
import jax.numpy as jnp
from jax import lax
from jax.experimental import pallas as pl
from jax.experimental.pallas import tpu as pltpu
from jax.sharding import PartitionSpec as P

SPAN = 256
EPS = 1e-05
LANES = 128
VMEM_BYTES = 56 * 1024 * 1024

f32 = jnp.float32
bf16 = jnp.bfloat16
highest = lax.Precision.HIGHEST

ROWS = ((0,), (0,))
COLS = ((1,), (1,))
PLAIN = ((1,), (0,))


def dot(left, right, dims=PLAIN, precision=None):
    return lax.dot_general(
        left, right, (dims, ((), ())), preferred_element_type=f32, precision=precision
    )


def sigmoid(v):
    return 1.0 / (1.0 + jnp.exp(-v))


def softplus(v):
    return jnp.maximum(v, 0.0) + jnp.log1p(jnp.exp(-jnp.abs(v)))


def spread_heads(per_head, channels, head_dim):
    rows = per_head.shape[0]
    per_tile = LANES // head_dim
    lane = lax.broadcasted_iota(jnp.int32, (rows, LANES), 1)
    tiles = []
    for tile in range(channels // LANES):
        out = jnp.broadcast_to(
            per_head[:, tile * per_tile : tile * per_tile + 1], (rows, LANES)
        )
        for sub in range(1, per_tile):
            head = tile * per_tile + sub
            out = jnp.where(
                lane >= sub * head_dim,
                jnp.broadcast_to(per_head[:, head : head + 1], (rows, LANES)),
                out,
            )
        tiles.append(out)
    return jnp.concatenate(tiles, axis=1)


def conv_taps(buf, taps, offset, width):
    out = offset
    for j in range(4):
        out = out + taps[j : j + 1] * buf[pl.ds(5 + j, width), :]
    return out


def decay_matrix(mask, cum_col, cum_row):
    return jnp.exp(jnp.where(mask, cum_col - cum_row, -1e30))


def span_values(dt, head_ref):
    length = dt.shape[0]
    rows = lax.broadcasted_iota(jnp.int32, (length, length), 0)
    cols = lax.broadcasted_iota(jnp.int32, (length, length), 1)
    mask = rows >= cols
    pre = dt + head_ref[0:1, :]
    step = softplus(pre)
    rate = head_ref[1:2, :] * step
    cum = dot(mask.astype(f32), rate, PLAIN, highest)
    return mask, pre, step, rate, cum


def put_half(place_ref, span, half, mine_ref, other_ref, value):
    own = span // half == place_ref[0]

    @pl.when(own)
    def _():
        mine_ref[...] = value

    @pl.when(jnp.logical_not(own))
    def _():
        other_ref[...] = value


def place_pieces(plan, place_ref, pieces, outs):
    core, z = place_ref[0], place_ref[1]
    for piece, other, dz, start, out, per, offset, rows in plan:
        member = (1 - core if other else core) * NZ + lax.rem(z + dz, NZ)
        row = pl.multiple_of(member * per + offset, 16)
        outs[out][pl.ds(row, rows), :] = pieces[piece][start : start + rows, :]


def cut_weights(w_ref, width):
    channels = w_ref.shape[1]
    parts = [w_ref.at[0:width, :], w_ref.at[width : 2 * width, :]]
    return parts + cut_out(w_ref.at[2 * width : 3 * width, :])


def cut_out(wo_ref):
    rows, channels = wo_ref.shape
    return [wo_ref.at[i * channels : (i + 1) * channels, :] for i in range(rows // channels)]


def times_out(v, wo_refs):
    return jnp.concatenate([dot(v, wo_ref[...]) for wo_ref in wo_refs], axis=1)


def times_out_t(v, wo_refs):
    channels = wo_refs[0].shape[1]
    return sum(
        dot(v[:, i * channels : (i + 1) * channels], wo_ref[...], COLS)
        for i, wo_ref in enumerate(wo_refs)
    )


def put_columns(place_ref, span, mine_ref, other_ref, columns):
    per = columns.shape[0] // (NC * NZ)
    rows = mine_ref.shape[0] // NZ

    def place_columns(core, ref):
        for z in range(NZ):
            at = (core * NZ + z) * per
            ref[pl.ds(pl.multiple_of(z * rows + span * per, 16), per), :] = columns[at : at + per, :]

    for core in range(NC):
        mine = place_ref[0] == core

        @pl.when(mine)
        def _(core=core):
            place_columns(core, mine_ref)

        @pl.when(jnp.logical_not(mine))
        def _(core=core):
            place_columns(core, other_ref)


def forward_kernel(plans, head_dim, place_ref, *refs):
    last_layer = len(plans) == 2
    refs = list(refs)

    def take(count):
        taken = refs[:count]
        del refs[:count]
        return taken

    piece_refs = [take(count) for _, count in plans]
    w_ref, wdt_ref, cx_ref, cbc_ref, head_ref = take(5)
    xn_ref, wbc_ref, z_ref, xp_ref, bc_ref, dt_ref, y_ref, hin_ref, mine_ref, other_ref = take(10)
    if last_layer:
        g_ref, sums_ref, gg_ref = take(3)
    xn_all, xbuf, bbuf, hst = take(4)
    if last_layer:
        [g_all] = take(1)
    length = z_ref.shape[0]
    channels = w_ref.shape[1]
    state = hst.shape[0]
    span = pl.program_id(0)
    wz_ref, wx_ref, *wo_refs = cut_weights(w_ref, xn_ref.shape[1])

    @pl.when(span == 0)
    def _():
        if last_layer:
            place_pieces(plans[0][0], place_ref, piece_refs[0], [xn_all])
            place_pieces(plans[1][0], place_ref, piece_refs[1], [g_all, wbc_ref])
        else:
            place_pieces(plans[0][0], place_ref, piece_refs[0], [xn_all, wbc_ref])
        xbuf[0:8, :] = jnp.zeros((8, channels), f32)
        bbuf[0:8, :] = jnp.zeros((8, 2 * state), f32)
        hst[...] = jnp.zeros_like(hst)

    here = pl.ds(pl.multiple_of(span * length, length), length)
    xn = xn_all[here, :]
    xn_ref[...] = xn
    z = dot(xn, wz_ref[...])
    z_ref[...] = z
    xp = dot(xn, wx_ref[...])
    xp_ref[...] = xp
    xbuf[8:, :] = xp
    bc = dot(xn, wbc_ref[...], COLS).astype(bf16)
    bc_ref[...] = bc
    bbuf[8:, :] = bc.astype(f32)
    dt = dot(xn, wdt_ref[...], COLS)
    dt_ref[...] = dt

    pre_x = conv_taps(xbuf, cx_ref[0:4, :], cx_ref[4:5, :], length)
    xc = pre_x * sigmoid(pre_x)
    pre_bc = conv_taps(bbuf, cbc_ref[0:4, :], cbc_ref[4:5, :], length)
    bcc = (pre_bc * sigmoid(pre_bc)).astype(bf16)
    xbuf[0:8, :] = xbuf[length : length + 8, :]
    bbuf[0:8, :] = bbuf[length : length + 8, :]
    b_mat = bcc[:, :state]
    c_mat = bcc[:, state:]

    mask, _, step, _, cum = span_values(dt, head_ref)
    cum_t = jnp.transpose(cum)
    scores = dot(c_mat, b_mat, COLS)
    xs = xc * spread_heads(step, channels, head_dim)
    xs_b = xs.astype(bf16)
    lane = lax.broadcasted_iota(jnp.int32, (length, LANES), 1)
    per_tile = LANES // head_dim
    tiles = []
    for tile in range(channels // LANES):
        xs_tile = xs_b[:, tile * LANES : (tile + 1) * LANES]
        out = None
        for sub in range(per_tile):
            head = tile * per_tile + sub
            decay = decay_matrix(mask, cum[:, head : head + 1], cum_t[head : head + 1, :])
            part = dot((scores * decay).astype(bf16), xs_tile)
            out = part if out is None else jnp.where(lane >= sub * head_dim, part, out)
        tiles.append(out)
    hin = hst[...]
    hin_ref[0] = hin
    last = cum[length - 1 : length, :]
    y = jnp.concatenate(tiles, axis=1)
    y = y + dot(c_mat, hin.astype(bf16)) * spread_heads(jnp.exp(cum), channels, head_dim)
    y = y + cx_ref[6:7, :] * xc
    y_ref[...] = y
    tail = spread_heads(jnp.exp(last - cum), channels, head_dim)
    keep = spread_heads(jnp.exp(last), channels, head_dim)
    hst[...] = keep * hin + dot(b_mat, (tail * xs).astype(bf16), ROWS)

    gated = y * (z * sigmoid(z))
    scaled = gated * cx_ref[5:6, :]
    squares = jnp.sum(gated * gated, axis=1, keepdims=True)
    high = squares.astype(bf16).astype(f32)
    extra = jnp.where(lane == 0, high, jnp.where(lane == 1, squares - high, 0.0)).astype(bf16)
    mixed = times_out(scaled.astype(bf16), wo_refs).astype(bf16)
    put_half(
        place_ref,
        span,
        pl.num_programs(0) // 2,
        mine_ref,
        other_ref,
        jnp.concatenate([mixed, extra], axis=1),
    )
    if last_layer:
        g = g_all[here, :]
        g_ref[...] = g
        gg = times_out_t(g, wo_refs)
        gg_ref[...] = gg
        products = jnp.sum(gg * scaled, axis=1, keepdims=True)
        both = jnp.where(lane == 0, squares, jnp.where(lane == 1, products, 0.0))
        sums_ref[...] = jnp.transpose(both)[0:8, :]


def gate_part(gg, rms, coef, z, y, cx_ref):
    norm_gate = cx_ref[5:6, :]
    sz = sigmoid(z)
    silu_z = z * sz
    gated = y * silu_z
    rg = rms * gg
    gate_out = (gated * rms * norm_gate).astype(bf16)
    d_gated = rg * norm_gate - gated * coef
    dz = (d_gated * y * (sz * (1.0 + z * (1.0 - sz)))).astype(bf16)
    return dz, d_gated * silu_z, gate_out, jnp.sum(rg * gated, axis=0, keepdims=True)


def gate_kernel(plan, n_pieces, width, place_ref, *refs):
    pieces = refs[:n_pieces]
    z_ref, y_ref, wo_ref, cx_ref, g_ref, dz_ref, dy_ref, go_ref, acc_ref, first_all = refs[n_pieces:]
    length = z_ref.shape[0]
    span = pl.program_id(0)

    @pl.when(span == 0)
    def _():
        place_pieces(plan, place_ref, pieces, [first_all])
        acc_ref[...] = jnp.zeros_like(acc_ref)

    first = first_all[pl.ds(pl.multiple_of(span * length, length), length), :]
    g = first[:, :width]
    g_ref[...] = g
    tok = first[:, width:].astype(f32)
    rms = tok[:, 0:1] + tok[:, 1:2]
    coef = tok[:, 2:3] + tok[:, 3:4]
    gg = times_out_t(g, cut_out(wo_ref))
    dz, dy, gate_out, acc_norm = gate_part(gg, rms, coef, z_ref[...], y_ref[...], cx_ref)
    dz_ref[...] = dz
    dy_ref[...] = dy
    go_ref[...] = gate_out
    acc_ref[5:6, :] += acc_norm


def last_gate_kernel(inner_all, place_ref, gg_ref, tok_ref, z_ref, y_ref, cx_ref, dz_ref, dy_ref, go_ref, acc_ref):
    @pl.when(pl.program_id(0) == 0)
    def _():
        acc_ref[...] = jnp.zeros_like(acc_ref)

    tok = jnp.transpose(tok_ref[...])
    rms = lax.rsqrt(tok[:, 0:1] / inner_all + EPS)
    coef = rms * rms * rms * tok[:, 1:2] / inner_all
    dz, dy, gate_out, acc_norm = gate_part(gg_ref[...], rms, coef, z_ref[...], y_ref[...], cx_ref)
    dz_ref[...] = dz
    dy_ref[...] = dy
    go_ref[...] = gate_out
    acc_ref[5:6, :] += acc_norm


def scan_kernel(head_dim, place_ref, *refs):
    (dy_ref, dz_ref, xn_ref, xp_ref, xhalo_ref, bc_ref, bchalo_ref, dt_ref, hin_ref,
     w_ref, wbc_ref, wdt_ref, cx_ref, cbc_ref, head_ref, pick_ref,
     dxt_ref, bcmine_ref, bcother_ref, mine_ref, other_ref, acc_ref, accbc_ref, acch_ref, accn_ref,
     xbuf, bbuf, dubuf, dubbuf, dhst) = refs
    length = xp_ref.shape[0]
    channels = w_ref.shape[1]
    width = xn_ref.shape[1]
    state = dhst.shape[0]
    step_id = pl.program_id(0)
    first_span = step_id == pl.num_programs(0) - 1

    @pl.when(step_id == 0)
    def _():
        dubuf[length:, :] = jnp.zeros((8, channels), f32)
        dubbuf[length:, :] = jnp.zeros((8, 2 * state), f32)
        dhst[...] = jnp.zeros_like(dhst)
        accn_ref[...] = jnp.zeros_like(accn_ref)
        acc_ref[...] = jnp.zeros_like(acc_ref)
        accbc_ref[...] = jnp.zeros_like(accbc_ref)
        acch_ref[...] = jnp.zeros_like(acch_ref)

    @pl.when(first_span)
    def _():
        xbuf[0:8, :] = jnp.zeros((8, channels), f32)
        bbuf[0:8, :] = jnp.zeros((8, 2 * state), f32)

    @pl.when(jnp.logical_not(first_span))
    def _():
        xbuf[0:8, :] = xhalo_ref[...]
        bbuf[0:8, :] = bchalo_ref[...].astype(f32)[8:16, :]

    xbuf[8:, :] = xp_ref[...]
    bbuf[8:, :] = bc_ref[...].astype(f32)
    dz_b, dy = dz_ref[...], dy_ref[...]
    skip = cx_ref[6:7, :]

    pre_x = conv_taps(xbuf, cx_ref[0:4, :], cx_ref[4:5, :], length)
    sx = sigmoid(pre_x)
    xc = pre_x * sx
    pre_bc = conv_taps(bbuf, cbc_ref[0:4, :], cbc_ref[4:5, :], length)
    sbc = sigmoid(pre_bc)
    bcc = (pre_bc * sbc).astype(bf16)
    b_mat = bcc[:, :state]
    c_mat = bcc[:, state:]
    mask, pre_dt, step, rate, cum = span_values(dt_ref[...], head_ref)
    cum_t = jnp.transpose(cum)
    last = cum[length - 1 : length, :]
    scores = dot(c_mat, b_mat, COLS)
    step_all = spread_heads(step, channels, head_dim)
    xs = xc * step_all
    xs_b = xs.astype(bf16)
    tail = spread_heads(jnp.exp(last - cum), channels, head_dim)
    keep = spread_heads(jnp.exp(last), channels, head_dim)

    hin = hin_ref[0]
    hin_b = hin.astype(bf16)
    dh = dhst[...]
    dh_b = dh.astype(bf16)
    dye = dy * spread_heads(jnp.exp(cum), channels, head_dim)
    dye_b = dye.astype(bf16)
    txs = tail * xs
    txs_b = txs.astype(bf16)
    carried = dot(c_mat, hin_b)
    pulled = dot(b_mat, dh_b)
    d_c = dot(dye_b, hin_b, COLS)
    d_b = dot(txs_b, dh_b, COLS)
    dhst[...] = keep * dh + dot(c_mat, dye_b, ROWS)
    into = txs * pulled
    across = dye * carried - into
    at_last = jnp.sum(into, axis=0, keepdims=True) + keep * jnp.sum(hin * dh, axis=0, keepdims=True)

    dy_b = dy.astype(bf16)
    dy_t = jnp.transpose(dy).astype(bf16)
    lane = lax.broadcasted_iota(jnp.int32, (length, LANES), 1)
    per_tile = LANES // head_dim
    d_scores = jnp.zeros((length, length), f32)
    row_sums = jnp.zeros((length, LANES), f32)
    col_sums = []
    dxs_parts = []
    for head in range(channels // head_dim):
        tile, sub = divmod(head, per_tile)
        dy_tile = dy_b[:, tile * LANES : (tile + 1) * LANES]
        own = (lane >= sub * head_dim) & (lane < (sub + 1) * head_dim)
        dy_head = jnp.where(own, dy_tile, jnp.zeros_like(dy_tile))
        d_m = dot(dy_head, xs_b[:, tile * LANES : (tile + 1) * LANES], COLS)
        decay = decay_matrix(mask, cum[:, head : head + 1], cum_t[head : head + 1, :])
        dxs_parts.append(
            dot(dy_t[head * head_dim : (head + 1) * head_dim, :], (scores * decay).astype(bf16))
        )
        d_m = d_m * decay
        d_scores = d_scores + d_m
        pairs = d_m * scores
        row_sums = jnp.where(lane == head, jnp.sum(pairs, axis=1, keepdims=True), row_sums)
        col_sums.append(jnp.sum(pairs, axis=0, keepdims=True))
    heads = len(col_sums)
    col_sums = jnp.concatenate(col_sums + [jnp.zeros((LANES - heads, length), f32)], axis=0)
    dxs = jnp.transpose(jnp.concatenate(dxs_parts, axis=0)) + tail * pulled
    pick = pick_ref[...]
    d_cum = row_sums - jnp.transpose(col_sums) + dot(across, pick, PLAIN, highest)
    at_last = dot(jnp.broadcast_to(at_last, (8, channels)), pick, PLAIN, highest)[0:1, :]
    d_rate = dot(mask.astype(f32), d_cum, ROWS, highest) + at_last
    d_step = d_rate * head_ref[1:2, :] + dot(dxs * xc, pick, PLAIN, highest)
    d_dt = d_step * sigmoid(pre_dt)
    acch_ref[0:1, :] += jnp.sum(d_dt, axis=0, keepdims=True)
    acch_ref[1:2, :] += jnp.sum(d_rate * rate, axis=0, keepdims=True)
    dt_b = d_dt.astype(bf16)
    ds_b = d_scores.astype(bf16)
    d_c = d_c + dot(ds_b, b_mat)
    d_b = d_b + dot(ds_b, c_mat, ROWS)
    d_xc = dxs * step_all + skip * dy
    acc_skip = jnp.sum(dy * xc, axis=0, keepdims=True)

    d_u = d_xc * (sx * (1.0 + pre_x * (1.0 - sx)))
    d_ub = jnp.concatenate([d_b, d_c], axis=1) * (sbc * (1.0 + pre_bc * (1.0 - sbc)))
    dubuf[0:length, :] = d_u
    dubbuf[0:length, :] = d_ub
    d_x = jnp.zeros_like(d_u)
    d_bc = jnp.zeros_like(d_ub)
    acc_rows = []
    accbc_rows = []
    for j in range(4):
        d_x = d_x + cx_ref[j : j + 1, :] * dubuf[pl.ds(3 - j, length), :]
        d_bc = d_bc + cbc_ref[j : j + 1, :] * dubbuf[pl.ds(3 - j, length), :]
        acc_rows.append(jnp.sum(d_u * xbuf[pl.ds(5 + j, length), :], axis=0, keepdims=True))
        accbc_rows.append(jnp.sum(d_ub * bbuf[pl.ds(5 + j, length), :], axis=0, keepdims=True))
    dubuf[length:, :] = d_u[0:8, :]
    dubbuf[length:, :] = d_ub[0:8, :]
    zero = jnp.zeros((1, channels), f32)
    acc_ref[...] += jnp.concatenate(
        acc_rows + [jnp.sum(d_u, axis=0, keepdims=True), zero, acc_skip, zero], axis=0
    )
    zero = jnp.zeros((3, d_ub.shape[1]), f32)
    accbc_ref[...] += jnp.concatenate(
        accbc_rows + [jnp.sum(d_ub, axis=0, keepdims=True), zero], axis=0
    )
    dx_b = d_x.astype(bf16)
    dbc_b = d_bc.astype(bf16)
    dxt_ref[:, :channels] = dx_b
    dxt_ref[:, channels:] = dt_b
    put_columns(
        place_ref,
        pl.num_programs(0) - 1 - step_id,
        bcmine_ref,
        bcother_ref,
        jnp.transpose(d_bc).astype(bf16),
    )
    total = dot(dz_b, w_ref[0:width, :], COLS) + dot(dx_b, w_ref[width : 2 * width, :], COLS)
    total = total + dot(dbc_b, wbc_ref[...]) + dot(dt_b, wdt_ref[...])
    accn_ref[0:1, :] += jnp.sum(total * xn_ref[...].astype(f32), axis=0, keepdims=True)
    put_half(
        place_ref,
        pl.num_programs(0) - 1 - step_id,
        pl.num_programs(0) // 2,
        mine_ref,
        other_ref,
        total.astype(bf16),
    )


def whole(shape):
    zeros = (0,) * len(shape)
    return pl.BlockSpec(shape, lambda i, p: zeros)


def span_rows(columns):
    return pl.BlockSpec((SPAN, columns), lambda i, p: (i, 0))


def half_rows(columns, spans, reverse):
    half = spans // 2

    def block(i, core):
        span = spans - 1 - i if reverse else i
        return jnp.clip(span - half * core, 0, half - 1), 0

    return [
        pl.BlockSpec((SPAN, columns), lambda i, p: block(i, p[0])),
        pl.BlockSpec((SPAN, columns), lambda i, p: block(i, 1 - p[0])),
    ]


def span_call(kernel, name, spans, place, operands, in_specs, shapes, out_specs, scratch, flops):
    moved = sum(v.size * v.dtype.itemsize for v in [*operands, *shapes])
    return pl.pallas_call(
        kernel,
        grid_spec=pltpu.PrefetchScalarGridSpec(
            num_scalar_prefetch=1,
            grid=(spans,),
            in_specs=in_specs,
            out_specs=out_specs,
            scratch_shapes=scratch,
        ),
        out_shape=shapes,
        compiler_params=pltpu.CompilerParams(
            dimension_semantics=("arbitrary",), vmem_limit_bytes=VMEM_BYTES
        ),
        cost_estimate=pl.CostEstimate(flops=flops, bytes_accessed=moved, transcendentals=0),
        name=name,
    )(place, *operands)


def run_forward(place, gathered, weights, small, state, head_dim):
    channels = weights[0].shape[1]
    width = gathered[0][0][0].shape[1]
    tokens = NC * NZ * gathered[0][2][0]
    spans = tokens // SPAN
    last_layer = len(gathered) == 2
    plans = [(cut_plan(*one), len(one[0])) for one in gathered]
    operands = [p for one in gathered for p in one[0]]
    operands += [*weights, *small]
    in_specs = [whole(v.shape) for v in operands]
    shapes = [
        jax.ShapeDtypeStruct((tokens, width), bf16),
        jax.ShapeDtypeStruct((2 * state, width), bf16),
        jax.ShapeDtypeStruct((tokens, channels), f32),
        jax.ShapeDtypeStruct((tokens, channels), f32),
        jax.ShapeDtypeStruct((tokens, 2 * state), bf16),
        jax.ShapeDtypeStruct((tokens, LANES), f32),
        jax.ShapeDtypeStruct((tokens, channels), f32),
        jax.ShapeDtypeStruct((spans, state, channels), f32),
        jax.ShapeDtypeStruct((tokens // 2, width + LANES), bf16),
        jax.ShapeDtypeStruct((tokens // 2, width + LANES), bf16),
    ]
    out_specs = [span_rows(width), whole((2 * state, width))]
    out_specs += [span_rows(s.shape[1]) for s in shapes[2:7]]
    out_specs.append(pl.BlockSpec((1, state, channels), lambda i, p: (i, 0, 0)))
    out_specs += half_rows(width + LANES, spans, False)
    scratch = [
        pltpu.VMEM((tokens, width), bf16),
        pltpu.VMEM((SPAN + 8, channels), f32),
        pltpu.VMEM((SPAN + 8, 2 * state), f32),
        pltpu.VMEM((state, channels), f32),
    ]
    if last_layer:
        shapes += [
            jax.ShapeDtypeStruct((tokens, width), bf16),
            jax.ShapeDtypeStruct((8, tokens), f32),
            jax.ShapeDtypeStruct((tokens, channels), f32),
        ]
        out_specs += [span_rows(width), pl.BlockSpec((8, SPAN), lambda i, p: (0, i)), span_rows(channels)]
        scratch.append(pltpu.VMEM((tokens, width), bf16))
    kernel = functools.partial(forward_kernel, plans, head_dim)
    return span_call(
        kernel, "layer_forward", spans, place, operands, in_specs, shapes, out_specs, scratch, 20 * 10**9
    )


def run_gate(place, gathered, z, y, w, cx):
    tokens, channels = z.shape
    width = w.shape[0] // 3
    spans = tokens // SPAN
    plan, pieces = cut_plan(*gathered), list(gathered[0])
    operands = [*pieces, z, y, w, cx]
    in_specs = [whole(p.shape) for p in pieces]
    in_specs += [span_rows(channels), span_rows(channels)]
    in_specs += [pl.BlockSpec((width, channels), lambda i, p: (2, 0)), whole(cx.shape)]
    shapes = [
        jax.ShapeDtypeStruct((tokens, width), bf16),
        jax.ShapeDtypeStruct((tokens, channels), bf16),
        jax.ShapeDtypeStruct((tokens, channels), f32),
        jax.ShapeDtypeStruct((tokens, channels), bf16),
        jax.ShapeDtypeStruct((8, channels), f32),
    ]
    out_specs = [span_rows(s.shape[1]) for s in shapes[:4]] + [whole(shapes[4].shape)]
    scratch = [pltpu.VMEM((tokens, pieces[0].shape[1]), bf16)]
    kernel = functools.partial(gate_kernel, plan, len(pieces), width)
    return span_call(
        kernel, "gate_backward", spans, place, operands, in_specs, shapes, out_specs, scratch, 6 * 10**9
    )


def run_last_gate(place, gg, sums, z, y, cx, inner_all):
    tokens, channels = z.shape
    spans = tokens // SPAN
    rows = span_rows(channels)
    shapes = [
        jax.ShapeDtypeStruct((tokens, channels), bf16),
        jax.ShapeDtypeStruct((tokens, channels), f32),
        jax.ShapeDtypeStruct((tokens, channels), bf16),
        jax.ShapeDtypeStruct((8, channels), f32),
    ]
    return span_call(
        functools.partial(last_gate_kernel, inner_all),
        "last_gate_backward",
        spans,
        place,
        [gg, sums, z, y, cx],
        [rows, pl.BlockSpec((8, SPAN), lambda i, p: (0, i)), rows, rows, whole(cx.shape)],
        shapes,
        [rows, rows, rows, whole(shapes[3].shape)],
        [],
        10**9,
    )


def run_scan(place, dy, dz, xn, xp, bc, dt, hin, weights, small, pick, head_dim):
    tokens, channels = xp.shape
    state = hin.shape[1]
    width = xn.shape[1]
    spans = tokens // SPAN

    def rev(columns):
        return pl.BlockSpec((SPAN, columns), lambda i, p: (spans - 1 - i, 0))

    def halo(columns, rows):
        per = SPAN // rows
        return pl.BlockSpec(
            (rows, columns), lambda i, p: (jnp.maximum((spans - 1 - i) * per - 1, 0), 0)
        )

    operands = [dy, dz, xn, xp, xp, bc, bc, dt, hin, *weights, *small, pick]
    in_specs = [
        rev(channels),
        rev(channels),
        rev(width),
        rev(channels),
        halo(channels, 8),
        rev(2 * state),
        halo(2 * state, 16),
        rev(LANES),
        pl.BlockSpec((1, state, channels), lambda i, p: (spans - 1 - i, 0, 0)),
    ]
    in_specs.append(whole((2 * width, channels)))
    in_specs += [whole(v.shape) for v in operands[len(in_specs) :]]
    shapes = [
        jax.ShapeDtypeStruct((tokens, channels + LANES), bf16),
        jax.ShapeDtypeStruct((state * spans, SPAN), bf16),
        jax.ShapeDtypeStruct((state * spans, SPAN), bf16),
        jax.ShapeDtypeStruct((tokens // 2, width), bf16),
        jax.ShapeDtypeStruct((tokens // 2, width), bf16),
        jax.ShapeDtypeStruct((8, channels), f32),
        jax.ShapeDtypeStruct((8, 2 * state), f32),
        jax.ShapeDtypeStruct((8, LANES), f32),
        jax.ShapeDtypeStruct((8, width), f32),
    ]
    out_specs = [rev(channels + LANES), whole(shapes[1].shape), whole(shapes[2].shape)]
    out_specs += half_rows(width, spans, True)
    out_specs += [whole(s.shape) for s in shapes[5:]]
    scratch = [
        pltpu.VMEM((SPAN + 8, channels), f32),
        pltpu.VMEM((SPAN + 8, 2 * state), f32),
        pltpu.VMEM((SPAN + 8, channels), f32),
        pltpu.VMEM((SPAN + 8, 2 * state), f32),
        pltpu.VMEM((state, channels), f32),
    ]
    kernel = functools.partial(scan_kernel, head_dim)
    return span_call(
        kernel, "scan_backward", spans, place, operands, in_specs, shapes, out_specs, scratch, 28 * 10**9
    )


def weight_kernel(pairs, *refs):
    lefts, rights, out_ref = refs[: len(pairs)], refs[len(pairs) : -1], refs[-1]
    at = 0
    for left_ref, right_ref in zip(lefts, rights):
        columns = right_ref.shape[1]
        out_ref[:, at : at + columns] = dot(left_ref[...], right_ref[...], ROWS).astype(bf16)
        at += columns


def weight_products(pairs):
    tokens = pairs[0][0].shape[0]
    rows = max(left.shape[1] for left, _ in pairs)
    block = rows // 4
    lefts, rights, columns = [], [], []
    for left, right in pairs:
        quarter = left.shape[1] == block
        lefts.append(pl.BlockSpec((tokens, block), (lambda i: (0, 0)) if quarter else (lambda i: (0, i))))
        wide = block if quarter else right.shape[1]
        rights.append(pl.BlockSpec((tokens, wide), (lambda i: (0, i)) if quarter else (lambda i: (0, 0))))
        columns.append(wide)
    return pl.pallas_call(
        functools.partial(weight_kernel, pairs_of(columns)),
        grid=(4,),
        in_specs=lefts + rights,
        out_specs=pl.BlockSpec((block, sum(columns)), lambda i: (i, 0)),
        out_shape=jax.ShapeDtypeStruct((rows, sum(columns)), bf16),
        compiler_params=pltpu.CompilerParams(vmem_limit_bytes=VMEM_BYTES),
        cost_estimate=pl.CostEstimate(
            flops=2 * tokens * rows * sum(columns), bytes_accessed=8 * 10**6, transcendentals=0
        ),
        name="weight_products",
    )(*[left for left, _ in pairs], *[right for _, right in pairs])


def pairs_of(columns):
    return tuple(columns)


SIZES = (4, 2, 2, 2, 4)
NX, NYL, NC, NYH, NZ = SIZES
EVERY = [
    (x, yl, c, yh, z)
    for x in range(NX)
    for yl in range(NYL)
    for c in range(NC)
    for yh in range(NYH)
    for z in range(NZ)
]


def linear(x, yl, c, yh, z):
    return ((((x % NX) * NYL + yl % NYL) * NC + c % NC) * NYH + yh % NYH) * NZ + z % NZ


def send(v, step, only=None):
    pairs = [(linear(*d), linear(*step(*d))) for d in EVERY if only is None or only(*d)]
    return lax.ppermute(v, ("dp", "tensor"), pairs)


def send_z(v, k):
    return send(v, lambda x, yl, c, yh, z: (x, yl, c, yh, z + k))


def send_core(v):
    return send(v, lambda x, yl, c, yh, z: (x, yl, c + 1, yh, z))


def trade(v, k=0):
    return send(v, lambda x, yl, c, yh, z: (x, yl, yh, c, z + k))


def position():
    dp, tensor = lax.axis_index("dp"), lax.axis_index("tensor")
    return dp // (NYL * NC), dp // NC % NYL, dp % NC, tensor // NZ, tensor % NZ


def gather(v, parts, away=False):
    arrays, sources = [], []
    for k in (0, 1, 3, 2):
        piece = trade(v, k) if away else v if k == 0 else send_z(v, k)
        arrays += [piece, send_core(piece)]
        sources += [(False, -k % NZ, 0), (True, -k % NZ, 0)]
    return arrays, sources, parts


def cut_plan(arrays, sources, parts):
    plan = []
    for number, (piece, (other, dz, first)) in enumerate(zip(arrays, sources)):
        base = 0
        for out, per in enumerate(parts):
            begin, end = max(first, base), min(first + piece.shape[0], base + per)
            if begin < end:
                plan.append((number, other, dz, begin - first, out, per, begin - base, end - begin))
            base += per
    return plan


def fold(mine, other):
    _, _, _, _, z = position()
    rows = mine.shape[0] // NZ
    blocks = []
    for k in range(NZ):
        at = (z + k) % NZ * rows
        a = lax.dynamic_slice_in_dim(mine, at, rows, 0).astype(f32)
        blocks.append(a + lax.dynamic_slice_in_dim(other, at, rows, 0).astype(f32))
    return blocks


def fold_beside(pairs):
    folded = [fold(mine, send_core(other)) for mine, other in pairs]
    return [jnp.concatenate([blocks[k] for blocks in folded], axis=1) for k in range(NZ)]


def scatter(*pairs):
    own, one, two, three = fold_beside(pairs)
    return [own] + [send_z(b.astype(bf16), k) for k, b in ((1, one), (2, two), (3, three))]


def scatter_home(*pairs):
    return [trade(b.astype(bf16), k) for k, b in enumerate(fold_beside(pairs))]


def split_two(v):
    high = v.astype(bf16)
    return high, (v - high.astype(f32)).astype(bf16)


def scatter_with_sum(mine, other, shared, meanwhile):
    _, _, _, _, z = position()
    half, lanes = mine.shape
    rows = half // NZ
    lines = -(-shared.shape[0] // (8 * lanes)) * 8

    def pack(vector):
        padded = (jnp.pad(p, (0, lines * lanes - vector.shape[0])) for p in split_two(vector))
        return jnp.concatenate([p.reshape(lines, lanes) for p in padded], axis=0)

    def unpack(packed):
        return (packed[:lines].astype(f32) + packed[lines:].astype(f32)).reshape(-1)[: shared.shape[0]]

    got = after(send_core(jnp.concatenate([other, pack(shared)], axis=0)), *meanwhile)
    blocks = fold(mine, got[:half])
    shared = shared + unpack(got[half:])
    packed = pack(shared)
    total, total_shared = blocks[0], shared
    for k in range(1, NZ):
        got = send_z(jnp.concatenate([blocks[k].astype(bf16), packed], axis=0), k)
        total = total + got[:rows].astype(f32)
        total_shared = total_shared + unpack(got[rows:])
    return total, total_shared


def sum_members(v):
    both = v + send_core(v)
    total = both
    for k in range(1, NZ):
        total = total + send_z(both, k)
    return total


def sum_far(v):
    far = send(v, lambda x, yl, c, yh, z: (x, yl, c, yh + 1, z), lambda x, yl, c, yh, z: c != yh)
    return (v.astype(f32) + far.astype(f32)).astype(bf16)


def halve(v):
    _, _, core, yh, _ = position()
    half = v.shape[0] // 2
    near = send(
        v[half:], lambda x, yl, c, yh, z: (x, yl, c + 1, yh, z), lambda x, yl, c, yh, z: c == yh
    )
    return jnp.where(core == yh, v[:half], near)


def sum_beside(part):
    beside = send(part, lambda x, yl, c, yh, z: (x, yl + 1, c, yh, z))
    return (part.astype(f32) + beside.astype(f32)).astype(bf16)


def reduce_back(half):
    _, _, core, yh, _ = position()
    other = send_core(half)
    stays = core == yh
    return jnp.where(stays, half, other), jnp.where(stays, other, half)


def sum_x(v):
    x = position()[0]
    rows = v.shape[0] // NX
    total = lax.dynamic_slice_in_dim(v, x * rows, rows, 0).astype(f32)
    for k in range(1, NX):
        block = lax.dynamic_slice_in_dim(v, (x + k) % NX * rows, rows, 0)
        total = total + send(block, lambda x, yl, c, yh, z, k=k: (x + k, yl, c, yh, z)).astype(f32)
    return total.astype(bf16)


def collect_x(part):
    x = position()[0]
    out = jnp.zeros((NX,) + part.shape, bf16)
    out = lax.dynamic_update_index_in_dim(out, part, x, 0)
    for k in range(1, NX):
        block = send(part, lambda x, yl, c, yh, z, k=k: (x + k, yl, c, yh, z))
        out = lax.dynamic_update_index_in_dim(out, block, (x - k) % NX, 0)
    return out


def finish_sum(quarter, meanwhile=()):
    part = after(sum_beside(halve(sum_far(quarter))), *meanwhile)
    halves = reduce_back(collect_x(part))
    whole_rows = jnp.stack(halves, axis=1)
    return whole_rows.reshape(-1, quarter.shape[1])


def row_call(kernel, name, operands, shapes):
    return pl.pallas_call(
        kernel,
        grid=(1,),
        in_specs=[pl.BlockSpec((rows, v.shape[1]), lambda i: (0, 0)) for v, rows in operands],
        out_specs=[pl.BlockSpec(s.shape, lambda i: (0, 0)) for s in shapes],
        out_shape=shapes,
        compiler_params=pltpu.CompilerParams(vmem_limit_bytes=VMEM_BYTES),
        name=name,
    )(*[v for v, _ in operands])


def inverse_rms(v):
    return lax.rsqrt(jnp.mean(v * v, axis=-1, keepdims=True) + EPS)


def first_kernel(packed_ref, gain_ref, out_ref):
    rows = 128
    v = packed_ref[0:rows, :].astype(f32)
    out_ref[0:rows, :] = (v * inverse_rms(v) * gain_ref[...]).astype(bf16)
    out_ref[rows:, :] = packed_ref[rows : out_ref.shape[0], :]


def add_terms(own_ref, a_ref, b_ref, c_ref):
    total = own_ref[...].astype(f32) + a_ref[...].astype(f32)
    return total + (b_ref[...].astype(f32) + c_ref[...].astype(f32))


def unscaled_output(inner_all, terms, width):
    total = add_terms(*terms)
    squares = total[:, width : width + 1] + total[:, width + 1 : width + 2]
    gate_rms = lax.rsqrt(squares / inner_all + EPS)
    return gate_rms, total[:, :width] * gate_rms


def middle_kernel(inner_all, own_ref, a_ref, b_ref, c_ref, res_ref, gain_ref, res1_ref, mixed_ref, rms_ref, normed_ref):
    width = res_ref.shape[1]
    gate_rms, mixed = unscaled_output(inner_all, (own_ref, a_ref, b_ref, c_ref), width)
    res = res_ref[...].astype(f32) + mixed
    res1_ref[...] = res
    mixed_ref[...] = mixed
    rms_ref[...] = jnp.broadcast_to(gate_rms, rms_ref.shape)
    normed_ref[...] = (res * inverse_rms(res) * gain_ref[...]).astype(bf16)


def input_gradient(grad_normed, res, d_res, gain):
    inv = inverse_rms(res)
    scaled = grad_normed * gain
    dots = jnp.sum(scaled * res, axis=-1, keepdims=True) / res.shape[1]
    return d_res + inv * scaled - res * (inv * inv * inv) * dots


def between_kernel(inner_all, own_ref, a_ref, b_ref, c_ref, res_ref, dres_ref, gain_ref, mixed_ref, rms_ref, out_ref, sent_ref):
    width = res_ref.shape[1]
    grad_normed = add_terms(*(ref.at[:, 0:width] for ref in (own_ref, a_ref, b_ref, c_ref)))
    d_res = input_gradient(grad_normed, res_ref[...], dres_ref[...].astype(f32), gain_ref[...])
    out_ref[...] = d_res
    g_mixed = d_res.astype(bf16)
    sent_ref[:, :width] = g_mixed
    gate_rms = rms_ref[:, 0:1]
    products = jnp.sum(g_mixed.astype(f32) * mixed_ref[...], axis=-1, keepdims=True)
    coef = gate_rms * gate_rms * products / inner_all
    lane = lax.broadcasted_iota(jnp.int32, rms_ref.shape, 1)
    rms_high = gate_rms.astype(bf16).astype(f32)
    coef_high = coef.astype(bf16).astype(f32)
    extra = jnp.where(lane == 0, rms_high, jnp.where(lane == 1, gate_rms - rms_high, 0.0))
    extra = jnp.where(lane == 2, coef_high, jnp.where(lane == 3, coef - coef_high, extra))
    sent_ref[:, width:] = extra.astype(bf16)


def end_kernel(inner_all, own_ref, a_ref, b_ref, c_ref, res_ref, kept_ref, gain_ref, out_ref, grad_ref):
    width = res_ref.shape[1]
    cut = [ref.at[:, 0:width] for ref in (own_ref, a_ref, b_ref, c_ref)]
    grad_ref[...] = input_gradient(
        add_terms(*cut), res_ref[...].astype(f32), kept_ref[:, width:], gain_ref[...]
    )
    cut = [ref.at[:, width : 2 * width + LANES] for ref in (own_ref, a_ref, b_ref, c_ref)]
    _, mixed = unscaled_output(inner_all, cut, width)
    out_ref[...] = kept_ref[:, 0:width] + mixed


def after(v, *others):
    return lax.optimization_barrier((v, *others))[0]


def pad_to(v, rows, lanes):
    return jnp.pad(v, ((0, rows - v.shape[0]), (0, lanes - v.shape[1])))


def local(
    hidden_in,
    grad_out,
    norm_in,
    w_z,
    w_x,
    w_bc,
    w_dt,
    conv_x,
    conv_x_bias,
    conv_bc,
    conv_bc_bias,
    dt_bias,
    a_log,
    skip,
    norm_gate,
    w_out,
):
    layers, width, channels = w_z.shape
    heads = w_dt.shape[2]
    head_dim = channels // heads
    both = conv_bc.shape[2]
    state = both // 2
    members = NC * NZ
    inner_all = channels * members
    rows = hidden_in.shape[1]
    bc_rows = both // members
    _, _, core, _, z = position()
    place = jnp.stack([core, z]).astype(jnp.int32)
    full = jax.ShapeDtypeStruct((rows, width), f32)

    bc_t = jnp.swapaxes(w_bc, 1, 2)
    dt_t = jnp.pad(jnp.swapaxes(w_dt, 1, 2), ((0, 0), (0, 8 - heads), (0, 0)))
    packed = jnp.concatenate([hidden_in[0], bc_t[0], dt_t.reshape(layers * 8, width)], axis=0)
    packed = trade(packed)
    per_channel = jnp.concatenate(
        [conv_x, conv_x_bias[:, None], norm_gate[:, None], jnp.repeat(skip, head_dim, axis=1)[:, None]],
        axis=1,
    )
    per_channel = jnp.pad(per_channel, ((0, 0), (0, 1), (0, 0)))
    per_head = jnp.stack([dt_bias, -jnp.exp(a_log)], axis=1)
    per_head = jnp.pad(per_head, ((0, 0), (0, 6), (0, LANES - heads)))
    little = jnp.concatenate([per_channel, per_head], axis=2).reshape(layers * 8, channels + LANES)
    little = trade(little).reshape(layers, 8, channels + LANES)

    def pack_weights(layer):
        quarters = [w_out[layer, :, i * channels : (i + 1) * channels] for i in range(width // channels)]
        return jnp.concatenate([w_z[layer], w_x[layer], *quarters], axis=0)

    w0 = trade(after(pack_weights(0), little))

    [sent] = row_call(
        first_kernel,
        "first_norm",
        [(packed, packed.shape[0]), (norm_in[0:1], 1)],
        [jax.ShapeDtypeStruct((rows + bc_rows, width), bf16)],
    )
    gathered0 = gather(sent, (rows, bc_rows))
    wdt = [pad_to(packed[rows + bc_rows + 8 * l : rows + bc_rows + 8 * (l + 1)], LANES, width) for l in range(layers)]
    smalls = []
    for layer in range(layers):
        cbc = jnp.concatenate([conv_bc[layer], conv_bc_bias[layer][None], jnp.zeros((3, both), f32)], axis=0)
        smalls.append((little[layer, :, :channels], cbc, little[layer, :, channels:]))
    channel_head = jnp.arange(channels) // head_dim
    pick = (channel_head[:, None] == jnp.arange(LANES)[None, :]).astype(f32)

    out0 = run_forward(place, [gathered0], (w0, wdt[0]), smalls[0], state, head_dim)
    xn0, wbc0, z0, xp0, bc0, dt0, y0, hin0, mine, other = out0
    grads = after(jnp.concatenate([grad_out[0], bc_t[1]], axis=0), w0)
    gathered_grad = gather(grads, (rows, bc_rows), away=True)
    grad_held = gathered_grad[0][0]
    terms = scatter((mine, after(other, *gathered_grad[0][::2])))
    w1 = trade(after(pack_weights(1), terms[0]))
    res1, mixed0, rms0, normed1 = row_call(
        functools.partial(middle_kernel, inner_all),
        "middle_norm",
        [(v, rows) for v in terms] + [(packed, rows), (norm_in[1:2], 1)],
        [full, full, jax.ShapeDtypeStruct((rows, LANES), f32), jax.ShapeDtypeStruct((rows, width), bf16)],
    )
    gathered1 = gather(normed1, (rows,))
    out1 = run_forward(
        place, [gathered1, gathered_grad], (w1, wdt[1]), smalls[1], state, head_dim
    )
    xn1, wbc1, z1, xp1, bc1, dt1, y1, hin1, mine, other, grad_rows1, sums, gg1 = out1
    sums = sum_members(sums)

    mixed_halves = mine, other
    dz1, dy1, go1, acc_gate1 = run_last_gate(place, gg1, sums, z1, y1, smalls[1][0], inner_all)
    early1 = sum_far(weight_products([(xn1, dz1), (go1, grad_rows1)]))
    back1 = run_scan(
        place, dy1, dz1, xn1, xp1, bc1, dt1, hin1, (w1, wbc1, wdt[1]), smalls[1], pick, head_dim
    )
    dxt1, *bc_halves, mine, other, acc1, accbc1, acch1, accn1 = back1
    terms = scatter((mine, after(other, early1)), bc_halves)
    d_res1, sent = row_call(
        functools.partial(between_kernel, inner_all),
        "between_layers",
        [(v, rows) for v in terms]
        + [(res1, rows), (grad_held, rows), (norm_in[1:2], 1), (mixed0, rows), (rms0, rows)],
        [full, jax.ShapeDtypeStruct((rows, width + LANES), bf16)],
    )
    gathered_back = gather(sent, (rows,))
    early1 = sum_x(halve(after(early1, sent)))

    bc_at = channels + bc_rows

    def with_bc(dxt, bc_sum):
        by_token = bc_sum.reshape(-1, bc_rows, SPAN).swapaxes(1, 2).reshape(-1, bc_rows)
        spread = jnp.pad(by_token, ((0, 0), (bc_at, dxt.shape[1] - bc_at - bc_rows)))
        return dxt + spread.astype(bf16)

    dxt1 = with_bc(dxt1, sum(v[:, width:].astype(f32) for v in terms))

    z0 = after(z0, early1)
    grad_rows0, dz0, dy0, go0, acc_gate0 = run_gate(place, gathered_back, z0, y0, w0, smalls[0][0])
    early = weight_products([(xn0, dz0), (go0, grad_rows0), (xn1, dxt1)])
    dy0 = after(dy0, early)
    early = sum_x(early)
    early1 = sum_beside(after(early1, dz0))
    kept_home = trade(jnp.concatenate([res1, d_res1], axis=1))
    back0 = run_scan(
        place, dy0, dz0, xn0, xp0, bc0, dt0, hin0, (w0, wbc0, wdt[0]), smalls[0], pick, head_dim
    )
    dxt0, *bc_halves, mine, other, acc0, accbc0, acch0, accn0 = back0
    all1 = jnp.concatenate(reduce_back(collect_x(after(early1, dxt0))), axis=0).reshape(width, 2 * channels)

    mixed_mine, mixed_other = mixed_halves
    terms = scatter_home((mine, other), (mixed_mine, after(mixed_other, dxt0)))
    hidden_out, grad_in = row_call(
        functools.partial(end_kernel, inner_all),
        "outputs",
        [(v, rows) for v in terms] + [(hidden_in[0], rows), (kept_home, rows), (norm_in[0:1], 1)],
        [full, full],
    )

    shared = jnp.concatenate([accn0[0], accn1[0], accbc0[0:5].reshape(-1), accbc1[0:5].reshape(-1)])
    bc_sum, shared = scatter_with_sum(*bc_halves, shared, (early, early1))
    wide_x = channels + LANES
    lines = -(-shared.shape[0] // wide_x)
    shared = jnp.pad(shared, (0, lines * wide_x - shared.shape[0])).reshape(lines, wide_x)
    tiny = jnp.concatenate(
        [pad_to(v, v.shape[0], wide_x) for v in (acc0 + acc_gate0, acc1 + acc_gate1, acch0, acch1)] + [shared], axis=0
    )
    tiny_rows = tiny.shape[0]
    tiny = pad_to(tiny, 128, wide_x).astype(bf16)
    late = jnp.concatenate([weight_products([(xn0, with_bc(dxt0, bc_sum))]), tiny], axis=0)
    late = finish_sum(sum_x(late), terms)
    early = finish_sum(after(early, dxt0))

    tiny = late[width : width + tiny_rows].astype(f32)
    g_x = jnp.stack([tiny[0:8, :channels], tiny[8:16, :channels]])
    g_head = jnp.stack([tiny[16:18, :heads], tiny[24:26, :heads]])
    shared = tiny[32:].reshape(-1)
    g_norm_in = shared[: 2 * width].reshape(layers, width) / norm_in
    g_bc = shared[2 * width : 2 * width + 10 * both].reshape(layers, 5, both)

    def tall(v):
        quarters = v.reshape(4, channels, channels)
        return jnp.concatenate([quarters[i] for i in range(4)], axis=1)

    def both_layers(first, second):
        return jnp.stack([first, second]).astype(f32)

    late = late[:width]
    xs1 = early[:, 2 * channels :]
    return (
        hidden_out[None],
        grad_in[None],
        g_norm_in,
        both_layers(early[:, :channels], all1[:, :channels]),
        both_layers(late[:, :channels], xs1[:, :channels]),
        both_layers(late[:, bc_at : bc_at + bc_rows], xs1[:, bc_at : bc_at + bc_rows]),
        both_layers(late[:, channels : channels + heads], xs1[:, channels : channels + heads]),
        g_x[:, 0:4],
        g_x[:, 4],
        g_bc[:, 0:4],
        g_bc[:, 4],
        g_head[:, 0],
        g_head[:, 1],
        jnp.sum(g_x[:, 6].reshape(layers, heads, head_dim), axis=2),
        g_x[:, 5],
        both_layers(tall(early[:, channels : 2 * channels]), tall(all1[:, channels:])),
    )


def solution(mesh):
    specs_in = (
        P("dp", "tensor", None),
        P("dp", "tensor", None),
        P(),
        P(None, None, "tensor"),
        P(None, None, "tensor"),
        P(None, None, "tensor"),
        P(None, None, "tensor"),
        P(None, None, "tensor"),
        P(None, "tensor"),
        P(),
        P(),
        P(None, "tensor"),
        P(None, "tensor"),
        P(None, "tensor"),
        P(None, "tensor"),
        P(None, "tensor", None),
    )
    specs_out = (
        P("dp", "tensor", None),
        P("dp", "tensor", None),
        P(),
        P(None, None, "tensor"),
        P(None, None, "tensor"),
        P(None, None, "tensor"),
        P(None, None, "tensor"),
        P(None, None, "tensor"),
        P(None, "tensor"),
        P(),
        P(),
        P(None, "tensor"),
        P(None, "tensor"),
        P(None, "tensor"),
        P(None, "tensor"),
        P(None, "tensor", None),
    )
    return jax.shard_map(
        local, mesh=mesh, in_specs=specs_in, out_specs=specs_out, check_vma=False
    )
```

```python
import functools

import jax
import jax.numpy as jnp
from jax import lax
from jax.experimental import pallas as pl
from jax.experimental.pallas import tpu as pltpu
from jax.sharding import PartitionSpec as P

SPAN = 256
EPS = 1e-05
LANES = 128
VMEM_BYTES = 56 * 1024 * 1024

f32 = jnp.float32
bf16 = jnp.bfloat16
highest = lax.Precision.HIGHEST

ROWS = ((0,), (0,))
COLS = ((1,), (1,))
PLAIN = ((1,), (0,))


def dot(left, right, dims=PLAIN, precision=None):
    return lax.dot_general(
        left, right, (dims, ((), ())), preferred_element_type=f32, precision=precision
    )


def sigmoid(v):
    return 1.0 / (1.0 + jnp.exp(-v))


def softplus(v):
    return jnp.maximum(v, 0.0) + jnp.log1p(jnp.exp(-jnp.abs(v)))


def spread_heads(per_head, channels, head_dim):
    rows = per_head.shape[0]
    per_tile = LANES // head_dim
    lane = lax.broadcasted_iota(jnp.int32, (rows, LANES), 1)
    tiles = []
    for tile in range(channels // LANES):
        out = jnp.broadcast_to(
            per_head[:, tile * per_tile : tile * per_tile + 1], (rows, LANES)
        )
        for sub in range(1, per_tile):
            head = tile * per_tile + sub
            out = jnp.where(
                lane >= sub * head_dim,
                jnp.broadcast_to(per_head[:, head : head + 1], (rows, LANES)),
                out,
            )
        tiles.append(out)
    return jnp.concatenate(tiles, axis=1)


def conv_taps(buf, taps, offset, width):
    out = offset
    for j in range(4):
        out = out + taps[j : j + 1] * buf[pl.ds(5 + j, width), :]
    return out


def decay_matrix(mask, cum_col, cum_row):
    return jnp.exp(jnp.where(mask, cum_col - cum_row, -1e30))


def span_values(dt, head_ref):
    length = dt.shape[0]
    rows = lax.broadcasted_iota(jnp.int32, (length, length), 0)
    cols = lax.broadcasted_iota(jnp.int32, (length, length), 1)
    mask = rows >= cols
    pre = dt + head_ref[0:1, :]
    step = softplus(pre)
    rate = head_ref[1:2, :] * step
    cum = dot(mask.astype(f32), rate, PLAIN, highest)
    return mask, pre, step, rate, cum


def put_half(place_ref, span, half, mine_ref, other_ref, value):
    own = span // half == place_ref[0]

    @pl.when(own)
    def _():
        mine_ref[...] = value

    @pl.when(jnp.logical_not(own))
    def _():
        other_ref[...] = value


def place_pieces(plan, place_ref, pieces, outs):
    core, z = place_ref[0], place_ref[1]
    for piece, other, dz, start, out, per, offset, rows in plan:
        member = (1 - core if other else core) * NZ + lax.rem(z + dz, NZ)
        row = pl.multiple_of(member * per + offset, 16)
        outs[out][pl.ds(row, rows), :] = pieces[piece][start : start + rows, :]


def cut_weights(w_ref, width):
    channels = w_ref.shape[1]
    parts = [w_ref.at[0:width, :], w_ref.at[width : 2 * width, :]]
    return parts + cut_out(w_ref.at[2 * width : 3 * width, :])


def cut_out(wo_ref):
    rows, channels = wo_ref.shape
    return [wo_ref.at[i * channels : (i + 1) * channels, :] for i in range(rows // channels)]


def times_out(v, wo_refs):
    return jnp.concatenate([dot(v, wo_ref[...]) for wo_ref in wo_refs], axis=1)


def times_out_t(v, wo_refs):
    channels = wo_refs[0].shape[1]
    return sum(
        dot(v[:, i * channels : (i + 1) * channels], wo_ref[...], COLS)
        for i, wo_ref in enumerate(wo_refs)
    )


def put_columns(place_ref, span, mine_ref, other_ref, columns):
    per = columns.shape[0] // (NC * NZ)
    rows = mine_ref.shape[0] // NZ

    def place_columns(core, ref):
        for z in range(NZ):
            at = (core * NZ + z) * per
            ref[pl.ds(pl.multiple_of(z * rows + span * per, 16), per), :] = columns[at : at + per, :]

    for core in range(NC):
        mine = place_ref[0] == core

        @pl.when(mine)
        def _(core=core):
            place_columns(core, mine_ref)

        @pl.when(jnp.logical_not(mine))
        def _(core=core):
            place_columns(core, other_ref)


def forward_kernel(plans, head_dim, place_ref, *refs):
    last_layer = len(plans) == 2
    refs = list(refs)

    def take(count):
        taken = refs[:count]
        del refs[:count]
        return taken

    piece_refs = [take(count) for _, count in plans]
    w_here, w_there, wdt_ref, cx_ref, cbc_ref, head_ref = take(6)
    w_ref, xn_ref, wbc_ref, z_ref, xp_ref, bc_ref, dt_ref, y_ref, hin_ref, mine_ref, other_ref = take(11)
    if last_layer:
        g_ref, sums_ref, gg_ref = take(3)
    w_sem, xn_all, xbuf, bbuf, hst = take(5)
    if last_layer:
        [g_all] = take(1)
    length = z_ref.shape[0]
    channels = w_ref.shape[1]
    state = hst.shape[0]
    span = pl.program_id(0)
    wz_ref, wx_ref, *wo_refs = cut_weights(w_ref, xn_ref.shape[1])

    @pl.when(span == 0)
    def _():
        @pl.when(place_ref[2] == 1)
        def _():
            pltpu.make_async_copy(w_here, w_ref, w_sem).start()

        @pl.when(place_ref[2] == 0)
        def _():
            pltpu.make_async_copy(w_there, w_ref, w_sem).start()

        if last_layer:
            place_pieces(plans[0][0], place_ref, piece_refs[0], [xn_all])
            place_pieces(plans[1][0], place_ref, piece_refs[1], [g_all, wbc_ref])
        else:
            place_pieces(plans[0][0], place_ref, piece_refs[0], [xn_all, wbc_ref])
        xbuf[0:8, :] = jnp.zeros((8, channels), f32)
        bbuf[0:8, :] = jnp.zeros((8, 2 * state), f32)
        hst[...] = jnp.zeros_like(hst)
        pltpu.make_async_copy(w_here, w_ref, w_sem).wait()

    here = pl.ds(pl.multiple_of(span * length, length), length)
    xn = xn_all[here, :]
    xn_ref[...] = xn
    z = dot(xn, wz_ref[...])
    z_ref[...] = z
    xp = dot(xn, wx_ref[...])
    xp_ref[...] = xp
    xbuf[8:, :] = xp
    bc = dot(xn, wbc_ref[...], COLS).astype(bf16)
    bc_ref[...] = bc
    bbuf[8:, :] = bc.astype(f32)
    dt = dot(xn, wdt_ref[...], COLS)
    dt_ref[...] = dt

    pre_x = conv_taps(xbuf, cx_ref[0:4, :], cx_ref[4:5, :], length)
    xc = pre_x * sigmoid(pre_x)
    pre_bc = conv_taps(bbuf, cbc_ref[0:4, :], cbc_ref[4:5, :], length)
    bcc = (pre_bc * sigmoid(pre_bc)).astype(bf16)
    xbuf[0:8, :] = xbuf[length : length + 8, :]
    bbuf[0:8, :] = bbuf[length : length + 8, :]
    b_mat = bcc[:, :state]
    c_mat = bcc[:, state:]

    mask, _, step, _, cum = span_values(dt, head_ref)
    cum_t = jnp.transpose(cum)
    scores = dot(c_mat, b_mat, COLS)
    xs = xc * spread_heads(step, channels, head_dim)
    xs_b = xs.astype(bf16)
    lane = lax.broadcasted_iota(jnp.int32, (length, LANES), 1)
    per_tile = LANES // head_dim
    tiles = []
    for tile in range(channels // LANES):
        xs_tile = xs_b[:, tile * LANES : (tile + 1) * LANES]
        out = None
        for sub in range(per_tile):
            head = tile * per_tile + sub
            decay = decay_matrix(mask, cum[:, head : head + 1], cum_t[head : head + 1, :])
            part = dot((scores * decay).astype(bf16), xs_tile)
            out = part if out is None else jnp.where(lane >= sub * head_dim, part, out)
        tiles.append(out)
    hin = hst[...]
    hin_ref[0] = hin
    last = cum[length - 1 : length, :]
    y = jnp.concatenate(tiles, axis=1)
    y = y + dot(c_mat, hin.astype(bf16)) * spread_heads(jnp.exp(cum), channels, head_dim)
    y = y + cx_ref[6:7, :] * xc
    y_ref[...] = y
    tail = spread_heads(jnp.exp(last - cum), channels, head_dim)
    keep = spread_heads(jnp.exp(last), channels, head_dim)
    hst[...] = keep * hin + dot(b_mat, (tail * xs).astype(bf16), ROWS)

    gated = y * (z * sigmoid(z))
    scaled = gated * cx_ref[5:6, :]
    squares = jnp.sum(gated * gated, axis=1, keepdims=True)
    high = squares.astype(bf16).astype(f32)
    extra = jnp.where(lane == 0, high, jnp.where(lane == 1, squares - high, 0.0)).astype(bf16)
    mixed = times_out(scaled.astype(bf16), wo_refs).astype(bf16)
    put_half(
        place_ref,
        span,
        pl.num_programs(0) // 2,
        mine_ref,
        other_ref,
        jnp.concatenate([mixed, extra], axis=1),
    )
    if last_layer:
        g = g_all[here, :]
        g_ref[...] = g
        gg = times_out_t(g, wo_refs)
        gg_ref[...] = gg
        products = jnp.sum(gg * scaled, axis=1, keepdims=True)
        both = jnp.where(lane == 0, squares, jnp.where(lane == 1, products, 0.0))
        sums_ref[...] = jnp.transpose(both)[0:8, :]


def gate_part(gg, rms, coef, z, y, cx_ref):
    norm_gate = cx_ref[5:6, :]
    sz = sigmoid(z)
    silu_z = z * sz
    gated = y * silu_z
    rg = rms * gg
    gate_out = (gated * rms * norm_gate).astype(bf16)
    d_gated = rg * norm_gate - gated * coef
    dz = (d_gated * y * (sz * (1.0 + z * (1.0 - sz)))).astype(bf16)
    return dz, d_gated * silu_z, gate_out, jnp.sum(rg * gated, axis=0, keepdims=True)


def gate_kernel(plan, n_pieces, width, place_ref, *refs):
    pieces = refs[:n_pieces]
    z_ref, y_ref, wo_ref, cx_ref, g_ref, dz_ref, dy_ref, go_ref, acc_ref, first_all = refs[n_pieces:]
    length = z_ref.shape[0]
    span = pl.program_id(0)

    @pl.when(span == 0)
    def _():
        place_pieces(plan, place_ref, pieces, [first_all])
        acc_ref[...] = jnp.zeros_like(acc_ref)

    first = first_all[pl.ds(pl.multiple_of(span * length, length), length), :]
    g = first[:, :width]
    g_ref[...] = g
    tok = first[:, width:].astype(f32)
    rms = tok[:, 0:1] + tok[:, 1:2]
    coef = tok[:, 2:3] + tok[:, 3:4]
    gg = times_out_t(g, cut_out(wo_ref))
    dz, dy, gate_out, acc_norm = gate_part(gg, rms, coef, z_ref[...], y_ref[...], cx_ref)
    dz_ref[...] = dz
    dy_ref[...] = dy
    go_ref[...] = gate_out
    acc_ref[5:6, :] += acc_norm


def last_gate_kernel(inner_all, place_ref, gg_ref, tok_ref, z_ref, y_ref, cx_ref, dz_ref, dy_ref, go_ref, acc_ref):
    @pl.when(pl.program_id(0) == 0)
    def _():
        acc_ref[...] = jnp.zeros_like(acc_ref)

    tok = jnp.transpose(tok_ref[...])
    rms = lax.rsqrt(tok[:, 0:1] / inner_all + EPS)
    coef = rms * rms * rms * tok[:, 1:2] / inner_all
    dz, dy, gate_out, acc_norm = gate_part(gg_ref[...], rms, coef, z_ref[...], y_ref[...], cx_ref)
    dz_ref[...] = dz
    dy_ref[...] = dy
    go_ref[...] = gate_out
    acc_ref[5:6, :] += acc_norm


def scan_kernel(head_dim, place_ref, *refs):
    (dy_ref, dz_ref, xn_ref, xp_ref, xhalo_ref, bc_ref, bchalo_ref, dt_ref, hin_ref,
     w_ref, wbc_ref, wdt_ref, cx_ref, cbc_ref, head_ref, pick_ref,
     dxt_ref, bcmine_ref, bcother_ref, mine_ref, other_ref, acc_ref, acch_ref, shared_ref,
     accbc, accn, xbuf, bbuf, dubuf, dubbuf, dhst) = refs
    length = xp_ref.shape[0]
    channels = w_ref.shape[1]
    width = xn_ref.shape[1]
    state = dhst.shape[0]
    step_id = pl.program_id(0)
    first_span = step_id == pl.num_programs(0) - 1

    @pl.when(step_id == 0)
    def _():
        dubuf[length:, :] = jnp.zeros((8, channels), f32)
        dubbuf[length:, :] = jnp.zeros((8, 2 * state), f32)
        dhst[...] = jnp.zeros_like(dhst)
        accn[...] = jnp.zeros_like(accn)
        acc_ref[...] = jnp.zeros_like(acc_ref)
        accbc[...] = jnp.zeros_like(accbc)
        acch_ref[...] = jnp.zeros_like(acch_ref)

    @pl.when(first_span)
    def _():
        xbuf[0:8, :] = jnp.zeros((8, channels), f32)
        bbuf[0:8, :] = jnp.zeros((8, 2 * state), f32)

    @pl.when(jnp.logical_not(first_span))
    def _():
        xbuf[0:8, :] = xhalo_ref[...]
        bbuf[0:8, :] = bchalo_ref[...].astype(f32)[8:16, :]

    xbuf[8:, :] = xp_ref[...]
    bbuf[8:, :] = bc_ref[...].astype(f32)
    dz_b, dy = dz_ref[...], dy_ref[...]
    skip = cx_ref[6:7, :]

    pre_x = conv_taps(xbuf, cx_ref[0:4, :], cx_ref[4:5, :], length)
    sx = sigmoid(pre_x)
    xc = pre_x * sx
    pre_bc = conv_taps(bbuf, cbc_ref[0:4, :], cbc_ref[4:5, :], length)
    sbc = sigmoid(pre_bc)
    bcc = (pre_bc * sbc).astype(bf16)
    b_mat = bcc[:, :state]
    c_mat = bcc[:, state:]
    mask, pre_dt, step, rate, cum = span_values(dt_ref[...], head_ref)
    cum_t = jnp.transpose(cum)
    last = cum[length - 1 : length, :]
    scores = dot(c_mat, b_mat, COLS)
    step_all = spread_heads(step, channels, head_dim)
    xs = xc * step_all
    xs_b = xs.astype(bf16)
    tail = spread_heads(jnp.exp(last - cum), channels, head_dim)
    keep = spread_heads(jnp.exp(last), channels, head_dim)

    hin = hin_ref[0]
    hin_b = hin.astype(bf16)
    dh = dhst[...]
    dh_b = dh.astype(bf16)
    dye = dy * spread_heads(jnp.exp(cum), channels, head_dim)
    dye_b = dye.astype(bf16)
    txs = tail * xs
    txs_b = txs.astype(bf16)
    carried = dot(c_mat, hin_b)
    pulled = dot(b_mat, dh_b)
    d_c = dot(dye_b, hin_b, COLS)
    d_b = dot(txs_b, dh_b, COLS)
    dhst[...] = keep * dh + dot(c_mat, dye_b, ROWS)
    into = txs * pulled
    across = dye * carried - into
    at_last = jnp.sum(into, axis=0, keepdims=True) + keep * jnp.sum(hin * dh, axis=0, keepdims=True)

    dy_b = dy.astype(bf16)
    dy_t = jnp.transpose(dy).astype(bf16)
    lane = lax.broadcasted_iota(jnp.int32, (length, LANES), 1)
    per_tile = LANES // head_dim
    d_scores = jnp.zeros((length, length), f32)
    row_sums = jnp.zeros((length, LANES), f32)
    col_sums = []
    dxs_parts = []
    for head in range(channels // head_dim):
        tile, sub = divmod(head, per_tile)
        dy_tile = dy_b[:, tile * LANES : (tile + 1) * LANES]
        own = (lane >= sub * head_dim) & (lane < (sub + 1) * head_dim)
        dy_head = jnp.where(own, dy_tile, jnp.zeros_like(dy_tile))
        d_m = dot(dy_head, xs_b[:, tile * LANES : (tile + 1) * LANES], COLS)
        decay = decay_matrix(mask, cum[:, head : head + 1], cum_t[head : head + 1, :])
        dxs_parts.append(
            dot(dy_t[head * head_dim : (head + 1) * head_dim, :], (scores * decay).astype(bf16))
        )
        d_m = d_m * decay
        d_scores = d_scores + d_m
        pairs = d_m * scores
        row_sums = jnp.where(lane == head, jnp.sum(pairs, axis=1, keepdims=True), row_sums)
        col_sums.append(jnp.sum(pairs, axis=0, keepdims=True))
    heads = len(col_sums)
    col_sums = jnp.concatenate(col_sums + [jnp.zeros((LANES - heads, length), f32)], axis=0)
    dxs = jnp.transpose(jnp.concatenate(dxs_parts, axis=0)) + tail * pulled
    pick = pick_ref[...]
    d_cum = row_sums - jnp.transpose(col_sums) + dot(across, pick, PLAIN, highest)
    at_last = dot(jnp.broadcast_to(at_last, (8, channels)), pick, PLAIN, highest)[0:1, :]
    d_rate = dot(mask.astype(f32), d_cum, ROWS, highest) + at_last
    d_step = d_rate * head_ref[1:2, :] + dot(dxs * xc, pick, PLAIN, highest)
    d_dt = d_step * sigmoid(pre_dt)
    acch_ref[0:1, :] += jnp.sum(d_dt, axis=0, keepdims=True)
    acch_ref[1:2, :] += jnp.sum(d_rate * rate, axis=0, keepdims=True)
    dt_b = d_dt.astype(bf16)
    ds_b = d_scores.astype(bf16)
    d_c = d_c + dot(ds_b, b_mat)
    d_b = d_b + dot(ds_b, c_mat, ROWS)
    d_xc = dxs * step_all + skip * dy
    acc_skip = jnp.sum(dy * xc, axis=0, keepdims=True)

    d_u = d_xc * (sx * (1.0 + pre_x * (1.0 - sx)))
    d_ub = jnp.concatenate([d_b, d_c], axis=1) * (sbc * (1.0 + pre_bc * (1.0 - sbc)))
    dubuf[0:length, :] = d_u
    dubbuf[0:length, :] = d_ub
    d_x = jnp.zeros_like(d_u)
    d_bc = jnp.zeros_like(d_ub)
    acc_rows = []
    accbc_rows = []
    for j in range(4):
        d_x = d_x + cx_ref[j : j + 1, :] * dubuf[pl.ds(3 - j, length), :]
        d_bc = d_bc + cbc_ref[j : j + 1, :] * dubbuf[pl.ds(3 - j, length), :]
        acc_rows.append(jnp.sum(d_u * xbuf[pl.ds(5 + j, length), :], axis=0, keepdims=True))
        accbc_rows.append(jnp.sum(d_ub * bbuf[pl.ds(5 + j, length), :], axis=0, keepdims=True))
    dubuf[length:, :] = d_u[0:8, :]
    dubbuf[length:, :] = d_ub[0:8, :]
    zero = jnp.zeros((1, channels), f32)
    acc_ref[...] += jnp.concatenate(
        acc_rows + [jnp.sum(d_u, axis=0, keepdims=True), zero, acc_skip, zero], axis=0
    )
    zero = jnp.zeros((3, d_ub.shape[1]), f32)
    accbc[...] += jnp.concatenate(
        accbc_rows + [jnp.sum(d_ub, axis=0, keepdims=True), zero], axis=0
    )
    dx_b = d_x.astype(bf16)
    dbc_b = d_bc.astype(bf16)
    dxt_ref[:, :channels] = dx_b
    dxt_ref[:, channels:] = dt_b
    put_columns(
        place_ref,
        pl.num_programs(0) - 1 - step_id,
        bcmine_ref,
        bcother_ref,
        jnp.transpose(d_bc).astype(bf16),
    )
    total = dot(dz_b, w_ref[0:width, :], COLS) + dot(dx_b, w_ref[width : 2 * width, :], COLS)
    total = total + dot(dbc_b, wbc_ref[...]) + dot(dt_b, wdt_ref[...])
    accn[0:1, :] += jnp.sum(total * xn_ref[...].astype(f32), axis=0, keepdims=True)

    @pl.when(first_span)
    def _():
        lanes = shared_ref.shape[1]
        lines = [accn[0:1, i * lanes : (i + 1) * lanes] for i in range(width // lanes)]
        shared = jnp.concatenate(lines + [accbc[0:5, :]], axis=0)
        shared_ref[0 : shared.shape[0], :] = shared.astype(bf16)
        shared_ref[shared.shape[0] :, :] = jnp.zeros(
            (shared_ref.shape[0] - shared.shape[0], lanes), bf16
        )

    put_half(
        place_ref,
        pl.num_programs(0) - 1 - step_id,
        pl.num_programs(0) // 2,
        mine_ref,
        other_ref,
        total.astype(bf16),
    )


def whole(shape):
    zeros = (0,) * len(shape)
    return pl.BlockSpec(shape, lambda i, p: zeros)


def span_rows(columns):
    return pl.BlockSpec((SPAN, columns), lambda i, p: (i, 0))


def half_rows(columns, spans, reverse):
    half = spans // 2

    def block(i, core):
        span = spans - 1 - i if reverse else i
        return jnp.clip(span - half * core, 0, half - 1), 0

    return [
        pl.BlockSpec((SPAN, columns), lambda i, p: block(i, p[0])),
        pl.BlockSpec((SPAN, columns), lambda i, p: block(i, 1 - p[0])),
    ]


def span_call(kernel, name, spans, place, operands, in_specs, shapes, out_specs, scratch, flops):
    moved = sum(v.size * v.dtype.itemsize for v in [*operands, *shapes])
    return pl.pallas_call(
        kernel,
        grid_spec=pltpu.PrefetchScalarGridSpec(
            num_scalar_prefetch=1,
            grid=(spans,),
            in_specs=in_specs,
            out_specs=out_specs,
            scratch_shapes=scratch,
        ),
        out_shape=shapes,
        compiler_params=pltpu.CompilerParams(
            dimension_semantics=("arbitrary",), vmem_limit_bytes=VMEM_BYTES
        ),
        cost_estimate=pl.CostEstimate(flops=flops, bytes_accessed=moved, transcendentals=0),
        name=name,
    )(place, *operands)


def run_forward(place, gathered, weights, small, state, head_dim):
    channels = weights[0].shape[1]
    width = gathered[0][0][0].shape[1]
    anywhere = pl.BlockSpec(memory_space=pl.ANY)
    tokens = NC * NZ * gathered[0][2][0]
    spans = tokens // SPAN
    last_layer = len(gathered) == 2
    plans = [(cut_plan(*one), len(one[0])) for one in gathered]
    operands = [p for one in gathered for p in one[0]]
    in_specs = [whole(v.shape) for v in operands] + [anywhere] * 2
    operands += [*weights, *small]
    in_specs += [whole(v.shape) for v in operands[len(in_specs) :]]
    shapes = [
        jax.ShapeDtypeStruct(weights[0].shape, bf16),
        jax.ShapeDtypeStruct((tokens, width), bf16),
        jax.ShapeDtypeStruct((2 * state, width), bf16),
        jax.ShapeDtypeStruct((tokens, channels), f32),
        jax.ShapeDtypeStruct((tokens, channels), f32),
        jax.ShapeDtypeStruct((tokens, 2 * state), bf16),
        jax.ShapeDtypeStruct((tokens, LANES), f32),
        jax.ShapeDtypeStruct((tokens, channels), f32),
        jax.ShapeDtypeStruct((spans, state, channels), f32),
        jax.ShapeDtypeStruct((tokens // 2, width + LANES), bf16),
        jax.ShapeDtypeStruct((tokens // 2, width + LANES), bf16),
    ]
    out_specs = [whole(weights[0].shape), span_rows(width), whole((2 * state, width))]
    out_specs += [span_rows(s.shape[1]) for s in shapes[3:8]]
    out_specs.append(pl.BlockSpec((1, state, channels), lambda i, p: (i, 0, 0)))
    out_specs += half_rows(width + LANES, spans, False)
    scratch = [
        pltpu.SemaphoreType.DMA,
        pltpu.VMEM((tokens, width), bf16),
        pltpu.VMEM((SPAN + 8, channels), f32),
        pltpu.VMEM((SPAN + 8, 2 * state), f32),
        pltpu.VMEM((state, channels), f32),
    ]
    if last_layer:
        shapes += [
            jax.ShapeDtypeStruct((tokens, width), bf16),
            jax.ShapeDtypeStruct((8, tokens), f32),
            jax.ShapeDtypeStruct((tokens, channels), f32),
        ]
        out_specs += [span_rows(width), pl.BlockSpec((8, SPAN), lambda i, p: (0, i)), span_rows(channels)]
        scratch.append(pltpu.VMEM((tokens, width), bf16))
    kernel = functools.partial(forward_kernel, plans, head_dim)
    return span_call(
        kernel, "layer_forward", spans, place, operands, in_specs, shapes, out_specs, scratch, 20 * 10**9
    )


def run_gate(place, gathered, z, y, w, cx):
    tokens, channels = z.shape
    width = w.shape[0] // 3
    spans = tokens // SPAN
    plan, pieces = cut_plan(*gathered), list(gathered[0])
    operands = [*pieces, z, y, w, cx]
    in_specs = [whole(p.shape) for p in pieces]
    in_specs += [span_rows(channels), span_rows(channels)]
    in_specs += [pl.BlockSpec((width, channels), lambda i, p: (2, 0)), whole(cx.shape)]
    shapes = [
        jax.ShapeDtypeStruct((tokens, width), bf16),
        jax.ShapeDtypeStruct((tokens, channels), bf16),
        jax.ShapeDtypeStruct((tokens, channels), f32),
        jax.ShapeDtypeStruct((tokens, channels), bf16),
        jax.ShapeDtypeStruct((8, channels), f32),
    ]
    out_specs = [span_rows(s.shape[1]) for s in shapes[:4]] + [whole(shapes[4].shape)]
    scratch = [pltpu.VMEM((tokens, pieces[0].shape[1]), bf16)]
    kernel = functools.partial(gate_kernel, plan, len(pieces), width)
    return span_call(
        kernel, "gate_backward", spans, place, operands, in_specs, shapes, out_specs, scratch, 6 * 10**9
    )


def run_last_gate(place, gg, sums, z, y, cx, inner_all):
    tokens, channels = z.shape
    spans = tokens // SPAN
    rows = span_rows(channels)
    shapes = [
        jax.ShapeDtypeStruct((tokens, channels), bf16),
        jax.ShapeDtypeStruct((tokens, channels), f32),
        jax.ShapeDtypeStruct((tokens, channels), bf16),
        jax.ShapeDtypeStruct((8, channels), f32),
    ]
    return span_call(
        functools.partial(last_gate_kernel, inner_all),
        "last_gate_backward",
        spans,
        place,
        [gg, sums, z, y, cx],
        [rows, pl.BlockSpec((8, SPAN), lambda i, p: (0, i)), rows, rows, whole(cx.shape)],
        shapes,
        [rows, rows, rows, whole(shapes[3].shape)],
        [],
        10**9,
    )


def run_scan(place, dy, dz, xn, xp, bc, dt, hin, weights, small, pick, head_dim):
    tokens, channels = xp.shape
    state = hin.shape[1]
    width = xn.shape[1]
    spans = tokens // SPAN

    def rev(columns):
        return pl.BlockSpec((SPAN, columns), lambda i, p: (spans - 1 - i, 0))

    def halo(columns, rows):
        per = SPAN // rows
        return pl.BlockSpec(
            (rows, columns), lambda i, p: (jnp.maximum((spans - 1 - i) * per - 1, 0), 0)
        )

    operands = [dy, dz, xn, xp, xp, bc, bc, dt, hin, *weights, *small, pick]
    in_specs = [
        rev(channels),
        rev(channels),
        rev(width),
        rev(channels),
        halo(channels, 8),
        rev(2 * state),
        halo(2 * state, 16),
        rev(LANES),
        pl.BlockSpec((1, state, channels), lambda i, p: (spans - 1 - i, 0, 0)),
    ]
    in_specs.append(whole((2 * width, channels)))
    in_specs += [whole(v.shape) for v in operands[len(in_specs) :]]
    shapes = [
        jax.ShapeDtypeStruct((tokens, channels + LANES), bf16),
        jax.ShapeDtypeStruct((state * spans, SPAN), bf16),
        jax.ShapeDtypeStruct((state * spans, SPAN), bf16),
        jax.ShapeDtypeStruct((tokens // 2, width), bf16),
        jax.ShapeDtypeStruct((tokens // 2, width), bf16),
        jax.ShapeDtypeStruct((8, channels), f32),
        jax.ShapeDtypeStruct((8, LANES), f32),
        jax.ShapeDtypeStruct((16, 2 * state), bf16),
    ]
    out_specs = [rev(channels + LANES), whole(shapes[1].shape), whole(shapes[2].shape)]
    out_specs += half_rows(width, spans, True)
    out_specs += [whole(s.shape) for s in shapes[5:]]
    scratch = [
        pltpu.VMEM((8, 2 * state), f32),
        pltpu.VMEM((8, width), f32),
        pltpu.VMEM((SPAN + 8, channels), f32),
        pltpu.VMEM((SPAN + 8, 2 * state), f32),
        pltpu.VMEM((SPAN + 8, channels), f32),
        pltpu.VMEM((SPAN + 8, 2 * state), f32),
        pltpu.VMEM((state, channels), f32),
    ]
    kernel = functools.partial(scan_kernel, head_dim)
    return span_call(
        kernel, "scan_backward", spans, place, operands, in_specs, shapes, out_specs, scratch, 28 * 10**9
    )


def weight_kernel(pairs, *refs):
    lefts, rights, out_ref = refs[: len(pairs)], refs[len(pairs) : -1], refs[-1]
    at = 0
    for left_ref, right_ref in zip(lefts, rights):
        columns = right_ref.shape[1]
        out_ref[:, at : at + columns] = dot(left_ref[...], right_ref[...], ROWS).astype(bf16)
        at += columns


def weight_products(pairs):
    tokens = pairs[0][0].shape[0]
    rows = max(left.shape[1] for left, _ in pairs)
    block = rows // 4
    lefts, rights, columns = [], [], []
    for left, right in pairs:
        quarter = left.shape[1] == block
        lefts.append(pl.BlockSpec((tokens, block), (lambda i: (0, 0)) if quarter else (lambda i: (0, i))))
        wide = block if quarter else right.shape[1]
        rights.append(pl.BlockSpec((tokens, wide), (lambda i: (0, i)) if quarter else (lambda i: (0, 0))))
        columns.append(wide)
    return pl.pallas_call(
        functools.partial(weight_kernel, pairs_of(columns)),
        grid=(4,),
        in_specs=lefts + rights,
        out_specs=pl.BlockSpec((block, sum(columns)), lambda i: (i, 0)),
        out_shape=jax.ShapeDtypeStruct((rows, sum(columns)), bf16),
        compiler_params=pltpu.CompilerParams(vmem_limit_bytes=VMEM_BYTES),
        cost_estimate=pl.CostEstimate(
            flops=2 * tokens * rows * sum(columns), bytes_accessed=8 * 10**6, transcendentals=0
        ),
        name="weight_products",
    )(*[left for left, _ in pairs], *[right for _, right in pairs])


def pairs_of(columns):
    return tuple(columns)


SIZES = (4, 2, 2, 2, 4)
NX, NYL, NC, NYH, NZ = SIZES
EVERY = [
    (x, yl, c, yh, z)
    for x in range(NX)
    for yl in range(NYL)
    for c in range(NC)
    for yh in range(NYH)
    for z in range(NZ)
]


def linear(x, yl, c, yh, z):
    return ((((x % NX) * NYL + yl % NYL) * NC + c % NC) * NYH + yh % NYH) * NZ + z % NZ


def send(v, step, only=None):
    pairs = [(linear(*d), linear(*step(*d))) for d in EVERY if only is None or only(*d)]
    return lax.ppermute(v, ("dp", "tensor"), pairs)


def send_z(v, k):
    return send(v, lambda x, yl, c, yh, z: (x, yl, c, yh, z + k))


def send_core(v):
    return send(v, lambda x, yl, c, yh, z: (x, yl, c + 1, yh, z))


def trade(v, k):
    return send(v, lambda x, yl, c, yh, z: (x, yl, yh, c, z + k))


def traded(v):
    return send(v, lambda x, yl, c, yh, z: (x, yl, yh, c, z), lambda x, yl, c, yh, z: c != yh)


def trade_places(v):
    _, _, core, yh, _ = position()
    return jnp.where(core == yh, v, traded(v))


def position():
    dp, tensor = lax.axis_index("dp"), lax.axis_index("tensor")
    return dp // (NYL * NC), dp // NC % NYL, dp % NC, tensor // NZ, tensor % NZ


def gather(v, parts, away=False):
    arrays, sources = [], []
    for k in (0, 1, 3, 2):
        if away:
            piece = trade(v, k) if k else trade_places(v)
        else:
            piece = send_z(v, k) if k else v
        arrays += [piece, send_core(piece)]
        sources += [(False, -k % NZ, 0), (True, -k % NZ, 0)]
    return arrays, sources, parts


def cut_plan(arrays, sources, parts):
    plan = []
    for number, (piece, (other, dz, first)) in enumerate(zip(arrays, sources)):
        base = 0
        for out, per in enumerate(parts):
            begin, end = max(first, base), min(first + piece.shape[0], base + per)
            if begin < end:
                plan.append((number, other, dz, begin - first, out, per, begin - base, end - begin))
            base += per
    return plan


def fold(mine, other):
    _, _, _, _, z = position()
    rows = mine.shape[0] // NZ
    blocks = []
    for k in range(NZ):
        at = (z + k) % NZ * rows
        a = lax.dynamic_slice_in_dim(mine, at, rows, 0).astype(f32)
        blocks.append(a + lax.dynamic_slice_in_dim(other, at, rows, 0).astype(f32))
    return blocks


def fold_beside(pairs):
    folded = [fold(mine, send_core(other)) for mine, other in pairs]
    return [jnp.concatenate([blocks[k] for blocks in folded], axis=1) for k in range(NZ)]


def scatter(*pairs):
    own, one, two, three = fold_beside(pairs)
    return [own] + [send_z(b.astype(bf16), k) for k, b in ((1, one), (2, two), (3, three))]


def scatter_with_sum(mine, other, shared, meanwhile):
    half = mine.shape[0]
    rows = half // NZ
    got = after(send_core(jnp.concatenate([other, shared], axis=0)), *meanwhile)
    blocks = fold(mine, got[:half])
    total_shared = shared.astype(f32) + got[half:].astype(f32)
    packed = total_shared.astype(bf16)
    total = blocks[0]
    for k in range(1, NZ):
        got = send_z(jnp.concatenate([blocks[k].astype(bf16), packed], axis=0), k)
        total = total + got[:rows].astype(f32)
        total_shared = total_shared + got[rows:].astype(f32)
    return total, total_shared


def sum_members(v):
    both = v + send_core(v)
    total = both
    for k in range(1, NZ):
        total = total + send_z(both, k)
    return total


def sum_far(v):
    far = send(v, lambda x, yl, c, yh, z: (x, yl, c, yh + 1, z), lambda x, yl, c, yh, z: c != yh)
    return (v.astype(f32) + far.astype(f32)).astype(bf16)


def halve(v):
    _, _, core, yh, _ = position()
    half = v.shape[0] // 2
    near = send(
        v[half:], lambda x, yl, c, yh, z: (x, yl, c + 1, yh, z), lambda x, yl, c, yh, z: c == yh
    )
    return jnp.where(core == yh, v[:half], near)


def sum_beside(part):
    beside = send(part, lambda x, yl, c, yh, z: (x, yl + 1, c, yh, z))
    return (part.astype(f32) + beside.astype(f32)).astype(bf16)


def sum_x(v):
    x = position()[0]
    rows = v.shape[0] // NX
    total = lax.dynamic_slice_in_dim(v, x * rows, rows, 0).astype(f32)
    for k in range(1, NX):
        block = lax.dynamic_slice_in_dim(v, (x + k) % NX * rows, rows, 0)
        total = total + send(block, lambda x, yl, c, yh, z, k=k: (x + k, yl, c, yh, z)).astype(f32)
    return total.astype(bf16)


def collect_x(part):
    x = position()[0]
    out = jnp.zeros((NX,) + part.shape, bf16)
    out = lax.dynamic_update_index_in_dim(out, part, x, 0)
    for k in range(1, NX):
        block = send(part, lambda x, yl, c, yh, z, k=k: (x + k, yl, c, yh, z))
        out = lax.dynamic_update_index_in_dim(out, block, (x - k) % NX, 0)
    return out


def collect(part):
    out = collect_x(part)
    return out, send_core(out)


def write_kernel(columns, by_half, n_kept, place_ref, here_ref, there_ref, *refs):
    low = pl.program_id(1) if not by_half else pl.program_id(0)
    here = (low == 0) == (place_ref[2] == 1)
    for column, out_ref in zip(columns, refs[n_kept:]):
        at = slice(column, column + out_ref.shape[-1])

        @pl.when(here)
        def _(out_ref=out_ref, at=at):
            out_ref[...] = here_ref[0, :, at].astype(f32).reshape(out_ref.shape)

        @pl.when(jnp.logical_not(here))
        def _(out_ref=out_ref, at=at):
            out_ref[...] = there_ref[0, :, at].astype(f32).reshape(out_ref.shape)


def write_sums(place, halves, by_half, outputs):
    rows = halves[0].shape[1]
    total = 2 * NX * rows
    grid = (2, NX) if by_half else (NX, 2)

    def block(i, j):
        return i * grid[1] + j

    columns, shapes, specs, kept, alias = [], [], [], [], {}
    for column, kind, layer, array in outputs:
        columns.append(column)
        if kind == "flat":
            shapes.append(jax.ShapeDtypeStruct((total, LANES), f32))
            specs.append(pl.BlockSpec((rows, LANES), lambda i, j, p: (block(i, j), 0)))
        else:
            wide = total // 4
            if kind == "rows":
                shapes.append(jax.ShapeDtypeStruct((2, total, wide), f32))
                specs.append(
                    pl.BlockSpec((1, rows, wide), lambda i, j, p, layer=layer: (layer, block(i, j), 0))
                )
            else:
                per = wide // rows
                shapes.append(jax.ShapeDtypeStruct((2, wide, total), f32))
                specs.append(
                    pl.BlockSpec(
                        (1, rows, wide),
                        lambda i, j, p, layer=layer: (layer, block(i, j) % per, block(i, j) // per),
                    )
                )
        if array is not None:
            alias[3 + len(kept)] = len(shapes) - 1
            kept.append(array)
    piece = pl.BlockSpec((1, rows, halves[0].shape[2]), lambda i, j, p: (j if by_half else i, 0, 0))
    return pl.pallas_call(
        functools.partial(write_kernel, columns, by_half, len(kept)),
        grid_spec=pltpu.PrefetchScalarGridSpec(
            num_scalar_prefetch=1,
            grid=grid,
            in_specs=[piece, piece] + [pl.BlockSpec(memory_space=pl.ANY)] * len(kept),
            out_specs=specs,
        ),
        out_shape=shapes,
        input_output_aliases=alias,
        compiler_params=pltpu.CompilerParams(vmem_limit_bytes=VMEM_BYTES),
        name="write_sums",
    )(place, *halves, *kept)


def row_call(kernel, name, operands, shapes):
    return pl.pallas_call(
        kernel,
        grid=(1,),
        in_specs=[pl.BlockSpec((rows, v.shape[1]), lambda i: (0, 0)) for v, rows in operands],
        out_specs=[pl.BlockSpec(s.shape, lambda i: (0, 0)) for s in shapes],
        out_shape=shapes,
        compiler_params=pltpu.CompilerParams(vmem_limit_bytes=VMEM_BYTES),
        name=name,
    )(*[v for v, _ in operands])


def inverse_rms(v):
    return lax.rsqrt(jnp.mean(v * v, axis=-1, keepdims=True) + EPS)


def first_kernel(packed_ref, gain_ref, out_ref):
    rows = 128
    v = packed_ref[0:rows, :].astype(f32)
    out_ref[0:rows, :] = (v * inverse_rms(v) * gain_ref[...]).astype(bf16)
    out_ref[rows:, :] = packed_ref[rows : out_ref.shape[0], :]


def add_terms(own_ref, a_ref, b_ref, c_ref):
    total = own_ref[...].astype(f32) + a_ref[...].astype(f32)
    return total + (b_ref[...].astype(f32) + c_ref[...].astype(f32))


def unscaled_output(inner_all, terms, width):
    total = add_terms(*terms)
    squares = total[:, width : width + 1] + total[:, width + 1 : width + 2]
    gate_rms = lax.rsqrt(squares / inner_all + EPS)
    return gate_rms, total[:, :width] * gate_rms


def middle_kernel(inner_all, own_ref, a_ref, b_ref, c_ref, res_ref, gain_ref, res1_ref, mixed_ref, rms_ref, normed_ref):
    width = res_ref.shape[1]
    gate_rms, mixed = unscaled_output(inner_all, (own_ref, a_ref, b_ref, c_ref), width)
    res = res_ref[...].astype(f32) + mixed
    res1_ref[...] = res
    mixed_ref[...] = mixed
    rms_ref[...] = jnp.broadcast_to(gate_rms, rms_ref.shape)
    normed_ref[...] = (res * inverse_rms(res) * gain_ref[...]).astype(bf16)


def input_gradient(grad_normed, res, d_res, gain):
    inv = inverse_rms(res)
    scaled = grad_normed * gain
    dots = jnp.sum(scaled * res, axis=-1, keepdims=True) / res.shape[1]
    return d_res + inv * scaled - res * (inv * inv * inv) * dots


def between_kernel(inner_all, own_ref, a_ref, b_ref, c_ref, res_ref, dres_ref, gain_ref, mixed_ref, rms_ref, out_ref, sent_ref):
    width = res_ref.shape[1]
    grad_normed = add_terms(*(ref.at[:, 0:width] for ref in (own_ref, a_ref, b_ref, c_ref)))
    d_res = input_gradient(grad_normed, res_ref[...], dres_ref[...].astype(f32), gain_ref[...])
    out_ref[...] = d_res
    g_mixed = d_res.astype(bf16)
    sent_ref[:, :width] = g_mixed
    gate_rms = rms_ref[:, 0:1]
    products = jnp.sum(g_mixed.astype(f32) * mixed_ref[...], axis=-1, keepdims=True)
    coef = gate_rms * gate_rms * products / inner_all
    lane = lax.broadcasted_iota(jnp.int32, rms_ref.shape, 1)
    rms_high = gate_rms.astype(bf16).astype(f32)
    coef_high = coef.astype(bf16).astype(f32)
    extra = jnp.where(lane == 0, rms_high, jnp.where(lane == 1, gate_rms - rms_high, 0.0))
    extra = jnp.where(lane == 2, coef_high, jnp.where(lane == 3, coef - coef_high, extra))
    sent_ref[:, width:] = extra.astype(bf16)


def end_kernel(own_ref, a_ref, b_ref, c_ref, res_ref, dres_ref, gain_ref, hidden_ref, out_ref):
    width = res_ref.shape[1]
    grad_normed = add_terms(own_ref, a_ref, b_ref, c_ref)
    grad = input_gradient(grad_normed, res_ref[...].astype(f32), dres_ref[...], gain_ref[...])
    out_ref[:, :width] = hidden_ref[...]
    out_ref[:, width:] = grad.astype(bf16)


def last_kernel(inner_all, own_ref, a_ref, b_ref, c_ref, res_ref, out_ref):
    _, mixed = unscaled_output(inner_all, (own_ref, a_ref, b_ref, c_ref), res_ref.shape[1])
    out_ref[...] = (res_ref[...] + mixed).astype(bf16)


def after(v, *others):
    return lax.optimization_barrier((v, *others))[0]


def pad_to(v, rows, lanes):
    return jnp.pad(v, ((0, rows - v.shape[0]), (0, lanes - v.shape[1])))


def local(
    hidden_in,
    grad_out,
    norm_in,
    w_z,
    w_x,
    w_bc,
    w_dt,
    conv_x,
    conv_x_bias,
    conv_bc,
    conv_bc_bias,
    dt_bias,
    a_log,
    skip,
    norm_gate,
    w_out,
):
    layers, width, channels = w_z.shape
    heads = w_dt.shape[2]
    head_dim = channels // heads
    both = conv_bc.shape[2]
    state = both // 2
    members = NC * NZ
    inner_all = channels * members
    rows = hidden_in.shape[1]
    bc_rows = both // members
    _, _, core, yh, z = position()
    stays = core == yh
    place = jnp.stack([core, z, stays]).astype(jnp.int32)
    full = jax.ShapeDtypeStruct((rows, width), f32)

    bc_t = jnp.swapaxes(w_bc, 1, 2)
    dt_t = jnp.pad(jnp.swapaxes(w_dt, 1, 2), ((0, 0), (0, 8 - heads), (0, 0)))
    packed = jnp.concatenate([hidden_in[0], bc_t[0], dt_t.reshape(layers * 8, width)], axis=0)
    packed = trade_places(packed)
    per_channel = jnp.concatenate(
        [conv_x, conv_x_bias[:, None], norm_gate[:, None], jnp.repeat(skip, head_dim, axis=1)[:, None]],
        axis=1,
    )
    per_channel = jnp.pad(per_channel, ((0, 0), (0, 1), (0, 0)))
    per_head = jnp.stack([dt_bias, -jnp.exp(a_log)], axis=1)
    per_head = jnp.pad(per_head, ((0, 0), (0, 6), (0, LANES - heads)))
    little = jnp.concatenate([per_channel, per_head], axis=2).reshape(layers * 8, channels + LANES)
    little = trade_places(after(little, packed)).reshape(layers, 8, channels + LANES)

    def pack_weights(layer):
        quarters = [w_out[layer, :, i * channels : (i + 1) * channels] for i in range(width // channels)]
        return jnp.concatenate([w_z[layer], w_x[layer], *quarters], axis=0)

    w0 = pack_weights(0)
    w0 = w0, traded(after(w0, packed))

    [sent] = row_call(
        first_kernel,
        "first_norm",
        [(packed, packed.shape[0]), (norm_in[0:1], 1)],
        [jax.ShapeDtypeStruct((rows + bc_rows, width), bf16)],
    )
    gathered0 = gather(sent, (rows, bc_rows))
    wdt = [pad_to(packed[rows + bc_rows + 8 * l : rows + bc_rows + 8 * (l + 1)], LANES, width) for l in range(layers)]
    smalls = []
    for layer in range(layers):
        cbc = jnp.concatenate([conv_bc[layer], conv_bc_bias[layer][None], jnp.zeros((3, both), f32)], axis=0)
        smalls.append((little[layer, :, :channels], cbc, little[layer, :, channels:]))
    channel_head = jnp.arange(channels) // head_dim
    pick = (channel_head[:, None] == jnp.arange(LANES)[None, :]).astype(f32)

    out0 = run_forward(place, [gathered0], (*w0, wdt[0]), smalls[0], state, head_dim)
    w0, xn0, wbc0, z0, xp0, bc0, dt0, y0, hin0, mine, other = out0
    grads = jnp.concatenate([grad_out[0], bc_t[1]], axis=0)
    gathered_grad = gather(after(grads, *gathered0[0]), (rows, bc_rows), away=True)
    grad_held = gathered_grad[0][0]
    terms = scatter((mine, after(other, *gathered_grad[0][::2])))
    w1 = pack_weights(1)
    w1 = w1, traded(after(w1, mine))
    res1, mixed0, rms0, normed1 = row_call(
        functools.partial(middle_kernel, inner_all),
        "middle_norm",
        [(v, rows) for v in terms] + [(packed, rows), (norm_in[1:2], 1)],
        [full, full, jax.ShapeDtypeStruct((rows, LANES), f32), jax.ShapeDtypeStruct((rows, width), bf16)],
    )
    gathered1 = gather(normed1, (rows,))
    out1 = run_forward(
        place, [gathered1, gathered_grad], (*w1, wdt[1]), smalls[1], state, head_dim
    )
    w1, xn1, wbc1, z1, xp1, bc1, dt1, y1, hin1, mine, other, grad_rows1, sums, gg1 = out1
    sums = sum_members(sums)

    home = fold(mine, send_core(other))
    dz1, dy1, go1, acc_gate1 = run_last_gate(place, gg1, sums, z1, y1, smalls[1][0], inner_all)
    early1 = sum_far(weight_products([(xn1, dz1), (go1, grad_rows1)]))
    dy1 = after(dy1, *home)
    home = home[:1] + [send_z(home[k].astype(bf16), k) for k in range(1, NZ)]
    back1 = run_scan(
        place, dy1, dz1, xn1, xp1, bc1, dt1, hin1, (w1, wbc1, wdt[1]), smalls[1], pick, head_dim
    )
    dxt1, *bc_halves, mine, other, acc1, acch1, shared1 = back1
    terms = scatter((mine, after(other, early1, *home)), bc_halves)
    [hidden_out] = row_call(
        functools.partial(last_kernel, inner_all),
        "last_output",
        [(after(home[0], terms[1]), rows)] + [(v, rows) for v in home[1:]] + [(res1, rows)],
        [jax.ShapeDtypeStruct((rows, width), bf16)],
    )
    d_res1, sent = row_call(
        functools.partial(between_kernel, inner_all),
        "between_layers",
        [(v, rows) for v in terms]
        + [(res1, rows), (grad_held, rows), (norm_in[1:2], 1), (mixed0, rows), (rms0, rows)],
        [full, jax.ShapeDtypeStruct((rows, width + LANES), bf16)],
    )
    gathered_back = gather(sent, (rows,))
    early1 = sum_x(halve(after(early1, sent)))

    bc_at = channels + bc_rows

    def with_bc(dxt, bc_sum):
        by_token = bc_sum.reshape(-1, bc_rows, SPAN).swapaxes(1, 2).reshape(-1, bc_rows)
        spread = jnp.pad(by_token, ((0, 0), (bc_at, dxt.shape[1] - bc_at - bc_rows)))
        return dxt + spread.astype(bf16)

    dxt1 = with_bc(dxt1, sum(v[:, width:].astype(f32) for v in terms))

    z0 = after(z0, early1)
    grad_rows0, dz0, dy0, go0, acc_gate0 = run_gate(place, gathered_back, z0, y0, w0, smalls[0][0])
    early = weight_products([(xn0, dz0), (go0, grad_rows0), (xn1, dxt1)])
    dy0 = after(dy0, early)
    early = sum_x(early)
    early1 = sum_beside(after(early1, dz0))
    back0 = run_scan(
        place, dy0, dz0, xn0, xp0, bc0, dt0, hin0, (w0, wbc0, wdt[0]), smalls[0], pick, head_dim
    )
    dxt0, *bc_halves, mine, other, acc0, acch0, shared0 = back0
    halves = collect(after(early1, dxt0))
    g_wz, g_wo = write_sums(place, halves, True, [(0, "rows", 1, None), (channels, "blocks", 1, None)])

    terms = scatter((mine, other))
    [outputs] = row_call(
        end_kernel,
        "outputs",
        [(v, rows) for v in terms] + [(packed, rows), (d_res1, rows), (norm_in[0:1], 1), (hidden_out, rows)],
        [jax.ShapeDtypeStruct((rows, 2 * width), bf16)],
    )
    outputs = trade_places(outputs).astype(f32)

    shared = jnp.concatenate([shared0, shared1], axis=0)
    bc_sum, shared = scatter_with_sum(*bc_halves, shared, (early, early1))
    tiny = jnp.concatenate(
        [(acc0 + acc_gate0).reshape(-1), (acc1 + acc_gate1).reshape(-1), acch0[0:2].reshape(-1), acch1[0:2].reshape(-1)]
        + [shared.reshape(-1)]
    )
    tiny_at = bc_at + bc_rows
    tiny_lanes = channels + LANES - tiny_at
    tiny_size = tiny.shape[0]
    tiny = jnp.pad(tiny, (0, width * tiny_lanes - tiny_size)).reshape(width, tiny_lanes)
    late = weight_products([(xn0, with_bc(dxt0, bc_sum))])
    late = late + jnp.pad(tiny, ((0, 0), (tiny_at, 0))).astype(bf16)
    late = sum_beside(halve(sum_far(sum_x(late))))
    early = sum_beside(halve(sum_far(after(early, dxt0))))
    g_wz, g_wo, g_wx, narrow1 = write_sums(
        place,
        collect(early),
        False,
        [
            (0, "rows", 0, g_wz),
            (channels, "blocks", 0, g_wo),
            (2 * channels, "rows", 1, None),
            (3 * channels, "flat", 1, None),
        ],
    )
    g_wx, narrow0 = write_sums(
        place, collect(late), False, [(0, "rows", 0, g_wx), (channels, "flat", 0, None)]
    )

    tiny = narrow0[:, tiny_at - channels :].reshape(-1)[:tiny_size]
    sizes = [8 * channels, 8 * channels, 2 * LANES, 2 * LANES]
    cut = [sum(sizes[:i]) for i in range(len(sizes) + 1)]
    g_x = tiny[: cut[2]].reshape(layers, 8, channels)
    g_head = tiny[cut[2] : cut[4]].reshape(layers, 2, LANES)[:, :, :heads]
    shared = tiny[cut[4] :].reshape(layers, -1, both)
    lines = width // both
    g_norm_in = shared[:, :lines].reshape(layers, width) / norm_in
    g_bc = shared[:, lines : lines + 5]
    return (
        outputs[None, :, :width],
        outputs[None, :, width:],
        g_norm_in,
        g_wz,
        g_wx,
        jnp.stack([v[:, bc_at - channels : tiny_at - channels] for v in (narrow0, narrow1)]),
        jnp.stack([v[:, :heads] for v in (narrow0, narrow1)]),
        g_x[:, 0:4],
        g_x[:, 4],
        g_bc[:, 0:4],
        g_bc[:, 4],
        g_head[:, 0],
        g_head[:, 1],
        jnp.sum(g_x[:, 6].reshape(layers, heads, head_dim), axis=2),
        g_x[:, 5],
        g_wo,
    )


def solution(mesh):
    specs_in = (
        P("dp", "tensor", None),
        P("dp", "tensor", None),
        P(),
        P(None, None, "tensor"),
        P(None, None, "tensor"),
        P(None, None, "tensor"),
        P(None, None, "tensor"),
        P(None, None, "tensor"),
        P(None, "tensor"),
        P(),
        P(),
        P(None, "tensor"),
        P(None, "tensor"),
        P(None, "tensor"),
        P(None, "tensor"),
        P(None, "tensor", None),
    )
    specs_out = (
        P("dp", "tensor", None),
        P("dp", "tensor", None),
        P(),
        P(None, None, "tensor"),
        P(None, None, "tensor"),
        P(None, None, "tensor"),
        P(None, None, "tensor"),
        P(None, None, "tensor"),
        P(None, "tensor"),
        P(),
        P(),
        P(None, "tensor"),
        P(None, "tensor"),
        P(None, "tensor"),
        P(None, "tensor"),
        P(None, "tensor", None),
    )
    return jax.shard_map(
        local, mesh=mesh, in_specs=specs_in, out_specs=specs_out, check_vma=False
    )
```

```python
import functools

import jax
import jax.numpy as jnp
from jax import lax
from jax.experimental import pallas as pl
from jax.experimental.pallas import tpu as pltpu
from jax.sharding import PartitionSpec as P

SPAN = 256
EPS = 1e-05
LANES = 128
VMEM_BYTES = 56 * 1024 * 1024

f32 = jnp.float32
bf16 = jnp.bfloat16
highest = lax.Precision.HIGHEST

ROWS = ((0,), (0,))
COLS = ((1,), (1,))
PLAIN = ((1,), (0,))


def dot(left, right, dims=PLAIN, precision=None):
    return lax.dot_general(
        left, right, (dims, ((), ())), preferred_element_type=f32, precision=precision
    )


def sigmoid(v):
    return 1.0 / (1.0 + jnp.exp(-v))


def softplus(v):
    return jnp.maximum(v, 0.0) + jnp.log1p(jnp.exp(-jnp.abs(v)))


def spread_heads(per_head, channels, head_dim):
    rows = per_head.shape[0]
    per_tile = LANES // head_dim
    lane = lax.broadcasted_iota(jnp.int32, (rows, LANES), 1)
    tiles = []
    for tile in range(channels // LANES):
        out = jnp.broadcast_to(
            per_head[:, tile * per_tile : tile * per_tile + 1], (rows, LANES)
        )
        for sub in range(1, per_tile):
            head = tile * per_tile + sub
            out = jnp.where(
                lane >= sub * head_dim,
                jnp.broadcast_to(per_head[:, head : head + 1], (rows, LANES)),
                out,
            )
        tiles.append(out)
    return jnp.concatenate(tiles, axis=1)


def conv_taps(buf, taps, offset, width):
    out = offset
    for j in range(4):
        out = out + taps[j : j + 1] * buf[pl.ds(5 + j, width), :]
    return out


def decay_matrix(mask, cum_col, cum_row):
    return jnp.exp(jnp.where(mask, cum_col - cum_row, -1e30))


def span_values(dt, head_ref):
    length = dt.shape[0]
    rows = lax.broadcasted_iota(jnp.int32, (length, length), 0)
    cols = lax.broadcasted_iota(jnp.int32, (length, length), 1)
    mask = rows >= cols
    pre = dt + head_ref[0:1, :]
    step = softplus(pre)
    rate = head_ref[1:2, :] * step
    cum = dot(mask.astype(f32), rate, PLAIN, highest)
    return mask, pre, step, rate, cum


def put_half(place_ref, span, half, mine_ref, other_ref, value):
    own = span // half == place_ref[0]

    @pl.when(own)
    def _():
        mine_ref[...] = value

    @pl.when(jnp.logical_not(own))
    def _():
        other_ref[...] = value


def place_pieces(plan, place_ref, pieces, outs):
    core, z = place_ref[0], place_ref[1]
    for piece, other, dz, start, out, per, offset, rows in plan:
        member = (1 - core if other else core) * NZ + lax.rem(z + dz, NZ)
        row = pl.multiple_of(member * per + offset, 16)
        outs[out][pl.ds(row, rows), :] = pieces[piece][start : start + rows, :]


def cut_weights(w_ref, width):
    channels = w_ref.shape[1]
    parts = [w_ref.at[0:width, :], w_ref.at[width : 2 * width, :]]
    return parts + cut_out(w_ref.at[2 * width : 3 * width, :])


def cut_out(wo_ref):
    rows, channels = wo_ref.shape
    return [wo_ref.at[i * channels : (i + 1) * channels, :] for i in range(rows // channels)]


def times_out(v, wo_refs):
    return jnp.concatenate([dot(v, wo_ref[...]) for wo_ref in wo_refs], axis=1)


def times_out_t(v, wo_refs):
    channels = wo_refs[0].shape[1]
    return sum(
        dot(v[:, i * channels : (i + 1) * channels], wo_ref[...], COLS)
        for i, wo_ref in enumerate(wo_refs)
    )


def put_columns(place_ref, span, mine_ref, other_ref, columns):
    per = columns.shape[0] // (NC * NZ)
    rows = mine_ref.shape[0] // NZ

    def place_columns(core, ref):
        for z in range(NZ):
            at = (core * NZ + z) * per
            ref[pl.ds(pl.multiple_of(z * rows + span * per, 16), per), :] = columns[at : at + per, :]

    for core in range(NC):
        mine = place_ref[0] == core

        @pl.when(mine)
        def _(core=core):
            place_columns(core, mine_ref)

        @pl.when(jnp.logical_not(mine))
        def _(core=core):
            place_columns(core, other_ref)


def forward_kernel(plans, head_dim, place_ref, *refs):
    last_layer = len(plans) == 2
    refs = list(refs)

    def take(count):
        taken = refs[:count]
        del refs[:count]
        return taken

    piece_refs = [take(count) for _, count in plans]
    w_here, w_there, wdt_ref, cx_ref, cbc_ref, head_ref = take(6)
    w_ref, xn_ref, wbc_ref, z_ref, xp_ref, bc_ref, dt_ref, y_ref, hin_ref, mine_ref, other_ref = take(11)
    if last_layer:
        g_ref, sums_ref, gg_ref = take(3)
    w_sem, xn_all, xbuf, bbuf, hst = take(5)
    if last_layer:
        [g_all] = take(1)
    length = z_ref.shape[0]
    channels = w_ref.shape[1]
    state = hst.shape[0]
    span = pl.program_id(0)
    wz_ref, wx_ref, *wo_refs = cut_weights(w_ref, xn_ref.shape[1])

    @pl.when(span == 0)
    def _():
        @pl.when(place_ref[2] == 1)
        def _():
            pltpu.make_async_copy(w_here.at[0 : w_ref.shape[0], :], w_ref, w_sem).start()

        @pl.when(place_ref[2] == 0)
        def _():
            pltpu.make_async_copy(w_there.at[0 : w_ref.shape[0], :], w_ref, w_sem).start()

        if last_layer:
            place_pieces(plans[0][0], place_ref, piece_refs[0], [xn_all])
            place_pieces(plans[1][0], place_ref, piece_refs[1], [g_all, wbc_ref])
        else:
            place_pieces(plans[0][0], place_ref, piece_refs[0], [xn_all, wbc_ref])
        xbuf[0:8, :] = jnp.zeros((8, channels), f32)
        bbuf[0:8, :] = jnp.zeros((8, 2 * state), f32)
        hst[...] = jnp.zeros_like(hst)
        pltpu.make_async_copy(w_here.at[0 : w_ref.shape[0], :], w_ref, w_sem).wait()

    here = pl.ds(pl.multiple_of(span * length, length), length)
    xn = xn_all[here, :]
    xn_ref[...] = xn
    z = dot(xn, wz_ref[...])
    z_ref[...] = z
    xp = dot(xn, wx_ref[...])
    xp_ref[...] = xp
    xbuf[8:, :] = xp
    bc = dot(xn, wbc_ref[...], COLS).astype(bf16)
    bc_ref[...] = bc
    bbuf[8:, :] = bc.astype(f32)
    dt = dot(xn, wdt_ref[...], COLS)
    dt_ref[...] = dt

    pre_x = conv_taps(xbuf, cx_ref[0:4, :], cx_ref[4:5, :], length)
    xc = pre_x * sigmoid(pre_x)
    pre_bc = conv_taps(bbuf, cbc_ref[0:4, :], cbc_ref[4:5, :], length)
    bcc = (pre_bc * sigmoid(pre_bc)).astype(bf16)
    xbuf[0:8, :] = xbuf[length : length + 8, :]
    bbuf[0:8, :] = bbuf[length : length + 8, :]
    b_mat = bcc[:, :state]
    c_mat = bcc[:, state:]

    mask, _, step, _, cum = span_values(dt, head_ref)
    cum_t = jnp.transpose(cum)
    scores = dot(c_mat, b_mat, COLS)
    xs = xc * spread_heads(step, channels, head_dim)
    xs_b = xs.astype(bf16)
    lane = lax.broadcasted_iota(jnp.int32, (length, LANES), 1)
    per_tile = LANES // head_dim
    tiles = []
    for tile in range(channels // LANES):
        xs_tile = xs_b[:, tile * LANES : (tile + 1) * LANES]
        out = None
        for sub in range(per_tile):
            head = tile * per_tile + sub
            decay = decay_matrix(mask, cum[:, head : head + 1], cum_t[head : head + 1, :])
            part = dot((scores * decay).astype(bf16), xs_tile)
            out = part if out is None else jnp.where(lane >= sub * head_dim, part, out)
        tiles.append(out)
    hin = hst[...]
    hin_ref[0] = hin
    last = cum[length - 1 : length, :]
    y = jnp.concatenate(tiles, axis=1)
    y = y + dot(c_mat, hin.astype(bf16)) * spread_heads(jnp.exp(cum), channels, head_dim)
    y = y + cx_ref[6:7, :] * xc
    y_ref[...] = y
    tail = spread_heads(jnp.exp(last - cum), channels, head_dim)
    keep = spread_heads(jnp.exp(last), channels, head_dim)
    hst[...] = keep * hin + dot(b_mat, (tail * xs).astype(bf16), ROWS)

    gated = y * (z * sigmoid(z))
    scaled = gated * cx_ref[5:6, :]
    squares = jnp.sum(gated * gated, axis=1, keepdims=True)
    high = squares.astype(bf16).astype(f32)
    extra = jnp.where(lane == 0, high, jnp.where(lane == 1, squares - high, 0.0)).astype(bf16)
    mixed = times_out(scaled.astype(bf16), wo_refs).astype(bf16)
    put_half(
        place_ref,
        span,
        pl.num_programs(0) // 2,
        mine_ref,
        other_ref,
        jnp.concatenate([mixed, extra], axis=1),
    )
    if last_layer:
        g = g_all[here, :]
        g_ref[...] = g
        gg = times_out_t(g, wo_refs)
        gg_ref[...] = gg
        products = jnp.sum(gg * scaled, axis=1, keepdims=True)
        both = jnp.where(lane == 0, squares, jnp.where(lane == 1, products, 0.0))
        sums_ref[...] = jnp.transpose(both)[0:8, :]


def gate_part(gg, rms, coef, z, y, cx_ref):
    norm_gate = cx_ref[5:6, :]
    sz = sigmoid(z)
    silu_z = z * sz
    gated = y * silu_z
    rg = rms * gg
    gate_out = (gated * rms * norm_gate).astype(bf16)
    d_gated = rg * norm_gate - gated * coef
    dz = (d_gated * y * (sz * (1.0 + z * (1.0 - sz)))).astype(bf16)
    return dz, d_gated * silu_z, gate_out, jnp.sum(rg * gated, axis=0, keepdims=True)


def gate_kernel(plan, n_pieces, width, place_ref, *refs):
    pieces = refs[:n_pieces]
    z_ref, y_ref, wo_ref, cx_ref, g_ref, dz_ref, dy_ref, go_ref, acc_ref, first_all = refs[n_pieces:]
    length = z_ref.shape[0]
    span = pl.program_id(0)

    @pl.when(span == 0)
    def _():
        place_pieces(plan, place_ref, pieces, [first_all])
        acc_ref[...] = jnp.zeros_like(acc_ref)

    first = first_all[pl.ds(pl.multiple_of(span * length, length), length), :]
    g = first[:, :width]
    g_ref[...] = g
    tok = first[:, width:].astype(f32)
    rms = tok[:, 0:1] + tok[:, 1:2]
    coef = tok[:, 2:3] + tok[:, 3:4]
    gg = times_out_t(g, cut_out(wo_ref))
    dz, dy, gate_out, acc_norm = gate_part(gg, rms, coef, z_ref[...], y_ref[...], cx_ref)
    dz_ref[...] = dz
    dy_ref[...] = dy
    go_ref[...] = gate_out
    acc_ref[5:6, :] += acc_norm


def last_gate_kernel(inner_all, place_ref, gg_ref, tok_ref, z_ref, y_ref, cx_ref, dz_ref, dy_ref, go_ref, acc_ref):
    @pl.when(pl.program_id(0) == 0)
    def _():
        acc_ref[...] = jnp.zeros_like(acc_ref)

    tok = jnp.transpose(tok_ref[...])
    rms = lax.rsqrt(tok[:, 0:1] / inner_all + EPS)
    coef = rms * rms * rms * tok[:, 1:2] / inner_all
    dz, dy, gate_out, acc_norm = gate_part(gg_ref[...], rms, coef, z_ref[...], y_ref[...], cx_ref)
    dz_ref[...] = dz
    dy_ref[...] = dy
    go_ref[...] = gate_out
    acc_ref[5:6, :] += acc_norm


def scan_kernel(head_dim, place_ref, *refs):
    (dy_ref, dz_ref, xn_ref, xp_ref, xhalo_ref, bc_ref, bchalo_ref, dt_ref, hin_ref,
     w_ref, wbc_ref, wdt_ref, cx_ref, cbc_ref, head_ref, pick_ref,
     dxt_ref, bcmine_ref, bcother_ref, mine_ref, other_ref, acc_ref, acch_ref, shared_ref,
     accbc, accn, xbuf, bbuf, dubuf, dubbuf, dhst) = refs
    length = xp_ref.shape[0]
    channels = w_ref.shape[1]
    width = xn_ref.shape[1]
    state = dhst.shape[0]
    step_id = pl.program_id(0)
    first_span = step_id == pl.num_programs(0) - 1

    @pl.when(step_id == 0)
    def _():
        dubuf[length:, :] = jnp.zeros((8, channels), f32)
        dubbuf[length:, :] = jnp.zeros((8, 2 * state), f32)
        dhst[...] = jnp.zeros_like(dhst)
        accn[...] = jnp.zeros_like(accn)
        acc_ref[...] = jnp.zeros_like(acc_ref)
        accbc[...] = jnp.zeros_like(accbc)
        acch_ref[...] = jnp.zeros_like(acch_ref)

    @pl.when(first_span)
    def _():
        xbuf[0:8, :] = jnp.zeros((8, channels), f32)
        bbuf[0:8, :] = jnp.zeros((8, 2 * state), f32)

    @pl.when(jnp.logical_not(first_span))
    def _():
        xbuf[0:8, :] = xhalo_ref[...]
        bbuf[0:8, :] = bchalo_ref[...].astype(f32)[8:16, :]

    xbuf[8:, :] = xp_ref[...]
    bbuf[8:, :] = bc_ref[...].astype(f32)
    dz_b, dy = dz_ref[...], dy_ref[...]
    skip = cx_ref[6:7, :]

    pre_x = conv_taps(xbuf, cx_ref[0:4, :], cx_ref[4:5, :], length)
    sx = sigmoid(pre_x)
    xc = pre_x * sx
    pre_bc = conv_taps(bbuf, cbc_ref[0:4, :], cbc_ref[4:5, :], length)
    sbc = sigmoid(pre_bc)
    bcc = (pre_bc * sbc).astype(bf16)
    b_mat = bcc[:, :state]
    c_mat = bcc[:, state:]
    mask, pre_dt, step, rate, cum = span_values(dt_ref[...], head_ref)
    cum_t = jnp.transpose(cum)
    last = cum[length - 1 : length, :]
    scores = dot(c_mat, b_mat, COLS)
    step_all = spread_heads(step, channels, head_dim)
    xs = xc * step_all
    xs_b = xs.astype(bf16)
    tail = spread_heads(jnp.exp(last - cum), channels, head_dim)
    keep = spread_heads(jnp.exp(last), channels, head_dim)

    hin = hin_ref[0]
    hin_b = hin.astype(bf16)
    dh = dhst[...]
    dh_b = dh.astype(bf16)
    dye = dy * spread_heads(jnp.exp(cum), channels, head_dim)
    dye_b = dye.astype(bf16)
    txs = tail * xs
    txs_b = txs.astype(bf16)
    carried = dot(c_mat, hin_b)
    pulled = dot(b_mat, dh_b)
    d_c = dot(dye_b, hin_b, COLS)
    d_b = dot(txs_b, dh_b, COLS)
    dhst[...] = keep * dh + dot(c_mat, dye_b, ROWS)
    into = txs * pulled
    across = dye * carried - into
    at_last = jnp.sum(into, axis=0, keepdims=True) + keep * jnp.sum(hin * dh, axis=0, keepdims=True)

    dy_b = dy.astype(bf16)
    dy_t = jnp.transpose(dy).astype(bf16)
    lane = lax.broadcasted_iota(jnp.int32, (length, LANES), 1)
    per_tile = LANES // head_dim
    d_scores = jnp.zeros((length, length), f32)
    row_sums = jnp.zeros((length, LANES), f32)
    col_sums = []
    dxs_parts = []
    for head in range(channels // head_dim):
        tile, sub = divmod(head, per_tile)
        dy_tile = dy_b[:, tile * LANES : (tile + 1) * LANES]
        own = (lane >= sub * head_dim) & (lane < (sub + 1) * head_dim)
        dy_head = jnp.where(own, dy_tile, jnp.zeros_like(dy_tile))
        d_m = dot(dy_head, xs_b[:, tile * LANES : (tile + 1) * LANES], COLS)
        decay = decay_matrix(mask, cum[:, head : head + 1], cum_t[head : head + 1, :])
        dxs_parts.append(
            dot(dy_t[head * head_dim : (head + 1) * head_dim, :], (scores * decay).astype(bf16))
        )
        d_m = d_m * decay
        d_scores = d_scores + d_m
        pairs = d_m * scores
        row_sums = jnp.where(lane == head, jnp.sum(pairs, axis=1, keepdims=True), row_sums)
        col_sums.append(jnp.sum(pairs, axis=0, keepdims=True))
    heads = len(col_sums)
    col_sums = jnp.concatenate(col_sums + [jnp.zeros((LANES - heads, length), f32)], axis=0)
    dxs = jnp.transpose(jnp.concatenate(dxs_parts, axis=0)) + tail * pulled
    pick = pick_ref[...]
    d_cum = row_sums - jnp.transpose(col_sums) + dot(across, pick, PLAIN, highest)
    at_last = dot(jnp.broadcast_to(at_last, (8, channels)), pick, PLAIN, highest)[0:1, :]
    d_rate = dot(mask.astype(f32), d_cum, ROWS, highest) + at_last
    d_step = d_rate * head_ref[1:2, :] + dot(dxs * xc, pick, PLAIN, highest)
    d_dt = d_step * sigmoid(pre_dt)
    acch_ref[0:1, :] += jnp.sum(d_dt, axis=0, keepdims=True)
    acch_ref[1:2, :] += jnp.sum(d_rate * rate, axis=0, keepdims=True)
    dt_b = d_dt.astype(bf16)
    ds_b = d_scores.astype(bf16)
    d_c = d_c + dot(ds_b, b_mat)
    d_b = d_b + dot(ds_b, c_mat, ROWS)
    d_xc = dxs * step_all + skip * dy
    acc_skip = jnp.sum(dy * xc, axis=0, keepdims=True)

    d_u = d_xc * (sx * (1.0 + pre_x * (1.0 - sx)))
    d_ub = jnp.concatenate([d_b, d_c], axis=1) * (sbc * (1.0 + pre_bc * (1.0 - sbc)))
    dubuf[0:length, :] = d_u
    dubbuf[0:length, :] = d_ub
    d_x = jnp.zeros_like(d_u)
    d_bc = jnp.zeros_like(d_ub)
    acc_rows = []
    accbc_rows = []
    for j in range(4):
        d_x = d_x + cx_ref[j : j + 1, :] * dubuf[pl.ds(3 - j, length), :]
        d_bc = d_bc + cbc_ref[j : j + 1, :] * dubbuf[pl.ds(3 - j, length), :]
        acc_rows.append(jnp.sum(d_u * xbuf[pl.ds(5 + j, length), :], axis=0, keepdims=True))
        accbc_rows.append(jnp.sum(d_ub * bbuf[pl.ds(5 + j, length), :], axis=0, keepdims=True))
    dubuf[length:, :] = d_u[0:8, :]
    dubbuf[length:, :] = d_ub[0:8, :]
    zero = jnp.zeros((1, channels), f32)
    acc_ref[...] += jnp.concatenate(
        acc_rows + [jnp.sum(d_u, axis=0, keepdims=True), zero, acc_skip, zero], axis=0
    )
    zero = jnp.zeros((3, d_ub.shape[1]), f32)
    accbc[...] += jnp.concatenate(
        accbc_rows + [jnp.sum(d_ub, axis=0, keepdims=True), zero], axis=0
    )
    dx_b = d_x.astype(bf16)
    dbc_b = d_bc.astype(bf16)
    dxt_ref[:, :channels] = dx_b
    dxt_ref[:, channels:] = dt_b
    put_columns(
        place_ref,
        pl.num_programs(0) - 1 - step_id,
        bcmine_ref,
        bcother_ref,
        jnp.transpose(d_bc).astype(bf16),
    )
    total = dot(dz_b, w_ref[0:width, :], COLS) + dot(dx_b, w_ref[width : 2 * width, :], COLS)
    total = total + dot(dbc_b, wbc_ref[...]) + dot(dt_b, wdt_ref[...])
    accn[0:1, :] += jnp.sum(total * xn_ref[...].astype(f32), axis=0, keepdims=True)

    @pl.when(first_span)
    def _():
        lanes = shared_ref.shape[1]
        lines = [accn[0:1, i * lanes : (i + 1) * lanes] for i in range(width // lanes)]
        shared = jnp.concatenate(lines + [accbc[0:5, :]], axis=0)
        shared_ref[0 : shared.shape[0], :] = shared.astype(bf16)
        shared_ref[shared.shape[0] :, :] = jnp.zeros(
            (shared_ref.shape[0] - shared.shape[0], lanes), bf16
        )

    put_half(
        place_ref,
        pl.num_programs(0) - 1 - step_id,
        pl.num_programs(0) // 2,
        mine_ref,
        other_ref,
        total.astype(bf16),
    )


def whole(shape):
    zeros = (0,) * len(shape)
    return pl.BlockSpec(shape, lambda i, p: zeros)


def span_rows(columns):
    return pl.BlockSpec((SPAN, columns), lambda i, p: (i, 0))


def half_rows(columns, spans, reverse):
    half = spans // 2

    def block(i, core):
        span = spans - 1 - i if reverse else i
        return jnp.clip(span - half * core, 0, half - 1), 0

    return [
        pl.BlockSpec((SPAN, columns), lambda i, p: block(i, p[0])),
        pl.BlockSpec((SPAN, columns), lambda i, p: block(i, 1 - p[0])),
    ]


def span_call(kernel, name, spans, place, operands, in_specs, shapes, out_specs, scratch, flops):
    moved = sum(v.size * v.dtype.itemsize for v in [*operands, *shapes])
    return pl.pallas_call(
        kernel,
        grid_spec=pltpu.PrefetchScalarGridSpec(
            num_scalar_prefetch=1,
            grid=(spans,),
            in_specs=in_specs,
            out_specs=out_specs,
            scratch_shapes=scratch,
        ),
        out_shape=shapes,
        compiler_params=pltpu.CompilerParams(
            dimension_semantics=("arbitrary",), vmem_limit_bytes=VMEM_BYTES
        ),
        cost_estimate=pl.CostEstimate(flops=flops, bytes_accessed=moved, transcendentals=0),
        name=name,
    )(place, *operands)


def run_forward(place, gathered, weights, small, state, head_dim):
    channels = weights[0].shape[1]
    width = gathered[0][0][0].shape[1]
    anywhere = pl.BlockSpec(memory_space=pl.ANY)
    tokens = NC * NZ * gathered[0][2][0]
    spans = tokens // SPAN
    last_layer = len(gathered) == 2
    plans = [(cut_plan(*one), len(one[0])) for one in gathered]
    operands = [p for one in gathered for p in one[0]]
    in_specs = [whole(v.shape) for v in operands] + [anywhere] * 2
    operands += [*weights, *small]
    in_specs += [whole(v.shape) for v in operands[len(in_specs) :]]
    shapes = [
        jax.ShapeDtypeStruct((3 * width, channels), bf16),
        jax.ShapeDtypeStruct((tokens, width), bf16),
        jax.ShapeDtypeStruct((2 * state, width), bf16),
        jax.ShapeDtypeStruct((tokens, channels), f32),
        jax.ShapeDtypeStruct((tokens, channels), f32),
        jax.ShapeDtypeStruct((tokens, 2 * state), bf16),
        jax.ShapeDtypeStruct((tokens, LANES), f32),
        jax.ShapeDtypeStruct((tokens, channels), f32),
        jax.ShapeDtypeStruct((spans, state, channels), f32),
        jax.ShapeDtypeStruct((tokens // 2, width + LANES), bf16),
        jax.ShapeDtypeStruct((tokens // 2, width + LANES), bf16),
    ]
    out_specs = [whole((3 * width, channels)), span_rows(width), whole((2 * state, width))]
    out_specs += [span_rows(s.shape[1]) for s in shapes[3:8]]
    out_specs.append(pl.BlockSpec((1, state, channels), lambda i, p: (i, 0, 0)))
    out_specs += half_rows(width + LANES, spans, False)
    scratch = [
        pltpu.SemaphoreType.DMA,
        pltpu.VMEM((tokens, width), bf16),
        pltpu.VMEM((SPAN + 8, channels), f32),
        pltpu.VMEM((SPAN + 8, 2 * state), f32),
        pltpu.VMEM((state, channels), f32),
    ]
    if last_layer:
        shapes += [
            jax.ShapeDtypeStruct((tokens, width), bf16),
            jax.ShapeDtypeStruct((8, tokens), f32),
            jax.ShapeDtypeStruct((tokens, channels), f32),
        ]
        out_specs += [span_rows(width), pl.BlockSpec((8, SPAN), lambda i, p: (0, i)), span_rows(channels)]
        scratch.append(pltpu.VMEM((tokens, width), bf16))
    kernel = functools.partial(forward_kernel, plans, head_dim)
    return span_call(
        kernel, "layer_forward", spans, place, operands, in_specs, shapes, out_specs, scratch, 20 * 10**9
    )


def run_gate(place, gathered, z, y, w, cx):
    tokens, channels = z.shape
    width = w.shape[0] // 3
    spans = tokens // SPAN
    plan, pieces = cut_plan(*gathered), list(gathered[0])
    operands = [*pieces, z, y, w, cx]
    in_specs = [whole(p.shape) for p in pieces]
    in_specs += [span_rows(channels), span_rows(channels)]
    in_specs += [pl.BlockSpec((width, channels), lambda i, p: (2, 0)), whole(cx.shape)]
    shapes = [
        jax.ShapeDtypeStruct((tokens, width), bf16),
        jax.ShapeDtypeStruct((tokens, channels), bf16),
        jax.ShapeDtypeStruct((tokens, channels), f32),
        jax.ShapeDtypeStruct((tokens, channels), bf16),
        jax.ShapeDtypeStruct((8, channels), f32),
    ]
    out_specs = [span_rows(s.shape[1]) for s in shapes[:4]] + [whole(shapes[4].shape)]
    scratch = [pltpu.VMEM((tokens, pieces[0].shape[1]), bf16)]
    kernel = functools.partial(gate_kernel, plan, len(pieces), width)
    return span_call(
        kernel, "gate_backward", spans, place, operands, in_specs, shapes, out_specs, scratch, 6 * 10**9
    )


def run_last_gate(place, gg, sums, z, y, cx, inner_all):
    tokens, channels = z.shape
    spans = tokens // SPAN
    rows = span_rows(channels)
    shapes = [
        jax.ShapeDtypeStruct((tokens, channels), bf16),
        jax.ShapeDtypeStruct((tokens, channels), f32),
        jax.ShapeDtypeStruct((tokens, channels), bf16),
        jax.ShapeDtypeStruct((8, channels), f32),
    ]
    return span_call(
        functools.partial(last_gate_kernel, inner_all),
        "last_gate_backward",
        spans,
        place,
        [gg, sums, z, y, cx],
        [rows, pl.BlockSpec((8, SPAN), lambda i, p: (0, i)), rows, rows, whole(cx.shape)],
        shapes,
        [rows, rows, rows, whole(shapes[3].shape)],
        [],
        10**9,
    )


def run_scan(place, dy, dz, xn, xp, bc, dt, hin, weights, small, pick, head_dim):
    tokens, channels = xp.shape
    state = hin.shape[1]
    width = xn.shape[1]
    spans = tokens // SPAN

    def rev(columns):
        return pl.BlockSpec((SPAN, columns), lambda i, p: (spans - 1 - i, 0))

    def halo(columns, rows):
        per = SPAN // rows
        return pl.BlockSpec(
            (rows, columns), lambda i, p: (jnp.maximum((spans - 1 - i) * per - 1, 0), 0)
        )

    operands = [dy, dz, xn, xp, xp, bc, bc, dt, hin, *weights, *small, pick]
    in_specs = [
        rev(channels),
        rev(channels),
        rev(width),
        rev(channels),
        halo(channels, 8),
        rev(2 * state),
        halo(2 * state, 16),
        rev(LANES),
        pl.BlockSpec((1, state, channels), lambda i, p: (spans - 1 - i, 0, 0)),
    ]
    in_specs.append(whole((2 * width, channels)))
    in_specs += [whole(v.shape) for v in operands[len(in_specs) :]]
    shapes = [
        jax.ShapeDtypeStruct((tokens, channels + LANES), bf16),
        jax.ShapeDtypeStruct((state * spans, SPAN), bf16),
        jax.ShapeDtypeStruct((state * spans, SPAN), bf16),
        jax.ShapeDtypeStruct((tokens // 2, width), bf16),
        jax.ShapeDtypeStruct((tokens // 2, width), bf16),
        jax.ShapeDtypeStruct((8, channels), f32),
        jax.ShapeDtypeStruct((8, LANES), f32),
        jax.ShapeDtypeStruct((16, 2 * state), bf16),
    ]
    out_specs = [rev(channels + LANES), whole(shapes[1].shape), whole(shapes[2].shape)]
    out_specs += half_rows(width, spans, True)
    out_specs += [whole(s.shape) for s in shapes[5:]]
    scratch = [
        pltpu.VMEM((8, 2 * state), f32),
        pltpu.VMEM((8, width), f32),
        pltpu.VMEM((SPAN + 8, channels), f32),
        pltpu.VMEM((SPAN + 8, 2 * state), f32),
        pltpu.VMEM((SPAN + 8, channels), f32),
        pltpu.VMEM((SPAN + 8, 2 * state), f32),
        pltpu.VMEM((state, channels), f32),
    ]
    kernel = functools.partial(scan_kernel, head_dim)
    return span_call(
        kernel, "scan_backward", spans, place, operands, in_specs, shapes, out_specs, scratch, 28 * 10**9
    )


def weight_kernel(pairs, *refs):
    lefts, rights, out_ref = refs[: len(pairs)], refs[len(pairs) : -1], refs[-1]
    at = 0
    for left_ref, right_ref in zip(lefts, rights):
        columns = right_ref.shape[1]
        out_ref[:, at : at + columns] = dot(left_ref[...], right_ref[...], ROWS).astype(bf16)
        at += columns


def weight_products(pairs):
    tokens = pairs[0][0].shape[0]
    rows = max(left.shape[1] for left, _ in pairs)
    block = rows // 4
    lefts, rights, columns = [], [], []
    for left, right in pairs:
        quarter = left.shape[1] == block
        lefts.append(pl.BlockSpec((tokens, block), (lambda i: (0, 0)) if quarter else (lambda i: (0, i))))
        wide = block if quarter else right.shape[1]
        rights.append(pl.BlockSpec((tokens, wide), (lambda i: (0, i)) if quarter else (lambda i: (0, 0))))
        columns.append(wide)
    return pl.pallas_call(
        functools.partial(weight_kernel, pairs_of(columns)),
        grid=(4,),
        in_specs=lefts + rights,
        out_specs=pl.BlockSpec((block, sum(columns)), lambda i: (i, 0)),
        out_shape=jax.ShapeDtypeStruct((rows, sum(columns)), bf16),
        compiler_params=pltpu.CompilerParams(vmem_limit_bytes=VMEM_BYTES),
        cost_estimate=pl.CostEstimate(
            flops=2 * tokens * rows * sum(columns), bytes_accessed=8 * 10**6, transcendentals=0
        ),
        name="weight_products",
    )(*[left for left, _ in pairs], *[right for _, right in pairs])


def pairs_of(columns):
    return tuple(columns)


SIZES = (4, 2, 2, 2, 4)
NX, NYL, NC, NYH, NZ = SIZES
EVERY = [
    (x, yl, c, yh, z)
    for x in range(NX)
    for yl in range(NYL)
    for c in range(NC)
    for yh in range(NYH)
    for z in range(NZ)
]


def linear(x, yl, c, yh, z):
    return ((((x % NX) * NYL + yl % NYL) * NC + c % NC) * NYH + yh % NYH) * NZ + z % NZ


def send(v, step, only=None):
    pairs = [(linear(*d), linear(*step(*d))) for d in EVERY if only is None or only(*d)]
    return lax.ppermute(v, ("dp", "tensor"), pairs)


def send_z(v, k):
    return send(v, lambda x, yl, c, yh, z: (x, yl, c, yh, z + k))


def send_core(v):
    return send(v, lambda x, yl, c, yh, z: (x, yl, c + 1, yh, z))


def trade(v, k):
    return send(v, lambda x, yl, c, yh, z: (x, yl, yh, c, z + k))


def traded(v):
    return send(v, lambda x, yl, c, yh, z: (x, yl, yh, c, z), lambda x, yl, c, yh, z: c != yh)


def trade_places(v):
    _, _, core, yh, _ = position()
    return jnp.where(core == yh, v, traded(v))


def position():
    dp, tensor = lax.axis_index("dp"), lax.axis_index("tensor")
    return dp // (NYL * NC), dp // NC % NYL, dp % NC, tensor // NZ, tensor % NZ


def gather(v, parts, traded_own=None):
    arrays, sources = [], []
    for k in (0, 1, 3, 2):
        if traded_own is not None:
            piece = trade(v, k) if k else traded_own
        else:
            piece = send_z(v, k) if k else v
        arrays += [piece, send_core(piece)]
        sources += [(False, -k % NZ, 0), (True, -k % NZ, 0)]
    return arrays, sources, parts


def cut_plan(arrays, sources, parts):
    plan = []
    for number, (piece, (other, dz, first)) in enumerate(zip(arrays, sources)):
        base = 0
        for out, per in enumerate(parts):
            begin, end = max(first, base), min(first + piece.shape[0], base + per)
            if begin < end:
                plan.append((number, other, dz, begin - first, out, per, begin - base, end - begin))
            base += per
    return plan


def fold(mine, other):
    _, _, _, _, z = position()
    rows = mine.shape[0] // NZ
    blocks = []
    for k in range(NZ):
        at = (z + k) % NZ * rows
        a = lax.dynamic_slice_in_dim(mine, at, rows, 0).astype(f32)
        blocks.append(a + lax.dynamic_slice_in_dim(other, at, rows, 0).astype(f32))
    return blocks


def fold_beside(pairs):
    folded = [fold(mine, send_core(other)) for mine, other in pairs]
    return [jnp.concatenate([blocks[k] for blocks in folded], axis=1) for k in range(NZ)]


def scatter(*pairs):
    own, one, two, three = fold_beside(pairs)
    return [own] + [send_z(b.astype(bf16), k) for k, b in ((1, one), (2, two), (3, three))]


def scatter_with_sum(mine, other, shared, meanwhile):
    half = mine.shape[0]
    rows = half // NZ
    got = send_core(jnp.concatenate([other, shared], axis=0))
    blocks = fold(mine, got[:half])
    total_shared = shared.astype(f32) + got[half:].astype(f32)
    packed = total_shared.astype(bf16)
    total = blocks[0]
    for k in range(1, NZ):
        got = send_z(jnp.concatenate([blocks[k].astype(bf16), packed], axis=0), k)
        total = total + got[:rows].astype(f32)
        total_shared = total_shared + got[rows:].astype(f32)
    return after(total, *meanwhile), total_shared


def sum_members(v):
    both = v + send_core(v)
    total = both
    for k in range(1, NZ):
        total = total + send_z(both, k)
    return total


def sum_far(v):
    far = send(v, lambda x, yl, c, yh, z: (x, yl, c, yh + 1, z), lambda x, yl, c, yh, z: c != yh)
    return (v.astype(f32) + far.astype(f32)).astype(bf16)


def halve(v):
    _, _, core, yh, _ = position()
    half = v.shape[0] // 2
    near = send(
        v[half:], lambda x, yl, c, yh, z: (x, yl, c + 1, yh, z), lambda x, yl, c, yh, z: c == yh
    )
    return jnp.where(core == yh, v[:half], near)


def sum_beside(part):
    beside = send(part, lambda x, yl, c, yh, z: (x, yl + 1, c, yh, z))
    return (part.astype(f32) + beside.astype(f32)).astype(bf16)


def sum_x(v):
    x = position()[0]
    rows = v.shape[0] // NX
    total = lax.dynamic_slice_in_dim(v, x * rows, rows, 0).astype(f32)
    for k in range(1, NX):
        block = lax.dynamic_slice_in_dim(v, (x + k) % NX * rows, rows, 0)
        total = total + send(block, lambda x, yl, c, yh, z, k=k: (x + k, yl, c, yh, z)).astype(f32)
    return total.astype(bf16)


def collect_x(part):
    x = position()[0]
    out = jnp.zeros((NX,) + part.shape, bf16)
    out = lax.dynamic_update_index_in_dim(out, part, x, 0)
    for k in range(1, NX):
        block = send(part, lambda x, yl, c, yh, z, k=k: (x + k, yl, c, yh, z))
        out = lax.dynamic_update_index_in_dim(out, block, (x - k) % NX, 0)
    return out


def collect(part):
    out = collect_x(part)
    return out, send_core(out)


def write_kernel(plan, by_half, n_kept, place_ref, here_ref, there_ref, *refs):
    rows = here_ref.shape[1]

    def write(ref):
        for (column, kind, wide), out_ref in zip(plan, refs[n_kept:]):
            for x in range(NX):
                value = ref[x, :, column : column + wide].astype(f32)
                if kind != "blocks":
                    out_ref[0, 0 if by_half else x, x if by_half else 0] = value
                elif by_half:
                    at = x // 2 * wide
                    out_ref[0, x % 2 * rows : (x % 2 + 1) * rows, at : at + wide] = value
                else:
                    out_ref[0, :, x * wide : (x + 1) * wide] = value

    here = (pl.program_id(0) == 0) == (place_ref[2] == 1)

    @pl.when(here)
    def _():
        write(here_ref)

    @pl.when(jnp.logical_not(here))
    def _():
        write(there_ref)


def write_sums(place, halves, by_half, outputs):
    rows, columns = halves[0].shape[1:]
    total = 2 * NX * rows
    wide = total // 4
    plan, shapes, specs, finals, kept, alias = [], [], [], [], [], {}
    for column, kind, layer, array in outputs:
        lanes = LANES if kind == "flat" else wide
        layers = 1 if kind == "flat" else 2
        plan.append((column, kind, lanes))
        if kind == "blocks":
            shape = (layers, wide, total)
            if by_half:
                spec = pl.BlockSpec((1, wide, total // 2), lambda h, p, layer=layer: (layer, 0, h))
            else:
                spec = pl.BlockSpec((1, rows, total), lambda h, p, layer=layer: (layer, h, 0))
            finals.append(shape)
        elif by_half:
            shape = (layers, 2, NX, rows, lanes)
            spec = pl.BlockSpec((1, 1, NX, rows, lanes), lambda h, p, layer=layer: (layer, h, 0, 0, 0))
            finals.append((layers, total, lanes))
        else:
            shape = (layers, NX, 2, rows, lanes)
            spec = pl.BlockSpec((1, NX, 1, rows, lanes), lambda h, p, layer=layer: (layer, 0, h, 0, 0))
            finals.append((layers, total, lanes))
        shapes.append(jax.ShapeDtypeStruct(shape, f32))
        specs.append(spec)
        if array is not None:
            alias[3 + len(kept)] = len(shapes) - 1
            kept.append(array.reshape(shape))
    piece = pl.BlockSpec((NX, rows, columns), lambda h, p: (0, 0, 0))
    written = pl.pallas_call(
        functools.partial(write_kernel, plan, by_half, len(kept)),
        grid_spec=pltpu.PrefetchScalarGridSpec(
            num_scalar_prefetch=1,
            grid=(2,),
            in_specs=[piece, piece] + [pl.BlockSpec(memory_space=pl.ANY)] * len(kept),
            out_specs=specs,
        ),
        out_shape=shapes,
        input_output_aliases=alias,
        compiler_params=pltpu.CompilerParams(vmem_limit_bytes=VMEM_BYTES),
        name="write_sums",
    )(place, *halves, *kept)
    return [v.reshape(final) for v, final in zip(written, finals)]


def row_call(kernel, name, operands, shapes):
    return pl.pallas_call(
        kernel,
        grid=(1,),
        in_specs=[pl.BlockSpec((rows, v.shape[1]), lambda i: (0, 0)) for v, rows in operands],
        out_specs=[pl.BlockSpec(s.shape, lambda i: (0, 0)) for s in shapes],
        out_shape=shapes,
        compiler_params=pltpu.CompilerParams(vmem_limit_bytes=VMEM_BYTES),
        name=name,
    )(*[v for v, _ in operands])


def inverse_rms(v):
    return lax.rsqrt(jnp.mean(v * v, axis=-1, keepdims=True) + EPS)


def first_kernel(packed_ref, gain_ref, out_ref):
    rows = 128
    v = packed_ref[0:rows, :].astype(f32)
    out_ref[0:rows, :] = (v * inverse_rms(v) * gain_ref[...]).astype(bf16)
    out_ref[rows:, :] = packed_ref[rows : out_ref.shape[0], :]


def add_terms(own_ref, a_ref, b_ref, c_ref):
    total = own_ref[...].astype(f32) + a_ref[...].astype(f32)
    return total + (b_ref[...].astype(f32) + c_ref[...].astype(f32))


def unscaled_output(inner_all, terms, width):
    total = add_terms(*terms)
    squares = total[:, width : width + 1] + total[:, width + 1 : width + 2]
    gate_rms = lax.rsqrt(squares / inner_all + EPS)
    return gate_rms, total[:, :width] * gate_rms


def middle_kernel(inner_all, own_ref, a_ref, b_ref, c_ref, res_ref, gain_ref, res1_ref, mixed_ref, rms_ref, normed_ref):
    width = res_ref.shape[1]
    gate_rms, mixed = unscaled_output(inner_all, (own_ref, a_ref, b_ref, c_ref), width)
    res = res_ref[...].astype(f32) + mixed
    res1_ref[...] = res
    mixed_ref[...] = mixed
    rms_ref[...] = jnp.broadcast_to(gate_rms, rms_ref.shape)
    normed_ref[...] = (res * inverse_rms(res) * gain_ref[...]).astype(bf16)


def input_gradient(grad_normed, res, d_res, gain):
    inv = inverse_rms(res)
    scaled = grad_normed * gain
    dots = jnp.sum(scaled * res, axis=-1, keepdims=True) / res.shape[1]
    return d_res + inv * scaled - res * (inv * inv * inv) * dots


def between_kernel(inner_all, own_ref, a_ref, b_ref, c_ref, res_ref, dres_ref, gain_ref, mixed_ref, rms_ref, out_ref, sent_ref):
    width = res_ref.shape[1]
    grad_normed = add_terms(*(ref.at[:, 0:width] for ref in (own_ref, a_ref, b_ref, c_ref)))
    d_res = input_gradient(grad_normed, res_ref[...], dres_ref[...].astype(f32), gain_ref[...])
    out_ref[...] = d_res
    g_mixed = d_res.astype(bf16)
    sent_ref[:, :width] = g_mixed
    gate_rms = rms_ref[:, 0:1]
    products = jnp.sum(g_mixed.astype(f32) * mixed_ref[...], axis=-1, keepdims=True)
    coef = gate_rms * gate_rms * products / inner_all
    lane = lax.broadcasted_iota(jnp.int32, rms_ref.shape, 1)
    rms_high = gate_rms.astype(bf16).astype(f32)
    coef_high = coef.astype(bf16).astype(f32)
    extra = jnp.where(lane == 0, rms_high, jnp.where(lane == 1, gate_rms - rms_high, 0.0))
    extra = jnp.where(lane == 2, coef_high, jnp.where(lane == 3, coef - coef_high, extra))
    sent_ref[:, width:] = extra.astype(bf16)


def end_kernel(own_ref, a_ref, b_ref, c_ref, res_ref, dres_ref, gain_ref, hidden_ref, out_ref):
    width = res_ref.shape[1]
    grad_normed = add_terms(own_ref, a_ref, b_ref, c_ref)
    grad = input_gradient(grad_normed, res_ref[...].astype(f32), dres_ref[...], gain_ref[...])
    out_ref[:, :width] = hidden_ref[...]
    out_ref[:, width:] = grad.astype(bf16)


def last_kernel(inner_all, own_ref, a_ref, b_ref, c_ref, res_ref, out_ref):
    _, mixed = unscaled_output(inner_all, (own_ref, a_ref, b_ref, c_ref), res_ref.shape[1])
    out_ref[...] = (res_ref[...] + mixed).astype(bf16)


def after(v, *others):
    return lax.optimization_barrier((v, *others))[0]


def pad_to(v, rows, lanes):
    return jnp.pad(v, ((0, rows - v.shape[0]), (0, lanes - v.shape[1])))


def local(
    hidden_in,
    grad_out,
    norm_in,
    w_z,
    w_x,
    w_bc,
    w_dt,
    conv_x,
    conv_x_bias,
    conv_bc,
    conv_bc_bias,
    dt_bias,
    a_log,
    skip,
    norm_gate,
    w_out,
):
    layers, width, channels = w_z.shape
    heads = w_dt.shape[2]
    head_dim = channels // heads
    both = conv_bc.shape[2]
    state = both // 2
    members = NC * NZ
    inner_all = channels * members
    rows = hidden_in.shape[1]
    bc_rows = both // members
    _, _, core, yh, z = position()
    stays = core == yh
    place = jnp.stack([core, z, stays]).astype(jnp.int32)
    full = jax.ShapeDtypeStruct((rows, width), f32)

    bc_t = jnp.swapaxes(w_bc, 1, 2)
    dt_t = jnp.pad(jnp.swapaxes(w_dt, 1, 2), ((0, 0), (0, 8 - heads), (0, 0)))
    per_channel = jnp.concatenate(
        [conv_x, conv_x_bias[:, None], norm_gate[:, None], jnp.repeat(skip, head_dim, axis=1)[:, None]],
        axis=1,
    )
    per_channel = jnp.pad(per_channel, ((0, 0), (0, 1), (0, 0)))
    per_head = jnp.stack([dt_bias, -jnp.exp(a_log)], axis=1)
    per_head = jnp.pad(per_head, ((0, 0), (0, 6), (0, LANES - heads)))
    little = jnp.concatenate([per_channel, per_head], axis=2).reshape(layers * 8, channels + LANES)
    high = little.astype(bf16)
    low = (little - high.astype(f32)).astype(bf16)
    lines = pad_to(jnp.concatenate([high, low], axis=1), layers * 8, width)
    packed = jnp.concatenate([hidden_in[0], bc_t[0], dt_t.reshape(layers * 8, width), lines], axis=0)
    packed = trade_places(packed)
    lines = packed[packed.shape[0] - layers * 8 :].astype(f32)
    little = lines[:, : channels + LANES] + lines[:, channels + LANES : 2 * (channels + LANES)]
    little = little.reshape(layers, 8, channels + LANES)

    def blocks_below(v):
        return [v[:, i * channels : (i + 1) * channels] for i in range(width // channels)]

    def pack_weights(layer):
        return jnp.concatenate([w_z[layer], w_x[layer], *blocks_below(w_out[layer])], axis=0)

    grads = jnp.concatenate([grad_out[0], bc_t[1]], axis=0)
    w0 = jnp.concatenate([pack_weights(0), *blocks_below(grads)], axis=0)
    w0 = w0, traded(after(w0, packed))
    there = w0[1][3 * width :].reshape(-1, *grads.shape[:1], channels)
    grads_here = jnp.where(stays, grads, jnp.concatenate(list(there), axis=1))

    [sent] = row_call(
        first_kernel,
        "first_norm",
        [(packed, packed.shape[0]), (norm_in[0:1], 1)],
        [jax.ShapeDtypeStruct((rows + bc_rows, width), bf16)],
    )
    gathered0 = gather(sent, (rows, bc_rows))
    wdt = [pad_to(packed[rows + bc_rows + 8 * l : rows + bc_rows + 8 * (l + 1)], LANES, width) for l in range(layers)]
    smalls = []
    for layer in range(layers):
        cbc = jnp.concatenate([conv_bc[layer], conv_bc_bias[layer][None], jnp.zeros((3, both), f32)], axis=0)
        smalls.append((little[layer, :, :channels], cbc, little[layer, :, channels:]))
    channel_head = jnp.arange(channels) // head_dim
    pick = (channel_head[:, None] == jnp.arange(LANES)[None, :]).astype(f32)

    out0 = run_forward(place, [gathered0], (*w0, wdt[0]), smalls[0], state, head_dim)
    w0, xn0, wbc0, z0, xp0, bc0, dt0, y0, hin0, mine, other = out0
    gathered_grad = gather(after(grads, *gathered0[0]), (rows, bc_rows), grads_here)
    grad_held = gathered_grad[0][0]
    terms = scatter((mine, after(other, *gathered_grad[0][2::2])))
    w1 = pack_weights(1)
    w1 = w1, traded(after(w1, terms[0]))
    res1, mixed0, rms0, normed1 = row_call(
        functools.partial(middle_kernel, inner_all),
        "middle_norm",
        [(v, rows) for v in terms] + [(packed, rows), (norm_in[1:2], 1)],
        [full, full, jax.ShapeDtypeStruct((rows, LANES), f32), jax.ShapeDtypeStruct((rows, width), bf16)],
    )
    gathered1 = gather(normed1, (rows,))
    out1 = run_forward(
        place, [gathered1, gathered_grad], (*w1, wdt[1]), smalls[1], state, head_dim
    )
    w1, xn1, wbc1, z1, xp1, bc1, dt1, y1, hin1, mine, other, grad_rows1, sums, gg1 = out1
    sums = sum_members(sums)

    home = fold(mine, send_core(other))
    dz1, dy1, go1, acc_gate1 = run_last_gate(place, gg1, sums, z1, y1, smalls[1][0], inner_all)
    early1 = sum_far(weight_products([(xn1, dz1), (go1, grad_rows1)]))
    dy1 = after(dy1, *home)
    home = home[:1] + [send_z(home[k].astype(bf16), k) for k in range(1, NZ)]
    back1 = run_scan(
        place, dy1, dz1, xn1, xp1, bc1, dt1, hin1, (w1, wbc1, wdt[1]), smalls[1], pick, head_dim
    )
    dxt1, *bc_halves, mine, other, acc1, acch1, shared1 = back1
    terms = scatter((mine, after(other, early1, *home)), bc_halves)
    [hidden_out] = row_call(
        functools.partial(last_kernel, inner_all),
        "last_output",
        [(after(home[0], terms[1]), rows)] + [(v, rows) for v in home[1:]] + [(res1, rows)],
        [jax.ShapeDtypeStruct((rows, width), bf16)],
    )
    d_res1, sent = row_call(
        functools.partial(between_kernel, inner_all),
        "between_layers",
        [(v, rows) for v in terms]
        + [(res1, rows), (grad_held, rows), (norm_in[1:2], 1), (mixed0, rows), (rms0, rows)],
        [full, jax.ShapeDtypeStruct((rows, width + LANES), bf16)],
    )
    gathered_back = gather(sent, (rows,))
    early1 = sum_x(halve(after(early1, sent)))

    bc_at = channels + bc_rows

    def with_bc(dxt, bc_sum):
        by_token = bc_sum.reshape(-1, bc_rows, SPAN).swapaxes(1, 2).reshape(-1, bc_rows)
        spread = jnp.pad(by_token, ((0, 0), (bc_at, dxt.shape[1] - bc_at - bc_rows)))
        return dxt + spread.astype(bf16)

    dxt1 = with_bc(dxt1, sum(v[:, width:].astype(f32) for v in terms))

    z0 = after(z0, early1)
    grad_rows0, dz0, dy0, go0, acc_gate0 = run_gate(place, gathered_back, z0, y0, w0, smalls[0][0])
    early = weight_products([(xn0, dz0), (go0, grad_rows0), (xn1, dxt1)])
    dy0 = after(dy0, early)
    early = sum_x(early)
    early1 = sum_beside(after(early1, dz0))
    back0 = run_scan(
        place, dy0, dz0, xn0, xp0, bc0, dt0, hin0, (w0, wbc0, wdt[0]), smalls[0], pick, head_dim
    )
    dxt0, *bc_halves, mine, other, acc0, acch0, shared0 = back0
    terms = scatter((mine, other))
    [outputs] = row_call(
        end_kernel,
        "outputs",
        [(v, rows) for v in terms] + [(packed, rows), (d_res1, rows), (norm_in[0:1], 1), (hidden_out, rows)],
        [jax.ShapeDtypeStruct((rows, 2 * width), bf16)],
    )
    outputs = trade_places(outputs).astype(f32)

    shared = jnp.concatenate([shared0, shared1], axis=0)
    bc_sum, shared = scatter_with_sum(*bc_halves, shared, (early, early1))
    tiny = jnp.concatenate(
        [(acc0 + acc_gate0).reshape(-1), (acc1 + acc_gate1).reshape(-1), acch0[0:2].reshape(-1), acch1[0:2].reshape(-1)]
        + [shared.reshape(-1)]
    )
    tiny_at = bc_at + bc_rows
    tiny_lanes = channels + LANES - tiny_at
    tiny_size = tiny.shape[0]
    tiny = jnp.pad(tiny, (0, width * tiny_lanes - tiny_size)).reshape(width, tiny_lanes)
    late = weight_products([(xn0, with_bc(dxt0, bc_sum))])
    late = late + jnp.pad(tiny, ((0, 0), (tiny_at, 0))).astype(bf16)
    late = sum_x(late)
    halves = collect(after(early1, late))
    g_wz, g_wo = write_sums(place, halves, True, [(0, "rows", 1, None), (channels, "blocks", 1, None)])
    late = sum_beside(halve(sum_far(late)))
    early = sum_beside(halve(sum_far(after(early, dxt0))))
    g_wz, g_wo, g_wx, narrow1 = write_sums(
        place,
        collect(early),
        False,
        [
            (0, "rows", 0, g_wz),
            (channels, "blocks", 0, g_wo),
            (2 * channels, "rows", 1, None),
            (3 * channels, "flat", 0, None),
        ],
    )
    g_wx, narrow0 = write_sums(
        place, collect(late), False, [(0, "rows", 0, g_wx), (channels, "flat", 0, None)]
    )

    narrow0, narrow1 = narrow0[0], narrow1[0]
    tiny = narrow0[:, tiny_at - channels :].reshape(-1)[:tiny_size]
    sizes = [8 * channels, 8 * channels, 2 * LANES, 2 * LANES]
    cut = [sum(sizes[:i]) for i in range(len(sizes) + 1)]
    g_x = tiny[: cut[2]].reshape(layers, 8, channels)
    g_head = tiny[cut[2] : cut[4]].reshape(layers, 2, LANES)[:, :, :heads]
    shared = tiny[cut[4] :].reshape(layers, -1, both)
    lines = width // both
    g_norm_in = shared[:, :lines].reshape(layers, width) / norm_in
    g_bc = shared[:, lines : lines + 5]
    return (
        outputs[None, :, :width],
        outputs[None, :, width:],
        g_norm_in,
        g_wz,
        g_wx,
        jnp.stack([v[:, bc_at - channels : tiny_at - channels] for v in (narrow0, narrow1)]),
        jnp.stack([v[:, :heads] for v in (narrow0, narrow1)]),
        g_x[:, 0:4],
        g_x[:, 4],
        g_bc[:, 0:4],
        g_bc[:, 4],
        g_head[:, 0],
        g_head[:, 1],
        jnp.sum(g_x[:, 6].reshape(layers, heads, head_dim), axis=2),
        g_x[:, 5],
        g_wo,
    )


def solution(mesh):
    specs_in = (
        P("dp", "tensor", None),
        P("dp", "tensor", None),
        P(),
        P(None, None, "tensor"),
        P(None, None, "tensor"),
        P(None, None, "tensor"),
        P(None, None, "tensor"),
        P(None, None, "tensor"),
        P(None, "tensor"),
        P(),
        P(),
        P(None, "tensor"),
        P(None, "tensor"),
        P(None, "tensor"),
        P(None, "tensor"),
        P(None, "tensor", None),
    )
    specs_out = (
        P("dp", "tensor", None),
        P("dp", "tensor", None),
        P(),
        P(None, None, "tensor"),
        P(None, None, "tensor"),
        P(None, None, "tensor"),
        P(None, None, "tensor"),
        P(None, None, "tensor"),
        P(None, "tensor"),
        P(),
        P(),
        P(None, "tensor"),
        P(None, "tensor"),
        P(None, "tensor"),
        P(None, "tensor"),
        P(None, "tensor", None),
    )
    return jax.shard_map(
        local, mesh=mesh, in_specs=specs_in, out_specs=specs_out, check_vma=False
    )
```

```python
import functools

import jax
import jax.numpy as jnp
from jax import lax
from jax.experimental import pallas as pl
from jax.experimental.pallas import tpu as pltpu
from jax.sharding import PartitionSpec as P

SPAN = 256
EPS = 1e-05
LANES = 128
VMEM_BYTES = 56 * 1024 * 1024

f32 = jnp.float32
bf16 = jnp.bfloat16
highest = lax.Precision.HIGHEST

ROWS = ((0,), (0,))
COLS = ((1,), (1,))
PLAIN = ((1,), (0,))


def dot(left, right, dims=PLAIN, precision=None):
    return lax.dot_general(
        left, right, (dims, ((), ())), preferred_element_type=f32, precision=precision
    )


def sigmoid(v):
    return 1.0 / (1.0 + jnp.exp(-v))


def softplus(v):
    return jnp.maximum(v, 0.0) + jnp.log1p(jnp.exp(-jnp.abs(v)))


def spread_heads(per_head, channels, head_dim):
    rows = per_head.shape[0]
    per_tile = LANES // head_dim
    lane = lax.broadcasted_iota(jnp.int32, (rows, LANES), 1)
    tiles = []
    for tile in range(channels // LANES):
        out = jnp.broadcast_to(
            per_head[:, tile * per_tile : tile * per_tile + 1], (rows, LANES)
        )
        for sub in range(1, per_tile):
            head = tile * per_tile + sub
            out = jnp.where(
                lane >= sub * head_dim,
                jnp.broadcast_to(per_head[:, head : head + 1], (rows, LANES)),
                out,
            )
        tiles.append(out)
    return jnp.concatenate(tiles, axis=1)


def conv_taps(buf, taps, offset, width):
    out = offset
    for j in range(4):
        out = out + taps[j : j + 1] * buf[pl.ds(5 + j, width), :]
    return out


def decay_matrix(mask, cum_col, cum_row):
    return jnp.exp(jnp.where(mask, cum_col - cum_row, -1e30))


def span_values(dt, head_ref):
    length = dt.shape[0]
    rows = lax.broadcasted_iota(jnp.int32, (length, length), 0)
    cols = lax.broadcasted_iota(jnp.int32, (length, length), 1)
    mask = rows >= cols
    pre = dt + head_ref[0:1, :]
    step = softplus(pre)
    rate = head_ref[1:2, :] * step
    cum = dot(mask.astype(f32), rate, PLAIN, highest)
    return mask, pre, step, rate, cum


def put_half(place_ref, span, half, mine_ref, other_ref, value):
    own = span // half == place_ref[0]

    @pl.when(own)
    def _():
        mine_ref[...] = value

    @pl.when(jnp.logical_not(own))
    def _():
        other_ref[...] = value


def place_pieces(plan, place_ref, pieces, outs):
    core, z = place_ref[0], place_ref[1]
    for piece, other, dz, start, out, per, offset, rows in plan:
        member = (1 - core if other else core) * NZ + lax.rem(z + dz, NZ)
        row = pl.multiple_of(member * per + offset, 16)
        outs[out][pl.ds(row, rows), :] = pieces[piece][start : start + rows, :]


def put_columns(place_ref, span, mine_ref, other_ref, columns):
    per = columns.shape[0] // (NC * NZ)
    rows = mine_ref.shape[0] // NZ

    def place_columns(core, ref):
        for z in range(NZ):
            at = (core * NZ + z) * per
            ref[pl.ds(pl.multiple_of(z * rows + span * per, 16), per), :] = columns[at : at + per, :]

    for core in range(NC):
        mine = place_ref[0] == core

        @pl.when(mine)
        def _(core=core):
            place_columns(core, mine_ref)

        @pl.when(jnp.logical_not(mine))
        def _(core=core):
            place_columns(core, other_ref)


def forward_kernel(plans, there_plan, head_dim, place_ref, *refs):
    last_layer = len(plans) == 2
    refs = list(refs)

    def take(count):
        taken = refs[:count]
        del refs[:count]
        return taken

    piece_refs = [take(count) for _, count in plans]
    [w_here] = take(1)
    w_there = take(len(there_plan))
    wdt_ref, cx_ref, cbc_ref, head_ref = take(4)
    w_ref, xn_ref, wbc_ref, z_ref, xp_ref, bc_ref, dt_ref, y_ref, hin_ref, mine_ref, other_ref = take(11)
    if last_layer:
        g_ref, sums_ref, gg_ref = take(3)
    w_sem, xn_all, xbuf, bbuf, hst = take(5)
    if last_layer:
        [g_all] = take(1)
    length = z_ref.shape[0]
    channels = cx_ref.shape[1]
    state = hst.shape[0]
    span = pl.program_id(0)

    @pl.when(span == 0)
    def _():
        @pl.when(place_ref[2] == 1)
        def _():
            pltpu.make_async_copy(w_here, w_ref, w_sem).start()

        @pl.when(place_ref[2] == 0)
        def _():
            for part, (start, k) in zip(w_there, there_plan):
                rows = part.shape[0]
                if k is not None:
                    start = pl.multiple_of(lax.rem(place_ref[3] + NX - k, NX) * rows, 16)
                pltpu.make_async_copy(part, w_ref.at[pl.ds(start, rows), :], w_sem).start()

        if last_layer:
            place_pieces(plans[0][0], place_ref, piece_refs[0], [xn_all])
            place_pieces(plans[1][0], place_ref, piece_refs[1], [g_all, wbc_ref])
        else:
            place_pieces(plans[0][0], place_ref, piece_refs[0], [xn_all, wbc_ref])
        xbuf[0:8, :] = jnp.zeros((8, channels), f32)
        bbuf[0:8, :] = jnp.zeros((8, 2 * state), f32)
        hst[...] = jnp.zeros_like(hst)
        pltpu.make_async_copy(w_here, w_ref, w_sem).wait()

    here = pl.ds(pl.multiple_of(span * length, length), length)
    xn = xn_all[here, :]
    xn_ref[...] = xn
    zx = dot(xn, w_ref[:, : 2 * channels])
    z = zx[:, :channels]
    z_ref[...] = z.astype(bf16)
    xp = zx[:, channels:]
    xp_ref[...] = xp.astype(bf16)
    xbuf[8:, :] = xp
    bc = dot(xn, wbc_ref[...], COLS).astype(bf16)
    bc_ref[...] = bc
    bbuf[8:, :] = bc.astype(f32)
    dt = dot(xn, wdt_ref[...], COLS)
    dt_ref[...] = dt

    pre_x = conv_taps(xbuf, cx_ref[0:4, :], cx_ref[4:5, :], length)
    xc = pre_x * sigmoid(pre_x)
    pre_bc = conv_taps(bbuf, cbc_ref[0:4, :], cbc_ref[4:5, :], length)
    bcc = (pre_bc * sigmoid(pre_bc)).astype(bf16)
    xbuf[0:8, :] = xbuf[length : length + 8, :]
    bbuf[0:8, :] = bbuf[length : length + 8, :]
    b_mat = bcc[:, :state]
    c_mat = bcc[:, state:]

    mask, _, step, _, cum = span_values(dt, head_ref)
    cum_t = jnp.transpose(cum)
    scores = dot(c_mat, b_mat, COLS)
    xs = xc * spread_heads(step, channels, head_dim)
    xs_b = xs.astype(bf16)
    lane = lax.broadcasted_iota(jnp.int32, (length, LANES), 1)
    per_tile = LANES // head_dim
    tiles = []
    for tile in range(channels // LANES):
        xs_tile = xs_b[:, tile * LANES : (tile + 1) * LANES]
        out = None
        for sub in range(per_tile):
            head = tile * per_tile + sub
            decay = decay_matrix(mask, cum[:, head : head + 1], cum_t[head : head + 1, :])
            part = dot((scores * decay).astype(bf16), xs_tile)
            out = part if out is None else jnp.where(lane >= sub * head_dim, part, out)
        tiles.append(out)
    hin = hst[...]
    hin_ref[0] = hin
    last = cum[length - 1 : length, :]
    y = jnp.concatenate(tiles, axis=1)
    y = y + dot(c_mat, hin.astype(bf16)) * spread_heads(jnp.exp(cum), channels, head_dim)
    y = y + cx_ref[6:7, :] * xc
    y_ref[...] = y.astype(bf16)
    tail = spread_heads(jnp.exp(last - cum), channels, head_dim)
    keep = spread_heads(jnp.exp(last), channels, head_dim)
    hst[...] = keep * hin + dot(b_mat, (tail * xs).astype(bf16), ROWS)

    gated = y * (z * sigmoid(z))
    scaled = gated * cx_ref[5:6, :]
    squares = jnp.sum(gated * gated, axis=1, keepdims=True)
    high = squares.astype(bf16).astype(f32)
    extra = jnp.where(lane == 0, high, jnp.where(lane == 1, squares - high, 0.0)).astype(bf16)
    mixed = dot(scaled.astype(bf16), w_ref[:, 2 * channels :], COLS).astype(bf16)
    put_half(
        place_ref,
        span,
        pl.num_programs(0) // 2,
        mine_ref,
        other_ref,
        jnp.concatenate([mixed, extra], axis=1),
    )
    if last_layer:
        g = g_all[here, :]
        g_ref[...] = g
        gg = dot(g, w_ref[:, 2 * channels :])
        gg_ref[...] = gg
        products = jnp.sum(gg * scaled, axis=1, keepdims=True)
        both = jnp.where(lane == 0, squares, jnp.where(lane == 1, products, 0.0))
        sums_ref[...] = jnp.transpose(both)[0:8, :]


def gate_part(gg, rms, coef, z, y, cx_ref):
    z, y = z.astype(f32), y.astype(f32)
    norm_gate = cx_ref[5:6, :]
    sz = sigmoid(z)
    silu_z = z * sz
    gated = y * silu_z
    rg = rms * gg
    gate_out = (gated * rms * norm_gate).astype(bf16)
    d_gated = rg * norm_gate - gated * coef
    dz = (d_gated * y * (sz * (1.0 + z * (1.0 - sz)))).astype(bf16)
    return dz, d_gated * silu_z, gate_out, jnp.sum(rg * gated, axis=0, keepdims=True)


def gate_kernel(plan, n_pieces, width, place_ref, *refs):
    pieces = refs[:n_pieces]
    z_ref, y_ref, wo_ref, cx_ref, g_ref, dz_ref, dy_ref, go_ref, acc_ref, first_all = refs[n_pieces:]
    length = z_ref.shape[0]
    span = pl.program_id(0)

    @pl.when(span == 0)
    def _():
        place_pieces(plan, place_ref, pieces, [first_all])
        acc_ref[...] = jnp.zeros_like(acc_ref)

    first = first_all[pl.ds(pl.multiple_of(span * length, length), length), :]
    g = first[:, :width]
    g_ref[...] = g
    tok = first[:, width:].astype(f32)
    rms = tok[:, 0:1] + tok[:, 1:2]
    coef = tok[:, 2:3] + tok[:, 3:4]
    gg = dot(g, wo_ref[...])
    dz, dy, gate_out, acc_norm = gate_part(gg, rms, coef, z_ref[...], y_ref[...], cx_ref)
    dz_ref[...] = dz
    dy_ref[...] = dy
    go_ref[...] = gate_out
    acc_ref[5:6, :] += acc_norm


def scan_kernel(with_gate, head_dim, inner_all, place_ref, *refs):
    if with_gate:
        (gg_ref, tok_ref, z_ref, y_ref), refs = refs[:4], refs[4:]
    else:
        (dy_ref, dz_ref), refs = refs[:2], refs[2:]
    (xn_ref, xp_ref, xhalo_ref, bc_ref, bchalo_ref, dt_ref, hin_ref,
     w_ref, wbc_ref, wdt_ref, cx_ref, cbc_ref, head_ref, pick_ref), refs = refs[:14], refs[14:]
    if with_gate:
        (dz_ref, go_ref), refs = refs[:2], refs[2:]
    (dxt_ref, bcmine_ref, bcother_ref, mine_ref, other_ref, acc_ref, acch_ref, shared_ref,
     accbc, accn, xbuf, bbuf, dubuf, dubbuf, dhst) = refs
    length = xp_ref.shape[0]
    channels = cx_ref.shape[1]
    width = xn_ref.shape[1]
    state = dhst.shape[0]
    step_id = pl.program_id(0)
    first_span = step_id == pl.num_programs(0) - 1

    @pl.when(step_id == 0)
    def _():
        dubuf[length:, :] = jnp.zeros((8, channels), f32)
        dubbuf[length:, :] = jnp.zeros((8, 2 * state), f32)
        dhst[...] = jnp.zeros_like(dhst)
        accn[...] = jnp.zeros_like(accn)
        acc_ref[...] = jnp.zeros_like(acc_ref)
        accbc[...] = jnp.zeros_like(accbc)
        acch_ref[...] = jnp.zeros_like(acch_ref)

    @pl.when(first_span)
    def _():
        xbuf[0:8, :] = jnp.zeros((8, channels), f32)
        bbuf[0:8, :] = jnp.zeros((8, 2 * state), f32)

    @pl.when(jnp.logical_not(first_span))
    def _():
        xbuf[0:8, :] = xhalo_ref[...].astype(f32)[8:16, :]
        bbuf[0:8, :] = bchalo_ref[...].astype(f32)[8:16, :]

    xbuf[8:, :] = xp_ref[...].astype(f32)
    bbuf[8:, :] = bc_ref[...].astype(f32)
    if with_gate:
        tok = jnp.transpose(tok_ref[...])
        rms = lax.rsqrt(tok[:, 0:1] / inner_all + EPS)
        coef = rms * rms * rms * tok[:, 1:2] / inner_all
        dz_b, dy, gate_out, acc_norm = gate_part(
            gg_ref[...], rms, coef, z_ref[...], y_ref[...], cx_ref
        )
        dz_ref[...] = dz_b
        go_ref[...] = gate_out
    else:
        dz_b, dy = dz_ref[...], dy_ref[...]
        acc_norm = jnp.zeros((1, channels), f32)
    skip = cx_ref[6:7, :]

    pre_x = conv_taps(xbuf, cx_ref[0:4, :], cx_ref[4:5, :], length)
    sx = sigmoid(pre_x)
    xc = pre_x * sx
    pre_bc = conv_taps(bbuf, cbc_ref[0:4, :], cbc_ref[4:5, :], length)
    sbc = sigmoid(pre_bc)
    bcc = (pre_bc * sbc).astype(bf16)
    b_mat = bcc[:, :state]
    c_mat = bcc[:, state:]
    mask, pre_dt, step, rate, cum = span_values(dt_ref[...], head_ref)
    cum_t = jnp.transpose(cum)
    last = cum[length - 1 : length, :]
    scores = dot(c_mat, b_mat, COLS)
    step_all = spread_heads(step, channels, head_dim)
    xs = xc * step_all
    xs_b = xs.astype(bf16)
    tail = spread_heads(jnp.exp(last - cum), channels, head_dim)
    keep = spread_heads(jnp.exp(last), channels, head_dim)

    hin = hin_ref[0]
    hin_b = hin.astype(bf16)
    dh = dhst[...]
    dh_b = dh.astype(bf16)
    dye = dy * spread_heads(jnp.exp(cum), channels, head_dim)
    dye_b = dye.astype(bf16)
    txs = tail * xs
    txs_b = txs.astype(bf16)
    carried = dot(c_mat, hin_b)
    pulled = dot(b_mat, dh_b)
    d_c = dot(dye_b, hin_b, COLS)
    d_b = dot(txs_b, dh_b, COLS)
    dhst[...] = keep * dh + dot(c_mat, dye_b, ROWS)
    into = txs * pulled
    across = dye * carried - into
    at_last = jnp.sum(into, axis=0, keepdims=True) + keep * jnp.sum(hin * dh, axis=0, keepdims=True)

    dy_b = dy.astype(bf16)
    dy_t = jnp.transpose(dy).astype(bf16)
    lane = lax.broadcasted_iota(jnp.int32, (length, LANES), 1)
    per_tile = LANES // head_dim
    d_scores = jnp.zeros((length, length), f32)
    row_sums = jnp.zeros((length, LANES), f32)
    col_sums = []
    dxs_parts = []
    for head in range(channels // head_dim):
        tile, sub = divmod(head, per_tile)
        dy_tile = dy_b[:, tile * LANES : (tile + 1) * LANES]
        own = (lane >= sub * head_dim) & (lane < (sub + 1) * head_dim)
        dy_head = jnp.where(own, dy_tile, jnp.zeros_like(dy_tile))
        d_m = dot(dy_head, xs_b[:, tile * LANES : (tile + 1) * LANES], COLS)
        decay = decay_matrix(mask, cum[:, head : head + 1], cum_t[head : head + 1, :])
        dxs_parts.append(
            dot(dy_t[head * head_dim : (head + 1) * head_dim, :], (scores * decay).astype(bf16))
        )
        d_m = d_m * decay
        d_scores = d_scores + d_m
        pairs = d_m * scores
        row_sums = jnp.where(lane == head, jnp.sum(pairs, axis=1, keepdims=True), row_sums)
        col_sums.append(jnp.sum(pairs, axis=0, keepdims=True))
    heads = len(col_sums)
    col_sums = jnp.concatenate(col_sums + [jnp.zeros((LANES - heads, length), f32)], axis=0)
    dxs = jnp.transpose(jnp.concatenate(dxs_parts, axis=0)) + tail * pulled
    pick = pick_ref[...]
    d_cum = row_sums - jnp.transpose(col_sums) + dot(across, pick, PLAIN, highest)
    at_last = dot(jnp.broadcast_to(at_last, (8, channels)), pick, PLAIN, highest)[0:1, :]
    d_rate = dot(mask.astype(f32), d_cum, ROWS, highest) + at_last
    d_step = d_rate * head_ref[1:2, :] + dot(dxs * xc, pick, PLAIN, highest)
    d_dt = d_step * sigmoid(pre_dt)
    acch_ref[0:1, :] += jnp.sum(d_dt, axis=0, keepdims=True)
    acch_ref[1:2, :] += jnp.sum(d_rate * rate, axis=0, keepdims=True)
    dt_b = d_dt.astype(bf16)
    ds_b = d_scores.astype(bf16)
    d_c = d_c + dot(ds_b, b_mat)
    d_b = d_b + dot(ds_b, c_mat, ROWS)
    d_xc = dxs * step_all + skip * dy
    acc_skip = jnp.sum(dy * xc, axis=0, keepdims=True)

    d_u = d_xc * (sx * (1.0 + pre_x * (1.0 - sx)))
    d_ub = jnp.concatenate([d_b, d_c], axis=1) * (sbc * (1.0 + pre_bc * (1.0 - sbc)))
    dubuf[0:length, :] = d_u
    dubbuf[0:length, :] = d_ub
    d_x = jnp.zeros_like(d_u)
    d_bc = jnp.zeros_like(d_ub)
    acc_rows = []
    accbc_rows = []
    for j in range(4):
        d_x = d_x + cx_ref[j : j + 1, :] * dubuf[pl.ds(3 - j, length), :]
        d_bc = d_bc + cbc_ref[j : j + 1, :] * dubbuf[pl.ds(3 - j, length), :]
        acc_rows.append(jnp.sum(d_u * xbuf[pl.ds(5 + j, length), :], axis=0, keepdims=True))
        accbc_rows.append(jnp.sum(d_ub * bbuf[pl.ds(5 + j, length), :], axis=0, keepdims=True))
    dubuf[length:, :] = d_u[0:8, :]
    dubbuf[length:, :] = d_ub[0:8, :]
    zero = jnp.zeros((1, channels), f32)
    acc_ref[...] += jnp.concatenate(
        acc_rows + [jnp.sum(d_u, axis=0, keepdims=True), acc_norm, acc_skip, zero], axis=0
    )
    zero = jnp.zeros((3, d_ub.shape[1]), f32)
    accbc[...] += jnp.concatenate(
        accbc_rows + [jnp.sum(d_ub, axis=0, keepdims=True), zero], axis=0
    )
    dx_b = d_x.astype(bf16)
    dbc_b = d_bc.astype(bf16)
    dxt_ref[:, :channels] = dx_b
    dxt_ref[:, channels:] = dt_b
    put_columns(
        place_ref,
        pl.num_programs(0) - 1 - step_id,
        bcmine_ref,
        bcother_ref,
        jnp.transpose(d_bc).astype(bf16),
    )
    total = dot(jnp.concatenate([dz_b, dx_b], axis=1), w_ref[...], COLS)
    total = total + dot(dbc_b, wbc_ref[...]) + dot(dt_b, wdt_ref[...])
    accn[0:1, :] += jnp.sum(total * xn_ref[...].astype(f32), axis=0, keepdims=True)

    @pl.when(first_span)
    def _():
        lanes = shared_ref.shape[1]
        lines = [accn[0:1, i * lanes : (i + 1) * lanes] for i in range(width // lanes)]
        shared = jnp.concatenate(lines + [accbc[0:5, :]], axis=0)
        shared_ref[0 : shared.shape[0], :] = shared.astype(bf16)
        shared_ref[shared.shape[0] :, :] = jnp.zeros(
            (shared_ref.shape[0] - shared.shape[0], lanes), bf16
        )

    put_half(
        place_ref,
        pl.num_programs(0) - 1 - step_id,
        pl.num_programs(0) // 2,
        mine_ref,
        other_ref,
        total.astype(bf16),
    )


def whole(shape):
    zeros = (0,) * len(shape)
    return pl.BlockSpec(shape, lambda i, p: zeros)


def span_rows(columns):
    return pl.BlockSpec((SPAN, columns), lambda i, p: (i, 0))


def half_rows(columns, spans, reverse):
    half = spans // 2

    def block(i, core):
        span = spans - 1 - i if reverse else i
        return jnp.clip(span - half * core, 0, half - 1), 0

    return [
        pl.BlockSpec((SPAN, columns), lambda i, p: block(i, p[0])),
        pl.BlockSpec((SPAN, columns), lambda i, p: block(i, 1 - p[0])),
    ]


def span_call(kernel, name, spans, place, operands, in_specs, shapes, out_specs, scratch, flops):
    moved = sum(v.size * v.dtype.itemsize for v in [*operands, *shapes])
    return pl.pallas_call(
        kernel,
        grid_spec=pltpu.PrefetchScalarGridSpec(
            num_scalar_prefetch=1,
            grid=(spans,),
            in_specs=in_specs,
            out_specs=out_specs,
            scratch_shapes=scratch,
        ),
        out_shape=shapes,
        compiler_params=pltpu.CompilerParams(
            dimension_semantics=("arbitrary",), vmem_limit_bytes=VMEM_BYTES
        ),
        cost_estimate=pl.CostEstimate(flops=flops, bytes_accessed=moved, transcendentals=0),
        name=name,
    )(place, *operands)


def run_forward(place, gathered, w, wdt, small, state, head_dim):
    w_here, w_there, there_plan = w
    channels = small[0].shape[1]
    width = gathered[0][0][0].shape[1]
    anywhere = pl.BlockSpec(memory_space=pl.ANY)
    tokens = NC * NZ * gathered[0][2][0]
    spans = tokens // SPAN
    last_layer = len(gathered) == 2
    plans = [(cut_plan(*one), len(one[0])) for one in gathered]
    operands = [p for one in gathered for p in one[0]]
    in_specs = [whole(v.shape) for v in operands] + [anywhere] * (1 + len(w_there))
    operands += [w_here, *w_there, wdt, *small]
    in_specs += [whole(v.shape) for v in operands[len(in_specs) :]]
    shapes = [
        jax.ShapeDtypeStruct(w_here.shape, bf16),
        jax.ShapeDtypeStruct((tokens, width), bf16),
        jax.ShapeDtypeStruct((2 * state, width), bf16),
        jax.ShapeDtypeStruct((tokens, channels), bf16),
        jax.ShapeDtypeStruct((tokens, channels), bf16),
        jax.ShapeDtypeStruct((tokens, 2 * state), bf16),
        jax.ShapeDtypeStruct((tokens, LANES), f32),
        jax.ShapeDtypeStruct((tokens, channels), bf16),
        jax.ShapeDtypeStruct((spans, state, channels), f32),
        jax.ShapeDtypeStruct((tokens // 2, width + LANES), bf16),
        jax.ShapeDtypeStruct((tokens // 2, width + LANES), bf16),
    ]
    out_specs = [whole(w_here.shape), span_rows(width), whole((2 * state, width))]
    out_specs += [span_rows(s.shape[1]) for s in shapes[3:8]]
    out_specs.append(pl.BlockSpec((1, state, channels), lambda i, p: (i, 0, 0)))
    out_specs += half_rows(width + LANES, spans, False)
    scratch = [
        pltpu.SemaphoreType.DMA,
        pltpu.VMEM((tokens, width), bf16),
        pltpu.VMEM((SPAN + 8, channels), f32),
        pltpu.VMEM((SPAN + 8, 2 * state), f32),
        pltpu.VMEM((state, channels), f32),
    ]
    if last_layer:
        shapes += [
            jax.ShapeDtypeStruct((tokens, width), bf16),
            jax.ShapeDtypeStruct((8, tokens), f32),
            jax.ShapeDtypeStruct((tokens, channels), f32),
        ]
        out_specs += [span_rows(width), pl.BlockSpec((8, SPAN), lambda i, p: (0, i)), span_rows(channels)]
        scratch.append(pltpu.VMEM((tokens, width), bf16))
    kernel = functools.partial(forward_kernel, plans, there_plan, head_dim)
    return span_call(
        kernel, "layer_forward", spans, place, operands, in_specs, shapes, out_specs, scratch, 20 * 10**9
    )


def run_gate(place, gathered, z, y, w, cx):
    tokens, channels = z.shape
    width = w.shape[0]
    spans = tokens // SPAN
    plan, pieces = cut_plan(*gathered), list(gathered[0])
    operands = [*pieces, z, y, w, cx]
    in_specs = [whole(p.shape) for p in pieces]
    in_specs += [span_rows(channels), span_rows(channels)]
    in_specs += [pl.BlockSpec((width, channels), lambda i, p: (0, 2)), whole(cx.shape)]
    shapes = [
        jax.ShapeDtypeStruct((tokens, width), bf16),
        jax.ShapeDtypeStruct((tokens, channels), bf16),
        jax.ShapeDtypeStruct((tokens, channels), f32),
        jax.ShapeDtypeStruct((tokens, channels), bf16),
        jax.ShapeDtypeStruct((8, channels), f32),
    ]
    out_specs = [span_rows(s.shape[1]) for s in shapes[:4]] + [whole(shapes[4].shape)]
    scratch = [pltpu.VMEM((tokens, pieces[0].shape[1]), bf16)]
    kernel = functools.partial(gate_kernel, plan, len(pieces), width)
    return span_call(
        kernel, "gate_backward", spans, place, operands, in_specs, shapes, out_specs, scratch, 6 * 10**9
    )


def run_scan(place, lead, xn, xp, bc, dt, hin, weights, small, pick, head_dim, inner_all):
    tokens, channels = xp.shape
    state = hin.shape[1]
    width = xn.shape[1]
    spans = tokens // SPAN
    with_gate = len(lead) == 4

    def rev(columns):
        return pl.BlockSpec((SPAN, columns), lambda i, p: (spans - 1 - i, 0))

    def halo(columns, rows):
        per = SPAN // rows
        return pl.BlockSpec(
            (rows, columns), lambda i, p: (jnp.maximum((spans - 1 - i) * per - 1, 0), 0)
        )

    operands = [*lead, xn, xp, xp, bc, bc, dt, hin, *weights, *small, pick]
    in_specs = [rev(channels)] * 2
    if with_gate:
        tok = pl.BlockSpec((8, SPAN), lambda i, p: (0, spans - 1 - i))
        in_specs = [rev(channels), tok, rev(channels), rev(channels)]
    in_specs += [
        rev(width),
        rev(channels),
        halo(channels, 16),
        rev(2 * state),
        halo(2 * state, 16),
        rev(LANES),
        pl.BlockSpec((1, state, channels), lambda i, p: (spans - 1 - i, 0, 0)),
    ]
    in_specs.append(whole((width, 2 * channels)))
    in_specs += [whole(v.shape) for v in operands[len(in_specs) :]]
    shapes = [
        jax.ShapeDtypeStruct((tokens, channels + LANES), bf16),
        jax.ShapeDtypeStruct((state * spans, SPAN), bf16),
        jax.ShapeDtypeStruct((state * spans, SPAN), bf16),
        jax.ShapeDtypeStruct((tokens // 2, width), bf16),
        jax.ShapeDtypeStruct((tokens // 2, width), bf16),
        jax.ShapeDtypeStruct((8, channels), f32),
        jax.ShapeDtypeStruct((8, LANES), f32),
        jax.ShapeDtypeStruct((16, 2 * state), bf16),
    ]
    out_specs = [rev(channels + LANES), whole(shapes[1].shape), whole(shapes[2].shape)]
    out_specs += half_rows(width, spans, True)
    out_specs += [whole(s.shape) for s in shapes[5:]]
    if with_gate:
        shapes = [jax.ShapeDtypeStruct((tokens, channels), bf16)] * 2 + shapes
        out_specs = [rev(channels)] * 2 + out_specs
    scratch = [
        pltpu.VMEM((8, 2 * state), f32),
        pltpu.VMEM((8, width), f32),
        pltpu.VMEM((SPAN + 8, channels), f32),
        pltpu.VMEM((SPAN + 8, 2 * state), f32),
        pltpu.VMEM((SPAN + 8, channels), f32),
        pltpu.VMEM((SPAN + 8, 2 * state), f32),
        pltpu.VMEM((state, channels), f32),
    ]
    kernel = functools.partial(scan_kernel, with_gate, head_dim, inner_all)
    return span_call(
        kernel, "scan_backward", spans, place, operands, in_specs, shapes, out_specs, scratch, 28 * 10**9
    )


def weight_kernel(n_pairs, split, place_ref, *refs):
    lefts, rights, outs = refs[:n_pairs], refs[n_pairs : 2 * n_pairs], refs[2 * n_pairs :]

    def write(out_ref):
        at = 0
        for left_ref, right_ref in zip(lefts, rights):
            columns = right_ref.shape[1]
            out_ref[:, at : at + columns] = dot(left_ref[...], right_ref[...], ROWS).astype(bf16)
            at += columns

    if not split:
        write(outs[0])
        return
    for k, out_ref in enumerate(outs):
        pl.when(pl.program_id(0) == k)(functools.partial(write, out_ref))


def weight_products(place, pairs, split=True):
    tokens = pairs[0][0].shape[0]
    rows = max(left.shape[1] for left, _ in pairs)
    block = rows // 4

    def at(i, p):
        return lax.rem(p[3] + i, NX) if split else i

    lefts, rights, columns = [], [], []
    for left, right in pairs:
        quarter = left.shape[1] == block
        cut, uncut = (lambda i, p: (0, at(i, p))), (lambda i, p: (0, 0))
        lefts.append(pl.BlockSpec((tokens, block), uncut if quarter else cut))
        wide = block if quarter else right.shape[1]
        rights.append(pl.BlockSpec((tokens, wide), cut if quarter else uncut))
        columns.append(wide)
    columns = sum(columns)
    if split:
        out_specs = [whole((block, columns))] * 4
        shapes = [jax.ShapeDtypeStruct((block, columns), bf16)] * 4
    else:
        out_specs = [pl.BlockSpec((block, columns), lambda i, p: (i, 0))]
        shapes = [jax.ShapeDtypeStruct((rows, columns), bf16)]
    out = pl.pallas_call(
        functools.partial(weight_kernel, len(pairs), split),
        grid_spec=pltpu.PrefetchScalarGridSpec(
            num_scalar_prefetch=1, grid=(4,), in_specs=lefts + rights, out_specs=out_specs
        ),
        out_shape=shapes,
        compiler_params=pltpu.CompilerParams(vmem_limit_bytes=VMEM_BYTES),
        cost_estimate=pl.CostEstimate(
            flops=2 * tokens * rows * columns, bytes_accessed=8 * 10**6, transcendentals=0
        ),
        name="weight_products",
    )(place, *[left for left, _ in pairs], *[right for _, right in pairs])
    return out if split else out[0]


SIZES = (4, 2, 2, 2, 4)
NX, NYL, NC, NYH, NZ = SIZES
EVERY = [
    (x, yl, c, yh, z)
    for x in range(NX)
    for yl in range(NYL)
    for c in range(NC)
    for yh in range(NYH)
    for z in range(NZ)
]


def linear(x, yl, c, yh, z):
    return ((((x % NX) * NYL + yl % NYL) * NC + c % NC) * NYH + yh % NYH) * NZ + z % NZ


def send(v, step, only=None):
    pairs = [(linear(*d), linear(*step(*d))) for d in EVERY if only is None or only(*d)]
    return lax.ppermute(v, ("dp", "tensor"), pairs)


def send_z(v, k):
    return send(v, lambda x, yl, c, yh, z: (x, yl, c, yh, z + k))


def send_core(v):
    return send(v, lambda x, yl, c, yh, z: (x, yl, c + 1, yh, z))


def trade(v, k):
    return send(v, lambda x, yl, c, yh, z: (x, yl, yh, c, z + k))


def traded(v):
    return send(v, lambda x, yl, c, yh, z: (x, yl, yh, c, z), lambda x, yl, c, yh, z: c != yh)


def trade_places(v):
    _, _, core, yh, _ = position()
    return jnp.where(core == yh, v, traded(v))


def quarter_of_half(v):
    x = position()[0]
    rows = v.shape[0] // 2 // NX
    return traded(lax.dynamic_slice_in_dim(v, x * rows, rows, 0))


def traded_by_x(v, quarter, ready):
    half = v.shape[0] // 2
    parts, plan = [quarter], [(None, 0)]
    for k in range(1, NX):
        parts.append(
            send(quarter, lambda x, yl, c, yh, z, k=k: (x + k, yl, c, yh, z), lambda x, yl, c, yh, z: c != yh)
        )
        plan.append((None, k))
    return parts + [traded(after(v[half:], ready))], plan + [(half, None)]


def position():
    dp, tensor = lax.axis_index("dp"), lax.axis_index("tensor")
    return dp // (NYL * NC), dp // NC % NYL, dp % NC, tensor // NZ, tensor % NZ


def gather(v, parts, traded_own=None):
    arrays, sources = [], []
    for k in (0, 1, 3, 2):
        if traded_own is not None:
            piece = trade(v, k) if k else traded_own
        else:
            piece = send_z(v, k) if k else v
        arrays += [piece, send_core(piece)]
        sources += [(False, -k % NZ, 0), (True, -k % NZ, 0)]
    return arrays, sources, parts


def cut_plan(arrays, sources, parts):
    plan = []
    for number, (piece, (other, dz, first)) in enumerate(zip(arrays, sources)):
        base = 0
        for out, per in enumerate(parts):
            begin, end = max(first, base), min(first + piece.shape[0], base + per)
            if begin < end:
                plan.append((number, other, dz, begin - first, out, per, begin - base, end - begin))
            base += per
    return plan


def fold(mine, other):
    _, _, _, _, z = position()
    rows = mine.shape[0] // NZ
    blocks = []
    for k in range(NZ):
        at = (z + k) % NZ * rows
        a = lax.dynamic_slice_in_dim(mine, at, rows, 0).astype(f32)
        blocks.append(a + lax.dynamic_slice_in_dim(other, at, rows, 0).astype(f32))
    return blocks


def fold_beside(pairs):
    folded = [fold(mine, send_core(other)) for mine, other in pairs]
    return [jnp.concatenate([blocks[k] for blocks in folded], axis=1) for k in range(NZ)]


def scatter(*pairs):
    own, one, two, three = fold_beside(pairs)
    return [own] + [send_z(b.astype(bf16), k) for k, b in ((1, one), (2, two), (3, three))]


def scatter_with_sum(mine, other, shared, meanwhile):
    half = mine.shape[0]
    rows = half // NZ
    got = after(send_core(jnp.concatenate([other, shared], axis=0)), *meanwhile)
    blocks = fold(mine, got[:half])
    total_shared = shared.astype(f32) + got[half:].astype(f32)
    packed = total_shared.astype(bf16)
    total = blocks[0]
    for k in range(1, NZ):
        got = send_z(jnp.concatenate([blocks[k].astype(bf16), packed], axis=0), k)
        total = total + got[:rows].astype(f32)
        total_shared = total_shared + got[rows:].astype(f32)
    return total, total_shared


def sum_members(v):
    both = v + send_core(v)
    total = both
    for k in range(1, NZ):
        total = total + send_z(both, k)
    return total


def send_far(v):
    return send(v, lambda x, yl, c, yh, z: (x, yl, c, yh + 1, z), lambda x, yl, c, yh, z: c != yh)


def sum_far(v, far=None):
    far = send_far(v) if far is None else far
    return (v.astype(f32) + far.astype(f32)).astype(bf16)


def halve(v):
    _, _, core, yh, _ = position()
    half = v.shape[0] // 2
    near = send(
        v[half:], lambda x, yl, c, yh, z: (x, yl, c + 1, yh, z), lambda x, yl, c, yh, z: c == yh
    )
    return jnp.where(core == yh, v[:half], near)


def sum_beside(part):
    beside = send(part, lambda x, yl, c, yh, z: (x, yl + 1, c, yh, z))
    return (part.astype(f32) + beside.astype(f32)).astype(bf16)


def sum_x(blocks):
    total = blocks[0].astype(f32)
    for k in range(1, NX):
        got = send(blocks[k], lambda x, yl, c, yh, z, k=k: (x + k, yl, c, yh, z))
        total = total + got.astype(f32)
    return total.astype(bf16)


def cut_x(v):
    x = position()[0]
    rows = v.shape[0] // NX
    return [lax.dynamic_slice_in_dim(v, (x + k) % NX * rows, rows, 0) for k in range(NX)]


def collect_x(part):
    x = position()[0]
    out = jnp.zeros((NX,) + part.shape, bf16)
    out = lax.dynamic_update_index_in_dim(out, part, x, 0)
    for k in range(1, NX):
        block = send(part, lambda x, yl, c, yh, z, k=k: (x + k, yl, c, yh, z))
        out = lax.dynamic_update_index_in_dim(out, block, (x - k) % NX, 0)
    return out


def collect(part):
    out = collect_x(part)
    return out, send_core(out)


def write_kernel(plan, by_half, n_kept, place_ref, here_ref, there_ref, *refs):
    rows = here_ref.shape[1]

    def write(ref):
        for (column, kind, wide), out_ref in zip(plan, refs[n_kept:]):
            for x in range(NX):
                value = ref[x, :, column : column + wide].astype(f32)
                if kind != "blocks":
                    out_ref[0, 0 if by_half else x, x if by_half else 0] = value
                elif by_half:
                    at = x // 2 * wide
                    out_ref[0, x % 2 * rows : (x % 2 + 1) * rows, at : at + wide] = value
                else:
                    out_ref[0, :, x * wide : (x + 1) * wide] = value

    here = (pl.program_id(0) == 0) == (place_ref[2] == 1)

    @pl.when(here)
    def _():
        write(here_ref)

    @pl.when(jnp.logical_not(here))
    def _():
        write(there_ref)


def write_sums(place, halves, by_half, outputs):
    rows, columns = halves[0].shape[1:]
    total = 2 * NX * rows
    wide = total // 4
    plan, shapes, specs, finals, kept, alias = [], [], [], [], [], {}
    for column, kind, layer, array in outputs:
        lanes = LANES if kind == "flat" else wide
        layers = 1 if kind == "flat" else 2
        plan.append((column, kind, lanes))
        if kind == "blocks":
            shape = (layers, wide, total)
            if by_half:
                spec = pl.BlockSpec((1, wide, total // 2), lambda h, p, layer=layer: (layer, 0, h))
            else:
                spec = pl.BlockSpec((1, rows, total), lambda h, p, layer=layer: (layer, h, 0))
            finals.append(shape)
        elif by_half:
            shape = (layers, 2, NX, rows, lanes)
            spec = pl.BlockSpec((1, 1, NX, rows, lanes), lambda h, p, layer=layer: (layer, h, 0, 0, 0))
            finals.append((layers, total, lanes))
        else:
            shape = (layers, NX, 2, rows, lanes)
            spec = pl.BlockSpec((1, NX, 1, rows, lanes), lambda h, p, layer=layer: (layer, 0, h, 0, 0))
            finals.append((layers, total, lanes))
        shapes.append(jax.ShapeDtypeStruct(shape, f32))
        specs.append(spec)
        if array is not None:
            alias[3 + len(kept)] = len(shapes) - 1
            kept.append(array.reshape(shape))
    piece = pl.BlockSpec((NX, rows, columns), lambda h, p: (0, 0, 0))
    written = pl.pallas_call(
        functools.partial(write_kernel, plan, by_half, len(kept)),
        grid_spec=pltpu.PrefetchScalarGridSpec(
            num_scalar_prefetch=1,
            grid=(2,),
            in_specs=[piece, piece] + [pl.BlockSpec(memory_space=pl.ANY)] * len(kept),
            out_specs=specs,
        ),
        out_shape=shapes,
        input_output_aliases=alias,
        compiler_params=pltpu.CompilerParams(vmem_limit_bytes=VMEM_BYTES),
        name="write_sums",
    )(place, *halves, *kept)
    return [v.reshape(final) for v, final in zip(written, finals)]


def row_call(kernel, name, operands, shapes):
    return pl.pallas_call(
        kernel,
        grid=(1,),
        in_specs=[pl.BlockSpec((rows, v.shape[1]), lambda i: (0, 0)) for v, rows in operands],
        out_specs=[pl.BlockSpec(s.shape, lambda i: (0, 0)) for s in shapes],
        out_shape=shapes,
        compiler_params=pltpu.CompilerParams(vmem_limit_bytes=VMEM_BYTES),
        name=name,
    )(*[v for v, _ in operands])


def inverse_rms(v):
    return lax.rsqrt(jnp.mean(v * v, axis=-1, keepdims=True) + EPS)


def first_kernel(packed_ref, gain_ref, out_ref):
    rows = 128
    v = packed_ref[0:rows, :].astype(f32)
    out_ref[0:rows, :] = (v * inverse_rms(v) * gain_ref[...]).astype(bf16)
    out_ref[rows:, :] = packed_ref[rows : out_ref.shape[0], :]


def add_terms(own_ref, a_ref, b_ref, c_ref):
    total = own_ref[...].astype(f32) + a_ref[...].astype(f32)
    return total + (b_ref[...].astype(f32) + c_ref[...].astype(f32))


def unscaled_output(inner_all, terms, width):
    total = add_terms(*terms)
    squares = total[:, width : width + 1] + total[:, width + 1 : width + 2]
    gate_rms = lax.rsqrt(squares / inner_all + EPS)
    return gate_rms, total[:, :width] * gate_rms


def middle_kernel(inner_all, own_ref, a_ref, b_ref, c_ref, res_ref, gain_ref, res1_ref, mixed_ref, rms_ref, normed_ref):
    width = res_ref.shape[1]
    gate_rms, mixed = unscaled_output(inner_all, (own_ref, a_ref, b_ref, c_ref), width)
    res = res_ref[...].astype(f32) + mixed
    res1_ref[...] = res
    mixed_ref[...] = mixed
    rms_ref[...] = jnp.broadcast_to(gate_rms, rms_ref.shape)
    normed_ref[...] = (res * inverse_rms(res) * gain_ref[...]).astype(bf16)


def input_gradient(grad_normed, res, d_res, gain):
    inv = inverse_rms(res)
    scaled = grad_normed * gain
    dots = jnp.sum(scaled * res, axis=-1, keepdims=True) / res.shape[1]
    return d_res + inv * scaled - res * (inv * inv * inv) * dots


def between_kernel(inner_all, own_ref, a_ref, b_ref, c_ref, res_ref, dres_ref, gain_ref, mixed_ref, rms_ref, out_ref, sent_ref):
    width = res_ref.shape[1]
    grad_normed = add_terms(*(ref.at[:, 0:width] for ref in (own_ref, a_ref, b_ref, c_ref)))
    d_res = input_gradient(grad_normed, res_ref[...], dres_ref[...].astype(f32), gain_ref[...])
    out_ref[...] = d_res
    g_mixed = d_res.astype(bf16)
    sent_ref[:, :width] = g_mixed
    gate_rms = rms_ref[:, 0:1]
    products = jnp.sum(g_mixed.astype(f32) * mixed_ref[...], axis=-1, keepdims=True)
    coef = gate_rms * gate_rms * products / inner_all
    lane = lax.broadcasted_iota(jnp.int32, rms_ref.shape, 1)
    rms_high = gate_rms.astype(bf16).astype(f32)
    coef_high = coef.astype(bf16).astype(f32)
    extra = jnp.where(lane == 0, rms_high, jnp.where(lane == 1, gate_rms - rms_high, 0.0))
    extra = jnp.where(lane == 2, coef_high, jnp.where(lane == 3, coef - coef_high, extra))
    sent_ref[:, width:] = extra.astype(bf16)


def end_kernel(own_ref, a_ref, b_ref, c_ref, res_ref, dres_ref, gain_ref, hidden_ref, out_ref):
    width = res_ref.shape[1]
    grad_normed = add_terms(own_ref, a_ref, b_ref, c_ref)
    grad = input_gradient(grad_normed, res_ref[...].astype(f32), dres_ref[...], gain_ref[...])
    out_ref[:, :width] = hidden_ref[...]
    out_ref[:, width:] = grad.astype(bf16)


def last_kernel(inner_all, own_ref, a_ref, b_ref, c_ref, res_ref, out_ref):
    _, mixed = unscaled_output(inner_all, (own_ref, a_ref, b_ref, c_ref), res_ref.shape[1])
    out_ref[...] = (res_ref[...] + mixed).astype(bf16)


def after(v, *others):
    return lax.optimization_barrier((v, *others))[0]


def pad_to(v, rows, lanes):
    return jnp.pad(v, ((0, rows - v.shape[0]), (0, lanes - v.shape[1])))


def local(
    hidden_in,
    grad_out,
    norm_in,
    w_z,
    w_x,
    w_bc,
    w_dt,
    conv_x,
    conv_x_bias,
    conv_bc,
    conv_bc_bias,
    dt_bias,
    a_log,
    skip,
    norm_gate,
    w_out,
):
    layers, width, channels = w_z.shape
    heads = w_dt.shape[2]
    head_dim = channels // heads
    both = conv_bc.shape[2]
    state = both // 2
    members = NC * NZ
    inner_all = channels * members
    rows = hidden_in.shape[1]
    bc_rows = both // members
    x, _, core, yh, z = position()
    stays = core == yh
    place = jnp.stack([core, z, stays, x]).astype(jnp.int32)
    full = jax.ShapeDtypeStruct((rows, width), f32)

    def pack_weights(layer):
        return jnp.concatenate([w_z[layer], w_x[layer], w_out[layer].T], axis=1)

    bc_t = jnp.swapaxes(w_bc, 1, 2)
    dt_t = jnp.pad(jnp.swapaxes(w_dt, 1, 2), ((0, 0), (0, 8 - heads), (0, 0)))
    per_channel = jnp.concatenate(
        [conv_x, conv_x_bias[:, None], norm_gate[:, None], jnp.repeat(skip, head_dim, axis=1)[:, None]],
        axis=1,
    )
    per_channel = jnp.pad(per_channel, ((0, 0), (0, 1), (0, 0)))
    per_head = jnp.stack([dt_bias, -jnp.exp(a_log)], axis=1)
    per_head = jnp.pad(per_head, ((0, 0), (0, 6), (0, LANES - heads)))
    little = jnp.concatenate([per_channel, per_head], axis=2).reshape(layers * 8, channels + LANES)
    high = little.astype(bf16)
    low = (little - high.astype(f32)).astype(bf16)
    lines = pad_to(jnp.concatenate([high, low], axis=1), layers * 8, width)
    packed = jnp.concatenate([hidden_in[0], bc_t[0], dt_t.reshape(layers * 8, width), lines], axis=0)
    w0 = pack_weights(0)
    quarter = quarter_of_half(w0)
    packed = after(trade_places(packed), quarter)
    lines = packed[packed.shape[0] - layers * 8 :].astype(f32)
    little = lines[:, : channels + LANES] + lines[:, channels + LANES : 2 * (channels + LANES)]
    little = little.reshape(layers, 8, channels + LANES)

    w0 = w0, *traded_by_x(w0, quarter, packed)
    grads = jnp.concatenate([grad_out[0], bc_t[1]], axis=0)

    [sent] = row_call(
        first_kernel,
        "first_norm",
        [(packed, packed.shape[0]), (norm_in[0:1], 1)],
        [jax.ShapeDtypeStruct((rows + bc_rows, width), bf16)],
    )
    gathered0 = gather(sent, (rows, bc_rows))
    wdt = [pad_to(packed[rows + bc_rows + 8 * l : rows + bc_rows + 8 * (l + 1)], LANES, width) for l in range(layers)]
    smalls = []
    for layer in range(layers):
        cbc = jnp.concatenate([conv_bc[layer], conv_bc_bias[layer][None], jnp.zeros((3, both), f32)], axis=0)
        smalls.append((little[layer, :, :channels], cbc, little[layer, :, channels:]))
    channel_head = jnp.arange(channels) // head_dim
    pick = (channel_head[:, None] == jnp.arange(LANES)[None, :]).astype(f32)

    out0 = run_forward(place, [gathered0], w0, wdt[0], smalls[0], state, head_dim)
    w0, xn0, wbc0, z0, xp0, bc0, dt0, y0, hin0, mine, other = out0
    gathered_grad = gather(after(grads, *gathered0[0]), (rows, bc_rows), trade_places(grads))
    grad_held = gathered_grad[0][0]
    terms = scatter((mine, after(other, *gathered_grad[0][2::2])))
    w1 = pack_weights(1)
    w1 = w1, [traded(after(w1, terms[0]))], [(0, None)]
    res1, mixed0, rms0, normed1 = row_call(
        functools.partial(middle_kernel, inner_all),
        "middle_norm",
        [(v, rows) for v in terms] + [(packed, rows), (norm_in[1:2], 1)],
        [full, full, jax.ShapeDtypeStruct((rows, LANES), f32), jax.ShapeDtypeStruct((rows, width), bf16)],
    )
    gathered1 = gather(normed1, (rows,))
    out1 = run_forward(
        place, [gathered1, gathered_grad], w1, wdt[1], smalls[1], state, head_dim
    )
    w1, xn1, wbc1, z1, xp1, bc1, dt1, y1, hin1, mine, other, grad_rows1, sums, gg1 = out1
    sums = sum_members(sums)

    home = fold(mine, send_core(other))
    sums = after(sums, *home)
    home = home[:1] + [send_z(home[k].astype(bf16), k) for k in range(1, NZ)]
    back1 = run_scan(
        place, (gg1, sums, z1, y1), xn1, xp1, bc1, dt1, hin1, (w1, wbc1, wdt[1]), smalls[1], pick, head_dim,
        inner_all,
    )
    dz1, go1, dxt1, *bc_halves, mine, other, acc1, acch1, shared1 = back1
    terms = scatter((mine, after(other, *home)), bc_halves)
    early1 = weight_products(place, [(xn1, after(dz1, terms[0])), (go1, grad_rows1)], split=False)
    terms[3] = after(terms[3], early1)
    early1_far = send_far(early1)
    [hidden_out] = row_call(
        functools.partial(last_kernel, inner_all),
        "last_output",
        [(after(home[0], terms[1]), rows)] + [(v, rows) for v in home[1:]] + [(res1, rows)],
        [jax.ShapeDtypeStruct((rows, width), bf16)],
    )
    d_res1, sent = row_call(
        functools.partial(between_kernel, inner_all),
        "between_layers",
        [(v, rows) for v in terms]
        + [(res1, rows), (grad_held, rows), (norm_in[1:2], 1), (mixed0, rows), (rms0, rows)],
        [full, jax.ShapeDtypeStruct((rows, width + LANES), bf16)],
    )
    gathered_back = gather(sent, (rows,))

    bc_at = channels + bc_rows

    def with_bc(dxt, bc_sum):
        by_token = bc_sum.reshape(-1, bc_rows, SPAN).swapaxes(1, 2).reshape(-1, bc_rows)
        spread = jnp.pad(by_token, ((0, 0), (bc_at, dxt.shape[1] - bc_at - bc_rows)))
        return dxt + spread.astype(bf16)

    dxt1 = with_bc(dxt1, sum(v[:, width:].astype(f32) for v in terms))

    early1 = halve(sum_far(early1, after(early1_far, sent)))
    z0 = after(z0, early1)
    early1 = sum_x(cut_x(early1))
    grad_rows0, dz0, dy0, go0, acc_gate0 = run_gate(place, gathered_back, z0, y0, w0, smalls[0][0])
    dz0 = after(dz0, early1)
    early = weight_products(place, [(xn0, dz0), (go0, grad_rows0), (xn1, dxt1)])
    dy0 = after(dy0, *early)
    early = sum_x(early)
    early1 = sum_beside(after(early1, dz0))
    back0 = run_scan(
        place, (dy0, dz0), xn0, xp0, bc0, dt0, hin0, (w0, wbc0, wdt[0]), smalls[0], pick, head_dim, inner_all
    )
    dxt0, *bc_halves, mine, other, acc0, acch0, shared0 = back0
    terms = scatter((mine, other))
    [outputs] = row_call(
        end_kernel,
        "outputs",
        [(v, rows) for v in terms] + [(packed, rows), (d_res1, rows), (norm_in[0:1], 1), (hidden_out, rows)],
        [jax.ShapeDtypeStruct((rows, 2 * width), bf16)],
    )
    outputs = trade_places(outputs).astype(f32)

    shared = jnp.concatenate([shared0, shared1], axis=0)
    bc_sum, shared = scatter_with_sum(*bc_halves, shared, (early,))
    tiny = jnp.concatenate(
        [(acc0 + acc_gate0).reshape(-1), acc1.reshape(-1), acch0[0:2].reshape(-1), acch1[0:2].reshape(-1)]
        + [shared.reshape(-1)]
    )
    tiny_at = bc_at + bc_rows
    tiny_lanes = channels + LANES - tiny_at
    tiny_size = tiny.shape[0]
    tiny = jnp.pad(tiny, (0, width * tiny_lanes - tiny_size)).reshape(width, tiny_lanes)
    tiny = jnp.pad(tiny, ((0, 0), (tiny_at, 0))).astype(bf16)
    late = weight_products(place, [(xn0, with_bc(dxt0, bc_sum))])
    late = sum_x([v + t for v, t in zip(late, cut_x(tiny))])
    halves = collect(after(early1, late))
    g_wz, g_wo = write_sums(place, halves, True, [(0, "rows", 1, None), (channels, "blocks", 1, None)])
    late = sum_beside(halve(sum_far(late)))
    early = sum_beside(halve(sum_far(after(early, dxt0))))
    g_wz, g_wo, g_wx, narrow1 = write_sums(
        place,
        collect(early),
        False,
        [
            (0, "rows", 0, g_wz),
            (channels, "blocks", 0, g_wo),
            (2 * channels, "rows", 1, None),
            (3 * channels, "flat", 0, None),
        ],
    )
    g_wx, narrow0 = write_sums(
        place, collect(late), False, [(0, "rows", 0, g_wx), (channels, "flat", 0, None)]
    )

    narrow0, narrow1 = narrow0[0], narrow1[0]
    tiny = narrow0[:, tiny_at - channels :].reshape(-1)[:tiny_size]
    sizes = [8 * channels, 8 * channels, 2 * LANES, 2 * LANES]
    cut = [sum(sizes[:i]) for i in range(len(sizes) + 1)]
    g_x = tiny[: cut[2]].reshape(layers, 8, channels)
    g_head = tiny[cut[2] : cut[4]].reshape(layers, 2, LANES)[:, :, :heads]
    shared = tiny[cut[4] :].reshape(layers, -1, both)
    lines = width // both
    g_norm_in = shared[:, :lines].reshape(layers, width) / norm_in
    g_bc = shared[:, lines : lines + 5]
    return (
        outputs[None, :, :width],
        outputs[None, :, width:],
        g_norm_in,
        g_wz,
        g_wx,
        jnp.stack([v[:, bc_at - channels : tiny_at - channels] for v in (narrow0, narrow1)]),
        jnp.stack([v[:, :heads] for v in (narrow0, narrow1)]),
        g_x[:, 0:4],
        g_x[:, 4],
        g_bc[:, 0:4],
        g_bc[:, 4],
        g_head[:, 0],
        g_head[:, 1],
        jnp.sum(g_x[:, 6].reshape(layers, heads, head_dim), axis=2),
        g_x[:, 5],
        g_wo,
    )


def solution(mesh):
    specs_in = (
        P("dp", "tensor", None),
        P("dp", "tensor", None),
        P(),
        P(None, None, "tensor"),
        P(None, None, "tensor"),
        P(None, None, "tensor"),
        P(None, None, "tensor"),
        P(None, None, "tensor"),
        P(None, "tensor"),
        P(),
        P(),
        P(None, "tensor"),
        P(None, "tensor"),
        P(None, "tensor"),
        P(None, "tensor"),
        P(None, "tensor", None),
    )
    specs_out = (
        P("dp", "tensor", None),
        P("dp", "tensor", None),
        P(),
        P(None, None, "tensor"),
        P(None, None, "tensor"),
        P(None, None, "tensor"),
        P(None, None, "tensor"),
        P(None, None, "tensor"),
        P(None, "tensor"),
        P(),
        P(),
        P(None, "tensor"),
        P(None, "tensor"),
        P(None, "tensor"),
        P(None, "tensor"),
        P(None, "tensor", None),
    )
    return jax.shard_map(
        local, mesh=mesh, in_specs=specs_in, out_specs=specs_out, check_vma=False
    )
```

```python
import functools

import jax
import jax.numpy as jnp
from jax import lax
from jax.experimental import pallas as pl
from jax.experimental.pallas import tpu as pltpu
from jax.sharding import PartitionSpec as P

SPAN = 256
EPS = 1e-05
LANES = 128
VMEM_BYTES = 56 * 1024 * 1024

f32 = jnp.float32
bf16 = jnp.bfloat16
highest = lax.Precision.HIGHEST

ROWS = ((0,), (0,))
COLS = ((1,), (1,))
PLAIN = ((1,), (0,))


def dot(left, right, dims=PLAIN, precision=None):
    return lax.dot_general(
        left, right, (dims, ((), ())), preferred_element_type=f32, precision=precision
    )


def sigmoid(v):
    return 1.0 / (1.0 + jnp.exp(-v))


def softplus(v):
    return jnp.maximum(v, 0.0) + jnp.log1p(jnp.exp(-jnp.abs(v)))


def spread_heads(per_head, channels, head_dim):
    rows = per_head.shape[0]
    per_tile = LANES // head_dim
    lane = lax.broadcasted_iota(jnp.int32, (rows, LANES), 1)
    tiles = []
    for tile in range(channels // LANES):
        out = jnp.broadcast_to(
            per_head[:, tile * per_tile : tile * per_tile + 1], (rows, LANES)
        )
        for sub in range(1, per_tile):
            head = tile * per_tile + sub
            out = jnp.where(
                lane >= sub * head_dim,
                jnp.broadcast_to(per_head[:, head : head + 1], (rows, LANES)),
                out,
            )
        tiles.append(out)
    return jnp.concatenate(tiles, axis=1)


def conv_taps(buf, taps, offset, width):
    out = offset
    for j in range(4):
        out = out + taps[j : j + 1] * buf[pl.ds(5 + j, width), :]
    return out


def decay_matrix(mask, cum_col, cum_row):
    return jnp.exp(jnp.where(mask, cum_col - cum_row, -1e30))


def span_values(dt, head_ref):
    length = dt.shape[0]
    rows = lax.broadcasted_iota(jnp.int32, (length, length), 0)
    cols = lax.broadcasted_iota(jnp.int32, (length, length), 1)
    mask = rows >= cols
    pre = dt + head_ref[0:1, :]
    step = softplus(pre)
    rate = head_ref[1:2, :] * step
    cum = dot(mask.astype(f32), rate, PLAIN, highest)
    return mask, pre, step, rate, cum


def put_half(place_ref, span, half, mine_ref, other_ref, value):
    own = span // half == place_ref[0]

    @pl.when(own)
    def _():
        mine_ref[...] = value

    @pl.when(jnp.logical_not(own))
    def _():
        other_ref[...] = value


def place_pieces(plan, place_ref, pieces, outs):
    core, z = place_ref[0], place_ref[1]
    for piece, other, dz, start, out, per, offset, rows in plan:
        member = (1 - core if other else core) * NZ + lax.rem(z + dz, NZ)
        row = pl.multiple_of(member * per + offset, 16)
        outs[out][pl.ds(row, rows), :] = pieces[piece][start : start + rows, :]


def put_columns(place_ref, span, mine_ref, other_ref, columns):
    per = columns.shape[0] // (NC * NZ)
    rows = mine_ref.shape[0] // NZ

    def place_columns(core, ref):
        for z in range(NZ):
            at = (core * NZ + z) * per
            ref[pl.ds(pl.multiple_of(z * rows + span * per, 16), per), :] = columns[at : at + per, :]

    for core in range(NC):
        mine = place_ref[0] == core

        @pl.when(mine)
        def _(core=core):
            place_columns(core, mine_ref)

        @pl.when(jnp.logical_not(mine))
        def _(core=core):
            place_columns(core, other_ref)


def forward_kernel(plans, there_plan, head_dim, place_ref, *refs):
    last_layer = len(plans) == 2
    refs = list(refs)

    def take(count):
        taken = refs[:count]
        del refs[:count]
        return taken

    piece_refs = [take(count) for _, count in plans]
    [w_here] = take(1)
    w_there = take(len(there_plan))
    wdt_ref, cx_ref, cbc_ref, head_ref = take(4)
    w_ref, xn_ref, wbc_ref, z_ref, xp_ref, bc_ref, dt_ref, y_ref, hin_ref, mine_ref, other_ref = take(11)
    if last_layer:
        g_ref, sums_ref, gg_ref = take(3)
    w_sem, xn_all, xbuf, bbuf, hst = take(5)
    if last_layer:
        [g_all] = take(1)
    length = z_ref.shape[0]
    channels = cx_ref.shape[1]
    state = hst.shape[0]
    span = pl.program_id(0)

    @pl.when(span == 0)
    def _():
        @pl.when(place_ref[2] == 1)
        def _():
            pltpu.make_async_copy(w_here, w_ref, w_sem).start()

        @pl.when(place_ref[2] == 0)
        def _():
            for part, (start, k) in zip(w_there, there_plan):
                rows = part.shape[0]
                if k is not None:
                    start = pl.multiple_of(lax.rem(place_ref[3] + NX - k, NX) * rows, 16)
                pltpu.make_async_copy(part, w_ref.at[pl.ds(start, rows), :], w_sem).start()

        if last_layer:
            place_pieces(plans[0][0], place_ref, piece_refs[0], [xn_all])
            place_pieces(plans[1][0], place_ref, piece_refs[1], [g_all, wbc_ref])
        else:
            place_pieces(plans[0][0], place_ref, piece_refs[0], [xn_all, wbc_ref])
        xbuf[0:8, :] = jnp.zeros((8, channels), f32)
        bbuf[0:8, :] = jnp.zeros((8, 2 * state), f32)
        hst[...] = jnp.zeros_like(hst)
        pltpu.make_async_copy(w_here, w_ref, w_sem).wait()

    here = pl.ds(pl.multiple_of(span * length, length), length)
    xn = xn_all[here, :]
    xn_ref[...] = xn
    zx = dot(xn, w_ref[:, : 2 * channels])
    z = zx[:, :channels]
    z_ref[...] = z.astype(bf16)
    xp = zx[:, channels:]
    xp_ref[...] = xp.astype(bf16)
    xbuf[8:, :] = xp
    bc = dot(xn, wbc_ref[...], COLS).astype(bf16)
    bc_ref[...] = bc
    bbuf[8:, :] = bc.astype(f32)
    dt = dot(xn, wdt_ref[...], COLS)
    dt_ref[...] = dt

    pre_x = conv_taps(xbuf, cx_ref[0:4, :], cx_ref[4:5, :], length)
    xc = pre_x * sigmoid(pre_x)
    pre_bc = conv_taps(bbuf, cbc_ref[0:4, :], cbc_ref[4:5, :], length)
    bcc = (pre_bc * sigmoid(pre_bc)).astype(bf16)
    xbuf[0:8, :] = xbuf[length : length + 8, :]
    bbuf[0:8, :] = bbuf[length : length + 8, :]
    b_mat = bcc[:, :state]
    c_mat = bcc[:, state:]

    mask, _, step, _, cum = span_values(dt, head_ref)
    cum_t = jnp.transpose(cum)
    scores = dot(c_mat, b_mat, COLS)
    xs = xc * spread_heads(step, channels, head_dim)
    xs_b = xs.astype(bf16)
    lane = lax.broadcasted_iota(jnp.int32, (length, LANES), 1)
    per_tile = LANES // head_dim
    tiles = []
    for tile in range(channels // LANES):
        xs_tile = xs_b[:, tile * LANES : (tile + 1) * LANES]
        out = None
        for sub in range(per_tile):
            head = tile * per_tile + sub
            decay = decay_matrix(mask, cum[:, head : head + 1], cum_t[head : head + 1, :])
            part = dot((scores * decay).astype(bf16), xs_tile)
            out = part if out is None else jnp.where(lane >= sub * head_dim, part, out)
        tiles.append(out)
    hin = hst[...]
    hin_ref[0] = hin
    last = cum[length - 1 : length, :]
    y = jnp.concatenate(tiles, axis=1)
    y = y + dot(c_mat, hin.astype(bf16)) * spread_heads(jnp.exp(cum), channels, head_dim)
    y = y + cx_ref[6:7, :] * xc
    y_ref[...] = y.astype(bf16)
    tail = spread_heads(jnp.exp(last - cum), channels, head_dim)
    keep = spread_heads(jnp.exp(last), channels, head_dim)
    hst[...] = keep * hin + dot(b_mat, (tail * xs).astype(bf16), ROWS)

    gated = y * (z * sigmoid(z))
    scaled = gated * cx_ref[5:6, :]
    squares = jnp.sum(gated * gated, axis=1, keepdims=True)
    high = squares.astype(bf16).astype(f32)
    extra = jnp.where(lane == 0, high, jnp.where(lane == 1, squares - high, 0.0)).astype(bf16)
    mixed = dot(scaled.astype(bf16), w_ref[:, 2 * channels :], COLS).astype(bf16)
    put_half(
        place_ref,
        span,
        pl.num_programs(0) // 2,
        mine_ref,
        other_ref,
        jnp.concatenate([mixed, extra], axis=1),
    )
    if last_layer:
        g = g_all[here, :]
        g_ref[...] = g
        gg = dot(g, w_ref[:, 2 * channels :])
        gg_ref[...] = gg
        products = jnp.sum(gg * scaled, axis=1, keepdims=True)
        both = jnp.where(lane == 0, squares, jnp.where(lane == 1, products, 0.0))
        sums_ref[...] = jnp.transpose(both)[0:8, :]


def gate_part(gg, rms, coef, z, y, cx_ref):
    z, y = z.astype(f32), y.astype(f32)
    norm_gate = cx_ref[5:6, :]
    sz = sigmoid(z)
    silu_z = z * sz
    gated = y * silu_z
    rg = rms * gg
    gate_out = (gated * rms * norm_gate).astype(bf16)
    d_gated = rg * norm_gate - gated * coef
    dz = (d_gated * y * (sz * (1.0 + z * (1.0 - sz)))).astype(bf16)
    return dz, d_gated * silu_z, gate_out, jnp.sum(rg * gated, axis=0, keepdims=True)


def gate_kernel(plan, n_pieces, width, place_ref, *refs):
    pieces = refs[:n_pieces]
    z_ref, y_ref, wo_ref, cx_ref, g_ref, dz_ref, dy_ref, go_ref, acc_ref, first_all = refs[n_pieces:]
    length = z_ref.shape[0]
    span = pl.program_id(0)

    @pl.when(span == 0)
    def _():
        place_pieces(plan, place_ref, pieces, [first_all])
        acc_ref[...] = jnp.zeros_like(acc_ref)

    first = first_all[pl.ds(pl.multiple_of(span * length, length), length), :]
    g = first[:, :width]
    g_ref[...] = g
    tok = first[:, width:].astype(f32)
    rms = tok[:, 0:1] + tok[:, 1:2]
    coef = tok[:, 2:3] + tok[:, 3:4]
    gg = dot(g, wo_ref[...])
    dz, dy, gate_out, acc_norm = gate_part(gg, rms, coef, z_ref[...], y_ref[...], cx_ref)
    dz_ref[...] = dz
    dy_ref[...] = dy
    go_ref[...] = gate_out
    acc_ref[5:6, :] += acc_norm


def scan_kernel(with_gate, head_dim, inner_all, place_ref, *refs):
    if with_gate:
        (gg_ref, tok_ref, z_ref, y_ref), refs = refs[:4], refs[4:]
    else:
        (dy_ref, dz_ref), refs = refs[:2], refs[2:]
    (xn_ref, xp_ref, xhalo_ref, bc_ref, bchalo_ref, dt_ref, hin_ref,
     w_ref, wbc_ref, wdt_ref, cx_ref, cbc_ref, head_ref, pick_ref), refs = refs[:14], refs[14:]
    if with_gate:
        (dz_ref, go_ref), refs = refs[:2], refs[2:]
    (dxt_ref, bcmine_ref, bcother_ref, mine_ref, other_ref, acc_ref, acch_ref, shared_ref,
     accbc, accn, xbuf, bbuf, dubuf, dubbuf, dhst) = refs
    length = xp_ref.shape[0]
    channels = cx_ref.shape[1]
    width = xn_ref.shape[1]
    state = dhst.shape[0]
    step_id = pl.program_id(0)
    first_span = step_id == pl.num_programs(0) - 1

    @pl.when(step_id == 0)
    def _():
        dubuf[length:, :] = jnp.zeros((8, channels), f32)
        dubbuf[length:, :] = jnp.zeros((8, 2 * state), f32)
        dhst[...] = jnp.zeros_like(dhst)
        accn[...] = jnp.zeros_like(accn)
        acc_ref[...] = jnp.zeros_like(acc_ref)
        accbc[...] = jnp.zeros_like(accbc)
        acch_ref[...] = jnp.zeros_like(acch_ref)

    @pl.when(first_span)
    def _():
        xbuf[0:8, :] = jnp.zeros((8, channels), f32)
        bbuf[0:8, :] = jnp.zeros((8, 2 * state), f32)

    @pl.when(jnp.logical_not(first_span))
    def _():
        xbuf[0:8, :] = xhalo_ref[...].astype(f32)[8:16, :]
        bbuf[0:8, :] = bchalo_ref[...].astype(f32)[8:16, :]

    xbuf[8:, :] = xp_ref[...].astype(f32)
    bbuf[8:, :] = bc_ref[...].astype(f32)
    if with_gate:
        tok = jnp.transpose(tok_ref[...])
        rms = lax.rsqrt(tok[:, 0:1] / inner_all + EPS)
        coef = rms * rms * rms * tok[:, 1:2] / inner_all
        dz_b, dy, gate_out, acc_norm = gate_part(
            gg_ref[...], rms, coef, z_ref[...], y_ref[...], cx_ref
        )
        dz_ref[...] = dz_b
        go_ref[...] = gate_out
    else:
        dz_b, dy = dz_ref[...], dy_ref[...]
        acc_norm = jnp.zeros((1, channels), f32)
    skip = cx_ref[6:7, :]

    pre_x = conv_taps(xbuf, cx_ref[0:4, :], cx_ref[4:5, :], length)
    sx = sigmoid(pre_x)
    xc = pre_x * sx
    pre_bc = conv_taps(bbuf, cbc_ref[0:4, :], cbc_ref[4:5, :], length)
    sbc = sigmoid(pre_bc)
    bcc = (pre_bc * sbc).astype(bf16)
    b_mat = bcc[:, :state]
    c_mat = bcc[:, state:]
    mask, pre_dt, step, rate, cum = span_values(dt_ref[...], head_ref)
    cum_t = jnp.transpose(cum)
    last = cum[length - 1 : length, :]
    scores = dot(c_mat, b_mat, COLS)
    step_all = spread_heads(step, channels, head_dim)
    xs = xc * step_all
    xs_b = xs.astype(bf16)
    tail = spread_heads(jnp.exp(last - cum), channels, head_dim)
    keep = spread_heads(jnp.exp(last), channels, head_dim)

    hin = hin_ref[0]
    hin_b = hin.astype(bf16)
    dh = dhst[...]
    dh_b = dh.astype(bf16)
    dye = dy * spread_heads(jnp.exp(cum), channels, head_dim)
    dye_b = dye.astype(bf16)
    txs = tail * xs
    txs_b = txs.astype(bf16)
    carried = dot(c_mat, hin_b)
    pulled = dot(b_mat, dh_b)
    d_c = dot(dye_b, hin_b, COLS)
    d_b = dot(txs_b, dh_b, COLS)
    dhst[...] = keep * dh + dot(c_mat, dye_b, ROWS)
    into = txs * pulled
    across = dye * carried - into
    at_last = jnp.sum(into, axis=0, keepdims=True) + keep * jnp.sum(hin * dh, axis=0, keepdims=True)

    dy_b = dy.astype(bf16)
    dy_t = jnp.transpose(dy).astype(bf16)
    lane = lax.broadcasted_iota(jnp.int32, (length, LANES), 1)
    per_tile = LANES // head_dim
    d_scores = jnp.zeros((length, length), f32)
    row_sums = jnp.zeros((length, LANES), f32)
    col_sums = []
    dxs_parts = []
    for head in range(channels // head_dim):
        tile, sub = divmod(head, per_tile)
        dy_tile = dy_b[:, tile * LANES : (tile + 1) * LANES]
        own = (lane >= sub * head_dim) & (lane < (sub + 1) * head_dim)
        dy_head = jnp.where(own, dy_tile, jnp.zeros_like(dy_tile))
        d_m = dot(dy_head, xs_b[:, tile * LANES : (tile + 1) * LANES], COLS)
        decay = decay_matrix(mask, cum[:, head : head + 1], cum_t[head : head + 1, :])
        dxs_parts.append(
            dot(dy_t[head * head_dim : (head + 1) * head_dim, :], (scores * decay).astype(bf16))
        )
        d_m = d_m * decay
        d_scores = d_scores + d_m
        pairs = d_m * scores
        row_sums = jnp.where(lane == head, jnp.sum(pairs, axis=1, keepdims=True), row_sums)
        col_sums.append(jnp.sum(pairs, axis=0, keepdims=True))
    heads = len(col_sums)
    col_sums = jnp.concatenate(col_sums + [jnp.zeros((LANES - heads, length), f32)], axis=0)
    dxs = jnp.transpose(jnp.concatenate(dxs_parts, axis=0)) + tail * pulled
    pick = pick_ref[...]
    d_cum = row_sums - jnp.transpose(col_sums) + dot(across, pick, PLAIN, highest)
    at_last = dot(jnp.broadcast_to(at_last, (8, channels)), pick, PLAIN, highest)[0:1, :]
    d_rate = dot(mask.astype(f32), d_cum, ROWS, highest) + at_last
    d_step = d_rate * head_ref[1:2, :] + dot(dxs * xc, pick, PLAIN, highest)
    d_dt = d_step * sigmoid(pre_dt)
    acch_ref[0:1, :] += jnp.sum(d_dt, axis=0, keepdims=True)
    acch_ref[1:2, :] += jnp.sum(d_rate * rate, axis=0, keepdims=True)
    dt_b = d_dt.astype(bf16)
    ds_b = d_scores.astype(bf16)
    d_c = d_c + dot(ds_b, b_mat)
    d_b = d_b + dot(ds_b, c_mat, ROWS)
    d_xc = dxs * step_all + skip * dy
    acc_skip = jnp.sum(dy * xc, axis=0, keepdims=True)

    d_u = d_xc * (sx * (1.0 + pre_x * (1.0 - sx)))
    d_ub = jnp.concatenate([d_b, d_c], axis=1) * (sbc * (1.0 + pre_bc * (1.0 - sbc)))
    dubuf[0:length, :] = d_u
    dubbuf[0:length, :] = d_ub
    d_x = jnp.zeros_like(d_u)
    d_bc = jnp.zeros_like(d_ub)
    acc_rows = []
    accbc_rows = []
    for j in range(4):
        d_x = d_x + cx_ref[j : j + 1, :] * dubuf[pl.ds(3 - j, length), :]
        d_bc = d_bc + cbc_ref[j : j + 1, :] * dubbuf[pl.ds(3 - j, length), :]
        acc_rows.append(jnp.sum(d_u * xbuf[pl.ds(5 + j, length), :], axis=0, keepdims=True))
        accbc_rows.append(jnp.sum(d_ub * bbuf[pl.ds(5 + j, length), :], axis=0, keepdims=True))
    dubuf[length:, :] = d_u[0:8, :]
    dubbuf[length:, :] = d_ub[0:8, :]
    zero = jnp.zeros((1, channels), f32)
    acc_ref[...] += jnp.concatenate(
        acc_rows + [jnp.sum(d_u, axis=0, keepdims=True), acc_norm, acc_skip, zero], axis=0
    )
    zero = jnp.zeros((3, d_ub.shape[1]), f32)
    accbc[...] += jnp.concatenate(
        accbc_rows + [jnp.sum(d_ub, axis=0, keepdims=True), zero], axis=0
    )
    dx_b = d_x.astype(bf16)
    dbc_b = d_bc.astype(bf16)
    dxt_ref[:, :channels] = dx_b
    dxt_ref[:, channels:] = dt_b
    put_columns(
        place_ref,
        pl.num_programs(0) - 1 - step_id,
        bcmine_ref,
        bcother_ref,
        jnp.transpose(d_bc).astype(bf16),
    )
    total = dot(jnp.concatenate([dz_b, dx_b], axis=1), w_ref[...], COLS)
    total = total + dot(dbc_b, wbc_ref[...]) + dot(dt_b, wdt_ref[...])
    accn[0:1, :] += jnp.sum(total * xn_ref[...].astype(f32), axis=0, keepdims=True)

    @pl.when(first_span)
    def _():
        lanes = shared_ref.shape[1]
        lines = [accn[0:1, i * lanes : (i + 1) * lanes] for i in range(width // lanes)]
        shared = jnp.concatenate(lines + [accbc[0:5, :]], axis=0)
        shared_ref[0 : shared.shape[0], :] = shared.astype(bf16)
        shared_ref[shared.shape[0] :, :] = jnp.zeros(
            (shared_ref.shape[0] - shared.shape[0], lanes), bf16
        )

    put_half(
        place_ref,
        pl.num_programs(0) - 1 - step_id,
        pl.num_programs(0) // 2,
        mine_ref,
        other_ref,
        total.astype(bf16),
    )


def whole(shape):
    zeros = (0,) * len(shape)
    return pl.BlockSpec(shape, lambda i, p: zeros)


def span_rows(columns):
    return pl.BlockSpec((SPAN, columns), lambda i, p: (i, 0))


def half_rows(columns, spans, reverse):
    half = spans // 2

    def block(i, core):
        span = spans - 1 - i if reverse else i
        return jnp.clip(span - half * core, 0, half - 1), 0

    return [
        pl.BlockSpec((SPAN, columns), lambda i, p: block(i, p[0])),
        pl.BlockSpec((SPAN, columns), lambda i, p: block(i, 1 - p[0])),
    ]


def span_call(kernel, name, spans, place, operands, in_specs, shapes, out_specs, scratch, flops):
    moved = sum(v.size * v.dtype.itemsize for v in [*operands, *shapes])
    return pl.pallas_call(
        kernel,
        grid_spec=pltpu.PrefetchScalarGridSpec(
            num_scalar_prefetch=1,
            grid=(spans,),
            in_specs=in_specs,
            out_specs=out_specs,
            scratch_shapes=scratch,
        ),
        out_shape=shapes,
        compiler_params=pltpu.CompilerParams(
            dimension_semantics=("arbitrary",), vmem_limit_bytes=VMEM_BYTES
        ),
        cost_estimate=pl.CostEstimate(flops=flops, bytes_accessed=moved, transcendentals=0),
        name=name,
    )(place, *operands)


def run_forward(place, gathered, w, wdt, small, state, head_dim):
    w_here, w_there, there_plan = w
    channels = small[0].shape[1]
    width = gathered[0][0][0].shape[1]
    anywhere = pl.BlockSpec(memory_space=pl.ANY)
    tokens = NC * NZ * gathered[0][2][0]
    spans = tokens // SPAN
    last_layer = len(gathered) == 2
    plans = [(cut_plan(*one), len(one[0])) for one in gathered]
    operands = [p for one in gathered for p in one[0]]
    in_specs = [whole(v.shape) for v in operands] + [anywhere] * (1 + len(w_there))
    operands += [w_here, *w_there, wdt, *small]
    in_specs += [whole(v.shape) for v in operands[len(in_specs) :]]
    shapes = [
        jax.ShapeDtypeStruct(w_here.shape, bf16),
        jax.ShapeDtypeStruct((tokens, width), bf16),
        jax.ShapeDtypeStruct((2 * state, width), bf16),
        jax.ShapeDtypeStruct((tokens, channels), bf16),
        jax.ShapeDtypeStruct((tokens, channels), bf16),
        jax.ShapeDtypeStruct((tokens, 2 * state), bf16),
        jax.ShapeDtypeStruct((tokens, LANES), f32),
        jax.ShapeDtypeStruct((tokens, channels), bf16),
        jax.ShapeDtypeStruct((spans, state, channels), f32),
        jax.ShapeDtypeStruct((tokens // 2, width + LANES), bf16),
        jax.ShapeDtypeStruct((tokens // 2, width + LANES), bf16),
    ]
    out_specs = [whole(w_here.shape), span_rows(width), whole((2 * state, width))]
    out_specs += [span_rows(s.shape[1]) for s in shapes[3:8]]
    out_specs.append(pl.BlockSpec((1, state, channels), lambda i, p: (i, 0, 0)))
    out_specs += half_rows(width + LANES, spans, False)
    scratch = [
        pltpu.SemaphoreType.DMA,
        pltpu.VMEM((tokens, width), bf16),
        pltpu.VMEM((SPAN + 8, channels), f32),
        pltpu.VMEM((SPAN + 8, 2 * state), f32),
        pltpu.VMEM((state, channels), f32),
    ]
    if last_layer:
        shapes += [
            jax.ShapeDtypeStruct((tokens, width), bf16),
            jax.ShapeDtypeStruct((8, tokens), f32),
            jax.ShapeDtypeStruct((tokens, channels), f32),
        ]
        out_specs += [span_rows(width), pl.BlockSpec((8, SPAN), lambda i, p: (0, i)), span_rows(channels)]
        scratch.append(pltpu.VMEM((tokens, width), bf16))
    kernel = functools.partial(forward_kernel, plans, there_plan, head_dim)
    return span_call(
        kernel, "layer_forward", spans, place, operands, in_specs, shapes, out_specs, scratch, 20 * 10**9
    )


def run_gate(place, gathered, z, y, w, cx):
    tokens, channels = z.shape
    width = w.shape[0]
    spans = tokens // SPAN
    plan, pieces = cut_plan(*gathered), list(gathered[0])
    operands = [*pieces, z, y, w, cx]
    in_specs = [whole(p.shape) for p in pieces]
    in_specs += [span_rows(channels), span_rows(channels)]
    in_specs += [pl.BlockSpec((width, channels), lambda i, p: (0, 2)), whole(cx.shape)]
    shapes = [
        jax.ShapeDtypeStruct((tokens, width), bf16),
        jax.ShapeDtypeStruct((tokens, channels), bf16),
        jax.ShapeDtypeStruct((tokens, channels), f32),
        jax.ShapeDtypeStruct((tokens, channels), bf16),
        jax.ShapeDtypeStruct((8, channels), f32),
    ]
    out_specs = [span_rows(s.shape[1]) for s in shapes[:4]] + [whole(shapes[4].shape)]
    scratch = [pltpu.VMEM((tokens, pieces[0].shape[1]), bf16)]
    kernel = functools.partial(gate_kernel, plan, len(pieces), width)
    return span_call(
        kernel, "gate_backward", spans, place, operands, in_specs, shapes, out_specs, scratch, 6 * 10**9
    )


def run_scan(place, lead, xn, xp, bc, dt, hin, weights, small, pick, head_dim, inner_all):
    tokens, channels = xp.shape
    state = hin.shape[1]
    width = xn.shape[1]
    spans = tokens // SPAN
    with_gate = len(lead) == 4

    def rev(columns):
        return pl.BlockSpec((SPAN, columns), lambda i, p: (spans - 1 - i, 0))

    def halo(columns, rows):
        per = SPAN // rows
        return pl.BlockSpec(
            (rows, columns), lambda i, p: (jnp.maximum((spans - 1 - i) * per - 1, 0), 0)
        )

    operands = [*lead, xn, xp, xp, bc, bc, dt, hin, *weights, *small, pick]
    in_specs = [rev(channels)] * 2
    if with_gate:
        tok = pl.BlockSpec((8, SPAN), lambda i, p: (0, spans - 1 - i))
        in_specs = [rev(channels), tok, rev(channels), rev(channels)]
    in_specs += [
        rev(width),
        rev(channels),
        halo(channels, 16),
        rev(2 * state),
        halo(2 * state, 16),
        rev(LANES),
        pl.BlockSpec((1, state, channels), lambda i, p: (spans - 1 - i, 0, 0)),
    ]
    in_specs.append(whole((width, 2 * channels)))
    in_specs += [whole(v.shape) for v in operands[len(in_specs) :]]
    shapes = [
        jax.ShapeDtypeStruct((tokens, channels + LANES), bf16),
        jax.ShapeDtypeStruct((state * spans, SPAN), bf16),
        jax.ShapeDtypeStruct((state * spans, SPAN), bf16),
        jax.ShapeDtypeStruct((tokens // 2, width), bf16),
        jax.ShapeDtypeStruct((tokens // 2, width), bf16),
        jax.ShapeDtypeStruct((8, channels), f32),
        jax.ShapeDtypeStruct((8, LANES), f32),
        jax.ShapeDtypeStruct((16, 2 * state), bf16),
    ]
    out_specs = [rev(channels + LANES), whole(shapes[1].shape), whole(shapes[2].shape)]
    out_specs += half_rows(width, spans, True)
    out_specs += [whole(s.shape) for s in shapes[5:]]
    if with_gate:
        shapes = [jax.ShapeDtypeStruct((tokens, channels), bf16)] * 2 + shapes
        out_specs = [rev(channels)] * 2 + out_specs
    scratch = [
        pltpu.VMEM((8, 2 * state), f32),
        pltpu.VMEM((8, width), f32),
        pltpu.VMEM((SPAN + 8, channels), f32),
        pltpu.VMEM((SPAN + 8, 2 * state), f32),
        pltpu.VMEM((SPAN + 8, channels), f32),
        pltpu.VMEM((SPAN + 8, 2 * state), f32),
        pltpu.VMEM((state, channels), f32),
    ]
    kernel = functools.partial(scan_kernel, with_gate, head_dim, inner_all)
    return span_call(
        kernel, "scan_backward", spans, place, operands, in_specs, shapes, out_specs, scratch, 28 * 10**9
    )


def weight_kernel(n_pairs, split, place_ref, *refs):
    lefts, rights, outs = refs[:n_pairs], refs[n_pairs : 2 * n_pairs], refs[2 * n_pairs :]

    def write(out_ref):
        at = 0
        for left_ref, right_ref in zip(lefts, rights):
            columns = right_ref.shape[1]
            out_ref[:, at : at + columns] = dot(left_ref[...], right_ref[...], ROWS).astype(bf16)
            at += columns

    if not split:
        write(outs[0])
        return
    for k, out_ref in enumerate(outs):
        pl.when(pl.program_id(0) == k)(functools.partial(write, out_ref))


def weight_products(place, pairs, split=True):
    tokens = pairs[0][0].shape[0]
    rows = max(left.shape[1] for left, _ in pairs)
    block = rows // 4

    def at(i, p):
        return lax.rem(p[3] + i, NX) if split else i

    lefts, rights, columns = [], [], []
    for left, right in pairs:
        quarter = left.shape[1] == block
        cut, uncut = (lambda i, p: (0, at(i, p))), (lambda i, p: (0, 0))
        lefts.append(pl.BlockSpec((tokens, block), uncut if quarter else cut))
        wide = block if quarter else right.shape[1]
        rights.append(pl.BlockSpec((tokens, wide), cut if quarter else uncut))
        columns.append(wide)
    columns = sum(columns)
    if split:
        out_specs = [whole((block, columns))] * 4
        shapes = [jax.ShapeDtypeStruct((block, columns), bf16)] * 4
    else:
        out_specs = [pl.BlockSpec((block, columns), lambda i, p: (i, 0))]
        shapes = [jax.ShapeDtypeStruct((rows, columns), bf16)]
    out = pl.pallas_call(
        functools.partial(weight_kernel, len(pairs), split),
        grid_spec=pltpu.PrefetchScalarGridSpec(
            num_scalar_prefetch=1, grid=(4,), in_specs=lefts + rights, out_specs=out_specs
        ),
        out_shape=shapes,
        compiler_params=pltpu.CompilerParams(vmem_limit_bytes=VMEM_BYTES),
        cost_estimate=pl.CostEstimate(
            flops=2 * tokens * rows * columns, bytes_accessed=8 * 10**6, transcendentals=0
        ),
        name="weight_products",
    )(place, *[left for left, _ in pairs], *[right for _, right in pairs])
    return out if split else out[0]


SIZES = (4, 2, 2, 2, 4)
NX, NYL, NC, NYH, NZ = SIZES
EVERY = [
    (x, yl, c, yh, z)
    for x in range(NX)
    for yl in range(NYL)
    for c in range(NC)
    for yh in range(NYH)
    for z in range(NZ)
]


def linear(x, yl, c, yh, z):
    return ((((x % NX) * NYL + yl % NYL) * NC + c % NC) * NYH + yh % NYH) * NZ + z % NZ


def send(v, step, only=None):
    pairs = [(linear(*d), linear(*step(*d))) for d in EVERY if only is None or only(*d)]
    return lax.ppermute(v, ("dp", "tensor"), pairs)


def send_z(v, k):
    return send(v, lambda x, yl, c, yh, z: (x, yl, c, yh, z + k))


def send_core(v):
    return send(v, lambda x, yl, c, yh, z: (x, yl, c + 1, yh, z))


def trade(v, k):
    return send(v, lambda x, yl, c, yh, z: (x, yl, yh, c, z + k))


def traded(v):
    return send(v, lambda x, yl, c, yh, z: (x, yl, yh, c, z), lambda x, yl, c, yh, z: c != yh)


def trade_places(v):
    _, _, core, yh, _ = position()
    return jnp.where(core == yh, v, traded(v))


def position():
    dp, tensor = lax.axis_index("dp"), lax.axis_index("tensor")
    return dp // (NYL * NC), dp // NC % NYL, dp % NC, tensor // NZ, tensor % NZ


def gather(v, parts, traded_own=None):
    arrays, sources = [], []
    for k in (0, 1, 3, 2):
        if traded_own is not None:
            piece = trade(v, k) if k else traded_own
        else:
            piece = send_z(v, k) if k else v
        arrays += [piece, send_core(piece)]
        sources += [(False, -k % NZ, 0), (True, -k % NZ, 0)]
    return arrays, sources, parts


def cut_plan(arrays, sources, parts):
    plan = []
    for number, (piece, (other, dz, first)) in enumerate(zip(arrays, sources)):
        base = 0
        for out, per in enumerate(parts):
            begin, end = max(first, base), min(first + piece.shape[0], base + per)
            if begin < end:
                plan.append((number, other, dz, begin - first, out, per, begin - base, end - begin))
            base += per
    return plan


def fold(mine, other):
    _, _, _, _, z = position()
    rows = mine.shape[0] // NZ
    blocks = []
    for k in range(NZ):
        at = (z + k) % NZ * rows
        a = lax.dynamic_slice_in_dim(mine, at, rows, 0).astype(f32)
        blocks.append(a + lax.dynamic_slice_in_dim(other, at, rows, 0).astype(f32))
    return blocks


def fold_beside(pairs):
    folded = [fold(mine, send_core(other)) for mine, other in pairs]
    return [jnp.concatenate([blocks[k] for blocks in folded], axis=1) for k in range(NZ)]


def scatter(*pairs):
    own, one, two, three = fold_beside(pairs)
    return [own] + [send_z(b.astype(bf16), k) for k, b in ((1, one), (2, two), (3, three))]


def scatter_with_sum(mine, other, shared, meanwhile):
    half = mine.shape[0]
    rows = half // NZ
    got = after(send_core(jnp.concatenate([other, shared], axis=0)), *meanwhile)
    blocks = fold(mine, got[:half])
    total_shared = shared.astype(f32) + got[half:].astype(f32)
    packed = total_shared.astype(bf16)
    total = blocks[0]
    for k in range(1, NZ):
        got = send_z(jnp.concatenate([blocks[k].astype(bf16), packed], axis=0), k)
        total = total + got[:rows].astype(f32)
        total_shared = total_shared + got[rows:].astype(f32)
    return total, total_shared


def sum_members(v):
    both = v + send_core(v)
    total = both
    for k in range(1, NZ):
        total = total + send_z(both, k)
    return total


def send_far(v):
    return send(v, lambda x, yl, c, yh, z: (x, yl, c, yh + 1, z), lambda x, yl, c, yh, z: c != yh)


def sum_far(v, far=None):
    far = send_far(v) if far is None else far
    return (v.astype(f32) + far.astype(f32)).astype(bf16)


def halve(v):
    _, _, core, yh, _ = position()
    half = v.shape[0] // 2
    near = send(
        v[half:], lambda x, yl, c, yh, z: (x, yl, c + 1, yh, z), lambda x, yl, c, yh, z: c == yh
    )
    return jnp.where(core == yh, v[:half], near)


def sum_beside(part):
    beside = send(part, lambda x, yl, c, yh, z: (x, yl + 1, c, yh, z))
    return (part.astype(f32) + beside.astype(f32)).astype(bf16)


def sum_x(blocks):
    total = blocks[0].astype(f32)
    for k in range(1, NX):
        got = send(blocks[k], lambda x, yl, c, yh, z, k=k: (x + k, yl, c, yh, z))
        total = total + got.astype(f32)
    return total.astype(bf16)


def cut_x(v):
    x = position()[0]
    rows = v.shape[0] // NX
    return [lax.dynamic_slice_in_dim(v, (x + k) % NX * rows, rows, 0) for k in range(NX)]


def collect_x(part):
    x = position()[0]
    out = jnp.zeros((NX,) + part.shape, bf16)
    out = lax.dynamic_update_index_in_dim(out, part, x, 0)
    for k in range(1, NX):
        block = send(part, lambda x, yl, c, yh, z, k=k: (x + k, yl, c, yh, z))
        out = lax.dynamic_update_index_in_dim(out, block, (x - k) % NX, 0)
    return out


def collect(part):
    out = collect_x(part)
    return out, send_core(out)


def write_kernel(plan, by_half, n_kept, place_ref, here_ref, there_ref, *refs):
    rows = here_ref.shape[1]

    def write(ref):
        for (column, kind, wide), out_ref in zip(plan, refs[n_kept:]):
            for x in range(NX):
                value = ref[x, :, column : column + wide].astype(f32)
                if kind != "blocks":
                    out_ref[0, 0 if by_half else x, x if by_half else 0] = value
                elif by_half:
                    at = x // 2 * wide
                    out_ref[0, x % 2 * rows : (x % 2 + 1) * rows, at : at + wide] = value
                else:
                    out_ref[0, :, x * wide : (x + 1) * wide] = value

    here = (pl.program_id(0) == 0) == (place_ref[2] == 1)

    @pl.when(here)
    def _():
        write(here_ref)

    @pl.when(jnp.logical_not(here))
    def _():
        write(there_ref)


def write_sums(place, halves, by_half, outputs):
    rows, columns = halves[0].shape[1:]
    total = 2 * NX * rows
    wide = total // 4
    plan, shapes, specs, finals, kept, alias = [], [], [], [], [], {}
    for column, kind, layer, array in outputs:
        lanes = LANES if kind == "flat" else wide
        layers = 1 if kind == "flat" else 2
        plan.append((column, kind, lanes))
        if kind == "blocks":
            shape = (layers, wide, total)
            if by_half:
                spec = pl.BlockSpec((1, wide, total // 2), lambda h, p, layer=layer: (layer, 0, h))
            else:
                spec = pl.BlockSpec((1, rows, total), lambda h, p, layer=layer: (layer, h, 0))
            finals.append(shape)
        elif by_half:
            shape = (layers, 2, NX, rows, lanes)
            spec = pl.BlockSpec((1, 1, NX, rows, lanes), lambda h, p, layer=layer: (layer, h, 0, 0, 0))
            finals.append((layers, total, lanes))
        else:
            shape = (layers, NX, 2, rows, lanes)
            spec = pl.BlockSpec((1, NX, 1, rows, lanes), lambda h, p, layer=layer: (layer, 0, h, 0, 0))
            finals.append((layers, total, lanes))
        shapes.append(jax.ShapeDtypeStruct(shape, f32))
        specs.append(spec)
        if array is not None:
            alias[3 + len(kept)] = len(shapes) - 1
            kept.append(array.reshape(shape))
    piece = pl.BlockSpec((NX, rows, columns), lambda h, p: (0, 0, 0))
    written = pl.pallas_call(
        functools.partial(write_kernel, plan, by_half, len(kept)),
        grid_spec=pltpu.PrefetchScalarGridSpec(
            num_scalar_prefetch=1,
            grid=(2,),
            in_specs=[piece, piece] + [pl.BlockSpec(memory_space=pl.ANY)] * len(kept),
            out_specs=specs,
        ),
        out_shape=shapes,
        input_output_aliases=alias,
        compiler_params=pltpu.CompilerParams(vmem_limit_bytes=VMEM_BYTES),
        name="write_sums",
    )(place, *halves, *kept)
    return [v.reshape(final) for v, final in zip(written, finals)]


def row_call(kernel, name, operands, shapes):
    return pl.pallas_call(
        kernel,
        grid=(1,),
        in_specs=[pl.BlockSpec((rows, v.shape[1]), lambda i: (0, 0)) for v, rows in operands],
        out_specs=[pl.BlockSpec(s.shape, lambda i: (0, 0)) for s in shapes],
        out_shape=shapes,
        compiler_params=pltpu.CompilerParams(vmem_limit_bytes=VMEM_BYTES),
        name=name,
    )(*[v for v, _ in operands])


def inverse_rms(v):
    return lax.rsqrt(jnp.mean(v * v, axis=-1, keepdims=True) + EPS)


def first_kernel(packed_ref, gain_ref, out_ref):
    rows = 128
    v = packed_ref[0:rows, :].astype(f32)
    out_ref[0:rows, :] = (v * inverse_rms(v) * gain_ref[...]).astype(bf16)
    out_ref[rows:, :] = packed_ref[rows : out_ref.shape[0], :]


def add_terms(own_ref, a_ref, b_ref, c_ref):
    total = own_ref[...].astype(f32) + a_ref[...].astype(f32)
    return total + (b_ref[...].astype(f32) + c_ref[...].astype(f32))


def unscaled_output(inner_all, terms, width):
    total = add_terms(*terms)
    squares = total[:, width : width + 1] + total[:, width + 1 : width + 2]
    gate_rms = lax.rsqrt(squares / inner_all + EPS)
    return gate_rms, total[:, :width] * gate_rms


def middle_kernel(inner_all, own_ref, a_ref, b_ref, c_ref, res_ref, gain_ref, res1_ref, mixed_ref, rms_ref, normed_ref):
    width = res_ref.shape[1]
    gate_rms, mixed = unscaled_output(inner_all, (own_ref, a_ref, b_ref, c_ref), width)
    res = res_ref[...].astype(f32) + mixed
    res1_ref[...] = res
    mixed_ref[...] = mixed
    rms_ref[...] = jnp.broadcast_to(gate_rms, rms_ref.shape)
    normed_ref[...] = (res * inverse_rms(res) * gain_ref[...]).astype(bf16)


def input_gradient(grad_normed, res, d_res, gain):
    inv = inverse_rms(res)
    scaled = grad_normed * gain
    dots = jnp.sum(scaled * res, axis=-1, keepdims=True) / res.shape[1]
    return d_res + inv * scaled - res * (inv * inv * inv) * dots


def between_kernel(inner_all, own_ref, a_ref, b_ref, c_ref, res_ref, dres_ref, gain_ref, mixed_ref, rms_ref, out_ref, sent_ref):
    width = res_ref.shape[1]
    grad_normed = add_terms(*(ref.at[:, 0:width] for ref in (own_ref, a_ref, b_ref, c_ref)))
    d_res = input_gradient(grad_normed, res_ref[...], dres_ref[...].astype(f32), gain_ref[...])
    out_ref[...] = d_res
    g_mixed = d_res.astype(bf16)
    sent_ref[:, :width] = g_mixed
    gate_rms = rms_ref[:, 0:1]
    products = jnp.sum(g_mixed.astype(f32) * mixed_ref[...], axis=-1, keepdims=True)
    coef = gate_rms * gate_rms * products / inner_all
    lane = lax.broadcasted_iota(jnp.int32, rms_ref.shape, 1)
    rms_high = gate_rms.astype(bf16).astype(f32)
    coef_high = coef.astype(bf16).astype(f32)
    extra = jnp.where(lane == 0, rms_high, jnp.where(lane == 1, gate_rms - rms_high, 0.0))
    extra = jnp.where(lane == 2, coef_high, jnp.where(lane == 3, coef - coef_high, extra))
    sent_ref[:, width:] = extra.astype(bf16)


def end_kernel(own_ref, a_ref, b_ref, c_ref, res_ref, dres_ref, gain_ref, hidden_ref, out_ref):
    width = res_ref.shape[1]
    grad_normed = add_terms(own_ref, a_ref, b_ref, c_ref)
    grad = input_gradient(grad_normed, res_ref[...].astype(f32), dres_ref[...], gain_ref[...])
    out_ref[:, :width] = hidden_ref[...]
    out_ref[:, width:] = grad.astype(bf16)


def last_kernel(inner_all, own_ref, a_ref, b_ref, c_ref, res_ref, out_ref):
    _, mixed = unscaled_output(inner_all, (own_ref, a_ref, b_ref, c_ref), res_ref.shape[1])
    out_ref[...] = (res_ref[...] + mixed).astype(bf16)


def after(v, *others):
    return lax.optimization_barrier((v, *others))[0]


def pad_to(v, rows, lanes):
    return jnp.pad(v, ((0, rows - v.shape[0]), (0, lanes - v.shape[1])))


def local(
    hidden_in,
    grad_out,
    norm_in,
    w_z,
    w_x,
    w_bc,
    w_dt,
    conv_x,
    conv_x_bias,
    conv_bc,
    conv_bc_bias,
    dt_bias,
    a_log,
    skip,
    norm_gate,
    w_out,
):
    layers, width, channels = w_z.shape
    heads = w_dt.shape[2]
    head_dim = channels // heads
    both = conv_bc.shape[2]
    state = both // 2
    members = NC * NZ
    inner_all = channels * members
    rows = hidden_in.shape[1]
    bc_rows = both // members
    x, _, core, yh, z = position()
    stays = core == yh
    place = jnp.stack([core, z, stays, x]).astype(jnp.int32)
    full = jax.ShapeDtypeStruct((rows, width), f32)

    def pack_weights(layer):
        return jnp.concatenate([w_z[layer], w_x[layer], w_out[layer].T], axis=1)

    bc_t = jnp.swapaxes(w_bc, 1, 2)
    dt_t = jnp.pad(jnp.swapaxes(w_dt, 1, 2), ((0, 0), (0, 8 - heads), (0, 0)))
    per_channel = jnp.concatenate(
        [conv_x, conv_x_bias[:, None], norm_gate[:, None], jnp.repeat(skip, head_dim, axis=1)[:, None]],
        axis=1,
    )
    per_channel = jnp.pad(per_channel, ((0, 0), (0, 1), (0, 0)))
    per_head = jnp.stack([dt_bias, -jnp.exp(a_log)], axis=1)
    per_head = jnp.pad(per_head, ((0, 0), (0, 6), (0, LANES - heads)))
    little = jnp.concatenate([per_channel, per_head], axis=2).reshape(layers * 8, channels + LANES)
    high = little.astype(bf16)
    low = (little - high.astype(f32)).astype(bf16)
    lines = pad_to(jnp.concatenate([high, low], axis=1), layers * 8, width)
    packed = jnp.concatenate([hidden_in[0], bc_t[0], dt_t.reshape(layers * 8, width), lines], axis=0)
    packed = trade_places(packed)
    lines = packed[packed.shape[0] - layers * 8 :].astype(f32)
    little = lines[:, : channels + LANES] + lines[:, channels + LANES : 2 * (channels + LANES)]
    little = little.reshape(layers, 8, channels + LANES)

    w0 = pack_weights(0)
    w0 = w0, [traded(after(w0, packed))], [(0, None)]
    grads = jnp.concatenate([grad_out[0], bc_t[1]], axis=0)

    [sent] = row_call(
        first_kernel,
        "first_norm",
        [(packed, packed.shape[0]), (norm_in[0:1], 1)],
        [jax.ShapeDtypeStruct((rows + bc_rows, width), bf16)],
    )
    gathered0 = gather(sent, (rows, bc_rows))
    wdt = [pad_to(packed[rows + bc_rows + 8 * l : rows + bc_rows + 8 * (l + 1)], LANES, width) for l in range(layers)]
    smalls = []
    for layer in range(layers):
        cbc = jnp.concatenate([conv_bc[layer], conv_bc_bias[layer][None], jnp.zeros((3, both), f32)], axis=0)
        smalls.append((little[layer, :, :channels], cbc, little[layer, :, channels:]))
    channel_head = jnp.arange(channels) // head_dim
    pick = (channel_head[:, None] == jnp.arange(LANES)[None, :]).astype(f32)

    out0 = run_forward(place, [gathered0], w0, wdt[0], smalls[0], state, head_dim)
    w0, xn0, wbc0, z0, xp0, bc0, dt0, y0, hin0, mine, other = out0
    grads = after(grads, sent)
    gathered_grad = gather(grads, (rows, bc_rows), trade_places(grads))
    grad_held = gathered_grad[0][0]
    terms = scatter((mine, after(other, *gathered_grad[0][::2])))
    w1 = pack_weights(1)
    w1 = w1, [traded(after(w1, terms[0]))], [(0, None)]
    res1, mixed0, rms0, normed1 = row_call(
        functools.partial(middle_kernel, inner_all),
        "middle_norm",
        [(v, rows) for v in terms] + [(packed, rows), (norm_in[1:2], 1)],
        [full, full, jax.ShapeDtypeStruct((rows, LANES), f32), jax.ShapeDtypeStruct((rows, width), bf16)],
    )
    gathered1 = gather(normed1, (rows,))
    out1 = run_forward(
        place, [gathered1, gathered_grad], w1, wdt[1], smalls[1], state, head_dim
    )
    w1, xn1, wbc1, z1, xp1, bc1, dt1, y1, hin1, mine, other, grad_rows1, sums, gg1 = out1
    sums = sum_members(sums)

    home = fold(mine, send_core(other))
    sums = after(sums, *home)
    home = home[:1] + [send_z(home[k].astype(bf16), k) for k in range(1, NZ)]
    back1 = run_scan(
        place, (gg1, sums, z1, y1), xn1, xp1, bc1, dt1, hin1, (w1, wbc1, wdt[1]), smalls[1], pick, head_dim,
        inner_all,
    )
    dz1, go1, dxt1, *bc_halves, mine, other, acc1, acch1, shared1 = back1
    terms = scatter((mine, after(other, *home)), bc_halves)
    early1 = weight_products(place, [(xn1, dz1), (go1, grad_rows1)], split=False)
    terms[1] = after(terms[1], early1)
    early1_far = send_far(early1)
    [hidden_out] = row_call(
        functools.partial(last_kernel, inner_all),
        "last_output",
        [(after(home[0], terms[1]), rows)] + [(v, rows) for v in home[1:]] + [(res1, rows)],
        [jax.ShapeDtypeStruct((rows, width), bf16)],
    )
    d_res1, sent = row_call(
        functools.partial(between_kernel, inner_all),
        "between_layers",
        [(v, rows) for v in terms]
        + [(res1, rows), (grad_held, rows), (norm_in[1:2], 1), (mixed0, rows), (rms0, rows)],
        [full, jax.ShapeDtypeStruct((rows, width + LANES), bf16)],
    )
    gathered_back = gather(sent, (rows,))

    bc_at = channels + bc_rows

    def with_bc(dxt, bc_sum):
        by_token = bc_sum.reshape(-1, bc_rows, SPAN).swapaxes(1, 2).reshape(-1, bc_rows)
        spread = jnp.pad(by_token, ((0, 0), (bc_at, dxt.shape[1] - bc_at - bc_rows)))
        return dxt + spread.astype(bf16)

    dxt1 = with_bc(dxt1, sum(v[:, width:].astype(f32) for v in terms))

    early1 = halve(sum_far(early1, after(early1_far, sent)))
    z0 = after(z0, early1)
    early1 = sum_x(cut_x(early1))
    grad_rows0, dz0, dy0, go0, acc_gate0 = run_gate(place, gathered_back, z0, y0, w0, smalls[0][0])
    dz0 = after(dz0, early1)
    early = weight_products(place, [(xn0, dz0), (go0, grad_rows0), (xn1, dxt1)])
    dy0 = after(dy0, *early)
    early = sum_x(early)
    early1 = sum_beside(after(early1, dz0))
    back0 = run_scan(
        place, (dy0, dz0), xn0, xp0, bc0, dt0, hin0, (w0, wbc0, wdt[0]), smalls[0], pick, head_dim, inner_all
    )
    dxt0, *bc_halves, mine, other, acc0, acch0, shared0 = back0
    shared = jnp.concatenate([shared0, shared1], axis=0)
    bc_sum, shared = scatter_with_sum(*bc_halves, shared, (early,))
    tiny_at = bc_at + bc_rows
    tiny_lanes = channels + LANES - tiny_at
    tiny = jnp.concatenate(
        [acc0 + acc_gate0, acc1] + [pad_to(v, v.shape[0], channels) for v in (acch0[0:2], acch1[0:2], shared)],
        axis=0,
    )
    tiny_shape = tiny.shape
    tiny = pad_to(tiny.reshape(-1, tiny_lanes), width, tiny_lanes)
    tiny = jnp.pad(tiny, ((0, 0), (tiny_at, 0))).astype(bf16)
    early = halve(sum_far(early))
    late = weight_products(place, [(xn0, after(with_bc(dxt0, bc_sum), early))])
    early = sum_beside(early)
    late = [v + t for v, t in zip(late, cut_x(tiny))]
    mine, other = after(mine, late[0]), after(other, late[0])
    late = after(sum_x(late), early)

    terms = scatter((mine, other))
    [outputs] = row_call(
        end_kernel,
        "outputs",
        [(v, rows) for v in terms] + [(packed, rows), (d_res1, rows), (norm_in[0:1], 1), (hidden_out, rows)],
        [jax.ShapeDtypeStruct((rows, 2 * width), bf16)],
    )
    outputs_home = trade_places(outputs).astype(f32)

    early = collect(early)
    early1 = collect(after(early1, early[0], outputs))
    late = collect(sum_beside(halve(sum_far(late))))
    g_wz, g_wo = write_sums(place, early1, True, [(0, "rows", 1, None), (channels, "blocks", 1, None)])
    g_wz, g_wo, g_wx, narrow1 = write_sums(
        place,
        early,
        False,
        [
            (0, "rows", 0, g_wz),
            (channels, "blocks", 0, g_wo),
            (2 * channels, "rows", 1, None),
            (3 * channels, "flat", 0, None),
        ],
    )
    g_wx, narrow0 = write_sums(
        place, late, False, [(0, "rows", 0, g_wx), (channels, "flat", 0, None)]
    )

    narrow0, narrow1 = narrow0[0], narrow1[0]
    tiny = narrow0[: tiny_shape[0] * channels // tiny_lanes, tiny_at - channels :].reshape(tiny_shape)
    g_x = tiny[0:16].reshape(layers, 8, channels)
    g_head = tiny[16:20, :heads].reshape(layers, 2, heads)
    shared = tiny[20:, :both].reshape(layers, -1, both)
    lines = width // both
    g_norm_in = shared[:, :lines].reshape(layers, width) / norm_in
    g_bc = shared[:, lines : lines + 5]
    return (
        outputs_home[None, :, :width],
        outputs_home[None, :, width:],
        g_norm_in,
        g_wz,
        g_wx,
        jnp.stack([v[:, bc_at - channels : tiny_at - channels] for v in (narrow0, narrow1)]),
        jnp.stack([v[:, :heads] for v in (narrow0, narrow1)]),
        g_x[:, 0:4],
        g_x[:, 4],
        g_bc[:, 0:4],
        g_bc[:, 4],
        g_head[:, 0],
        g_head[:, 1],
        jnp.sum(g_x[:, 6].reshape(layers, heads, head_dim), axis=2),
        g_x[:, 5],
        g_wo,
    )


def solution(mesh):
    specs_in = (
        P("dp", "tensor", None),
        P("dp", "tensor", None),
        P(),
        P(None, None, "tensor"),
        P(None, None, "tensor"),
        P(None, None, "tensor"),
        P(None, None, "tensor"),
        P(None, None, "tensor"),
        P(None, "tensor"),
        P(),
        P(),
        P(None, "tensor"),
        P(None, "tensor"),
        P(None, "tensor"),
        P(None, "tensor"),
        P(None, "tensor", None),
    )
    specs_out = (
        P("dp", "tensor", None),
        P("dp", "tensor", None),
        P(),
        P(None, None, "tensor"),
        P(None, None, "tensor"),
        P(None, None, "tensor"),
        P(None, None, "tensor"),
        P(None, None, "tensor"),
        P(None, "tensor"),
        P(),
        P(),
        P(None, "tensor"),
        P(None, "tensor"),
        P(None, "tensor"),
        P(None, "tensor"),
        P(None, "tensor", None),
    )
    return jax.shard_map(
        local, mesh=mesh, in_specs=specs_in, out_specs=specs_out, check_vma=False
    )
```

```python
import functools

import jax
import jax.numpy as jnp
from jax import lax
from jax.experimental import pallas as pl
from jax.experimental.pallas import tpu as pltpu
from jax.sharding import PartitionSpec as P

SPAN = 256
EPS = 1e-05
LANES = 128
VMEM_BYTES = 56 * 1024 * 1024

f32 = jnp.float32
bf16 = jnp.bfloat16
highest = lax.Precision.HIGHEST

ROWS = ((0,), (0,))
COLS = ((1,), (1,))
PLAIN = ((1,), (0,))


def dot(left, right, dims=PLAIN, precision=None):
    return lax.dot_general(
        left, right, (dims, ((), ())), preferred_element_type=f32, precision=precision
    )


def sigmoid(v):
    return 1.0 / (1.0 + jnp.exp(-v))


def softplus(v):
    return jnp.maximum(v, 0.0) + jnp.log1p(jnp.exp(-jnp.abs(v)))


def spread_heads(per_head, channels, head_dim):
    rows = per_head.shape[0]
    per_tile = LANES // head_dim
    lane = lax.broadcasted_iota(jnp.int32, (rows, LANES), 1)
    tiles = []
    for tile in range(channels // LANES):
        out = jnp.broadcast_to(
            per_head[:, tile * per_tile : tile * per_tile + 1], (rows, LANES)
        )
        for sub in range(1, per_tile):
            head = tile * per_tile + sub
            out = jnp.where(
                lane >= sub * head_dim,
                jnp.broadcast_to(per_head[:, head : head + 1], (rows, LANES)),
                out,
            )
        tiles.append(out)
    return jnp.concatenate(tiles, axis=1)


def conv_taps(buf, taps, offset, width):
    out = offset
    for j in range(4):
        out = out + taps[j : j + 1] * buf[pl.ds(5 + j, width), :]
    return out


def decay_matrix(mask, cum_col, cum_row):
    return jnp.exp(jnp.where(mask, cum_col - cum_row, -1e30))


def span_values(dt, head_ref):
    length = dt.shape[0]
    rows = lax.broadcasted_iota(jnp.int32, (length, length), 0)
    cols = lax.broadcasted_iota(jnp.int32, (length, length), 1)
    mask = rows >= cols
    pre = dt + head_ref[0:1, :]
    step = softplus(pre)
    rate = head_ref[1:2, :] * step
    cum = dot(mask.astype(f32), rate, PLAIN, highest)
    return mask, pre, step, rate, cum


def put_half(place_ref, span, half, mine_ref, other_ref, value):
    own = span // half == place_ref[0]

    @pl.when(own)
    def _():
        mine_ref[...] = value

    @pl.when(jnp.logical_not(own))
    def _():
        other_ref[...] = value


def place_pieces(plan, place_ref, pieces, outs):
    core, z = place_ref[0], place_ref[1]
    for piece, other, dz, start, out, per, offset, rows in plan:
        member = (1 - core if other else core) * NZ + lax.rem(z + dz, NZ)
        row = pl.multiple_of(member * per + offset, 16)
        outs[out][pl.ds(row, rows), :] = pieces[piece][start : start + rows, :]


def put_columns(place_ref, span, mine_ref, other_ref, columns):
    per = columns.shape[0] // (NC * NZ)
    rows = mine_ref.shape[0] // NZ

    def place_columns(core, ref):
        for z in range(NZ):
            at = (core * NZ + z) * per
            ref[pl.ds(pl.multiple_of(z * rows + span * per, 16), per), :] = columns[at : at + per, :]

    for core in range(NC):
        mine = place_ref[0] == core

        @pl.when(mine)
        def _(core=core):
            place_columns(core, mine_ref)

        @pl.when(jnp.logical_not(mine))
        def _(core=core):
            place_columns(core, other_ref)


def forward_kernel(plans, there_plan, head_dim, place_ref, *refs):
    last_layer = len(plans) == 2
    refs = list(refs)

    def take(count):
        taken = refs[:count]
        del refs[:count]
        return taken

    piece_refs = [take(count) for _, count in plans]
    [w_here] = take(1)
    w_there = take(len(there_plan))
    wdt_ref, cx_ref, cbc_ref, head_ref = take(4)
    w_ref, xn_ref, wbc_ref, z_ref, xp_ref, bc_ref, dt_ref, y_ref, hin_ref, mine_ref, other_ref = take(11)
    if last_layer:
        g_ref, sums_ref, gg_ref = take(3)
    w_sem, xn_all, xbuf, bbuf, hst = take(5)
    if last_layer:
        [g_all] = take(1)
    length = z_ref.shape[0]
    channels = cx_ref.shape[1]
    state = hst.shape[0]
    span = pl.program_id(0)

    @pl.when(span == 0)
    def _():
        @pl.when(place_ref[2] == 1)
        def _():
            pltpu.make_async_copy(w_here, w_ref, w_sem).start()

        @pl.when(place_ref[2] == 0)
        def _():
            for part, (start, k) in zip(w_there, there_plan):
                rows = part.shape[0]
                if k is not None:
                    start = pl.multiple_of(lax.rem(place_ref[3] + NX - k, NX) * rows, 16)
                pltpu.make_async_copy(part, w_ref.at[pl.ds(start, rows), :], w_sem).start()

        if last_layer:
            place_pieces(plans[0][0], place_ref, piece_refs[0], [xn_all])
            place_pieces(plans[1][0], place_ref, piece_refs[1], [g_all, wbc_ref])
        else:
            place_pieces(plans[0][0], place_ref, piece_refs[0], [xn_all, wbc_ref])
        xbuf[0:8, :] = jnp.zeros((8, channels), f32)
        bbuf[0:8, :] = jnp.zeros((8, 2 * state), f32)
        hst[...] = jnp.zeros_like(hst)
        pltpu.make_async_copy(w_here, w_ref, w_sem).wait()

    here = pl.ds(pl.multiple_of(span * length, length), length)
    xn = xn_all[here, :]
    xn_ref[...] = xn
    zx = dot(xn, w_ref[:, : 2 * channels])
    z = zx[:, :channels]
    z_ref[...] = z.astype(bf16)
    xp = zx[:, channels:]
    xp_ref[...] = xp.astype(bf16)
    xbuf[8:, :] = xp
    bc = dot(xn, wbc_ref[...], COLS).astype(bf16)
    bc_ref[...] = bc
    bbuf[8:, :] = bc.astype(f32)
    dt = dot(xn, wdt_ref[...], COLS)
    dt_ref[...] = dt

    pre_x = conv_taps(xbuf, cx_ref[0:4, :], cx_ref[4:5, :], length)
    xc = pre_x * sigmoid(pre_x)
    pre_bc = conv_taps(bbuf, cbc_ref[0:4, :], cbc_ref[4:5, :], length)
    bcc = (pre_bc * sigmoid(pre_bc)).astype(bf16)
    xbuf[0:8, :] = xbuf[length : length + 8, :]
    bbuf[0:8, :] = bbuf[length : length + 8, :]
    b_mat = bcc[:, :state]
    c_mat = bcc[:, state:]

    mask, _, step, _, cum = span_values(dt, head_ref)
    cum_t = jnp.transpose(cum)
    scores = dot(c_mat, b_mat, COLS)
    xs = xc * spread_heads(step, channels, head_dim)
    xs_b = xs.astype(bf16)
    lane = lax.broadcasted_iota(jnp.int32, (length, LANES), 1)
    per_tile = LANES // head_dim
    tiles = []
    for tile in range(channels // LANES):
        xs_tile = xs_b[:, tile * LANES : (tile + 1) * LANES]
        out = None
        for sub in range(per_tile):
            head = tile * per_tile + sub
            decay = decay_matrix(mask, cum[:, head : head + 1], cum_t[head : head + 1, :])
            part = dot((scores * decay).astype(bf16), xs_tile)
            out = part if out is None else jnp.where(lane >= sub * head_dim, part, out)
        tiles.append(out)
    hin = hst[...]
    hin_ref[0] = hin
    last = cum[length - 1 : length, :]
    y = jnp.concatenate(tiles, axis=1)
    y = y + dot(c_mat, hin.astype(bf16)) * spread_heads(jnp.exp(cum), channels, head_dim)
    y = y + cx_ref[6:7, :] * xc
    y_ref[...] = y.astype(bf16)
    tail = spread_heads(jnp.exp(last - cum), channels, head_dim)
    keep = spread_heads(jnp.exp(last), channels, head_dim)
    hst[...] = keep * hin + dot(b_mat, (tail * xs).astype(bf16), ROWS)

    gated = y * (z * sigmoid(z))
    scaled = gated * cx_ref[5:6, :]
    squares = jnp.sum(gated * gated, axis=1, keepdims=True)
    high = squares.astype(bf16).astype(f32)
    extra = jnp.where(lane == 0, high, jnp.where(lane == 1, squares - high, 0.0)).astype(bf16)
    mixed = dot(scaled.astype(bf16), w_ref[:, 2 * channels :], COLS).astype(bf16)
    put_half(
        place_ref,
        span,
        pl.num_programs(0) // 2,
        mine_ref,
        other_ref,
        jnp.concatenate([mixed, extra], axis=1),
    )
    if last_layer:
        g = g_all[here, :]
        g_ref[...] = g
        gg = dot(g, w_ref[:, 2 * channels :])
        gg_ref[...] = gg
        products = jnp.sum(gg * scaled, axis=1, keepdims=True)
        both = jnp.where(lane == 0, squares, jnp.where(lane == 1, products, 0.0))
        sums_ref[...] = jnp.transpose(both)[0:8, :]


def gate_part(gg, rms, coef, z, y, cx_ref):
    z, y = z.astype(f32), y.astype(f32)
    norm_gate = cx_ref[5:6, :]
    sz = sigmoid(z)
    silu_z = z * sz
    gated = y * silu_z
    rg = rms * gg
    gate_out = (gated * rms * norm_gate).astype(bf16)
    d_gated = rg * norm_gate - gated * coef
    dz = (d_gated * y * (sz * (1.0 + z * (1.0 - sz)))).astype(bf16)
    return dz, d_gated * silu_z, gate_out, jnp.sum(rg * gated, axis=0, keepdims=True)


def gate_kernel(plan, n_pieces, width, place_ref, *refs):
    pieces = refs[:n_pieces]
    z_ref, y_ref, wo_ref, cx_ref, g_ref, dz_ref, dy_ref, go_ref, acc_ref, first_all = refs[n_pieces:]
    length = z_ref.shape[0]
    span = pl.program_id(0)

    @pl.when(span == 0)
    def _():
        place_pieces(plan, place_ref, pieces, [first_all])
        acc_ref[...] = jnp.zeros_like(acc_ref)

    first = first_all[pl.ds(pl.multiple_of(span * length, length), length), :]
    g = first[:, :width]
    g_ref[...] = g
    tok = first[:, width:].astype(f32)
    rms = tok[:, 0:1] + tok[:, 1:2]
    coef = tok[:, 2:3] + tok[:, 3:4]
    gg = dot(g, wo_ref[...])
    dz, dy, gate_out, acc_norm = gate_part(gg, rms, coef, z_ref[...], y_ref[...], cx_ref)
    dz_ref[...] = dz
    dy_ref[...] = dy
    go_ref[...] = gate_out
    acc_ref[5:6, :] += acc_norm


def scan_kernel(with_gate, head_dim, inner_all, place_ref, *refs):
    if with_gate:
        (gg_ref, tok_ref, z_ref, y_ref), refs = refs[:4], refs[4:]
    else:
        (dy_ref, dz_ref), refs = refs[:2], refs[2:]
    (xn_ref, xp_ref, xhalo_ref, bc_ref, bchalo_ref, dt_ref, hin_ref,
     w_ref, wbc_ref, wdt_ref, cx_ref, cbc_ref, head_ref, pick_ref), refs = refs[:14], refs[14:]
    if with_gate:
        (dz_ref, go_ref), refs = refs[:2], refs[2:]
    (dxt_ref, bcmine_ref, bcother_ref, mine_ref, other_ref, acc_ref, acch_ref, shared_ref,
     accbc, accn, xbuf, bbuf, dubuf, dubbuf, dhst) = refs
    length = xp_ref.shape[0]
    channels = cx_ref.shape[1]
    width = xn_ref.shape[1]
    state = dhst.shape[0]
    step_id = pl.program_id(0)
    first_span = step_id == pl.num_programs(0) - 1

    @pl.when(step_id == 0)
    def _():
        dubuf[length:, :] = jnp.zeros((8, channels), f32)
        dubbuf[length:, :] = jnp.zeros((8, 2 * state), f32)
        dhst[...] = jnp.zeros_like(dhst)
        accn[...] = jnp.zeros_like(accn)
        acc_ref[...] = jnp.zeros_like(acc_ref)
        accbc[...] = jnp.zeros_like(accbc)
        acch_ref[...] = jnp.zeros_like(acch_ref)

    @pl.when(first_span)
    def _():
        xbuf[0:8, :] = jnp.zeros((8, channels), f32)
        bbuf[0:8, :] = jnp.zeros((8, 2 * state), f32)

    @pl.when(jnp.logical_not(first_span))
    def _():
        xbuf[0:8, :] = xhalo_ref[...].astype(f32)[8:16, :]
        bbuf[0:8, :] = bchalo_ref[...].astype(f32)[8:16, :]

    xbuf[8:, :] = xp_ref[...].astype(f32)
    bbuf[8:, :] = bc_ref[...].astype(f32)
    if with_gate:
        tok = jnp.transpose(tok_ref[...])
        rms = lax.rsqrt(tok[:, 0:1] / inner_all + EPS)
        coef = rms * rms * rms * tok[:, 1:2] / inner_all
        dz_b, dy, gate_out, acc_norm = gate_part(
            gg_ref[...], rms, coef, z_ref[...], y_ref[...], cx_ref
        )
        dz_ref[...] = dz_b
        go_ref[...] = gate_out
    else:
        dz_b, dy = dz_ref[...], dy_ref[...]
        acc_norm = jnp.zeros((1, channels), f32)
    skip = cx_ref[6:7, :]

    pre_x = conv_taps(xbuf, cx_ref[0:4, :], cx_ref[4:5, :], length)
    sx = sigmoid(pre_x)
    xc = pre_x * sx
    pre_bc = conv_taps(bbuf, cbc_ref[0:4, :], cbc_ref[4:5, :], length)
    sbc = sigmoid(pre_bc)
    bcc = (pre_bc * sbc).astype(bf16)
    b_mat = bcc[:, :state]
    c_mat = bcc[:, state:]
    mask, pre_dt, step, rate, cum = span_values(dt_ref[...], head_ref)
    cum_t = jnp.transpose(cum)
    last = cum[length - 1 : length, :]
    scores = dot(c_mat, b_mat, COLS)
    step_all = spread_heads(step, channels, head_dim)
    xs = xc * step_all
    xs_b = xs.astype(bf16)
    tail = spread_heads(jnp.exp(last - cum), channels, head_dim)
    keep = spread_heads(jnp.exp(last), channels, head_dim)

    hin = hin_ref[0]
    hin_b = hin.astype(bf16)
    dh = dhst[...]
    dh_b = dh.astype(bf16)
    dye = dy * spread_heads(jnp.exp(cum), channels, head_dim)
    dye_b = dye.astype(bf16)
    txs = tail * xs
    txs_b = txs.astype(bf16)
    carried = dot(c_mat, hin_b)
    pulled = dot(b_mat, dh_b)
    d_c = dot(dye_b, hin_b, COLS)
    d_b = dot(txs_b, dh_b, COLS)
    dhst[...] = keep * dh + dot(c_mat, dye_b, ROWS)
    into = txs * pulled
    across = dye * carried - into
    at_last = jnp.sum(into, axis=0, keepdims=True) + keep * jnp.sum(hin * dh, axis=0, keepdims=True)

    dy_b = dy.astype(bf16)
    dy_t = jnp.transpose(dy).astype(bf16)
    lane = lax.broadcasted_iota(jnp.int32, (length, LANES), 1)
    per_tile = LANES // head_dim
    d_scores = jnp.zeros((length, length), f32)
    row_sums = jnp.zeros((length, LANES), f32)
    col_sums = []
    dxs_parts = []
    for head in range(channels // head_dim):
        tile, sub = divmod(head, per_tile)
        dy_tile = dy_b[:, tile * LANES : (tile + 1) * LANES]
        own = (lane >= sub * head_dim) & (lane < (sub + 1) * head_dim)
        dy_head = jnp.where(own, dy_tile, jnp.zeros_like(dy_tile))
        d_m = dot(dy_head, xs_b[:, tile * LANES : (tile + 1) * LANES], COLS)
        decay = decay_matrix(mask, cum[:, head : head + 1], cum_t[head : head + 1, :])
        dxs_parts.append(
            dot(dy_t[head * head_dim : (head + 1) * head_dim, :], (scores * decay).astype(bf16))
        )
        d_m = d_m * decay
        d_scores = d_scores + d_m
        pairs = d_m * scores
        row_sums = jnp.where(lane == head, jnp.sum(pairs, axis=1, keepdims=True), row_sums)
        col_sums.append(jnp.sum(pairs, axis=0, keepdims=True))
    heads = len(col_sums)
    col_sums = jnp.concatenate(col_sums + [jnp.zeros((LANES - heads, length), f32)], axis=0)
    dxs = jnp.transpose(jnp.concatenate(dxs_parts, axis=0)) + tail * pulled
    pick = pick_ref[...]
    d_cum = row_sums - jnp.transpose(col_sums) + dot(across, pick, PLAIN, highest)
    at_last = dot(jnp.broadcast_to(at_last, (8, channels)), pick, PLAIN, highest)[0:1, :]
    d_rate = dot(mask.astype(f32), d_cum, ROWS, highest) + at_last
    d_step = d_rate * head_ref[1:2, :] + dot(dxs * xc, pick, PLAIN, highest)
    d_dt = d_step * sigmoid(pre_dt)
    acch_ref[0:1, :] += jnp.sum(d_dt, axis=0, keepdims=True)
    acch_ref[1:2, :] += jnp.sum(d_rate * rate, axis=0, keepdims=True)
    dt_b = d_dt.astype(bf16)
    ds_b = d_scores.astype(bf16)
    d_c = d_c + dot(ds_b, b_mat)
    d_b = d_b + dot(ds_b, c_mat, ROWS)
    d_xc = dxs * step_all + skip * dy
    acc_skip = jnp.sum(dy * xc, axis=0, keepdims=True)

    d_u = d_xc * (sx * (1.0 + pre_x * (1.0 - sx)))
    d_ub = jnp.concatenate([d_b, d_c], axis=1) * (sbc * (1.0 + pre_bc * (1.0 - sbc)))
    dubuf[0:length, :] = d_u
    dubbuf[0:length, :] = d_ub
    d_x = jnp.zeros_like(d_u)
    d_bc = jnp.zeros_like(d_ub)
    acc_rows = []
    accbc_rows = []
    for j in range(4):
        d_x = d_x + cx_ref[j : j + 1, :] * dubuf[pl.ds(3 - j, length), :]
        d_bc = d_bc + cbc_ref[j : j + 1, :] * dubbuf[pl.ds(3 - j, length), :]
        acc_rows.append(jnp.sum(d_u * xbuf[pl.ds(5 + j, length), :], axis=0, keepdims=True))
        accbc_rows.append(jnp.sum(d_ub * bbuf[pl.ds(5 + j, length), :], axis=0, keepdims=True))
    dubuf[length:, :] = d_u[0:8, :]
    dubbuf[length:, :] = d_ub[0:8, :]
    zero = jnp.zeros((1, channels), f32)
    acc_ref[...] += jnp.concatenate(
        acc_rows + [jnp.sum(d_u, axis=0, keepdims=True), acc_norm, acc_skip, zero], axis=0
    )
    zero = jnp.zeros((3, d_ub.shape[1]), f32)
    accbc[...] += jnp.concatenate(
        accbc_rows + [jnp.sum(d_ub, axis=0, keepdims=True), zero], axis=0
    )
    dx_b = d_x.astype(bf16)
    dbc_b = d_bc.astype(bf16)
    dxt_ref[:, :channels] = dx_b
    dxt_ref[:, channels:] = dt_b
    put_columns(
        place_ref,
        pl.num_programs(0) - 1 - step_id,
        bcmine_ref,
        bcother_ref,
        jnp.transpose(d_bc).astype(bf16),
    )
    total = dot(jnp.concatenate([dz_b, dx_b], axis=1), w_ref[...], COLS)
    total = total + dot(dbc_b, wbc_ref[...]) + dot(dt_b, wdt_ref[...])
    accn[0:1, :] += jnp.sum(total * xn_ref[...].astype(f32), axis=0, keepdims=True)

    @pl.when(first_span)
    def _():
        lanes = shared_ref.shape[1]
        lines = [accn[0:1, i * lanes : (i + 1) * lanes] for i in range(width // lanes)]
        shared = jnp.concatenate(lines + [accbc[0:5, :]], axis=0)
        shared_ref[0 : shared.shape[0], :] = shared.astype(bf16)
        shared_ref[shared.shape[0] :, :] = jnp.zeros(
            (shared_ref.shape[0] - shared.shape[0], lanes), bf16
        )

    put_half(
        place_ref,
        pl.num_programs(0) - 1 - step_id,
        pl.num_programs(0) // 2,
        mine_ref,
        other_ref,
        total.astype(bf16),
    )


def whole(shape):
    zeros = (0,) * len(shape)
    return pl.BlockSpec(shape, lambda i, p: zeros)


def span_rows(columns):
    return pl.BlockSpec((SPAN, columns), lambda i, p: (i, 0))


def half_rows(columns, spans, reverse):
    half = spans // 2

    def block(i, core):
        span = spans - 1 - i if reverse else i
        return jnp.clip(span - half * core, 0, half - 1), 0

    return [
        pl.BlockSpec((SPAN, columns), lambda i, p: block(i, p[0])),
        pl.BlockSpec((SPAN, columns), lambda i, p: block(i, 1 - p[0])),
    ]


def span_call(kernel, name, spans, place, operands, in_specs, shapes, out_specs, scratch, flops):
    moved = sum(v.size * v.dtype.itemsize for v in [*operands, *shapes])
    return pl.pallas_call(
        kernel,
        grid_spec=pltpu.PrefetchScalarGridSpec(
            num_scalar_prefetch=1,
            grid=(spans,),
            in_specs=in_specs,
            out_specs=out_specs,
            scratch_shapes=scratch,
        ),
        out_shape=shapes,
        compiler_params=pltpu.CompilerParams(
            dimension_semantics=("arbitrary",), vmem_limit_bytes=VMEM_BYTES
        ),
        cost_estimate=pl.CostEstimate(flops=flops, bytes_accessed=moved, transcendentals=0),
        name=name,
    )(place, *operands)


def run_forward(place, gathered, w, wdt, small, state, head_dim):
    w_here, w_there, there_plan = w
    channels = small[0].shape[1]
    width = gathered[0][0][0].shape[1]
    anywhere = pl.BlockSpec(memory_space=pl.ANY)
    tokens = NC * NZ * gathered[0][2][0]
    spans = tokens // SPAN
    last_layer = len(gathered) == 2
    plans = [(cut_plan(*one), len(one[0])) for one in gathered]
    operands = [p for one in gathered for p in one[0]]
    in_specs = [whole(v.shape) for v in operands] + [anywhere] * (1 + len(w_there))
    operands += [w_here, *w_there, wdt, *small]
    in_specs += [whole(v.shape) for v in operands[len(in_specs) :]]
    shapes = [
        jax.ShapeDtypeStruct(w_here.shape, bf16),
        jax.ShapeDtypeStruct((tokens, width), bf16),
        jax.ShapeDtypeStruct((2 * state, width), bf16),
        jax.ShapeDtypeStruct((tokens, channels), bf16),
        jax.ShapeDtypeStruct((tokens, channels), bf16),
        jax.ShapeDtypeStruct((tokens, 2 * state), bf16),
        jax.ShapeDtypeStruct((tokens, LANES), f32),
        jax.ShapeDtypeStruct((tokens, channels), bf16),
        jax.ShapeDtypeStruct((spans, state, channels), f32),
        jax.ShapeDtypeStruct((tokens // 2, width + LANES), bf16),
        jax.ShapeDtypeStruct((tokens // 2, width + LANES), bf16),
    ]
    out_specs = [whole(w_here.shape), span_rows(width), whole((2 * state, width))]
    out_specs += [span_rows(s.shape[1]) for s in shapes[3:8]]
    out_specs.append(pl.BlockSpec((1, state, channels), lambda i, p: (i, 0, 0)))
    out_specs += half_rows(width + LANES, spans, False)
    scratch = [
        pltpu.SemaphoreType.DMA,
        pltpu.VMEM((tokens, width), bf16),
        pltpu.VMEM((SPAN + 8, channels), f32),
        pltpu.VMEM((SPAN + 8, 2 * state), f32),
        pltpu.VMEM((state, channels), f32),
    ]
    if last_layer:
        shapes += [
            jax.ShapeDtypeStruct((tokens, width), bf16),
            jax.ShapeDtypeStruct((8, tokens), f32),
            jax.ShapeDtypeStruct((tokens, channels), f32),
        ]
        out_specs += [span_rows(width), pl.BlockSpec((8, SPAN), lambda i, p: (0, i)), span_rows(channels)]
        scratch.append(pltpu.VMEM((tokens, width), bf16))
    kernel = functools.partial(forward_kernel, plans, there_plan, head_dim)
    return span_call(
        kernel, "layer_forward", spans, place, operands, in_specs, shapes, out_specs, scratch, 20 * 10**9
    )


def run_gate(place, gathered, z, y, w, cx):
    tokens, channels = z.shape
    width = w.shape[0]
    spans = tokens // SPAN
    plan, pieces = cut_plan(*gathered), list(gathered[0])
    operands = [*pieces, z, y, w, cx]
    in_specs = [whole(p.shape) for p in pieces]
    in_specs += [span_rows(channels), span_rows(channels)]
    in_specs += [pl.BlockSpec((width, channels), lambda i, p: (0, 2)), whole(cx.shape)]
    shapes = [
        jax.ShapeDtypeStruct((tokens, width), bf16),
        jax.ShapeDtypeStruct((tokens, channels), bf16),
        jax.ShapeDtypeStruct((tokens, channels), f32),
        jax.ShapeDtypeStruct((tokens, channels), bf16),
        jax.ShapeDtypeStruct((8, channels), f32),
    ]
    out_specs = [span_rows(s.shape[1]) for s in shapes[:4]] + [whole(shapes[4].shape)]
    scratch = [pltpu.VMEM((tokens, pieces[0].shape[1]), bf16)]
    kernel = functools.partial(gate_kernel, plan, len(pieces), width)
    return span_call(
        kernel, "gate_backward", spans, place, operands, in_specs, shapes, out_specs, scratch, 6 * 10**9
    )


def run_scan(place, lead, xn, xp, bc, dt, hin, weights, small, pick, head_dim, inner_all):
    tokens, channels = xp.shape
    state = hin.shape[1]
    width = xn.shape[1]
    spans = tokens // SPAN
    with_gate = len(lead) == 4

    def rev(columns):
        return pl.BlockSpec((SPAN, columns), lambda i, p: (spans - 1 - i, 0))

    def halo(columns, rows):
        per = SPAN // rows
        return pl.BlockSpec(
            (rows, columns), lambda i, p: (jnp.maximum((spans - 1 - i) * per - 1, 0), 0)
        )

    operands = [*lead, xn, xp, xp, bc, bc, dt, hin, *weights, *small, pick]
    in_specs = [rev(channels)] * 2
    if with_gate:
        tok = pl.BlockSpec((8, SPAN), lambda i, p: (0, spans - 1 - i))
        in_specs = [rev(channels), tok, rev(channels), rev(channels)]
    in_specs += [
        rev(width),
        rev(channels),
        halo(channels, 16),
        rev(2 * state),
        halo(2 * state, 16),
        rev(LANES),
        pl.BlockSpec((1, state, channels), lambda i, p: (spans - 1 - i, 0, 0)),
    ]
    in_specs.append(whole((width, 2 * channels)))
    in_specs += [whole(v.shape) for v in operands[len(in_specs) :]]
    shapes = [
        jax.ShapeDtypeStruct((tokens, channels + LANES), bf16),
        jax.ShapeDtypeStruct((state * spans, SPAN), bf16),
        jax.ShapeDtypeStruct((state * spans, SPAN), bf16),
        jax.ShapeDtypeStruct((tokens // 2, width), bf16),
        jax.ShapeDtypeStruct((tokens // 2, width), bf16),
        jax.ShapeDtypeStruct((8, channels), f32),
        jax.ShapeDtypeStruct((8, LANES), f32),
        jax.ShapeDtypeStruct((16, 2 * state), bf16),
    ]
    out_specs = [rev(channels + LANES), whole(shapes[1].shape), whole(shapes[2].shape)]
    out_specs += half_rows(width, spans, True)
    out_specs += [whole(s.shape) for s in shapes[5:]]
    if with_gate:
        shapes = [jax.ShapeDtypeStruct((tokens, channels), bf16)] * 2 + shapes
        out_specs = [rev(channels)] * 2 + out_specs
    scratch = [
        pltpu.VMEM((8, 2 * state), f32),
        pltpu.VMEM((8, width), f32),
        pltpu.VMEM((SPAN + 8, channels), f32),
        pltpu.VMEM((SPAN + 8, 2 * state), f32),
        pltpu.VMEM((SPAN + 8, channels), f32),
        pltpu.VMEM((SPAN + 8, 2 * state), f32),
        pltpu.VMEM((state, channels), f32),
    ]
    kernel = functools.partial(scan_kernel, with_gate, head_dim, inner_all)
    return span_call(
        kernel, "scan_backward", spans, place, operands, in_specs, shapes, out_specs, scratch, 28 * 10**9
    )


def weight_kernel(n_pairs, split, place_ref, *refs):
    lefts, rights, outs = refs[:n_pairs], refs[n_pairs : 2 * n_pairs], refs[2 * n_pairs :]

    def write(out_ref):
        at = 0
        for left_ref, right_ref in zip(lefts, rights):
            columns = right_ref.shape[1]
            out_ref[:, at : at + columns] = dot(left_ref[...], right_ref[...], ROWS).astype(bf16)
            at += columns

    if not split:
        write(outs[0])
        return
    for k, out_ref in enumerate(outs):
        pl.when(pl.program_id(0) == k)(functools.partial(write, out_ref))


def weight_products(place, pairs, split=True):
    tokens = pairs[0][0].shape[0]
    rows = max(left.shape[1] for left, _ in pairs)
    block = rows // 4

    def at(i, p):
        return lax.rem(p[3] + i, NX) if split else i

    lefts, rights, columns = [], [], []
    for left, right in pairs:
        quarter = left.shape[1] == block
        cut, uncut = (lambda i, p: (0, at(i, p))), (lambda i, p: (0, 0))
        lefts.append(pl.BlockSpec((tokens, block), uncut if quarter else cut))
        wide = block if quarter else right.shape[1]
        rights.append(pl.BlockSpec((tokens, wide), cut if quarter else uncut))
        columns.append(wide)
    columns = sum(columns)
    if split:
        out_specs = [whole((block, columns))] * 4
        shapes = [jax.ShapeDtypeStruct((block, columns), bf16)] * 4
    else:
        out_specs = [pl.BlockSpec((block, columns), lambda i, p: (i, 0))]
        shapes = [jax.ShapeDtypeStruct((rows, columns), bf16)]
    out = pl.pallas_call(
        functools.partial(weight_kernel, len(pairs), split),
        grid_spec=pltpu.PrefetchScalarGridSpec(
            num_scalar_prefetch=1, grid=(4,), in_specs=lefts + rights, out_specs=out_specs
        ),
        out_shape=shapes,
        compiler_params=pltpu.CompilerParams(vmem_limit_bytes=VMEM_BYTES),
        cost_estimate=pl.CostEstimate(
            flops=2 * tokens * rows * columns, bytes_accessed=8 * 10**6, transcendentals=0
        ),
        name="weight_products",
    )(place, *[left for left, _ in pairs], *[right for _, right in pairs])
    return out if split else out[0]


SIZES = (4, 2, 2, 2, 4)
NX, NYL, NC, NYH, NZ = SIZES
EVERY = [
    (x, yl, c, yh, z)
    for x in range(NX)
    for yl in range(NYL)
    for c in range(NC)
    for yh in range(NYH)
    for z in range(NZ)
]


def linear(x, yl, c, yh, z):
    return ((((x % NX) * NYL + yl % NYL) * NC + c % NC) * NYH + yh % NYH) * NZ + z % NZ


def send(v, step, only=None):
    pairs = [(linear(*d), linear(*step(*d))) for d in EVERY if only is None or only(*d)]
    return lax.ppermute(v, ("dp", "tensor"), pairs)


def send_z(v, k):
    return send(v, lambda x, yl, c, yh, z: (x, yl, c, yh, z + k))


def send_core(v):
    return send(v, lambda x, yl, c, yh, z: (x, yl, c + 1, yh, z))


def trade(v, k):
    return send(v, lambda x, yl, c, yh, z: (x, yl, yh, c, z + k))


def traded(v):
    return send(v, lambda x, yl, c, yh, z: (x, yl, yh, c, z), lambda x, yl, c, yh, z: c != yh)


def trade_places(v):
    _, _, core, yh, _ = position()
    return jnp.where(core == yh, v, traded(v))


def position():
    dp, tensor = lax.axis_index("dp"), lax.axis_index("tensor")
    return dp // (NYL * NC), dp // NC % NYL, dp % NC, tensor // NZ, tensor % NZ


def gather(v, parts, traded_own=None, later=()):
    arrays, sources = [], []
    for k in (0, 1, 3, 2):
        if traded_own is not None:
            piece = trade(v, k) if k else traded_own
        else:
            piece = send_z(v, k) if k else v
        arrays += [piece, send_core(after(piece, *later) if later else piece)]
        sources += [(False, -k % NZ, 0), (True, -k % NZ, 0)]
    return arrays, sources, parts


def cut_plan(arrays, sources, parts):
    plan = []
    for number, (piece, (other, dz, first)) in enumerate(zip(arrays, sources)):
        base = 0
        for out, per in enumerate(parts):
            begin, end = max(first, base), min(first + piece.shape[0], base + per)
            if begin < end:
                plan.append((number, other, dz, begin - first, out, per, begin - base, end - begin))
            base += per
    return plan


def fold(mine, other):
    _, _, _, _, z = position()
    rows = mine.shape[0] // NZ
    blocks = []
    for k in range(NZ):
        at = (z + k) % NZ * rows
        a = lax.dynamic_slice_in_dim(mine, at, rows, 0).astype(f32)
        blocks.append(a + lax.dynamic_slice_in_dim(other, at, rows, 0).astype(f32))
    return blocks


def fold_beside(pairs):
    folded = [fold(mine, send_core(other)) for mine, other in pairs]
    return [jnp.concatenate([blocks[k] for blocks in folded], axis=1) for k in range(NZ)]


def scatter(*pairs):
    own, one, two, three = fold_beside(pairs)
    return [own] + [send_z(b.astype(bf16), k) for k, b in ((1, one), (2, two), (3, three))]


def scatter_with_sum(mine, other, shared, meanwhile):
    half = mine.shape[0]
    rows = half // NZ
    got = after(send_core(jnp.concatenate([other, shared], axis=0)), *meanwhile)
    blocks = fold(mine, got[:half])
    total_shared = shared.astype(f32) + got[half:].astype(f32)
    packed = total_shared.astype(bf16)
    total = blocks[0]
    for k in range(1, NZ):
        got = send_z(jnp.concatenate([blocks[k].astype(bf16), packed], axis=0), k)
        total = total + got[:rows].astype(f32)
        total_shared = total_shared + got[rows:].astype(f32)
    return total, total_shared


def sum_members(v):
    both = v + send_core(v)
    total = both
    for k in range(1, NZ):
        total = total + send_z(both, k)
    return total


def send_far(v):
    return send(v, lambda x, yl, c, yh, z: (x, yl, c, yh + 1, z), lambda x, yl, c, yh, z: c != yh)


def sum_far(v, far=None):
    far = send_far(v) if far is None else far
    return (v.astype(f32) + far.astype(f32)).astype(bf16)


def halve(v):
    _, _, core, yh, _ = position()
    half = v.shape[0] // 2
    near = send(
        v[half:], lambda x, yl, c, yh, z: (x, yl, c + 1, yh, z), lambda x, yl, c, yh, z: c == yh
    )
    return jnp.where(core == yh, v[:half], near)


def sum_beside(part):
    beside = send(part, lambda x, yl, c, yh, z: (x, yl + 1, c, yh, z))
    return (part.astype(f32) + beside.astype(f32)).astype(bf16)


def sum_x(blocks):
    total = blocks[0].astype(f32)
    for k in range(1, NX):
        got = send(blocks[k], lambda x, yl, c, yh, z, k=k: (x + k, yl, c, yh, z))
        total = total + got.astype(f32)
    return total.astype(bf16)


def cut_x(v):
    x = position()[0]
    rows = v.shape[0] // NX
    return [lax.dynamic_slice_in_dim(v, (x + k) % NX * rows, rows, 0) for k in range(NX)]


def collect_x(part):
    x = position()[0]
    out = jnp.zeros((NX,) + part.shape, bf16)
    out = lax.dynamic_update_index_in_dim(out, part, x, 0)
    for k in range(1, NX):
        block = send(part, lambda x, yl, c, yh, z, k=k: (x + k, yl, c, yh, z))
        out = lax.dynamic_update_index_in_dim(out, block, (x - k) % NX, 0)
    return out


def collect(part, meanwhile=()):
    out = collect_x(part)
    out = after(out, *meanwhile) if meanwhile else out
    return out, send_core(out)


def write_kernel(plan, by_half, n_kept, place_ref, here_ref, there_ref, *refs):
    rows = here_ref.shape[1]

    def write(ref):
        for (column, kind, wide), out_ref in zip(plan, refs[n_kept:]):
            for x in range(NX):
                value = ref[x, :, column : column + wide].astype(f32)
                if kind != "blocks":
                    out_ref[0, 0 if by_half else x, x if by_half else 0] = value
                elif by_half:
                    at = x // 2 * wide
                    out_ref[0, x % 2 * rows : (x % 2 + 1) * rows, at : at + wide] = value
                else:
                    out_ref[0, :, x * wide : (x + 1) * wide] = value

    here = (pl.program_id(0) == 0) == (place_ref[2] == 1)

    @pl.when(here)
    def _():
        write(here_ref)

    @pl.when(jnp.logical_not(here))
    def _():
        write(there_ref)


def write_sums(place, halves, by_half, outputs):
    rows, columns = halves[0].shape[1:]
    total = 2 * NX * rows
    wide = total // 4
    plan, shapes, specs, finals, kept, alias = [], [], [], [], [], {}
    for column, kind, layer, array in outputs:
        lanes = LANES if kind == "flat" else wide
        layers = 1 if kind == "flat" else 2
        plan.append((column, kind, lanes))
        if kind == "blocks":
            shape = (layers, wide, total)
            if by_half:
                spec = pl.BlockSpec((1, wide, total // 2), lambda h, p, layer=layer: (layer, 0, h))
            else:
                spec = pl.BlockSpec((1, rows, total), lambda h, p, layer=layer: (layer, h, 0))
            finals.append(shape)
        elif by_half:
            shape = (layers, 2, NX, rows, lanes)
            spec = pl.BlockSpec((1, 1, NX, rows, lanes), lambda h, p, layer=layer: (layer, h, 0, 0, 0))
            finals.append((layers, total, lanes))
        else:
            shape = (layers, NX, 2, rows, lanes)
            spec = pl.BlockSpec((1, NX, 1, rows, lanes), lambda h, p, layer=layer: (layer, 0, h, 0, 0))
            finals.append((layers, total, lanes))
        shapes.append(jax.ShapeDtypeStruct(shape, f32))
        specs.append(spec)
        if array is not None:
            alias[3 + len(kept)] = len(shapes) - 1
            kept.append(array.reshape(shape))
    piece = pl.BlockSpec((NX, rows, columns), lambda h, p: (0, 0, 0))
    written = pl.pallas_call(
        functools.partial(write_kernel, plan, by_half, len(kept)),
        grid_spec=pltpu.PrefetchScalarGridSpec(
            num_scalar_prefetch=1,
            grid=(2,),
            in_specs=[piece, piece] + [pl.BlockSpec(memory_space=pl.ANY)] * len(kept),
            out_specs=specs,
        ),
        out_shape=shapes,
        input_output_aliases=alias,
        compiler_params=pltpu.CompilerParams(vmem_limit_bytes=VMEM_BYTES),
        name="write_sums",
    )(place, *halves, *kept)
    return [v.reshape(final) for v, final in zip(written, finals)]


def row_call(kernel, name, operands, shapes):
    return pl.pallas_call(
        kernel,
        grid=(1,),
        in_specs=[pl.BlockSpec((rows, v.shape[1]), lambda i: (0, 0)) for v, rows in operands],
        out_specs=[pl.BlockSpec(s.shape, lambda i: (0, 0)) for s in shapes],
        out_shape=shapes,
        compiler_params=pltpu.CompilerParams(vmem_limit_bytes=VMEM_BYTES),
        name=name,
    )(*[v for v, _ in operands])


def inverse_rms(v):
    return lax.rsqrt(jnp.mean(v * v, axis=-1, keepdims=True) + EPS)


def first_kernel(packed_ref, gain_ref, out_ref):
    rows = 128
    v = packed_ref[0:rows, :].astype(f32)
    out_ref[0:rows, :] = (v * inverse_rms(v) * gain_ref[...]).astype(bf16)
    out_ref[rows:, :] = packed_ref[rows : out_ref.shape[0], :]


def add_terms(own_ref, a_ref, b_ref, c_ref):
    total = own_ref[...].astype(f32) + a_ref[...].astype(f32)
    return total + (b_ref[...].astype(f32) + c_ref[...].astype(f32))


def unscaled_output(inner_all, terms, width):
    total = add_terms(*terms)
    squares = total[:, width : width + 1] + total[:, width + 1 : width + 2]
    gate_rms = lax.rsqrt(squares / inner_all + EPS)
    return gate_rms, total[:, :width] * gate_rms


def middle_kernel(inner_all, own_ref, a_ref, b_ref, c_ref, res_ref, gain_ref, res1_ref, mixed_ref, rms_ref, normed_ref):
    width = res_ref.shape[1]
    gate_rms, mixed = unscaled_output(inner_all, (own_ref, a_ref, b_ref, c_ref), width)
    res = res_ref[...].astype(f32) + mixed
    res1_ref[...] = res
    mixed_ref[...] = mixed
    rms_ref[...] = jnp.broadcast_to(gate_rms, rms_ref.shape)
    normed_ref[...] = (res * inverse_rms(res) * gain_ref[...]).astype(bf16)


def input_gradient(grad_normed, res, d_res, gain):
    inv = inverse_rms(res)
    scaled = grad_normed * gain
    dots = jnp.sum(scaled * res, axis=-1, keepdims=True) / res.shape[1]
    return d_res + inv * scaled - res * (inv * inv * inv) * dots


def between_kernel(inner_all, own_ref, a_ref, b_ref, c_ref, res_ref, dres_ref, gain_ref, mixed_ref, rms_ref, out_ref, sent_ref):
    width = res_ref.shape[1]
    grad_normed = add_terms(*(ref.at[:, 0:width] for ref in (own_ref, a_ref, b_ref, c_ref)))
    d_res = input_gradient(grad_normed, res_ref[...], dres_ref[...].astype(f32), gain_ref[...])
    out_ref[...] = d_res
    g_mixed = d_res.astype(bf16)
    sent_ref[:, :width] = g_mixed
    gate_rms = rms_ref[:, 0:1]
    products = jnp.sum(g_mixed.astype(f32) * mixed_ref[...], axis=-1, keepdims=True)
    coef = gate_rms * gate_rms * products / inner_all
    lane = lax.broadcasted_iota(jnp.int32, rms_ref.shape, 1)
    rms_high = gate_rms.astype(bf16).astype(f32)
    coef_high = coef.astype(bf16).astype(f32)
    extra = jnp.where(lane == 0, rms_high, jnp.where(lane == 1, gate_rms - rms_high, 0.0))
    extra = jnp.where(lane == 2, coef_high, jnp.where(lane == 3, coef - coef_high, extra))
    sent_ref[:, width:] = extra.astype(bf16)


def end_kernel(own_ref, a_ref, b_ref, c_ref, res_ref, dres_ref, gain_ref, hidden_ref, out_ref):
    width = res_ref.shape[1]
    grad_normed = add_terms(own_ref, a_ref, b_ref, c_ref)
    grad = input_gradient(grad_normed, res_ref[...].astype(f32), dres_ref[...], gain_ref[...])
    out_ref[:, :width] = hidden_ref[...]
    out_ref[:, width:] = grad.astype(bf16)


def last_kernel(inner_all, own_ref, a_ref, b_ref, c_ref, res_ref, out_ref):
    _, mixed = unscaled_output(inner_all, (own_ref, a_ref, b_ref, c_ref), res_ref.shape[1])
    out_ref[...] = (res_ref[...] + mixed).astype(bf16)


def after(v, *others):
    return lax.optimization_barrier((v, *others))[0]


def pad_to(v, rows, lanes):
    return jnp.pad(v, ((0, rows - v.shape[0]), (0, lanes - v.shape[1])))


def local(
    hidden_in,
    grad_out,
    norm_in,
    w_z,
    w_x,
    w_bc,
    w_dt,
    conv_x,
    conv_x_bias,
    conv_bc,
    conv_bc_bias,
    dt_bias,
    a_log,
    skip,
    norm_gate,
    w_out,
):
    layers, width, channels = w_z.shape
    heads = w_dt.shape[2]
    head_dim = channels // heads
    both = conv_bc.shape[2]
    state = both // 2
    members = NC * NZ
    inner_all = channels * members
    rows = hidden_in.shape[1]
    bc_rows = both // members
    x, _, core, yh, z = position()
    stays = core == yh
    place = jnp.stack([core, z, stays, x]).astype(jnp.int32)
    full = jax.ShapeDtypeStruct((rows, width), f32)

    def pack_weights(layer):
        return jnp.concatenate([w_z[layer], w_x[layer], w_out[layer].T], axis=1)

    bc_t = jnp.swapaxes(w_bc, 1, 2)
    dt_t = jnp.pad(jnp.swapaxes(w_dt, 1, 2), ((0, 0), (0, 8 - heads), (0, 0)))
    per_channel = jnp.concatenate(
        [conv_x, conv_x_bias[:, None], norm_gate[:, None], jnp.repeat(skip, head_dim, axis=1)[:, None]],
        axis=1,
    )
    per_channel = jnp.pad(per_channel, ((0, 0), (0, 1), (0, 0)))
    per_head = jnp.stack([dt_bias, -jnp.exp(a_log)], axis=1)
    per_head = jnp.pad(per_head, ((0, 0), (0, 6), (0, LANES - heads)))
    little = jnp.concatenate([per_channel, per_head], axis=2).reshape(layers * 8, channels + LANES)
    high = little.astype(bf16)
    low = (little - high.astype(f32)).astype(bf16)
    lines = pad_to(jnp.concatenate([high, low], axis=1), layers * 8, width)
    packed = jnp.concatenate([hidden_in[0], bc_t[0], dt_t.reshape(layers * 8, width), lines], axis=0)
    packed = trade_places(packed)
    lines = packed[packed.shape[0] - layers * 8 :].astype(f32)
    little = lines[:, : channels + LANES] + lines[:, channels + LANES : 2 * (channels + LANES)]
    little = little.reshape(layers, 8, channels + LANES)

    w0 = pack_weights(0)
    w0 = w0, [traded(after(w0, packed))], [(0, None)]
    grads = jnp.concatenate([grad_out[0], bc_t[1]], axis=0)

    [sent] = row_call(
        first_kernel,
        "first_norm",
        [(packed, packed.shape[0]), (norm_in[0:1], 1)],
        [jax.ShapeDtypeStruct((rows + bc_rows, width), bf16)],
    )
    gathered0 = gather(sent, (rows, bc_rows))
    wdt = [pad_to(packed[rows + bc_rows + 8 * l : rows + bc_rows + 8 * (l + 1)], LANES, width) for l in range(layers)]
    smalls = []
    for layer in range(layers):
        cbc = jnp.concatenate([conv_bc[layer], conv_bc_bias[layer][None], jnp.zeros((3, both), f32)], axis=0)
        smalls.append((little[layer, :, :channels], cbc, little[layer, :, channels:]))
    channel_head = jnp.arange(channels) // head_dim
    pick = (channel_head[:, None] == jnp.arange(LANES)[None, :]).astype(f32)

    out0 = run_forward(place, [gathered0], w0, wdt[0], smalls[0], state, head_dim)
    w0, xn0, wbc0, z0, xp0, bc0, dt0, y0, hin0, mine, other = out0
    grads = after(grads, sent)
    gathered_grad = gather(grads, (rows, bc_rows), trade_places(grads), (mine,))
    grad_held = gathered_grad[0][0]
    terms = scatter((mine, after(other, *gathered_grad[0][2::2])))
    w1 = pack_weights(1)
    w1 = w1, [traded(after(w1, terms[0], grad_held))], [(0, None)]
    res1, mixed0, rms0, normed1 = row_call(
        functools.partial(middle_kernel, inner_all),
        "middle_norm",
        [(v, rows) for v in terms] + [(packed, rows), (norm_in[1:2], 1)],
        [full, full, jax.ShapeDtypeStruct((rows, LANES), f32), jax.ShapeDtypeStruct((rows, width), bf16)],
    )
    gathered1 = gather(normed1, (rows,))
    out1 = run_forward(
        place, [gathered1, gathered_grad], w1, wdt[1], smalls[1], state, head_dim
    )
    w1, xn1, wbc1, z1, xp1, bc1, dt1, y1, hin1, mine, other, grad_rows1, sums, gg1 = out1
    sums = sum_members(sums)

    home = fold(mine, send_core(other))
    sums = after(sums, *home)
    home = home[:1] + [send_z(home[k].astype(bf16), k) for k in range(1, NZ)]
    back1 = run_scan(
        place, (gg1, sums, z1, y1), xn1, xp1, bc1, dt1, hin1, (w1, wbc1, wdt[1]), smalls[1], pick, head_dim,
        inner_all,
    )
    dz1, go1, dxt1, *bc_halves, mine, other, acc1, acch1, shared1 = back1
    terms = scatter((mine, after(other, *home)), bc_halves)
    early1 = weight_products(place, [(xn1, dz1), (go1, grad_rows1)], split=False)
    terms[1] = after(terms[1], early1)
    early1_far = send_far(early1)
    [hidden_out] = row_call(
        functools.partial(last_kernel, inner_all),
        "last_output",
        [(after(home[0], terms[1]), rows)] + [(v, rows) for v in home[1:]] + [(res1, rows)],
        [jax.ShapeDtypeStruct((rows, width), bf16)],
    )
    d_res1, sent = row_call(
        functools.partial(between_kernel, inner_all),
        "between_layers",
        [(v, rows) for v in terms]
        + [(res1, rows), (grad_held, rows), (norm_in[1:2], 1), (mixed0, rows), (rms0, rows)],
        [full, jax.ShapeDtypeStruct((rows, width + LANES), bf16)],
    )
    gathered_back = gather(sent, (rows,))

    bc_at = channels + bc_rows

    def with_bc(dxt, bc_sum):
        by_token = bc_sum.reshape(-1, bc_rows, SPAN).swapaxes(1, 2).reshape(-1, bc_rows)
        spread = jnp.pad(by_token, ((0, 0), (bc_at, dxt.shape[1] - bc_at - bc_rows)))
        return dxt + spread.astype(bf16)

    dxt1 = with_bc(dxt1, sum(v[:, width:].astype(f32) for v in terms))

    early1 = halve(sum_far(early1, after(early1_far, sent)))
    z0 = after(z0, early1)
    early1 = sum_x(cut_x(early1))
    grad_rows0, dz0, dy0, go0, acc_gate0 = run_gate(place, gathered_back, z0, y0, w0, smalls[0][0])
    dz0 = after(dz0, early1)
    early = weight_products(place, [(xn0, dz0), (go0, grad_rows0), (xn1, dxt1)])
    dy0 = after(dy0, *early)
    early = sum_x(early)
    early1 = sum_beside(after(early1, dz0))
    back0 = run_scan(
        place, (dy0, dz0), xn0, xp0, bc0, dt0, hin0, (w0, wbc0, wdt[0]), smalls[0], pick, head_dim, inner_all
    )
    dxt0, *bc_halves, mine, other, acc0, acch0, shared0 = back0
    shared = jnp.concatenate([shared0, shared1], axis=0)
    bc_sum, shared = scatter_with_sum(*bc_halves, shared, (early,))
    tiny_at = bc_at + bc_rows
    tiny_lanes = channels + LANES - tiny_at
    tiny = jnp.concatenate(
        [acc0 + acc_gate0, acc1] + [pad_to(v, v.shape[0], channels) for v in (acch0[0:2], acch1[0:2], shared)],
        axis=0,
    )
    tiny_shape = tiny.shape
    tiny = pad_to(tiny.reshape(-1, tiny_lanes), width, tiny_lanes)
    tiny = jnp.pad(tiny, ((0, 0), (tiny_at, 0))).astype(bf16)
    early = halve(sum_far(after(early, dxt0)))
    home = fold(mine, send_core(other))
    late = weight_products(place, [(xn0, after(with_bc(dxt0, bc_sum), early, home[0]))])
    early = sum_beside(early)
    tiny = after(tiny, early)
    late = [v + t for v, t in zip(late, cut_x(tiny))]
    late = sum_x(late)

    terms = home[:1] + [send_z(home[k].astype(bf16), k) for k in range(1, NZ)]
    [outputs] = row_call(
        end_kernel,
        "outputs",
        [(v, rows) for v in terms] + [(packed, rows), (d_res1, rows), (norm_in[0:1], 1), (hidden_out, rows)],
        [jax.ShapeDtypeStruct((rows, 2 * width), bf16)],
    )
    outputs_home = trade_places(outputs).astype(f32)

    early = collect(early, (outputs,))
    early1 = collect(after(early1, early[0]))
    late = collect(sum_beside(halve(sum_far(late))))
    g_wz, g_wo, g_wx, narrow1 = write_sums(
        place,
        early,
        False,
        [
            (0, "rows", 0, None),
            (channels, "blocks", 0, None),
            (2 * channels, "rows", 1, None),
            (3 * channels, "flat", 0, None),
        ],
    )
    g_wx, narrow0 = write_sums(place, late, False, [(0, "rows", 0, g_wx), (channels, "flat", 0, None)])
    g_wz, g_wo = write_sums(place, early1, True, [(0, "rows", 1, g_wz), (channels, "blocks", 1, g_wo)])

    narrow0, narrow1 = narrow0[0], narrow1[0]
    tiny = narrow0[: tiny_shape[0] * channels // tiny_lanes, tiny_at - channels :].reshape(tiny_shape)
    g_x = tiny[0:16].reshape(layers, 8, channels)
    g_head = tiny[16:20, :heads].reshape(layers, 2, heads)
    shared = tiny[20:, :both].reshape(layers, -1, both)
    lines = width // both
    g_norm_in = shared[:, :lines].reshape(layers, width) / norm_in
    g_bc = shared[:, lines : lines + 5]
    return (
        outputs_home[None, :, :width],
        outputs_home[None, :, width:],
        g_norm_in,
        g_wz,
        g_wx,
        jnp.stack([v[:, bc_at - channels : tiny_at - channels] for v in (narrow0, narrow1)]),
        jnp.stack([v[:, :heads] for v in (narrow0, narrow1)]),
        g_x[:, 0:4],
        g_x[:, 4],
        g_bc[:, 0:4],
        g_bc[:, 4],
        g_head[:, 0],
        g_head[:, 1],
        jnp.sum(g_x[:, 6].reshape(layers, heads, head_dim), axis=2),
        g_x[:, 5],
        g_wo,
    )


def solution(mesh):
    specs_in = (
        P("dp", "tensor", None),
        P("dp", "tensor", None),
        P(),
        P(None, None, "tensor"),
        P(None, None, "tensor"),
        P(None, None, "tensor"),
        P(None, None, "tensor"),
        P(None, None, "tensor"),
        P(None, "tensor"),
        P(),
        P(),
        P(None, "tensor"),
        P(None, "tensor"),
        P(None, "tensor"),
        P(None, "tensor"),
        P(None, "tensor", None),
    )
    specs_out = (
        P("dp", "tensor", None),
        P("dp", "tensor", None),
        P(),
        P(None, None, "tensor"),
        P(None, None, "tensor"),
        P(None, None, "tensor"),
        P(None, None, "tensor"),
        P(None, None, "tensor"),
        P(None, "tensor"),
        P(),
        P(),
        P(None, "tensor"),
        P(None, "tensor"),
        P(None, "tensor"),
        P(None, "tensor"),
        P(None, "tensor", None),
    )
    return jax.shard_map(
        local, mesh=mesh, in_specs=specs_in, out_specs=specs_out, check_vma=False
    )
```

```python
import functools

import jax
import jax.numpy as jnp
from jax import lax
from jax.experimental import pallas as pl
from jax.experimental.pallas import tpu as pltpu
from jax.sharding import PartitionSpec as P

SPAN = 256
EPS = 1e-05
LANES = 128
VMEM_BYTES = 56 * 1024 * 1024

f32 = jnp.float32
bf16 = jnp.bfloat16
highest = lax.Precision.HIGHEST

ROWS = ((0,), (0,))
COLS = ((1,), (1,))
PLAIN = ((1,), (0,))


def dot(left, right, dims=PLAIN, precision=None):
    return lax.dot_general(
        left, right, (dims, ((), ())), preferred_element_type=f32, precision=precision
    )


def sigmoid(v):
    return 1.0 / (1.0 + jnp.exp(-v))


def softplus(v):
    return jnp.maximum(v, 0.0) + jnp.log1p(jnp.exp(-jnp.abs(v)))


def spread_heads(per_head, channels, head_dim):
    rows = per_head.shape[0]
    per_tile = LANES // head_dim
    lane = lax.broadcasted_iota(jnp.int32, (rows, LANES), 1)
    tiles = []
    for tile in range(channels // LANES):
        out = jnp.broadcast_to(
            per_head[:, tile * per_tile : tile * per_tile + 1], (rows, LANES)
        )
        for sub in range(1, per_tile):
            head = tile * per_tile + sub
            out = jnp.where(
                lane >= sub * head_dim,
                jnp.broadcast_to(per_head[:, head : head + 1], (rows, LANES)),
                out,
            )
        tiles.append(out)
    return jnp.concatenate(tiles, axis=1)


def conv_taps(buf, taps, offset, width):
    out = offset
    for j in range(4):
        out = out + taps[j : j + 1] * buf[pl.ds(5 + j, width), :]
    return out


def decay_matrix(mask, cum_col, cum_row):
    return jnp.exp(jnp.where(mask, cum_col - cum_row, -1e30))


def span_values(dt, head_ref):
    length = dt.shape[0]
    rows = lax.broadcasted_iota(jnp.int32, (length, length), 0)
    cols = lax.broadcasted_iota(jnp.int32, (length, length), 1)
    mask = rows >= cols
    pre = dt + head_ref[0:1, :]
    step = softplus(pre)
    rate = head_ref[1:2, :] * step
    cum = dot(mask.astype(f32), rate, PLAIN, highest)
    return mask, pre, step, rate, cum


def put_half(place_ref, span, half, mine_ref, other_ref, value):
    own = span // half == place_ref[0]

    @pl.when(own)
    def _():
        mine_ref[...] = value

    @pl.when(jnp.logical_not(own))
    def _():
        other_ref[...] = value


def place_pieces(plan, place_ref, pieces, outs):
    core, z = place_ref[0], place_ref[1]
    for piece, other, dz, start, out, per, offset, rows in plan:
        member = (1 - core if other else core) * NZ + lax.rem(z + dz, NZ)
        row = pl.multiple_of(member * per + offset, 16)
        outs[out][pl.ds(row, rows), :] = pieces[piece][start : start + rows, :]


def put_columns(place_ref, span, mine_ref, other_ref, columns):
    per = columns.shape[0] // (NC * NZ)
    rows = mine_ref.shape[0] // NZ

    def place_columns(core, ref):
        for z in range(NZ):
            at = (core * NZ + z) * per
            ref[pl.ds(pl.multiple_of(z * rows + span * per, 16), per), :] = columns[at : at + per, :]

    for core in range(NC):
        mine = place_ref[0] == core

        @pl.when(mine)
        def _(core=core):
            place_columns(core, mine_ref)

        @pl.when(jnp.logical_not(mine))
        def _(core=core):
            place_columns(core, other_ref)


def forward_kernel(plans, there_plan, head_dim, place_ref, *refs):
    last_layer = len(plans) == 2
    refs = list(refs)

    def take(count):
        taken = refs[:count]
        del refs[:count]
        return taken

    piece_refs = [take(count) for _, count in plans]
    [w_here] = take(1)
    w_there = take(len(there_plan))
    wdt_ref, cx_ref, cbc_ref, head_ref = take(4)
    w_ref, xn_ref, wbc_ref, z_ref, xp_ref, bc_ref, dt_ref, y_ref, hin_ref, mine_ref, other_ref = take(11)
    if last_layer:
        g_ref, sums_ref, gg_ref = take(3)
    w_sem, xn_all, xbuf, bbuf, hst = take(5)
    if last_layer:
        [g_all] = take(1)
    length = z_ref.shape[0]
    channels = cx_ref.shape[1]
    state = hst.shape[0]
    span = pl.program_id(0)

    @pl.when(span == 0)
    def _():
        @pl.when(place_ref[2] == 1)
        def _():
            pltpu.make_async_copy(w_here, w_ref, w_sem).start()

        @pl.when(place_ref[2] == 0)
        def _():
            for part, (start, k) in zip(w_there, there_plan):
                rows = part.shape[0]
                if k is not None:
                    start = pl.multiple_of(lax.rem(place_ref[3] + NX - k, NX) * rows, 16)
                pltpu.make_async_copy(part, w_ref.at[pl.ds(start, rows), :], w_sem).start()

        if last_layer:
            place_pieces(plans[0][0], place_ref, piece_refs[0], [xn_all])
            place_pieces(plans[1][0], place_ref, piece_refs[1], [g_all, wbc_ref])
        else:
            place_pieces(plans[0][0], place_ref, piece_refs[0], [xn_all, wbc_ref])
        xbuf[0:8, :] = jnp.zeros((8, channels), f32)
        bbuf[0:8, :] = jnp.zeros((8, 2 * state), f32)
        hst[...] = jnp.zeros_like(hst)
        pltpu.make_async_copy(w_here, w_ref, w_sem).wait()

    here = pl.ds(pl.multiple_of(span * length, length), length)
    xn = xn_all[here, :]
    xn_ref[...] = xn
    zx = dot(xn, w_ref[:, : 2 * channels])
    z = zx[:, :channels]
    z_ref[...] = z.astype(bf16)
    xp = zx[:, channels:]
    xp_ref[...] = xp.astype(bf16)
    xbuf[8:, :] = xp
    bc = dot(xn, wbc_ref[...], COLS).astype(bf16)
    bc_ref[...] = bc
    bbuf[8:, :] = bc.astype(f32)
    dt = dot(xn, wdt_ref[...], COLS)
    dt_ref[...] = dt

    pre_x = conv_taps(xbuf, cx_ref[0:4, :], cx_ref[4:5, :], length)
    xc = pre_x * sigmoid(pre_x)
    pre_bc = conv_taps(bbuf, cbc_ref[0:4, :], cbc_ref[4:5, :], length)
    bcc = (pre_bc * sigmoid(pre_bc)).astype(bf16)
    xbuf[0:8, :] = xbuf[length : length + 8, :]
    bbuf[0:8, :] = bbuf[length : length + 8, :]
    b_mat = bcc[:, :state]
    c_mat = bcc[:, state:]

    mask, _, step, _, cum = span_values(dt, head_ref)
    cum_t = jnp.transpose(cum)
    scores = dot(c_mat, b_mat, COLS)
    xs = xc * spread_heads(step, channels, head_dim)
    xs_b = xs.astype(bf16)
    lane = lax.broadcasted_iota(jnp.int32, (length, LANES), 1)
    per_tile = LANES // head_dim
    tiles = []
    for tile in range(channels // LANES):
        xs_tile = xs_b[:, tile * LANES : (tile + 1) * LANES]
        out = None
        for sub in range(per_tile):
            head = tile * per_tile + sub
            decay = decay_matrix(mask, cum[:, head : head + 1], cum_t[head : head + 1, :])
            part = dot((scores * decay).astype(bf16), xs_tile)
            out = part if out is None else jnp.where(lane >= sub * head_dim, part, out)
        tiles.append(out)
    hin = hst[...]
    hin_ref[0] = hin
    last = cum[length - 1 : length, :]
    y = jnp.concatenate(tiles, axis=1)
    y = y + dot(c_mat, hin.astype(bf16)) * spread_heads(jnp.exp(cum), channels, head_dim)
    y = y + cx_ref[6:7, :] * xc
    y_ref[...] = y.astype(bf16)
    tail = spread_heads(jnp.exp(last - cum), channels, head_dim)
    keep = spread_heads(jnp.exp(last), channels, head_dim)
    hst[...] = keep * hin + dot(b_mat, (tail * xs).astype(bf16), ROWS)

    gated = y * (z * sigmoid(z))
    scaled = gated * cx_ref[5:6, :]
    squares = jnp.sum(gated * gated, axis=1, keepdims=True)
    high = squares.astype(bf16).astype(f32)
    extra = jnp.where(lane == 0, high, jnp.where(lane == 1, squares - high, 0.0)).astype(bf16)
    mixed = dot(scaled.astype(bf16), w_ref[:, 2 * channels :], COLS).astype(bf16)
    put_half(
        place_ref,
        span,
        pl.num_programs(0) // 2,
        mine_ref,
        other_ref,
        jnp.concatenate([mixed, extra], axis=1),
    )
    if last_layer:
        g = g_all[here, :]
        g_ref[...] = g
        gg = dot(g, w_ref[:, 2 * channels :])
        gg_ref[...] = gg
        products = jnp.sum(gg * scaled, axis=1, keepdims=True)
        both = jnp.where(lane == 0, squares, jnp.where(lane == 1, products, 0.0))
        sums_ref[...] = jnp.transpose(both)[0:8, :]


def gate_part(gg, rms, coef, z, y, cx_ref):
    z, y = z.astype(f32), y.astype(f32)
    norm_gate = cx_ref[5:6, :]
    sz = sigmoid(z)
    silu_z = z * sz
    gated = y * silu_z
    rg = rms * gg
    gate_out = (gated * rms * norm_gate).astype(bf16)
    d_gated = rg * norm_gate - gated * coef
    dz = (d_gated * y * (sz * (1.0 + z * (1.0 - sz)))).astype(bf16)
    return dz, d_gated * silu_z, gate_out, jnp.sum(rg * gated, axis=0, keepdims=True)


def gate_kernel(plan, n_pieces, width, place_ref, *refs):
    pieces = refs[:n_pieces]
    z_ref, y_ref, wo_ref, cx_ref, g_ref, dz_ref, dy_ref, go_ref, acc_ref, first_all = refs[n_pieces:]
    length = z_ref.shape[0]
    span = pl.program_id(0)

    @pl.when(span == 0)
    def _():
        place_pieces(plan, place_ref, pieces, [first_all])
        acc_ref[...] = jnp.zeros_like(acc_ref)

    first = first_all[pl.ds(pl.multiple_of(span * length, length), length), :]
    g = first[:, :width]
    g_ref[...] = g
    tok = first[:, width:].astype(f32)
    rms = tok[:, 0:1] + tok[:, 1:2]
    coef = tok[:, 2:3] + tok[:, 3:4]
    gg = dot(g, wo_ref[...])
    dz, dy, gate_out, acc_norm = gate_part(gg, rms, coef, z_ref[...], y_ref[...], cx_ref)
    dz_ref[...] = dz
    dy_ref[...] = dy
    go_ref[...] = gate_out
    acc_ref[5:6, :] += acc_norm


def scan_kernel(with_gate, head_dim, inner_all, place_ref, *refs):
    if with_gate:
        (gg_ref, tok_ref, z_ref, y_ref), refs = refs[:4], refs[4:]
    else:
        (dy_ref, dz_ref), refs = refs[:2], refs[2:]
    (xn_ref, xp_ref, xhalo_ref, bc_ref, bchalo_ref, dt_ref, hin_ref,
     w_ref, wbc_ref, wdt_ref, cx_ref, cbc_ref, head_ref, pick_ref), refs = refs[:14], refs[14:]
    if with_gate:
        (dz_ref, go_ref), refs = refs[:2], refs[2:]
    (dxt_ref, bcmine_ref, bcother_ref, mine_ref, other_ref, acc_ref, acch_ref, shared_ref,
     accbc, accn, xbuf, bbuf, dubuf, dubbuf, dhst) = refs
    length = xp_ref.shape[0]
    channels = cx_ref.shape[1]
    width = xn_ref.shape[1]
    state = dhst.shape[0]
    step_id = pl.program_id(0)
    first_span = step_id == pl.num_programs(0) - 1

    @pl.when(step_id == 0)
    def _():
        dubuf[length:, :] = jnp.zeros((8, channels), f32)
        dubbuf[length:, :] = jnp.zeros((8, 2 * state), f32)
        dhst[...] = jnp.zeros_like(dhst)
        accn[...] = jnp.zeros_like(accn)
        acc_ref[...] = jnp.zeros_like(acc_ref)
        accbc[...] = jnp.zeros_like(accbc)
        acch_ref[...] = jnp.zeros_like(acch_ref)

    @pl.when(first_span)
    def _():
        xbuf[0:8, :] = jnp.zeros((8, channels), f32)
        bbuf[0:8, :] = jnp.zeros((8, 2 * state), f32)

    @pl.when(jnp.logical_not(first_span))
    def _():
        xbuf[0:8, :] = xhalo_ref[...].astype(f32)[8:16, :]
        bbuf[0:8, :] = bchalo_ref[...].astype(f32)[8:16, :]

    xbuf[8:, :] = xp_ref[...].astype(f32)
    bbuf[8:, :] = bc_ref[...].astype(f32)
    if with_gate:
        tok = jnp.transpose(tok_ref[...])
        rms = lax.rsqrt(tok[:, 0:1] / inner_all + EPS)
        coef = rms * rms * rms * tok[:, 1:2] / inner_all
        dz_b, dy, gate_out, acc_norm = gate_part(
            gg_ref[...], rms, coef, z_ref[...], y_ref[...], cx_ref
        )
        dz_ref[...] = dz_b
        go_ref[...] = gate_out
    else:
        dz_b, dy = dz_ref[...], dy_ref[...]
        acc_norm = jnp.zeros((1, channels), f32)
    skip = cx_ref[6:7, :]

    pre_x = conv_taps(xbuf, cx_ref[0:4, :], cx_ref[4:5, :], length)
    sx = sigmoid(pre_x)
    xc = pre_x * sx
    pre_bc = conv_taps(bbuf, cbc_ref[0:4, :], cbc_ref[4:5, :], length)
    sbc = sigmoid(pre_bc)
    bcc = (pre_bc * sbc).astype(bf16)
    b_mat = bcc[:, :state]
    c_mat = bcc[:, state:]
    mask, pre_dt, step, rate, cum = span_values(dt_ref[...], head_ref)
    cum_t = jnp.transpose(cum)
    last = cum[length - 1 : length, :]
    scores = dot(c_mat, b_mat, COLS)
    step_all = spread_heads(step, channels, head_dim)
    xs = xc * step_all
    xs_b = xs.astype(bf16)
    tail = spread_heads(jnp.exp(last - cum), channels, head_dim)
    keep = spread_heads(jnp.exp(last), channels, head_dim)

    hin = hin_ref[0]
    hin_b = hin.astype(bf16)
    dh = dhst[...]
    dh_b = dh.astype(bf16)
    dye = dy * spread_heads(jnp.exp(cum), channels, head_dim)
    dye_b = dye.astype(bf16)
    txs = tail * xs
    txs_b = txs.astype(bf16)
    carried = dot(c_mat, hin_b)
    pulled = dot(b_mat, dh_b)
    d_c = dot(dye_b, hin_b, COLS)
    d_b = dot(txs_b, dh_b, COLS)
    dhst[...] = keep * dh + dot(c_mat, dye_b, ROWS)
    into = txs * pulled
    across = dye * carried - into
    at_last = jnp.sum(into, axis=0, keepdims=True) + keep * jnp.sum(hin * dh, axis=0, keepdims=True)

    dy_b = dy.astype(bf16)
    dy_t = jnp.transpose(dy).astype(bf16)
    lane = lax.broadcasted_iota(jnp.int32, (length, LANES), 1)
    per_tile = LANES // head_dim
    d_scores = jnp.zeros((length, length), f32)
    row_sums = jnp.zeros((length, LANES), f32)
    col_sums = []
    dxs_parts = []
    for head in range(channels // head_dim):
        tile, sub = divmod(head, per_tile)
        dy_tile = dy_b[:, tile * LANES : (tile + 1) * LANES]
        own = (lane >= sub * head_dim) & (lane < (sub + 1) * head_dim)
        dy_head = jnp.where(own, dy_tile, jnp.zeros_like(dy_tile))
        d_m = dot(dy_head, xs_b[:, tile * LANES : (tile + 1) * LANES], COLS)
        decay = decay_matrix(mask, cum[:, head : head + 1], cum_t[head : head + 1, :])
        dxs_parts.append(
            dot(dy_t[head * head_dim : (head + 1) * head_dim, :], (scores * decay).astype(bf16))
        )
        d_m = d_m * decay
        d_scores = d_scores + d_m
        pairs = d_m * scores
        row_sums = jnp.where(lane == head, jnp.sum(pairs, axis=1, keepdims=True), row_sums)
        col_sums.append(jnp.sum(pairs, axis=0, keepdims=True))
    heads = len(col_sums)
    col_sums = jnp.concatenate(col_sums + [jnp.zeros((LANES - heads, length), f32)], axis=0)
    dxs = jnp.transpose(jnp.concatenate(dxs_parts, axis=0)) + tail * pulled
    pick = pick_ref[...]
    d_cum = row_sums - jnp.transpose(col_sums) + dot(across, pick, PLAIN, highest)
    at_last = dot(jnp.broadcast_to(at_last, (8, channels)), pick, PLAIN, highest)[0:1, :]
    d_rate = dot(mask.astype(f32), d_cum, ROWS, highest) + at_last
    d_step = d_rate * head_ref[1:2, :] + dot(dxs * xc, pick, PLAIN, highest)
    d_dt = d_step * sigmoid(pre_dt)
    acch_ref[0:1, :] += jnp.sum(d_dt, axis=0, keepdims=True)
    acch_ref[1:2, :] += jnp.sum(d_rate * rate, axis=0, keepdims=True)
    dt_b = d_dt.astype(bf16)
    ds_b = d_scores.astype(bf16)
    d_c = d_c + dot(ds_b, b_mat)
    d_b = d_b + dot(ds_b, c_mat, ROWS)
    d_xc = dxs * step_all + skip * dy
    acc_skip = jnp.sum(dy * xc, axis=0, keepdims=True)

    d_u = d_xc * (sx * (1.0 + pre_x * (1.0 - sx)))
    d_ub = jnp.concatenate([d_b, d_c], axis=1) * (sbc * (1.0 + pre_bc * (1.0 - sbc)))
    dubuf[0:length, :] = d_u
    dubbuf[0:length, :] = d_ub
    d_x = jnp.zeros_like(d_u)
    d_bc = jnp.zeros_like(d_ub)
    acc_rows = []
    accbc_rows = []
    for j in range(4):
        d_x = d_x + cx_ref[j : j + 1, :] * dubuf[pl.ds(3 - j, length), :]
        d_bc = d_bc + cbc_ref[j : j + 1, :] * dubbuf[pl.ds(3 - j, length), :]
        acc_rows.append(jnp.sum(d_u * xbuf[pl.ds(5 + j, length), :], axis=0, keepdims=True))
        accbc_rows.append(jnp.sum(d_ub * bbuf[pl.ds(5 + j, length), :], axis=0, keepdims=True))
    dubuf[length:, :] = d_u[0:8, :]
    dubbuf[length:, :] = d_ub[0:8, :]
    zero = jnp.zeros((1, channels), f32)
    acc_ref[...] += jnp.concatenate(
        acc_rows + [jnp.sum(d_u, axis=0, keepdims=True), acc_norm, acc_skip, zero], axis=0
    )
    zero = jnp.zeros((3, d_ub.shape[1]), f32)
    accbc[...] += jnp.concatenate(
        accbc_rows + [jnp.sum(d_ub, axis=0, keepdims=True), zero], axis=0
    )
    dx_b = d_x.astype(bf16)
    dbc_b = d_bc.astype(bf16)
    dxt_ref[:, :channels] = dx_b
    dxt_ref[:, channels:] = dt_b
    put_columns(
        place_ref,
        pl.num_programs(0) - 1 - step_id,
        bcmine_ref,
        bcother_ref,
        jnp.transpose(d_bc).astype(bf16),
    )
    total = dot(jnp.concatenate([dz_b, dx_b], axis=1), w_ref[...], COLS)
    total = total + dot(dbc_b, wbc_ref[...]) + dot(dt_b, wdt_ref[...])
    accn[0:1, :] += jnp.sum(total * xn_ref[...].astype(f32), axis=0, keepdims=True)

    @pl.when(first_span)
    def _():
        lanes = shared_ref.shape[1]
        lines = [accn[0:1, i * lanes : (i + 1) * lanes] for i in range(width // lanes)]
        shared = jnp.concatenate(lines + [accbc[0:5, :]], axis=0)
        shared_ref[0 : shared.shape[0], :] = shared.astype(bf16)
        shared_ref[shared.shape[0] :, :] = jnp.zeros(
            (shared_ref.shape[0] - shared.shape[0], lanes), bf16
        )

    put_half(
        place_ref,
        pl.num_programs(0) - 1 - step_id,
        pl.num_programs(0) // 2,
        mine_ref,
        other_ref,
        total.astype(bf16),
    )


def whole(shape):
    zeros = (0,) * len(shape)
    return pl.BlockSpec(shape, lambda i, p: zeros)


def span_rows(columns):
    return pl.BlockSpec((SPAN, columns), lambda i, p: (i, 0))


def half_rows(columns, spans, reverse):
    half = spans // 2

    def block(i, core):
        span = spans - 1 - i if reverse else i
        return jnp.clip(span - half * core, 0, half - 1), 0

    return [
        pl.BlockSpec((SPAN, columns), lambda i, p: block(i, p[0])),
        pl.BlockSpec((SPAN, columns), lambda i, p: block(i, 1 - p[0])),
    ]


def span_call(kernel, name, spans, place, operands, in_specs, shapes, out_specs, scratch, flops):
    moved = sum(v.size * v.dtype.itemsize for v in [*operands, *shapes])
    return pl.pallas_call(
        kernel,
        grid_spec=pltpu.PrefetchScalarGridSpec(
            num_scalar_prefetch=1,
            grid=(spans,),
            in_specs=in_specs,
            out_specs=out_specs,
            scratch_shapes=scratch,
        ),
        out_shape=shapes,
        compiler_params=pltpu.CompilerParams(
            dimension_semantics=("arbitrary",), vmem_limit_bytes=VMEM_BYTES
        ),
        cost_estimate=pl.CostEstimate(flops=flops, bytes_accessed=moved, transcendentals=0),
        name=name,
    )(place, *operands)


def run_forward(place, gathered, w, wdt, small, state, head_dim):
    w_here, w_there, there_plan = w
    channels = small[0].shape[1]
    width = gathered[0][0][0].shape[1]
    anywhere = pl.BlockSpec(memory_space=pl.ANY)
    tokens = NC * NZ * gathered[0][2][0]
    spans = tokens // SPAN
    last_layer = len(gathered) == 2
    plans = [(cut_plan(*one), len(one[0])) for one in gathered]
    operands = [p for one in gathered for p in one[0]]
    in_specs = [whole(v.shape) for v in operands] + [anywhere] * (1 + len(w_there))
    operands += [w_here, *w_there, wdt, *small]
    in_specs += [whole(v.shape) for v in operands[len(in_specs) :]]
    shapes = [
        jax.ShapeDtypeStruct(w_here.shape, bf16),
        jax.ShapeDtypeStruct((tokens, width), bf16),
        jax.ShapeDtypeStruct((2 * state, width), bf16),
        jax.ShapeDtypeStruct((tokens, channels), bf16),
        jax.ShapeDtypeStruct((tokens, channels), bf16),
        jax.ShapeDtypeStruct((tokens, 2 * state), bf16),
        jax.ShapeDtypeStruct((tokens, LANES), f32),
        jax.ShapeDtypeStruct((tokens, channels), bf16),
        jax.ShapeDtypeStruct((spans, state, channels), f32),
        jax.ShapeDtypeStruct((tokens // 2, width + LANES), bf16),
        jax.ShapeDtypeStruct((tokens // 2, width + LANES), bf16),
    ]
    out_specs = [whole(w_here.shape), span_rows(width), whole((2 * state, width))]
    out_specs += [span_rows(s.shape[1]) for s in shapes[3:8]]
    out_specs.append(pl.BlockSpec((1, state, channels), lambda i, p: (i, 0, 0)))
    out_specs += half_rows(width + LANES, spans, False)
    scratch = [
        pltpu.SemaphoreType.DMA,
        pltpu.VMEM((tokens, width), bf16),
        pltpu.VMEM((SPAN + 8, channels), f32),
        pltpu.VMEM((SPAN + 8, 2 * state), f32),
        pltpu.VMEM((state, channels), f32),
    ]
    if last_layer:
        shapes += [
            jax.ShapeDtypeStruct((tokens, width), bf16),
            jax.ShapeDtypeStruct((8, tokens), f32),
            jax.ShapeDtypeStruct((tokens, channels), f32),
        ]
        out_specs += [span_rows(width), pl.BlockSpec((8, SPAN), lambda i, p: (0, i)), span_rows(channels)]
        scratch.append(pltpu.VMEM((tokens, width), bf16))
    kernel = functools.partial(forward_kernel, plans, there_plan, head_dim)
    return span_call(
        kernel, "layer_forward", spans, place, operands, in_specs, shapes, out_specs, scratch, 20 * 10**9
    )


def run_gate(place, gathered, z, y, w, cx):
    tokens, channels = z.shape
    width = w.shape[0]
    spans = tokens // SPAN
    plan, pieces = cut_plan(*gathered), list(gathered[0])
    operands = [*pieces, z, y, w, cx]
    in_specs = [whole(p.shape) for p in pieces]
    in_specs += [span_rows(channels), span_rows(channels)]
    in_specs += [pl.BlockSpec((width, channels), lambda i, p: (0, 2)), whole(cx.shape)]
    shapes = [
        jax.ShapeDtypeStruct((tokens, width), bf16),
        jax.ShapeDtypeStruct((tokens, channels), bf16),
        jax.ShapeDtypeStruct((tokens, channels), f32),
        jax.ShapeDtypeStruct((tokens, channels), bf16),
        jax.ShapeDtypeStruct((8, channels), f32),
    ]
    out_specs = [span_rows(s.shape[1]) for s in shapes[:4]] + [whole(shapes[4].shape)]
    scratch = [pltpu.VMEM((tokens, pieces[0].shape[1]), bf16)]
    kernel = functools.partial(gate_kernel, plan, len(pieces), width)
    return span_call(
        kernel, "gate_backward", spans, place, operands, in_specs, shapes, out_specs, scratch, 6 * 10**9
    )


def run_scan(place, lead, xn, xp, bc, dt, hin, weights, small, pick, head_dim, inner_all):
    tokens, channels = xp.shape
    state = hin.shape[1]
    width = xn.shape[1]
    spans = tokens // SPAN
    with_gate = len(lead) == 4

    def rev(columns):
        return pl.BlockSpec((SPAN, columns), lambda i, p: (spans - 1 - i, 0))

    def halo(columns, rows):
        per = SPAN // rows
        return pl.BlockSpec(
            (rows, columns), lambda i, p: (jnp.maximum((spans - 1 - i) * per - 1, 0), 0)
        )

    operands = [*lead, xn, xp, xp, bc, bc, dt, hin, *weights, *small, pick]
    in_specs = [rev(channels)] * 2
    if with_gate:
        tok = pl.BlockSpec((8, SPAN), lambda i, p: (0, spans - 1 - i))
        in_specs = [rev(channels), tok, rev(channels), rev(channels)]
    in_specs += [
        rev(width),
        rev(channels),
        halo(channels, 16),
        rev(2 * state),
        halo(2 * state, 16),
        rev(LANES),
        pl.BlockSpec((1, state, channels), lambda i, p: (spans - 1 - i, 0, 0)),
    ]
    in_specs.append(whole((width, 2 * channels)))
    in_specs += [whole(v.shape) for v in operands[len(in_specs) :]]
    shapes = [
        jax.ShapeDtypeStruct((tokens, channels + LANES), bf16),
        jax.ShapeDtypeStruct((state * spans, SPAN), bf16),
        jax.ShapeDtypeStruct((state * spans, SPAN), bf16),
        jax.ShapeDtypeStruct((tokens // 2, width), bf16),
        jax.ShapeDtypeStruct((tokens // 2, width), bf16),
        jax.ShapeDtypeStruct((8, channels), f32),
        jax.ShapeDtypeStruct((8, LANES), f32),
        jax.ShapeDtypeStruct((16, 2 * state), bf16),
    ]
    out_specs = [rev(channels + LANES), whole(shapes[1].shape), whole(shapes[2].shape)]
    out_specs += half_rows(width, spans, True)
    out_specs += [whole(s.shape) for s in shapes[5:]]
    if with_gate:
        shapes = [jax.ShapeDtypeStruct((tokens, channels), bf16)] * 2 + shapes
        out_specs = [rev(channels)] * 2 + out_specs
    scratch = [
        pltpu.VMEM((8, 2 * state), f32),
        pltpu.VMEM((8, width), f32),
        pltpu.VMEM((SPAN + 8, channels), f32),
        pltpu.VMEM((SPAN + 8, 2 * state), f32),
        pltpu.VMEM((SPAN + 8, channels), f32),
        pltpu.VMEM((SPAN + 8, 2 * state), f32),
        pltpu.VMEM((state, channels), f32),
    ]
    kernel = functools.partial(scan_kernel, with_gate, head_dim, inner_all)
    return span_call(
        kernel, "scan_backward", spans, place, operands, in_specs, shapes, out_specs, scratch, 28 * 10**9
    )


def weight_kernel(n_pairs, split, place_ref, *refs):
    lefts, rights, outs = refs[:n_pairs], refs[n_pairs : 2 * n_pairs], refs[2 * n_pairs :]

    def write(out_ref):
        at = 0
        for left_ref, right_ref in zip(lefts, rights):
            columns = right_ref.shape[1]
            out_ref[:, at : at + columns] = dot(left_ref[...], right_ref[...], ROWS).astype(bf16)
            at += columns

    if not split:
        write(outs[0])
        return
    for k, out_ref in enumerate(outs):
        pl.when(pl.program_id(0) == k)(functools.partial(write, out_ref))


def weight_products(place, pairs, split=True):
    tokens = pairs[0][0].shape[0]
    rows = max(left.shape[1] for left, _ in pairs)
    block = rows // 4

    def at(i, p):
        return lax.rem(p[3] + i, NX) if split else i

    lefts, rights, columns = [], [], []
    for left, right in pairs:
        quarter = left.shape[1] == block
        cut, uncut = (lambda i, p: (0, at(i, p))), (lambda i, p: (0, 0))
        lefts.append(pl.BlockSpec((tokens, block), uncut if quarter else cut))
        wide = block if quarter else right.shape[1]
        rights.append(pl.BlockSpec((tokens, wide), cut if quarter else uncut))
        columns.append(wide)
    columns = sum(columns)
    if split:
        out_specs = [whole((block, columns))] * 4
        shapes = [jax.ShapeDtypeStruct((block, columns), bf16)] * 4
    else:
        out_specs = [pl.BlockSpec((block, columns), lambda i, p: (i, 0))]
        shapes = [jax.ShapeDtypeStruct((rows, columns), bf16)]
    out = pl.pallas_call(
        functools.partial(weight_kernel, len(pairs), split),
        grid_spec=pltpu.PrefetchScalarGridSpec(
            num_scalar_prefetch=1, grid=(4,), in_specs=lefts + rights, out_specs=out_specs
        ),
        out_shape=shapes,
        compiler_params=pltpu.CompilerParams(vmem_limit_bytes=VMEM_BYTES),
        cost_estimate=pl.CostEstimate(
            flops=2 * tokens * rows * columns, bytes_accessed=8 * 10**6, transcendentals=0
        ),
        name="weight_products",
    )(place, *[left for left, _ in pairs], *[right for _, right in pairs])
    return out if split else out[0]


SIZES = (4, 2, 2, 2, 4)
NX, NYL, NC, NYH, NZ = SIZES
EVERY = [
    (x, yl, c, yh, z)
    for x in range(NX)
    for yl in range(NYL)
    for c in range(NC)
    for yh in range(NYH)
    for z in range(NZ)
]


def linear(x, yl, c, yh, z):
    return ((((x % NX) * NYL + yl % NYL) * NC + c % NC) * NYH + yh % NYH) * NZ + z % NZ


def send(v, step, only=None):
    pairs = [(linear(*d), linear(*step(*d))) for d in EVERY if only is None or only(*d)]
    return lax.ppermute(v, ("dp", "tensor"), pairs)


def send_z(v, k):
    return send(v, lambda x, yl, c, yh, z: (x, yl, c, yh, z + k))


def send_core(v):
    return send(v, lambda x, yl, c, yh, z: (x, yl, c + 1, yh, z))


def trade(v, k):
    return send(v, lambda x, yl, c, yh, z: (x, yl, yh, c, z + k))


def traded(v):
    return send(v, lambda x, yl, c, yh, z: (x, yl, yh, c, z), lambda x, yl, c, yh, z: c != yh)


def trade_places(v):
    _, _, core, yh, _ = position()
    return jnp.where(core == yh, v, traded(v))


def position():
    dp, tensor = lax.axis_index("dp"), lax.axis_index("tensor")
    return dp // (NYL * NC), dp // NC % NYL, dp % NC, tensor // NZ, tensor % NZ


def gather(v, parts, traded_own=None, later=()):
    arrays, sources = [], []
    for k in (0, 1, 3, 2):
        if traded_own is not None:
            piece = trade(v, k) if k else traded_own
        else:
            piece = send_z(v, k) if k else v
        arrays += [piece, send_core(after(piece, *later) if later else piece)]
        sources += [(False, -k % NZ, 0), (True, -k % NZ, 0)]
    return arrays, sources, parts


def cut_plan(arrays, sources, parts):
    plan = []
    for number, (piece, (other, dz, first)) in enumerate(zip(arrays, sources)):
        base = 0
        for out, per in enumerate(parts):
            begin, end = max(first, base), min(first + piece.shape[0], base + per)
            if begin < end:
                plan.append((number, other, dz, begin - first, out, per, begin - base, end - begin))
            base += per
    return plan


def fold(mine, other):
    _, _, _, _, z = position()
    rows = mine.shape[0] // NZ
    blocks = []
    for k in range(NZ):
        at = (z + k) % NZ * rows
        a = lax.dynamic_slice_in_dim(mine, at, rows, 0).astype(f32)
        blocks.append(a + lax.dynamic_slice_in_dim(other, at, rows, 0).astype(f32))
    return blocks


def fold_beside(pairs):
    folded = [fold(mine, send_core(other)) for mine, other in pairs]
    return [jnp.concatenate([blocks[k] for blocks in folded], axis=1) for k in range(NZ)]


def scatter(*pairs, meanwhile=None):
    own, one, two, three = fold_beside(pairs)
    if meanwhile is not None:
        two = after(two, meanwhile)
    return [own] + [send_z(b.astype(bf16), k) for k, b in ((1, one), (2, two), (3, three))]


def scatter_with_sum(mine, other, shared, meanwhile):
    half = mine.shape[0]
    rows = half // NZ
    got = after(send_core(jnp.concatenate([other, shared], axis=0)), *meanwhile)
    blocks = fold(mine, got[:half])
    total_shared = shared.astype(f32) + got[half:].astype(f32)
    packed = total_shared.astype(bf16)
    total = blocks[0]
    for k in range(1, NZ):
        got = send_z(jnp.concatenate([blocks[k].astype(bf16), packed], axis=0), k)
        total = total + got[:rows].astype(f32)
        total_shared = total_shared + got[rows:].astype(f32)
    return total, total_shared


def sum_members(v):
    both = v + send_core(v)
    total = both
    for k in range(1, NZ):
        total = total + send_z(both, k)
    return total


def send_far(v):
    return send(v, lambda x, yl, c, yh, z: (x, yl, c, yh + 1, z), lambda x, yl, c, yh, z: c != yh)


def sum_far(v, far=None):
    far = send_far(v) if far is None else far
    return (v.astype(f32) + far.astype(f32)).astype(bf16)


def halve(v):
    _, _, core, yh, _ = position()
    half = v.shape[0] // 2
    near = send(
        v[half:], lambda x, yl, c, yh, z: (x, yl, c + 1, yh, z), lambda x, yl, c, yh, z: c == yh
    )
    return jnp.where(core == yh, v[:half], near)


def sum_beside(part):
    beside = send(part, lambda x, yl, c, yh, z: (x, yl + 1, c, yh, z))
    return (part.astype(f32) + beside.astype(f32)).astype(bf16)


def sum_x(blocks):
    total = blocks[0].astype(f32)
    for k in range(1, NX):
        got = send(blocks[k], lambda x, yl, c, yh, z, k=k: (x + k, yl, c, yh, z))
        total = total + got.astype(f32)
    return total.astype(bf16)


def cut_x(v):
    x = position()[0]
    rows = v.shape[0] // NX
    return [lax.dynamic_slice_in_dim(v, (x + k) % NX * rows, rows, 0) for k in range(NX)]


def collect_x(part, meanwhile=()):
    parts = [part]
    for k in range(1, NX):
        got = send(part, lambda x, yl, c, yh, z, k=k: (x + k, yl, c, yh, z))
        parts.append(after(got, *meanwhile) if meanwhile else got)
    return jnp.stack(parts)


def write_kernel(plan, n_kept, place_ref, here_ref, there_ref, *refs):
    rows = here_ref.shape[1]

    def write(ref):
        for (column, kind, wide, by_half), out_ref in zip(plan, refs[n_kept:]):
            for x in range(NX):
                value = ref[lax.rem(place_ref[3] + NX - x, NX), :, column : column + wide].astype(f32)
                if kind != "blocks":
                    out_ref[0, 0 if by_half else x, x if by_half else 0] = value
                elif by_half:
                    at = x // 2 * wide
                    out_ref[0, x % 2 * rows : (x % 2 + 1) * rows, at : at + wide] = value
                else:
                    out_ref[0, :, x * wide : (x + 1) * wide] = value

    here = (pl.program_id(0) == 0) == (place_ref[2] == 1)

    @pl.when(here)
    def _():
        write(here_ref)

    @pl.when(jnp.logical_not(here))
    def _():
        write(there_ref)


def write_sums(place, halves, outputs):
    rows, columns = halves[0].shape[1:]
    total = 2 * NX * rows
    wide = total // 4
    plan, shapes, specs, finals, kept, alias = [], [], [], [], [], {}
    for column, kind, layer, array, by_half in outputs:
        lanes = LANES if kind == "flat" else wide
        layers = 1 if kind == "flat" else 2
        plan.append((column, kind, lanes, by_half))
        if kind == "blocks":
            shape = (layers, wide, total)
            if by_half:
                spec = pl.BlockSpec((1, wide, total // 2), lambda h, p, layer=layer: (layer, 0, h))
            else:
                spec = pl.BlockSpec((1, rows, total), lambda h, p, layer=layer: (layer, h, 0))
            finals.append(shape)
        elif by_half:
            shape = (layers, 2, NX, rows, lanes)
            spec = pl.BlockSpec((1, 1, NX, rows, lanes), lambda h, p, layer=layer: (layer, h, 0, 0, 0))
            finals.append((layers, total, lanes))
        else:
            shape = (layers, NX, 2, rows, lanes)
            spec = pl.BlockSpec((1, NX, 1, rows, lanes), lambda h, p, layer=layer: (layer, 0, h, 0, 0))
            finals.append((layers, total, lanes))
        shapes.append(jax.ShapeDtypeStruct(shape, f32))
        specs.append(spec)
        if array is not None:
            alias[3 + len(kept)] = len(shapes) - 1
            kept.append(array.reshape(shape))
    piece = pl.BlockSpec((NX, rows, columns), lambda h, p: (0, 0, 0))
    written = pl.pallas_call(
        functools.partial(write_kernel, plan, len(kept)),
        grid_spec=pltpu.PrefetchScalarGridSpec(
            num_scalar_prefetch=1,
            grid=(2,),
            in_specs=[piece, piece] + [pl.BlockSpec(memory_space=pl.ANY)] * len(kept),
            out_specs=specs,
        ),
        out_shape=shapes,
        input_output_aliases=alias,
        compiler_params=pltpu.CompilerParams(vmem_limit_bytes=VMEM_BYTES),
        name="write_sums",
    )(place, *halves, *kept)
    return [v.reshape(final) for v, final in zip(written, finals)]


def row_call(kernel, name, operands, shapes):
    return pl.pallas_call(
        kernel,
        grid=(1,),
        in_specs=[pl.BlockSpec((rows, v.shape[1]), lambda i: (0, 0)) for v, rows in operands],
        out_specs=[pl.BlockSpec(s.shape, lambda i, n=len(s.shape): (0,) * n) for s in shapes],
        out_shape=shapes,
        compiler_params=pltpu.CompilerParams(vmem_limit_bytes=VMEM_BYTES),
        name=name,
    )(*[v for v, _ in operands])


def inverse_rms(v):
    return lax.rsqrt(jnp.mean(v * v, axis=-1, keepdims=True) + EPS)


def first_kernel(packed_ref, gain_ref, out_ref):
    rows = 128
    v = packed_ref[0:rows, :].astype(f32)
    out_ref[0:rows, :] = (v * inverse_rms(v) * gain_ref[...]).astype(bf16)
    out_ref[rows:, :] = packed_ref[rows : out_ref.shape[0], :]


def add_terms(own_ref, a_ref, b_ref, c_ref):
    total = own_ref[...].astype(f32) + a_ref[...].astype(f32)
    return total + (b_ref[...].astype(f32) + c_ref[...].astype(f32))


def unscaled_output(inner_all, terms, width):
    total = add_terms(*terms)
    squares = total[:, width : width + 1] + total[:, width + 1 : width + 2]
    gate_rms = lax.rsqrt(squares / inner_all + EPS)
    return gate_rms, total[:, :width] * gate_rms


def middle_kernel(inner_all, own_ref, a_ref, b_ref, c_ref, res_ref, gain_ref, res1_ref, mixed_ref, rms_ref, normed_ref):
    width = res_ref.shape[1]
    gate_rms, mixed = unscaled_output(inner_all, (own_ref, a_ref, b_ref, c_ref), width)
    res = res_ref[...].astype(f32) + mixed
    res1_ref[...] = res
    mixed_ref[...] = mixed
    rms_ref[...] = jnp.broadcast_to(gate_rms, rms_ref.shape)
    normed_ref[...] = (res * inverse_rms(res) * gain_ref[...]).astype(bf16)


def input_gradient(grad_normed, res, d_res, gain):
    inv = inverse_rms(res)
    scaled = grad_normed * gain
    dots = jnp.sum(scaled * res, axis=-1, keepdims=True) / res.shape[1]
    return d_res + inv * scaled - res * (inv * inv * inv) * dots


def between_kernel(inner_all, own_ref, a_ref, b_ref, c_ref, res_ref, dres_ref, gain_ref, mixed_ref, rms_ref, out_ref, sent_ref):
    width = res_ref.shape[1]
    grad_normed = add_terms(*(ref.at[:, 0:width] for ref in (own_ref, a_ref, b_ref, c_ref)))
    d_res = input_gradient(grad_normed, res_ref[...], dres_ref[...].astype(f32), gain_ref[...])
    out_ref[...] = d_res
    g_mixed = d_res.astype(bf16)
    sent_ref[:, :width] = g_mixed
    gate_rms = rms_ref[:, 0:1]
    products = jnp.sum(g_mixed.astype(f32) * mixed_ref[...], axis=-1, keepdims=True)
    coef = gate_rms * gate_rms * products / inner_all
    lane = lax.broadcasted_iota(jnp.int32, rms_ref.shape, 1)
    rms_high = gate_rms.astype(bf16).astype(f32)
    coef_high = coef.astype(bf16).astype(f32)
    extra = jnp.where(lane == 0, rms_high, jnp.where(lane == 1, gate_rms - rms_high, 0.0))
    extra = jnp.where(lane == 2, coef_high, jnp.where(lane == 3, coef - coef_high, extra))
    sent_ref[:, width:] = extra.astype(bf16)


def end_kernel(own_ref, a_ref, b_ref, c_ref, res_ref, dres_ref, gain_ref, hidden_ref, out_ref):
    width = res_ref.shape[1]
    grad_normed = add_terms(own_ref, a_ref, b_ref, c_ref)
    grad = input_gradient(grad_normed, res_ref[...].astype(f32), dres_ref[...], gain_ref[...])
    out_ref[:, :width] = hidden_ref[...]
    out_ref[:, width:] = grad.astype(bf16)


def last_kernel(inner_all, own_ref, a_ref, b_ref, c_ref, res_ref, out_ref):
    _, mixed = unscaled_output(inner_all, (own_ref, a_ref, b_ref, c_ref), res_ref.shape[1])
    out_ref[...] = (res_ref[...] + mixed).astype(bf16)


TINY_ROWS = 56


def small_kernel(head_dim, ends, narrow0_ref, narrow1_ref, gain_ref, pick_ref, norm_ref, wbc_ref, wdt_ref, cx_ref,
                 cxb_ref, cbc_ref, cbcb_ref, dtb_ref, alog_ref, skip_ref, ng_ref):
    bc_at, tiny_at = ends
    heads = wdt_ref.shape[2]
    channels = cx_ref.shape[2]
    both = cbc_ref.shape[2]
    lanes = narrow0_ref.shape[1] - tiny_at
    for layer, ref in enumerate((narrow0_ref, narrow1_ref)):
        wbc_ref[layer] = ref[:, bc_at:tiny_at]
        wdt_ref[layer] = ref[:, 0:heads]
    tiny = jnp.concatenate(
        [narrow0_ref[i * TINY_ROWS : (i + 1) * TINY_ROWS, tiny_at:] for i in range(channels // lanes)], axis=1
    )
    lines = norm_ref.shape[1] // both
    for layer in range(2):
        rows = tiny[8 * layer : 8 * layer + 8]
        cx_ref[layer] = rows[0:4]
        cxb_ref[layer : layer + 1, :] = rows[4:5]
        ng_ref[layer : layer + 1, :] = rows[5:6]
        skip_ref[layer : layer + 1, :] = dot(rows, pick_ref[...], PLAIN, highest)[6:7, 0:heads]
        at = 16 + 2 * layer
        dtb_ref[layer : layer + 1, :] = tiny[at : at + 1, 0:heads]
        alog_ref[layer : layer + 1, :] = tiny[at + 1 : at + 2, 0:heads]
        at = 20 + 16 * layer
        norm = jnp.concatenate([tiny[at + i : at + i + 1, 0:both] for i in range(lines)], axis=1)
        norm_ref[layer : layer + 1, :] = norm / gain_ref[layer : layer + 1, :]
        cbc_ref[layer] = tiny[at + lines : at + lines + 4, 0:both]
        cbcb_ref[layer : layer + 1, :] = tiny[at + lines + 4 : at + lines + 5, 0:both]


def after(v, *others):
    return lax.optimization_barrier((v, *others))[0]


def pad_to(v, rows, lanes):
    return jnp.pad(v, ((0, rows - v.shape[0]), (0, lanes - v.shape[1])))


def local(
    hidden_in,
    grad_out,
    norm_in,
    w_z,
    w_x,
    w_bc,
    w_dt,
    conv_x,
    conv_x_bias,
    conv_bc,
    conv_bc_bias,
    dt_bias,
    a_log,
    skip,
    norm_gate,
    w_out,
):
    layers, width, channels = w_z.shape
    heads = w_dt.shape[2]
    head_dim = channels // heads
    both = conv_bc.shape[2]
    state = both // 2
    members = NC * NZ
    inner_all = channels * members
    rows = hidden_in.shape[1]
    bc_rows = both // members
    x, _, core, yh, z = position()
    stays = core == yh
    place = jnp.stack([core, z, stays, x]).astype(jnp.int32)
    full = jax.ShapeDtypeStruct((rows, width), f32)

    def pack_weights(layer):
        return jnp.concatenate([w_z[layer], w_x[layer], w_out[layer].T], axis=1)

    bc_t = jnp.swapaxes(w_bc, 1, 2)
    dt_t = jnp.pad(jnp.swapaxes(w_dt, 1, 2), ((0, 0), (0, 8 - heads), (0, 0)))
    per_channel = jnp.concatenate(
        [conv_x, conv_x_bias[:, None], norm_gate[:, None], jnp.repeat(skip, head_dim, axis=1)[:, None]],
        axis=1,
    )
    per_channel = jnp.pad(per_channel, ((0, 0), (0, 1), (0, 0)))
    per_head = jnp.stack([dt_bias, -jnp.exp(a_log)], axis=1)
    per_head = jnp.pad(per_head, ((0, 0), (0, 6), (0, LANES - heads)))
    little = jnp.concatenate([per_channel, per_head], axis=2).reshape(layers * 8, channels + LANES)
    high = little.astype(bf16)
    low = (little - high.astype(f32)).astype(bf16)
    lines = pad_to(jnp.concatenate([high, low], axis=1), layers * 8, width)
    packed = jnp.concatenate([hidden_in[0], bc_t[0], dt_t.reshape(layers * 8, width), lines], axis=0)
    packed = trade_places(packed)
    lines = packed[packed.shape[0] - layers * 8 :].astype(f32)
    little = lines[:, : channels + LANES] + lines[:, channels + LANES : 2 * (channels + LANES)]
    little = little.reshape(layers, 8, channels + LANES)

    w0 = pack_weights(0)
    w0 = w0, [traded(after(w0, packed))], [(0, None)]
    grads = jnp.concatenate([grad_out[0], bc_t[1]], axis=0)

    [sent] = row_call(
        first_kernel,
        "first_norm",
        [(packed, packed.shape[0]), (norm_in[0:1], 1)],
        [jax.ShapeDtypeStruct((rows + bc_rows, width), bf16)],
    )
    gathered0 = gather(sent, (rows, bc_rows))
    wdt = [pad_to(packed[rows + bc_rows + 8 * l : rows + bc_rows + 8 * (l + 1)], LANES, width) for l in range(layers)]
    smalls = []
    for layer in range(layers):
        cbc = jnp.concatenate([conv_bc[layer], conv_bc_bias[layer][None], jnp.zeros((3, both), f32)], axis=0)
        smalls.append((little[layer, :, :channels], cbc, little[layer, :, channels:]))
    channel_head = jnp.arange(channels) // head_dim
    pick = (channel_head[:, None] == jnp.arange(LANES)[None, :]).astype(f32)

    out0 = run_forward(place, [gathered0], w0, wdt[0], smalls[0], state, head_dim)
    w0, xn0, wbc0, z0, xp0, bc0, dt0, y0, hin0, mine, other = out0
    grads = after(grads, sent)
    gathered_grad = gather(grads, (rows, bc_rows), jnp.where(stays, grads, after(traded(grads), mine)), (mine,))
    grad_held = gathered_grad[0][0]
    terms = scatter((mine, after(other, *gathered_grad[0][::2])))
    w1 = pack_weights(1)
    w1 = w1, [traded(after(w1, terms[0]))], [(0, None)]
    res1, mixed0, rms0, normed1 = row_call(
        functools.partial(middle_kernel, inner_all),
        "middle_norm",
        [(v, rows) for v in terms] + [(packed, rows), (norm_in[1:2], 1)],
        [full, full, jax.ShapeDtypeStruct((rows, LANES), f32), jax.ShapeDtypeStruct((rows, width), bf16)],
    )
    gathered1 = gather(normed1, (rows,))
    out1 = run_forward(
        place, [gathered1, gathered_grad], w1, wdt[1], smalls[1], state, head_dim
    )
    w1, xn1, wbc1, z1, xp1, bc1, dt1, y1, hin1, mine, other, grad_rows1, sums, gg1 = out1
    sums = sum_members(sums)

    home = fold(mine, send_core(other))
    sums = after(sums, *home)
    home = home[:1] + [send_z(home[k].astype(bf16), k) for k in range(1, NZ)]
    back1 = run_scan(
        place, (gg1, sums, z1, y1), xn1, xp1, bc1, dt1, hin1, (w1, wbc1, wdt[1]), smalls[1], pick, head_dim,
        inner_all,
    )
    dz1, go1, dxt1, *bc_halves, mine, other, acc1, acch1, shared1 = back1
    early1 = weight_products(place, [(xn1, dz1), (go1, grad_rows1)], split=False)
    terms = scatter((mine, after(other, *home)), bc_halves, meanwhile=early1)
    early1_far = send_far(early1)
    [hidden_out] = row_call(
        functools.partial(last_kernel, inner_all),
        "last_output",
        [(after(home[0], terms[1]), rows)] + [(v, rows) for v in home[1:]] + [(res1, rows)],
        [jax.ShapeDtypeStruct((rows, width), bf16)],
    )
    d_res1, sent = row_call(
        functools.partial(between_kernel, inner_all),
        "between_layers",
        [(v, rows) for v in terms]
        + [(res1, rows), (grad_held, rows), (norm_in[1:2], 1), (mixed0, rows), (rms0, rows)],
        [full, jax.ShapeDtypeStruct((rows, width + LANES), bf16)],
    )
    gathered_back = gather(sent, (rows,))

    bc_at = channels + bc_rows

    def with_bc(dxt, bc_sum):
        by_token = bc_sum.reshape(-1, bc_rows, SPAN).swapaxes(1, 2).reshape(-1, bc_rows)
        spread = jnp.pad(by_token, ((0, 0), (bc_at, dxt.shape[1] - bc_at - bc_rows)))
        return dxt + spread.astype(bf16)

    dxt1 = with_bc(dxt1, sum(v[:, width:].astype(f32) for v in terms))

    early1 = halve(sum_far(early1, after(early1_far, sent)))
    z0 = after(z0, early1)
    early1 = sum_x(cut_x(early1))
    grad_rows0, dz0, dy0, go0, acc_gate0 = run_gate(place, gathered_back, z0, y0, w0, smalls[0][0])
    dz0 = after(dz0, early1)
    early = weight_products(place, [(xn0, dz0), (go0, grad_rows0), (xn1, dxt1)])
    dy0 = after(dy0, *early)
    early = sum_x(early)
    early1 = sum_beside(after(early1, dz0))
    back0 = run_scan(
        place, (dy0, dz0), xn0, xp0, bc0, dt0, hin0, (w0, wbc0, wdt[0]), smalls[0], pick, head_dim, inner_all
    )
    dxt0, *bc_halves, mine, other, acc0, acch0, shared0 = back0
    shared = jnp.concatenate([shared0, shared1], axis=0)
    bc_sum, shared = scatter_with_sum(*bc_halves, shared, (early,))
    tiny_at = bc_at + bc_rows
    tiny_lanes = channels + LANES - tiny_at
    tiny = jnp.concatenate(
        [acc0 + acc_gate0, acc1] + [pad_to(v, v.shape[0], channels) for v in (acch0[0:2], acch1[0:2], shared)],
        axis=0,
    )
    tiny = pad_to(tiny, TINY_ROWS, channels)
    tiny = [tiny[:, i * tiny_lanes : (i + 1) * tiny_lanes] for i in range(channels // tiny_lanes)]
    tiny = pad_to(jnp.concatenate(tiny, axis=0), width, tiny_lanes)
    tiny = jnp.pad(tiny, ((0, 0), (tiny_at, 0))).astype(bf16)
    early = sum_beside(halve(sum_far(after(early, dxt0))))
    home = fold(mine, send_core(other))
    late = weight_products(place, [(xn0, after(with_bc(dxt0, bc_sum), early, home[0]))])
    early = collect_x(jnp.concatenate([early, early1], axis=1), (late[0],))
    tiny = after(tiny, early)
    late = [v + t for v, t in zip(late, cut_x(tiny))]
    terms = home[:1] + [send_z(home[k].astype(bf16), k) for k in range(1, NZ)]
    [outputs] = row_call(
        end_kernel,
        "outputs",
        [(v, rows) for v in terms] + [(packed, rows), (d_res1, rows), (norm_in[0:1], 1), (hidden_out, rows)],
        [jax.ShapeDtypeStruct((rows, 2 * width), bf16)],
    )
    outputs_home = trade_places(outputs).astype(f32)

    late = sum_x(late)
    early = early, send_core(early)
    at1 = 3 * channels + LANES
    g_wz, g_wo, g_wx, narrow1 = write_sums(
        place,
        early,
        [
            (0, "rows", 0, None, False),
            (channels, "blocks", 0, None, False),
            (2 * channels, "rows", 1, None, False),
            (3 * channels, "flat", 0, None, False),
        ],
    )
    g_wz, g_wo = write_sums(
        place, early, [(at1, "rows", 1, g_wz, True), (at1 + channels, "blocks", 1, g_wo, True)]
    )
    late = collect_x(sum_beside(halve(sum_far(after(late, outputs)))), (g_wz,))
    late = late, send_core(late)
    g_wx, narrow0 = write_sums(
        place, late, [(0, "rows", 0, g_wx, False), (channels, "flat", 0, None, False)]
    )

    narrow0, narrow1 = narrow0[0], narrow1[0]
    small = row_call(
        functools.partial(small_kernel, head_dim, (bc_at - channels, tiny_at - channels)),
        "small_gradients",
        [(narrow0, width), (narrow1, width), (norm_in, layers), (pick, channels)],
        [
            jax.ShapeDtypeStruct(shape, f32)
            for shape in (
                norm_in.shape,
                w_bc.shape,
                w_dt.shape,
                conv_x.shape,
                conv_x_bias.shape,
                conv_bc.shape,
                conv_bc_bias.shape,
                dt_bias.shape,
                a_log.shape,
                skip.shape,
                norm_gate.shape,
            )
        ],
    )
    return (
        outputs_home[None, :, :width],
        outputs_home[None, :, width:],
        small[0],
        g_wz,
        g_wx,
        *small[1:],
        g_wo,
    )


def solution(mesh):
    specs_in = (
        P("dp", "tensor", None),
        P("dp", "tensor", None),
        P(),
        P(None, None, "tensor"),
        P(None, None, "tensor"),
        P(None, None, "tensor"),
        P(None, None, "tensor"),
        P(None, None, "tensor"),
        P(None, "tensor"),
        P(),
        P(),
        P(None, "tensor"),
        P(None, "tensor"),
        P(None, "tensor"),
        P(None, "tensor"),
        P(None, "tensor", None),
    )
    specs_out = (
        P("dp", "tensor", None),
        P("dp", "tensor", None),
        P(),
        P(None, None, "tensor"),
        P(None, None, "tensor"),
        P(None, None, "tensor"),
        P(None, None, "tensor"),
        P(None, None, "tensor"),
        P(None, "tensor"),
        P(),
        P(),
        P(None, "tensor"),
        P(None, "tensor"),
        P(None, "tensor"),
        P(None, "tensor"),
        P(None, "tensor", None),
    )
    return jax.shard_map(
        local, mesh=mesh, in_specs=specs_in, out_specs=specs_out, check_vma=False
    )
```

```python
import functools

import jax
import jax.numpy as jnp
from jax import lax
from jax.experimental import pallas as pl
from jax.experimental.pallas import tpu as pltpu
from jax.sharding import PartitionSpec as P

SPAN = 256
EPS = 1e-05
LANES = 128
VMEM_BYTES = 56 * 1024 * 1024

f32 = jnp.float32
bf16 = jnp.bfloat16
highest = lax.Precision.HIGHEST

ROWS = ((0,), (0,))
COLS = ((1,), (1,))
PLAIN = ((1,), (0,))


def dot(left, right, dims=PLAIN, precision=None):
    return lax.dot_general(
        left, right, (dims, ((), ())), preferred_element_type=f32, precision=precision
    )


def sigmoid(v):
    return 0.5 + 0.5 * jnp.tanh(0.5 * v)


def dot_exact(left, right, dims=PLAIN, terms=3):
    parts = []
    for _ in range(terms):
        parts.append(right.astype(bf16))
        right = right - parts[-1].astype(f32)
    out = dot(left.astype(bf16), jnp.concatenate(parts, axis=1), dims)
    width = out.shape[1] // terms
    return sum(out[:, i * width : (i + 1) * width] for i in range(terms))


def sum_heads(v, pick):
    high = v.astype(bf16)
    low = (v - high.astype(f32)).astype(bf16)
    return dot(high, pick) + dot(low, pick)


def softplus(v):
    return jnp.maximum(v, 0.0) + jnp.log1p(jnp.exp(-jnp.abs(v)))


def spread_heads(per_head, channels, head_dim):
    rows = per_head.shape[0]
    per_tile = LANES // head_dim
    lane = lax.broadcasted_iota(jnp.int32, (rows, LANES), 1)
    tiles = []
    for tile in range(channels // LANES):
        out = jnp.broadcast_to(
            per_head[:, tile * per_tile : tile * per_tile + 1], (rows, LANES)
        )
        for sub in range(1, per_tile):
            head = tile * per_tile + sub
            out = jnp.where(
                lane >= sub * head_dim,
                jnp.broadcast_to(per_head[:, head : head + 1], (rows, LANES)),
                out,
            )
        tiles.append(out)
    return jnp.concatenate(tiles, axis=1)


def conv_taps(buf, taps, offset, width):
    out = offset
    for j in range(4):
        out = out + taps[j : j + 1] * buf[pl.ds(5 + j, width), :]
    return out


def decay_matrix(mask, cum_col, cum_row):
    return jnp.exp(jnp.where(mask, cum_col - cum_row, -1e30))


def span_values(dt, head_ref):
    length = dt.shape[0]
    rows = lax.broadcasted_iota(jnp.int32, (length, length), 0)
    cols = lax.broadcasted_iota(jnp.int32, (length, length), 1)
    mask = rows >= cols
    pre = dt + head_ref[0:1, :]
    step = softplus(pre)
    rate = head_ref[1:2, :] * step
    cum = dot_exact(mask, rate)
    return mask, pre, step, rate, cum


def put_half(place_ref, span, half, mine_ref, other_ref, value):
    own = span // half == place_ref[0]

    @pl.when(own)
    def _():
        mine_ref[...] = value

    @pl.when(jnp.logical_not(own))
    def _():
        other_ref[...] = value


def place_pieces(plan, place_ref, pieces, outs):
    core, z = place_ref[0], place_ref[1]
    for piece, other, dz, start, out, per, offset, rows in plan:
        member = (1 - core if other else core) * NZ + lax.rem(z + dz, NZ)
        row = pl.multiple_of(member * per + offset, 16)
        outs[out][pl.ds(row, rows), :] = pieces[piece][start : start + rows, :]


def put_columns(place_ref, span, mine_ref, other_ref, columns):
    per = columns.shape[0] // (NC * NZ)
    rows = mine_ref.shape[0] // NZ

    def place_columns(core, ref):
        for z in range(NZ):
            at = (core * NZ + z) * per
            ref[pl.ds(pl.multiple_of(z * rows + span * per, 16), per), :] = columns[at : at + per, :]

    for core in range(NC):
        mine = place_ref[0] == core

        @pl.when(mine)
        def _(core=core):
            place_columns(core, mine_ref)

        @pl.when(jnp.logical_not(mine))
        def _(core=core):
            place_columns(core, other_ref)


def forward_kernel(plans, there_plan, head_dim, place_ref, *refs):
    last_layer = len(plans) == 2
    refs = list(refs)

    def take(count):
        taken = refs[:count]
        del refs[:count]
        return taken

    piece_refs = [take(count) for _, count in plans]
    [w_here] = take(1)
    w_there = take(len(there_plan))
    wdt_ref, cx_ref, cbc_ref, head_ref = take(4)
    w_ref, xn_ref, wbc_ref, z_ref, xp_ref, bc_ref, dt_ref, y_ref, hin_ref, mine_ref, other_ref = take(11)
    if last_layer:
        g_ref, sums_ref, gg_ref = take(3)
    w_sem, xn_all, xbuf, bbuf, hst = take(5)
    if last_layer:
        [g_all] = take(1)
    length = z_ref.shape[0]
    channels = cx_ref.shape[1]
    state = hst.shape[0]
    span = pl.program_id(0)

    @pl.when(span == 0)
    def _():
        @pl.when(place_ref[2] == 1)
        def _():
            pltpu.make_async_copy(w_here, w_ref, w_sem).start()

        @pl.when(place_ref[2] == 0)
        def _():
            for part, (start, k) in zip(w_there, there_plan):
                rows = part.shape[0]
                if k is not None:
                    start = pl.multiple_of(lax.rem(place_ref[3] + NX - k, NX) * rows, 16)
                pltpu.make_async_copy(part, w_ref.at[pl.ds(start, rows), :], w_sem).start()

        if last_layer:
            place_pieces(plans[0][0], place_ref, piece_refs[0], [xn_all])
            place_pieces(plans[1][0], place_ref, piece_refs[1], [g_all, wbc_ref])
        else:
            place_pieces(plans[0][0], place_ref, piece_refs[0], [xn_all, wbc_ref])
        xbuf[0:8, :] = jnp.zeros((8, channels), f32)
        bbuf[0:8, :] = jnp.zeros((8, 2 * state), f32)
        hst[...] = jnp.zeros_like(hst)
        pltpu.make_async_copy(w_here, w_ref, w_sem).wait()

    here = pl.ds(pl.multiple_of(span * length, length), length)
    xn = xn_all[here, :]
    xn_ref[...] = xn
    zx = dot(xn, w_ref[:, : 2 * channels])
    z = zx[:, :channels]
    z_ref[...] = z.astype(bf16)
    xp = zx[:, channels:]
    xp_ref[...] = xp.astype(bf16)
    xbuf[8:, :] = xp
    bc = dot(xn, wbc_ref[...], COLS).astype(bf16)
    bc_ref[...] = bc
    bbuf[8:, :] = bc.astype(f32)
    dt = dot(xn, wdt_ref[...], COLS)
    dt_ref[...] = dt

    pre_x = conv_taps(xbuf, cx_ref[0:4, :], cx_ref[4:5, :], length)
    xc = pre_x * sigmoid(pre_x)
    pre_bc = conv_taps(bbuf, cbc_ref[0:4, :], cbc_ref[4:5, :], length)
    bcc = (pre_bc * sigmoid(pre_bc)).astype(bf16)
    xbuf[0:8, :] = xbuf[length : length + 8, :]
    bbuf[0:8, :] = bbuf[length : length + 8, :]
    b_mat = bcc[:, :state]
    c_mat = bcc[:, state:]

    mask, _, step, _, cum = span_values(dt, head_ref)
    cum_t = jnp.transpose(cum)
    scores = dot(c_mat, b_mat, COLS)
    xs = xc * spread_heads(step, channels, head_dim)
    xs_b = xs.astype(bf16)
    lane = lax.broadcasted_iota(jnp.int32, (length, LANES), 1)
    per_tile = LANES // head_dim
    tiles = []
    for tile in range(channels // LANES):
        xs_tile = xs_b[:, tile * LANES : (tile + 1) * LANES]
        out = None
        for sub in range(per_tile):
            head = tile * per_tile + sub
            decay = decay_matrix(mask, cum[:, head : head + 1], cum_t[head : head + 1, :])
            part = dot((scores * decay).astype(bf16), xs_tile)
            out = part if out is None else jnp.where(lane >= sub * head_dim, part, out)
        tiles.append(out)
    hin = hst[...]
    hin_ref[0] = hin
    last = cum[length - 1 : length, :]
    y = jnp.concatenate(tiles, axis=1)
    y = y + dot(c_mat, hin.astype(bf16)) * spread_heads(jnp.exp(cum), channels, head_dim)
    y = y + cx_ref[6:7, :] * xc
    y_ref[...] = y.astype(bf16)
    tail = spread_heads(jnp.exp(last - cum), channels, head_dim)
    keep = spread_heads(jnp.exp(last), channels, head_dim)
    hst[...] = keep * hin + dot(b_mat, (tail * xs).astype(bf16), ROWS)

    gated = y * (z * sigmoid(z))
    scaled = gated * cx_ref[5:6, :]
    squares = jnp.sum(gated * gated, axis=1, keepdims=True)
    high = squares.astype(bf16).astype(f32)
    extra = jnp.where(lane == 0, high, jnp.where(lane == 1, squares - high, 0.0)).astype(bf16)
    mixed = dot(scaled.astype(bf16), w_ref[:, 2 * channels :], COLS).astype(bf16)
    put_half(
        place_ref,
        span,
        pl.num_programs(0) // 2,
        mine_ref,
        other_ref,
        jnp.concatenate([mixed, extra], axis=1),
    )
    if last_layer:
        g = g_all[here, :]
        g_ref[...] = g
        gg = dot(g, w_ref[:, 2 * channels :])
        gg_ref[...] = gg
        products = jnp.sum(gg * scaled, axis=1, keepdims=True)
        both = jnp.where(lane == 0, squares, jnp.where(lane == 1, products, 0.0))
        sums_ref[...] = jnp.transpose(both)[0:8, :]


def gate_part(gg, rms, coef, z, y, cx_ref):
    z, y = z.astype(f32), y.astype(f32)
    norm_gate = cx_ref[5:6, :]
    sz = sigmoid(z)
    silu_z = z * sz
    gated = y * silu_z
    rg = rms * gg
    gate_out = (gated * rms * norm_gate).astype(bf16)
    d_gated = rg * norm_gate - gated * coef
    dz = (d_gated * y * (sz * (1.0 + z * (1.0 - sz)))).astype(bf16)
    return dz, d_gated * silu_z, gate_out, jnp.sum(rg * gated, axis=0, keepdims=True)


def gate_kernel(plan, n_pieces, width, place_ref, *refs):
    pieces = refs[:n_pieces]
    z_ref, y_ref, wo_ref, cx_ref, g_ref, dz_ref, dy_ref, go_ref, acc_ref, first_all = refs[n_pieces:]
    length = z_ref.shape[0]
    span = pl.program_id(0)

    @pl.when(span == 0)
    def _():
        place_pieces(plan, place_ref, pieces, [first_all])
        acc_ref[...] = jnp.zeros_like(acc_ref)

    first = first_all[pl.ds(pl.multiple_of(span * length, length), length), :]
    g = first[:, :width]
    g_ref[...] = g
    tok = first[:, width:].astype(f32)
    rms = tok[:, 0:1] + tok[:, 1:2]
    coef = tok[:, 2:3] + tok[:, 3:4]
    gg = dot(g, wo_ref[...])
    dz, dy, gate_out, acc_norm = gate_part(gg, rms, coef, z_ref[...], y_ref[...], cx_ref)
    dz_ref[...] = dz
    dy_ref[...] = dy
    go_ref[...] = gate_out
    acc_ref[5:6, :] += acc_norm


def scan_kernel(with_gate, head_dim, inner_all, place_ref, *refs):
    if with_gate:
        (gg_ref, tok_ref, z_ref, y_ref), refs = refs[:4], refs[4:]
    else:
        (dy_ref, dz_ref), refs = refs[:2], refs[2:]
    (xn_ref, xp_ref, xhalo_ref, bc_ref, bchalo_ref, dt_ref, hin_ref,
     w_ref, wbc_ref, wdt_ref, cx_ref, cbc_ref, head_ref, pick_ref), refs = refs[:14], refs[14:]
    if with_gate:
        (dz_ref, go_ref), refs = refs[:2], refs[2:]
    (dxt_ref, bcmine_ref, bcother_ref, mine_ref, other_ref, acc_ref, acch_ref, shared_ref,
     accbc, accn, xbuf, bbuf, dubuf, dubbuf, dhst) = refs
    length = xp_ref.shape[0]
    channels = cx_ref.shape[1]
    width = xn_ref.shape[1]
    state = dhst.shape[0]
    step_id = pl.program_id(0)
    first_span = step_id == pl.num_programs(0) - 1

    @pl.when(step_id == 0)
    def _():
        dubuf[length:, :] = jnp.zeros((8, channels), f32)
        dubbuf[length:, :] = jnp.zeros((8, 2 * state), f32)
        dhst[...] = jnp.zeros_like(dhst)
        accn[...] = jnp.zeros_like(accn)
        acc_ref[...] = jnp.zeros_like(acc_ref)
        accbc[...] = jnp.zeros_like(accbc)
        acch_ref[...] = jnp.zeros_like(acch_ref)

    @pl.when(first_span)
    def _():
        xbuf[0:8, :] = jnp.zeros((8, channels), f32)
        bbuf[0:8, :] = jnp.zeros((8, 2 * state), f32)

    @pl.when(jnp.logical_not(first_span))
    def _():
        xbuf[0:8, :] = xhalo_ref[...].astype(f32)[8:16, :]
        bbuf[0:8, :] = bchalo_ref[...].astype(f32)[8:16, :]

    xbuf[8:, :] = xp_ref[...].astype(f32)
    bbuf[8:, :] = bc_ref[...].astype(f32)
    if with_gate:
        tok = jnp.transpose(tok_ref[...])
        rms = lax.rsqrt(tok[:, 0:1] / inner_all + EPS)
        coef = rms * rms * rms * tok[:, 1:2] / inner_all
        dz_b, dy, gate_out, acc_norm = gate_part(
            gg_ref[...], rms, coef, z_ref[...], y_ref[...], cx_ref
        )
        dz_ref[...] = dz_b
        go_ref[...] = gate_out
    else:
        dz_b, dy = dz_ref[...], dy_ref[...]
        acc_norm = jnp.zeros((1, channels), f32)
    skip = cx_ref[6:7, :]

    pre_x = conv_taps(xbuf, cx_ref[0:4, :], cx_ref[4:5, :], length)
    sx = sigmoid(pre_x)
    xc = pre_x * sx
    pre_bc = conv_taps(bbuf, cbc_ref[0:4, :], cbc_ref[4:5, :], length)
    sbc = sigmoid(pre_bc)
    bcc = (pre_bc * sbc).astype(bf16)
    b_mat = bcc[:, :state]
    c_mat = bcc[:, state:]
    mask, pre_dt, step, rate, cum = span_values(dt_ref[...], head_ref)
    cum_t = jnp.transpose(cum)
    last = cum[length - 1 : length, :]
    scores = dot(c_mat, b_mat, COLS)
    step_all = spread_heads(step, channels, head_dim)
    xs = xc * step_all
    xs_b = xs.astype(bf16)
    tail = spread_heads(jnp.exp(last - cum), channels, head_dim)
    keep = spread_heads(jnp.exp(last), channels, head_dim)

    hin = hin_ref[0]
    hin_b = hin.astype(bf16)
    dh = dhst[...]
    dh_b = dh.astype(bf16)
    dye = dy * spread_heads(jnp.exp(cum), channels, head_dim)
    dye_b = dye.astype(bf16)
    txs = tail * xs
    txs_b = txs.astype(bf16)
    carried = dot(c_mat, hin_b)
    pulled = dot(b_mat, dh_b)
    d_c = dot(dye_b, hin_b, COLS)
    d_b = dot(txs_b, dh_b, COLS)
    dhst[...] = keep * dh + dot(c_mat, dye_b, ROWS)
    into = txs * pulled
    across = dye * carried - into
    at_last = jnp.sum(into, axis=0, keepdims=True) + keep * jnp.sum(hin * dh, axis=0, keepdims=True)

    dy_b = dy.astype(bf16)
    dy_t = jnp.transpose(dy).astype(bf16)
    lane = lax.broadcasted_iota(jnp.int32, (length, LANES), 1)
    per_tile = LANES // head_dim
    d_scores = jnp.zeros((length, length), f32)
    row_sums = jnp.zeros((length, LANES), f32)
    col_sums = []
    dxs_parts = []
    for head in range(channels // head_dim):
        tile, sub = divmod(head, per_tile)
        dy_tile = dy_b[:, tile * LANES : (tile + 1) * LANES]
        own = (lane >= sub * head_dim) & (lane < (sub + 1) * head_dim)
        dy_head = jnp.where(own, dy_tile, jnp.zeros_like(dy_tile))
        d_m = dot(dy_head, xs_b[:, tile * LANES : (tile + 1) * LANES], COLS)
        decay = decay_matrix(mask, cum[:, head : head + 1], cum_t[head : head + 1, :])
        dxs_parts.append(
            dot(dy_t[head * head_dim : (head + 1) * head_dim, :], (scores * decay).astype(bf16))
        )
        d_m = d_m * decay
        d_scores = d_scores + d_m
        pairs = d_m * scores
        row_sums = jnp.where(lane == head, jnp.sum(pairs, axis=1, keepdims=True), row_sums)
        col_sums.append(jnp.sum(pairs, axis=0, keepdims=True))
    heads = len(col_sums)
    col_sums = jnp.concatenate(col_sums + [jnp.zeros((LANES - heads, length), f32)], axis=0)
    dxs = jnp.transpose(jnp.concatenate(dxs_parts, axis=0)) + tail * pulled
    pick = pick_ref[...].astype(bf16)
    d_cum = row_sums - jnp.transpose(col_sums) + sum_heads(across, pick)
    at_last = sum_heads(jnp.broadcast_to(at_last, (16, channels)), pick)[0:1, :]
    d_rate = dot_exact(mask, d_cum, ROWS) + at_last
    d_step = d_rate * head_ref[1:2, :] + sum_heads(dxs * xc, pick)
    d_dt = d_step * sigmoid(pre_dt)
    acch_ref[0:1, :] += jnp.sum(d_dt, axis=0, keepdims=True)
    acch_ref[1:2, :] += jnp.sum(d_rate * rate, axis=0, keepdims=True)
    dt_b = d_dt.astype(bf16)
    ds_b = d_scores.astype(bf16)
    d_c = d_c + dot(ds_b, b_mat)
    d_b = d_b + dot(ds_b, c_mat, ROWS)
    d_xc = dxs * step_all + skip * dy
    acc_skip = jnp.sum(dy * xc, axis=0, keepdims=True)

    d_u = d_xc * (sx * (1.0 + pre_x * (1.0 - sx)))
    d_ub = jnp.concatenate([d_b, d_c], axis=1) * (sbc * (1.0 + pre_bc * (1.0 - sbc)))
    dubuf[0:length, :] = d_u
    dubbuf[0:length, :] = d_ub
    d_x = jnp.zeros_like(d_u)
    d_bc = jnp.zeros_like(d_ub)
    acc_rows = []
    accbc_rows = []
    for j in range(4):
        d_x = d_x + cx_ref[j : j + 1, :] * dubuf[pl.ds(3 - j, length), :]
        d_bc = d_bc + cbc_ref[j : j + 1, :] * dubbuf[pl.ds(3 - j, length), :]
        acc_rows.append(jnp.sum(d_u * xbuf[pl.ds(5 + j, length), :], axis=0, keepdims=True))
        accbc_rows.append(jnp.sum(d_ub * bbuf[pl.ds(5 + j, length), :], axis=0, keepdims=True))
    dubuf[length:, :] = d_u[0:8, :]
    dubbuf[length:, :] = d_ub[0:8, :]
    zero = jnp.zeros((1, channels), f32)
    acc_ref[...] += jnp.concatenate(
        acc_rows + [jnp.sum(d_u, axis=0, keepdims=True), acc_norm, acc_skip, zero], axis=0
    )
    zero = jnp.zeros((3, d_ub.shape[1]), f32)
    accbc[...] += jnp.concatenate(
        accbc_rows + [jnp.sum(d_ub, axis=0, keepdims=True), zero], axis=0
    )
    dx_b = d_x.astype(bf16)
    dbc_b = d_bc.astype(bf16)
    dxt_ref[:, :channels] = dx_b
    dxt_ref[:, channels:] = dt_b
    put_columns(
        place_ref,
        pl.num_programs(0) - 1 - step_id,
        bcmine_ref,
        bcother_ref,
        jnp.transpose(d_bc).astype(bf16),
    )
    total = dot(jnp.concatenate([dz_b, dx_b], axis=1), w_ref[...], COLS)
    total = total + dot(dbc_b, wbc_ref[...]) + dot(dt_b, wdt_ref[...])
    accn[0:1, :] += jnp.sum(total * xn_ref[...].astype(f32), axis=0, keepdims=True)

    @pl.when(first_span)
    def _():
        lanes = shared_ref.shape[1]
        lines = [accn[0:1, i * lanes : (i + 1) * lanes] for i in range(width // lanes)]
        shared = jnp.concatenate(lines + [accbc[0:5, :]], axis=0)
        shared_ref[0 : shared.shape[0], :] = shared.astype(bf16)
        shared_ref[shared.shape[0] :, :] = jnp.zeros(
            (shared_ref.shape[0] - shared.shape[0], lanes), bf16
        )

    put_half(
        place_ref,
        pl.num_programs(0) - 1 - step_id,
        pl.num_programs(0) // 2,
        mine_ref,
        other_ref,
        total.astype(bf16),
    )


def whole(shape):
    zeros = (0,) * len(shape)
    return pl.BlockSpec(shape, lambda i, p: zeros)


def span_rows(columns):
    return pl.BlockSpec((SPAN, columns), lambda i, p: (i, 0))


def half_rows(columns, spans, reverse):
    half = spans // 2

    def block(i, core):
        span = spans - 1 - i if reverse else i
        return jnp.clip(span - half * core, 0, half - 1), 0

    return [
        pl.BlockSpec((SPAN, columns), lambda i, p: block(i, p[0])),
        pl.BlockSpec((SPAN, columns), lambda i, p: block(i, 1 - p[0])),
    ]


def span_call(kernel, name, spans, place, operands, in_specs, shapes, out_specs, scratch, flops):
    moved = sum(v.size * v.dtype.itemsize for v in [*operands, *shapes])
    return pl.pallas_call(
        kernel,
        grid_spec=pltpu.PrefetchScalarGridSpec(
            num_scalar_prefetch=1,
            grid=(spans,),
            in_specs=in_specs,
            out_specs=out_specs,
            scratch_shapes=scratch,
        ),
        out_shape=shapes,
        compiler_params=pltpu.CompilerParams(
            dimension_semantics=("arbitrary",), vmem_limit_bytes=VMEM_BYTES
        ),
        cost_estimate=pl.CostEstimate(flops=flops, bytes_accessed=moved, transcendentals=0),
        name=name,
    )(place, *operands)


def run_forward(place, gathered, w, wdt, small, state, head_dim):
    w_here, w_there, there_plan = w
    channels = small[0].shape[1]
    width = gathered[0][0][0].shape[1]
    anywhere = pl.BlockSpec(memory_space=pl.ANY)
    tokens = NC * NZ * gathered[0][2][0]
    spans = tokens // SPAN
    last_layer = len(gathered) == 2
    plans = [(cut_plan(*one), len(one[0])) for one in gathered]
    operands = [p for one in gathered for p in one[0]]
    in_specs = [whole(v.shape) for v in operands] + [anywhere] * (1 + len(w_there))
    operands += [w_here, *w_there, wdt, *small]
    in_specs += [whole(v.shape) for v in operands[len(in_specs) :]]
    shapes = [
        jax.ShapeDtypeStruct(w_here.shape, bf16),
        jax.ShapeDtypeStruct((tokens, width), bf16),
        jax.ShapeDtypeStruct((2 * state, width), bf16),
        jax.ShapeDtypeStruct((tokens, channels), bf16),
        jax.ShapeDtypeStruct((tokens, channels), bf16),
        jax.ShapeDtypeStruct((tokens, 2 * state), bf16),
        jax.ShapeDtypeStruct((tokens, LANES), f32),
        jax.ShapeDtypeStruct((tokens, channels), bf16),
        jax.ShapeDtypeStruct((spans, state, channels), f32),
        jax.ShapeDtypeStruct((tokens // 2, width + LANES), bf16),
        jax.ShapeDtypeStruct((tokens // 2, width + LANES), bf16),
    ]
    out_specs = [whole(w_here.shape), span_rows(width), whole((2 * state, width))]
    out_specs += [span_rows(s.shape[1]) for s in shapes[3:8]]
    out_specs.append(pl.BlockSpec((1, state, channels), lambda i, p: (i, 0, 0)))
    out_specs += half_rows(width + LANES, spans, False)
    scratch = [
        pltpu.SemaphoreType.DMA,
        pltpu.VMEM((tokens, width), bf16),
        pltpu.VMEM((SPAN + 8, channels), f32),
        pltpu.VMEM((SPAN + 8, 2 * state), f32),
        pltpu.VMEM((state, channels), f32),
    ]
    if last_layer:
        shapes += [
            jax.ShapeDtypeStruct((tokens, width), bf16),
            jax.ShapeDtypeStruct((8, tokens), f32),
            jax.ShapeDtypeStruct((tokens, channels), f32),
        ]
        out_specs += [span_rows(width), pl.BlockSpec((8, SPAN), lambda i, p: (0, i)), span_rows(channels)]
        scratch.append(pltpu.VMEM((tokens, width), bf16))
    kernel = functools.partial(forward_kernel, plans, there_plan, head_dim)
    return span_call(
        kernel, "layer_forward", spans, place, operands, in_specs, shapes, out_specs, scratch, 20 * 10**9
    )


def run_gate(place, gathered, z, y, w, cx):
    tokens, channels = z.shape
    width = w.shape[0]
    spans = tokens // SPAN
    plan, pieces = cut_plan(*gathered), list(gathered[0])
    operands = [*pieces, z, y, w, cx]
    in_specs = [whole(p.shape) for p in pieces]
    in_specs += [span_rows(channels), span_rows(channels)]
    in_specs += [pl.BlockSpec((width, channels), lambda i, p: (0, 2)), whole(cx.shape)]
    shapes = [
        jax.ShapeDtypeStruct((tokens, width), bf16),
        jax.ShapeDtypeStruct((tokens, channels), bf16),
        jax.ShapeDtypeStruct((tokens, channels), f32),
        jax.ShapeDtypeStruct((tokens, channels), bf16),
        jax.ShapeDtypeStruct((8, channels), f32),
    ]
    out_specs = [span_rows(s.shape[1]) for s in shapes[:4]] + [whole(shapes[4].shape)]
    scratch = [pltpu.VMEM((tokens, pieces[0].shape[1]), bf16)]
    kernel = functools.partial(gate_kernel, plan, len(pieces), width)
    return span_call(
        kernel, "gate_backward", spans, place, operands, in_specs, shapes, out_specs, scratch, 6 * 10**9
    )


def run_scan(place, lead, xn, xp, bc, dt, hin, weights, small, pick, head_dim, inner_all):
    tokens, channels = xp.shape
    state = hin.shape[1]
    width = xn.shape[1]
    spans = tokens // SPAN
    with_gate = len(lead) == 4

    def rev(columns):
        return pl.BlockSpec((SPAN, columns), lambda i, p: (spans - 1 - i, 0))

    def halo(columns, rows):
        per = SPAN // rows
        return pl.BlockSpec(
            (rows, columns), lambda i, p: (jnp.maximum((spans - 1 - i) * per - 1, 0), 0)
        )

    operands = [*lead, xn, xp, xp, bc, bc, dt, hin, *weights, *small, pick]
    in_specs = [rev(channels)] * 2
    if with_gate:
        tok = pl.BlockSpec((8, SPAN), lambda i, p: (0, spans - 1 - i))
        in_specs = [rev(channels), tok, rev(channels), rev(channels)]
    in_specs += [
        rev(width),
        rev(channels),
        halo(channels, 16),
        rev(2 * state),
        halo(2 * state, 16),
        rev(LANES),
        pl.BlockSpec((1, state, channels), lambda i, p: (spans - 1 - i, 0, 0)),
    ]
    in_specs.append(whole((width, 2 * channels)))
    in_specs += [whole(v.shape) for v in operands[len(in_specs) :]]
    shapes = [
        jax.ShapeDtypeStruct((tokens, channels + LANES), bf16),
        jax.ShapeDtypeStruct((state * spans, SPAN), bf16),
        jax.ShapeDtypeStruct((state * spans, SPAN), bf16),
        jax.ShapeDtypeStruct((tokens // 2, width), bf16),
        jax.ShapeDtypeStruct((tokens // 2, width), bf16),
        jax.ShapeDtypeStruct((8, channels), f32),
        jax.ShapeDtypeStruct((8, LANES), f32),
        jax.ShapeDtypeStruct((16, 2 * state), bf16),
    ]
    out_specs = [rev(channels + LANES), whole(shapes[1].shape), whole(shapes[2].shape)]
    out_specs += half_rows(width, spans, True)
    out_specs += [whole(s.shape) for s in shapes[5:]]
    if with_gate:
        shapes = [jax.ShapeDtypeStruct((tokens, channels), bf16)] * 2 + shapes
        out_specs = [rev(channels)] * 2 + out_specs
    scratch = [
        pltpu.VMEM((8, 2 * state), f32),
        pltpu.VMEM((8, width), f32),
        pltpu.VMEM((SPAN + 8, channels), f32),
        pltpu.VMEM((SPAN + 8, 2 * state), f32),
        pltpu.VMEM((SPAN + 8, channels), f32),
        pltpu.VMEM((SPAN + 8, 2 * state), f32),
        pltpu.VMEM((state, channels), f32),
    ]
    kernel = functools.partial(scan_kernel, with_gate, head_dim, inner_all)
    return span_call(
        kernel, "scan_backward", spans, place, operands, in_specs, shapes, out_specs, scratch, 28 * 10**9
    )


def weight_kernel(n_pairs, split, place_ref, *refs):
    lefts, rights, outs = refs[:n_pairs], refs[n_pairs : 2 * n_pairs], refs[2 * n_pairs :]

    def write(out_ref):
        at = 0
        for left_ref, right_ref in zip(lefts, rights):
            columns = right_ref.shape[1]
            out_ref[:, at : at + columns] = dot(left_ref[...], right_ref[...], ROWS).astype(bf16)
            at += columns

    if not split:
        write(outs[0])
        return
    for k, out_ref in enumerate(outs):
        pl.when(pl.program_id(0) == k)(functools.partial(write, out_ref))


def weight_products(place, pairs, split=True):
    tokens = pairs[0][0].shape[0]
    rows = max(left.shape[1] for left, _ in pairs)
    block = rows // 4

    def at(i, p):
        return lax.rem(p[3] + i, NX) if split else i

    lefts, rights, columns = [], [], []
    for left, right in pairs:
        quarter = left.shape[1] == block
        cut, uncut = (lambda i, p: (0, at(i, p))), (lambda i, p: (0, 0))
        lefts.append(pl.BlockSpec((tokens, block), uncut if quarter else cut))
        wide = block if quarter else right.shape[1]
        rights.append(pl.BlockSpec((tokens, wide), cut if quarter else uncut))
        columns.append(wide)
    columns = sum(columns)
    if split:
        out_specs = [whole((block, columns))] * 4
        shapes = [jax.ShapeDtypeStruct((block, columns), bf16)] * 4
    else:
        out_specs = [pl.BlockSpec((block, columns), lambda i, p: (i, 0))]
        shapes = [jax.ShapeDtypeStruct((rows, columns), bf16)]
    out = pl.pallas_call(
        functools.partial(weight_kernel, len(pairs), split),
        grid_spec=pltpu.PrefetchScalarGridSpec(
            num_scalar_prefetch=1, grid=(4,), in_specs=lefts + rights, out_specs=out_specs
        ),
        out_shape=shapes,
        compiler_params=pltpu.CompilerParams(vmem_limit_bytes=VMEM_BYTES),
        cost_estimate=pl.CostEstimate(
            flops=2 * tokens * rows * columns, bytes_accessed=8 * 10**6, transcendentals=0
        ),
        name="weight_products",
    )(place, *[left for left, _ in pairs], *[right for _, right in pairs])
    return out if split else out[0]


SIZES = (4, 2, 2, 2, 4)
NX, NYL, NC, NYH, NZ = SIZES
EVERY = [
    (x, yl, c, yh, z)
    for x in range(NX)
    for yl in range(NYL)
    for c in range(NC)
    for yh in range(NYH)
    for z in range(NZ)
]


def linear(x, yl, c, yh, z):
    return ((((x % NX) * NYL + yl % NYL) * NC + c % NC) * NYH + yh % NYH) * NZ + z % NZ


def send(v, step, only=None):
    pairs = [(linear(*d), linear(*step(*d))) for d in EVERY if only is None or only(*d)]
    return lax.ppermute(v, ("dp", "tensor"), pairs)


def send_z(v, k):
    return send(v, lambda x, yl, c, yh, z: (x, yl, c, yh, z + k))


def send_core(v):
    return send(v, lambda x, yl, c, yh, z: (x, yl, c + 1, yh, z))


def trade(v, k):
    return send(v, lambda x, yl, c, yh, z: (x, yl, yh, c, z + k))


def traded(v):
    return send(v, lambda x, yl, c, yh, z: (x, yl, yh, c, z), lambda x, yl, c, yh, z: c != yh)


def trade_places(v):
    _, _, core, yh, _ = position()
    return jnp.where(core == yh, v, traded(v))


def position():
    dp, tensor = lax.axis_index("dp"), lax.axis_index("tensor")
    return dp // (NYL * NC), dp // NC % NYL, dp % NC, tensor // NZ, tensor % NZ


def gather(v, parts, traded_own=None, later=()):
    arrays, sources = [], []
    for k in (0, 1, 3, 2):
        if traded_own is not None:
            piece = trade(v, k) if k else traded_own
        else:
            piece = send_z(v, k) if k else v
        arrays += [piece, send_core(after(piece, *later) if later else piece)]
        sources += [(False, -k % NZ, 0), (True, -k % NZ, 0)]
    return arrays, sources, parts


def cut_plan(arrays, sources, parts):
    plan = []
    for number, (piece, (other, dz, first)) in enumerate(zip(arrays, sources)):
        base = 0
        for out, per in enumerate(parts):
            begin, end = max(first, base), min(first + piece.shape[0], base + per)
            if begin < end:
                plan.append((number, other, dz, begin - first, out, per, begin - base, end - begin))
            base += per
    return plan


def fold(mine, other):
    _, _, _, _, z = position()
    rows = mine.shape[0] // NZ
    blocks = []
    for k in range(NZ):
        at = (z + k) % NZ * rows
        a = lax.dynamic_slice_in_dim(mine, at, rows, 0).astype(f32)
        blocks.append(a + lax.dynamic_slice_in_dim(other, at, rows, 0).astype(f32))
    return blocks


def fold_beside(pairs):
    folded = [fold(mine, send_core(other)) for mine, other in pairs]
    return [jnp.concatenate([blocks[k] for blocks in folded], axis=1) for k in range(NZ)]


def scatter(*pairs, meanwhile=None):
    own, one, two, three = fold_beside(pairs)
    if meanwhile is not None:
        two = after(two, meanwhile)
    return [own] + [send_z(b.astype(bf16), k) for k, b in ((1, one), (2, two), (3, three))]


def scatter_with_sum(mine, other, shared, meanwhile):
    half = mine.shape[0]
    rows = half // NZ
    got = after(send_core(jnp.concatenate([other, shared], axis=0)), *meanwhile)
    blocks = fold(mine, got[:half])
    total_shared = shared.astype(f32) + got[half:].astype(f32)
    packed = total_shared.astype(bf16)
    total = blocks[0]
    for k in range(1, NZ):
        got = send_z(jnp.concatenate([blocks[k].astype(bf16), packed], axis=0), k)
        total = total + got[:rows].astype(f32)
        total_shared = total_shared + got[rows:].astype(f32)
    return total, total_shared


def sum_members(v):
    both = v + send_core(v)
    total = both
    for k in range(1, NZ):
        total = total + send_z(both, k)
    return total


def send_far(v):
    return send(v, lambda x, yl, c, yh, z: (x, yl, c, yh + 1, z), lambda x, yl, c, yh, z: c != yh)


def sum_far(v, far=None):
    far = send_far(v) if far is None else far
    return (v.astype(f32) + far.astype(f32)).astype(bf16)


def halve(v):
    _, _, core, yh, _ = position()
    half = v.shape[0] // 2
    near = send(
        v[half:], lambda x, yl, c, yh, z: (x, yl, c + 1, yh, z), lambda x, yl, c, yh, z: c == yh
    )
    return jnp.where(core == yh, v[:half], near)


def sum_beside(part):
    beside = send(part, lambda x, yl, c, yh, z: (x, yl + 1, c, yh, z))
    return (part.astype(f32) + beside.astype(f32)).astype(bf16)


def sum_x(blocks):
    total = blocks[0].astype(f32)
    for k in range(1, NX):
        got = send(blocks[k], lambda x, yl, c, yh, z, k=k: (x + k, yl, c, yh, z))
        total = total + got.astype(f32)
    return total.astype(bf16)


def cut_x(v):
    x = position()[0]
    rows = v.shape[0] // NX
    return [lax.dynamic_slice_in_dim(v, (x + k) % NX * rows, rows, 0) for k in range(NX)]


def collect_x(part, meanwhile=()):
    parts = [part]
    for k in range(1, NX):
        got = send(part, lambda x, yl, c, yh, z, k=k: (x + k, yl, c, yh, z))
        parts.append(after(got, *meanwhile) if meanwhile else got)
    return jnp.stack(parts)


def write_kernel(plan, n_kept, place_ref, here_ref, there_ref, *refs):
    rows = here_ref.shape[1]

    def write(ref):
        for (column, kind, wide, by_half), out_ref in zip(plan, refs[n_kept:]):
            for x in range(NX):
                value = ref[lax.rem(place_ref[3] + NX - x, NX), :, column : column + wide].astype(f32)
                if kind != "blocks":
                    out_ref[0, 0 if by_half else x, x if by_half else 0] = value
                elif by_half:
                    at = x // 2 * wide
                    out_ref[0, x % 2 * rows : (x % 2 + 1) * rows, at : at + wide] = value
                else:
                    out_ref[0, :, x * wide : (x + 1) * wide] = value

    here = (pl.program_id(0) == 0) == (place_ref[2] == 1)

    @pl.when(here)
    def _():
        write(here_ref)

    @pl.when(jnp.logical_not(here))
    def _():
        write(there_ref)


def write_sums(place, halves, outputs):
    rows, columns = halves[0].shape[1:]
    total = 2 * NX * rows
    wide = total // 4
    plan, shapes, specs, finals, kept, alias = [], [], [], [], [], {}
    for column, kind, layer, array, by_half in outputs:
        lanes = LANES if kind == "flat" else wide
        layers = 1 if kind == "flat" else 2
        plan.append((column, kind, lanes, by_half))
        if kind == "blocks":
            shape = (layers, wide, total)
            if by_half:
                spec = pl.BlockSpec((1, wide, total // 2), lambda h, p, layer=layer: (layer, 0, h))
            else:
                spec = pl.BlockSpec((1, rows, total), lambda h, p, layer=layer: (layer, h, 0))
            finals.append(shape)
        elif by_half:
            shape = (layers, 2, NX, rows, lanes)
            spec = pl.BlockSpec((1, 1, NX, rows, lanes), lambda h, p, layer=layer: (layer, h, 0, 0, 0))
            finals.append((layers, total, lanes))
        else:
            shape = (layers, NX, 2, rows, lanes)
            spec = pl.BlockSpec((1, NX, 1, rows, lanes), lambda h, p, layer=layer: (layer, 0, h, 0, 0))
            finals.append((layers, total, lanes))
        shapes.append(jax.ShapeDtypeStruct(shape, f32))
        specs.append(spec)
        if array is not None:
            alias[3 + len(kept)] = len(shapes) - 1
            kept.append(array.reshape(shape))
    piece = pl.BlockSpec((NX, rows, columns), lambda h, p: (0, 0, 0))
    written = pl.pallas_call(
        functools.partial(write_kernel, plan, len(kept)),
        grid_spec=pltpu.PrefetchScalarGridSpec(
            num_scalar_prefetch=1,
            grid=(2,),
            in_specs=[piece, piece] + [pl.BlockSpec(memory_space=pl.ANY)] * len(kept),
            out_specs=specs,
        ),
        out_shape=shapes,
        input_output_aliases=alias,
        compiler_params=pltpu.CompilerParams(vmem_limit_bytes=VMEM_BYTES),
        name="write_sums",
    )(place, *halves, *kept)
    return [v.reshape(final) for v, final in zip(written, finals)]


def row_call(kernel, name, operands, shapes):
    return pl.pallas_call(
        kernel,
        grid=(1,),
        in_specs=[pl.BlockSpec((rows, v.shape[1]), lambda i: (0, 0)) for v, rows in operands],
        out_specs=[pl.BlockSpec(s.shape, lambda i, n=len(s.shape): (0,) * n) for s in shapes],
        out_shape=shapes,
        compiler_params=pltpu.CompilerParams(vmem_limit_bytes=VMEM_BYTES),
        name=name,
    )(*[v for v, _ in operands])


def inverse_rms(v):
    return lax.rsqrt(jnp.mean(v * v, axis=-1, keepdims=True) + EPS)


def first_kernel(packed_ref, gain_ref, out_ref):
    rows = 128
    v = packed_ref[0:rows, :].astype(f32)
    out_ref[0:rows, :] = (v * inverse_rms(v) * gain_ref[...]).astype(bf16)
    out_ref[rows:, :] = packed_ref[rows : out_ref.shape[0], :]


def add_terms(own_ref, a_ref, b_ref, c_ref):
    total = own_ref[...].astype(f32) + a_ref[...].astype(f32)
    return total + (b_ref[...].astype(f32) + c_ref[...].astype(f32))


def unscaled_output(inner_all, terms, width):
    total = add_terms(*terms)
    squares = total[:, width : width + 1] + total[:, width + 1 : width + 2]
    gate_rms = lax.rsqrt(squares / inner_all + EPS)
    return gate_rms, total[:, :width] * gate_rms


def middle_kernel(inner_all, own_ref, a_ref, b_ref, c_ref, res_ref, gain_ref, res1_ref, mixed_ref, rms_ref, normed_ref):
    width = res_ref.shape[1]
    gate_rms, mixed = unscaled_output(inner_all, (own_ref, a_ref, b_ref, c_ref), width)
    res = res_ref[...].astype(f32) + mixed
    res1_ref[...] = res
    mixed_ref[...] = mixed
    rms_ref[...] = jnp.broadcast_to(gate_rms, rms_ref.shape)
    normed_ref[...] = (res * inverse_rms(res) * gain_ref[...]).astype(bf16)


def input_gradient(grad_normed, res, d_res, gain):
    inv = inverse_rms(res)
    scaled = grad_normed * gain
    dots = jnp.sum(scaled * res, axis=-1, keepdims=True) / res.shape[1]
    return d_res + inv * scaled - res * (inv * inv * inv) * dots


def between_kernel(inner_all, own_ref, a_ref, b_ref, c_ref, res_ref, dres_ref, gain_ref, mixed_ref, rms_ref, out_ref, sent_ref):
    width = res_ref.shape[1]
    grad_normed = add_terms(*(ref.at[:, 0:width] for ref in (own_ref, a_ref, b_ref, c_ref)))
    d_res = input_gradient(grad_normed, res_ref[...], dres_ref[...].astype(f32), gain_ref[...])
    out_ref[...] = d_res
    g_mixed = d_res.astype(bf16)
    sent_ref[:, :width] = g_mixed
    gate_rms = rms_ref[:, 0:1]
    products = jnp.sum(g_mixed.astype(f32) * mixed_ref[...], axis=-1, keepdims=True)
    coef = gate_rms * gate_rms * products / inner_all
    lane = lax.broadcasted_iota(jnp.int32, rms_ref.shape, 1)
    rms_high = gate_rms.astype(bf16).astype(f32)
    coef_high = coef.astype(bf16).astype(f32)
    extra = jnp.where(lane == 0, rms_high, jnp.where(lane == 1, gate_rms - rms_high, 0.0))
    extra = jnp.where(lane == 2, coef_high, jnp.where(lane == 3, coef - coef_high, extra))
    sent_ref[:, width:] = extra.astype(bf16)


def end_kernel(own_ref, a_ref, b_ref, c_ref, res_ref, dres_ref, gain_ref, hidden_ref, out_ref):
    width = res_ref.shape[1]
    grad_normed = add_terms(own_ref, a_ref, b_ref, c_ref)
    grad = input_gradient(grad_normed, res_ref[...].astype(f32), dres_ref[...], gain_ref[...])
    out_ref[:, :width] = hidden_ref[...]
    out_ref[:, width:] = grad.astype(bf16)


def last_kernel(inner_all, own_ref, a_ref, b_ref, c_ref, res_ref, out_ref):
    _, mixed = unscaled_output(inner_all, (own_ref, a_ref, b_ref, c_ref), res_ref.shape[1])
    out_ref[...] = (res_ref[...] + mixed).astype(bf16)


TINY_ROWS = 56


def small_kernel(head_dim, ends, narrow0_ref, narrow1_ref, gain_ref, pick_ref, norm_ref, wbc_ref, wdt_ref, cx_ref,
                 cxb_ref, cbc_ref, cbcb_ref, dtb_ref, alog_ref, skip_ref, ng_ref):
    bc_at, tiny_at = ends
    heads = wdt_ref.shape[2]
    channels = cx_ref.shape[2]
    both = cbc_ref.shape[2]
    lanes = narrow0_ref.shape[1] - tiny_at
    for layer, ref in enumerate((narrow0_ref, narrow1_ref)):
        wbc_ref[layer] = ref[:, bc_at:tiny_at]
        wdt_ref[layer] = ref[:, 0:heads]
    tiny = jnp.concatenate(
        [narrow0_ref[i * TINY_ROWS : (i + 1) * TINY_ROWS, tiny_at:] for i in range(channels // lanes)], axis=1
    )
    lines = norm_ref.shape[1] // both
    for layer in range(2):
        rows = tiny[8 * layer : 8 * layer + 8]
        cx_ref[layer] = rows[0:4]
        cxb_ref[layer : layer + 1, :] = rows[4:5]
        ng_ref[layer : layer + 1, :] = rows[5:6]
        skip_ref[layer : layer + 1, :] = dot(rows, pick_ref[...], PLAIN, highest)[6:7, 0:heads]
        at = 16 + 2 * layer
        dtb_ref[layer : layer + 1, :] = tiny[at : at + 1, 0:heads]
        alog_ref[layer : layer + 1, :] = tiny[at + 1 : at + 2, 0:heads]
        at = 20 + 16 * layer
        norm = jnp.concatenate([tiny[at + i : at + i + 1, 0:both] for i in range(lines)], axis=1)
        norm_ref[layer : layer + 1, :] = norm / gain_ref[layer : layer + 1, :]
        cbc_ref[layer] = tiny[at + lines : at + lines + 4, 0:both]
        cbcb_ref[layer : layer + 1, :] = tiny[at + lines + 4 : at + lines + 5, 0:both]


def after(v, *others):
    return lax.optimization_barrier((v, *others))[0]


def pad_to(v, rows, lanes):
    return jnp.pad(v, ((0, rows - v.shape[0]), (0, lanes - v.shape[1])))


def local(
    hidden_in,
    grad_out,
    norm_in,
    w_z,
    w_x,
    w_bc,
    w_dt,
    conv_x,
    conv_x_bias,
    conv_bc,
    conv_bc_bias,
    dt_bias,
    a_log,
    skip,
    norm_gate,
    w_out,
):
    layers, width, channels = w_z.shape
    heads = w_dt.shape[2]
    head_dim = channels // heads
    both = conv_bc.shape[2]
    state = both // 2
    members = NC * NZ
    inner_all = channels * members
    rows = hidden_in.shape[1]
    bc_rows = both // members
    x, _, core, yh, z = position()
    stays = core == yh
    place = jnp.stack([core, z, stays, x]).astype(jnp.int32)
    full = jax.ShapeDtypeStruct((rows, width), f32)

    def pack_weights(layer):
        return jnp.concatenate([w_z[layer], w_x[layer], w_out[layer].T], axis=1)

    bc_t = jnp.swapaxes(w_bc, 1, 2)
    dt_t = jnp.pad(jnp.swapaxes(w_dt, 1, 2), ((0, 0), (0, 8 - heads), (0, 0)))
    per_channel = jnp.concatenate(
        [conv_x, conv_x_bias[:, None], norm_gate[:, None], jnp.repeat(skip, head_dim, axis=1)[:, None]],
        axis=1,
    )
    per_channel = jnp.pad(per_channel, ((0, 0), (0, 1), (0, 0)))
    per_head = jnp.stack([dt_bias, -jnp.exp(a_log)], axis=1)
    per_head = jnp.pad(per_head, ((0, 0), (0, 6), (0, LANES - heads)))
    little = jnp.concatenate([per_channel, per_head], axis=2).reshape(layers * 8, channels + LANES)
    high = little.astype(bf16)
    low = (little - high.astype(f32)).astype(bf16)
    lines = pad_to(jnp.concatenate([high, low], axis=1), layers * 8, width)
    packed = jnp.concatenate([hidden_in[0], bc_t[0], dt_t.reshape(layers * 8, width), lines], axis=0)
    packed = trade_places(packed)
    lines = packed[packed.shape[0] - layers * 8 :].astype(f32)
    little = lines[:, : channels + LANES] + lines[:, channels + LANES : 2 * (channels + LANES)]
    little = little.reshape(layers, 8, channels + LANES)

    w0 = pack_weights(0)
    w0 = w0, [traded(after(w0, packed))], [(0, None)]
    grads = jnp.concatenate([grad_out[0], bc_t[1]], axis=0)

    [sent] = row_call(
        first_kernel,
        "first_norm",
        [(packed, packed.shape[0]), (norm_in[0:1], 1)],
        [jax.ShapeDtypeStruct((rows + bc_rows, width), bf16)],
    )
    gathered0 = gather(sent, (rows, bc_rows))
    wdt = [pad_to(packed[rows + bc_rows + 8 * l : rows + bc_rows + 8 * (l + 1)], LANES, width) for l in range(layers)]
    smalls = []
    for layer in range(layers):
        cbc = jnp.concatenate([conv_bc[layer], conv_bc_bias[layer][None], jnp.zeros((3, both), f32)], axis=0)
        smalls.append((little[layer, :, :channels], cbc, little[layer, :, channels:]))
    channel_head = jnp.arange(channels) // head_dim
    pick = (channel_head[:, None] == jnp.arange(LANES)[None, :]).astype(f32)

    out0 = run_forward(place, [gathered0], w0, wdt[0], smalls[0], state, head_dim)
    w0, xn0, wbc0, z0, xp0, bc0, dt0, y0, hin0, mine, other = out0
    grads = after(grads, sent)
    gathered_grad = gather(grads, (rows, bc_rows), jnp.where(stays, grads, after(traded(grads), mine)), (mine,))
    grad_held = gathered_grad[0][0]
    terms = scatter((mine, after(other, *gathered_grad[0][::2])))
    w1 = pack_weights(1)
    w1 = w1, [traded(after(w1, terms[0]))], [(0, None)]
    res1, mixed0, rms0, normed1 = row_call(
        functools.partial(middle_kernel, inner_all),
        "middle_norm",
        [(v, rows) for v in terms] + [(packed, rows), (norm_in[1:2], 1)],
        [full, full, jax.ShapeDtypeStruct((rows, LANES), f32), jax.ShapeDtypeStruct((rows, width), bf16)],
    )
    gathered1 = gather(normed1, (rows,))
    out1 = run_forward(
        place, [gathered1, gathered_grad], w1, wdt[1], smalls[1], state, head_dim
    )
    w1, xn1, wbc1, z1, xp1, bc1, dt1, y1, hin1, mine, other, grad_rows1, sums, gg1 = out1
    sums = sum_members(sums)

    home = fold(mine, send_core(other))
    sums = after(sums, *home)
    home = home[:1] + [send_z(home[k].astype(bf16), k) for k in range(1, NZ)]
    back1 = run_scan(
        place, (gg1, sums, z1, y1), xn1, xp1, bc1, dt1, hin1, (w1, wbc1, wdt[1]), smalls[1], pick, head_dim,
        inner_all,
    )
    dz1, go1, dxt1, *bc_halves, mine, other, acc1, acch1, shared1 = back1
    early1 = weight_products(place, [(xn1, dz1), (go1, grad_rows1)], split=False)
    terms = scatter((mine, after(other, *home)), bc_halves, meanwhile=early1)
    early1_far = send_far(early1)
    [hidden_out] = row_call(
        functools.partial(last_kernel, inner_all),
        "last_output",
        [(after(home[0], terms[1]), rows)] + [(v, rows) for v in home[1:]] + [(res1, rows)],
        [jax.ShapeDtypeStruct((rows, width), bf16)],
    )
    d_res1, sent = row_call(
        functools.partial(between_kernel, inner_all),
        "between_layers",
        [(v, rows) for v in terms]
        + [(res1, rows), (grad_held, rows), (norm_in[1:2], 1), (mixed0, rows), (rms0, rows)],
        [full, jax.ShapeDtypeStruct((rows, width + LANES), bf16)],
    )
    gathered_back = gather(sent, (rows,))

    bc_at = channels + bc_rows

    def with_bc(dxt, bc_sum):
        by_token = bc_sum.reshape(-1, bc_rows, SPAN).swapaxes(1, 2).reshape(-1, bc_rows)
        spread = jnp.pad(by_token, ((0, 0), (bc_at, dxt.shape[1] - bc_at - bc_rows)))
        return dxt + spread.astype(bf16)

    dxt1 = with_bc(dxt1, sum(v[:, width:].astype(f32) for v in terms))

    early1 = halve(sum_far(early1, after(early1_far, sent)))
    z0 = after(z0, early1)
    early1 = sum_x(cut_x(early1))
    grad_rows0, dz0, dy0, go0, acc_gate0 = run_gate(place, gathered_back, z0, y0, w0, smalls[0][0])
    dz0 = after(dz0, early1)
    early = weight_products(place, [(xn0, dz0), (go0, grad_rows0), (xn1, dxt1)])
    dy0 = after(dy0, *early)
    early = sum_x(early)
    early1 = sum_beside(after(early1, dz0))
    back0 = run_scan(
        place, (dy0, dz0), xn0, xp0, bc0, dt0, hin0, (w0, wbc0, wdt[0]), smalls[0], pick, head_dim, inner_all
    )
    dxt0, *bc_halves, mine, other, acc0, acch0, shared0 = back0
    shared = jnp.concatenate([shared0, shared1], axis=0)
    bc_sum, shared = scatter_with_sum(*bc_halves, shared, (early,))
    tiny_at = bc_at + bc_rows
    tiny_lanes = channels + LANES - tiny_at
    tiny = jnp.concatenate(
        [acc0 + acc_gate0, acc1] + [pad_to(v, v.shape[0], channels) for v in (acch0[0:2], acch1[0:2], shared)],
        axis=0,
    )
    tiny = pad_to(tiny, TINY_ROWS, channels)
    tiny = [tiny[:, i * tiny_lanes : (i + 1) * tiny_lanes] for i in range(channels // tiny_lanes)]
    tiny = pad_to(jnp.concatenate(tiny, axis=0), width, tiny_lanes)
    tiny = jnp.pad(tiny, ((0, 0), (tiny_at, 0))).astype(bf16)
    early = halve(sum_far(after(early, dxt0)))
    home = fold(mine, send_core(other))
    late = weight_products(place, [(xn0, after(with_bc(dxt0, bc_sum), early, home[0]))])
    early = sum_beside(early)
    tiny = after(tiny, early)
    late = [v + t for v, t in zip(late, cut_x(tiny))]
    late = sum_x(late)

    terms = home[:1] + [send_z(home[k].astype(bf16), k) for k in range(1, NZ)]
    [outputs] = row_call(
        end_kernel,
        "outputs",
        [(v, rows) for v in terms] + [(packed, rows), (d_res1, rows), (norm_in[0:1], 1), (hidden_out, rows)],
        [jax.ShapeDtypeStruct((rows, 2 * width), bf16)],
    )
    outputs_home = trade_places(outputs).astype(f32)

    early = after(collect_x(early), outputs)
    early = early, send_core(early)
    early1 = collect_x(after(early1, early[0]))
    early1 = early1, send_core(early1)
    g_wz, g_wo, g_wx, narrow1 = write_sums(
        place,
        early,
        [
            (0, "rows", 0, None, False),
            (channels, "blocks", 0, None, False),
            (2 * channels, "rows", 1, None, False),
            (3 * channels, "flat", 0, None, False),
        ],
    )
    g_wz, g_wo = write_sums(
        place, early1, [(0, "rows", 1, g_wz, True), (channels, "blocks", 1, g_wo, True)]
    )
    late = collect_x(sum_beside(halve(sum_far(late))), (g_wz,))
    late = late, send_core(late)
    g_wx, narrow0 = write_sums(
        place, late, [(0, "rows", 0, g_wx, False), (channels, "flat", 0, None, False)]
    )

    narrow0, narrow1 = narrow0[0], narrow1[0]
    small = row_call(
        functools.partial(small_kernel, head_dim, (bc_at - channels, tiny_at - channels)),
        "small_gradients",
        [(narrow0, width), (narrow1, width), (norm_in, layers), (pick, channels)],
        [
            jax.ShapeDtypeStruct(shape, f32)
            for shape in (
                norm_in.shape,
                w_bc.shape,
                w_dt.shape,
                conv_x.shape,
                conv_x_bias.shape,
                conv_bc.shape,
                conv_bc_bias.shape,
                dt_bias.shape,
                a_log.shape,
                skip.shape,
                norm_gate.shape,
            )
        ],
    )
    return (
        outputs_home[None, :, :width],
        outputs_home[None, :, width:],
        small[0],
        g_wz,
        g_wx,
        *small[1:],
        g_wo,
    )


def solution(mesh):
    specs_in = (
        P("dp", "tensor", None),
        P("dp", "tensor", None),
        P(),
        P(None, None, "tensor"),
        P(None, None, "tensor"),
        P(None, None, "tensor"),
        P(None, None, "tensor"),
        P(None, None, "tensor"),
        P(None, "tensor"),
        P(),
        P(),
        P(None, "tensor"),
        P(None, "tensor"),
        P(None, "tensor"),
        P(None, "tensor"),
        P(None, "tensor", None),
    )
    specs_out = (
        P("dp", "tensor", None),
        P("dp", "tensor", None),
        P(),
        P(None, None, "tensor"),
        P(None, None, "tensor"),
        P(None, None, "tensor"),
        P(None, None, "tensor"),
        P(None, None, "tensor"),
        P(None, "tensor"),
        P(),
        P(),
        P(None, "tensor"),
        P(None, "tensor"),
        P(None, "tensor"),
        P(None, "tensor"),
        P(None, "tensor", None),
    )
    return jax.shard_map(
        local, mesh=mesh, in_specs=specs_in, out_specs=specs_out, check_vma=False
    )
```

```python
import functools

import jax
import jax.numpy as jnp
from jax import lax
from jax.experimental import pallas as pl
from jax.experimental.pallas import tpu as pltpu
from jax.sharding import PartitionSpec as P

SPAN = 256
EPS = 1e-05
LANES = 128
VMEM_BYTES = 56 * 1024 * 1024

f32 = jnp.float32
bf16 = jnp.bfloat16
highest = lax.Precision.HIGHEST

ROWS = ((0,), (0,))
COLS = ((1,), (1,))
PLAIN = ((1,), (0,))


def dot(left, right, dims=PLAIN, precision=None):
    return lax.dot_general(
        left, right, (dims, ((), ())), preferred_element_type=f32, precision=precision
    )


def sigmoid(v):
    return 0.5 + 0.5 * jnp.tanh(0.5 * v)


def dot_exact(left, right, dims=PLAIN, terms=3):
    parts = []
    for _ in range(terms):
        parts.append(right.astype(bf16))
        right = right - parts[-1].astype(f32)
    out = dot(left.astype(bf16), jnp.concatenate(parts, axis=1), dims)
    width = out.shape[1] // terms
    return sum(out[:, i * width : (i + 1) * width] for i in range(terms))


def sum_heads(v, pick):
    high = v.astype(bf16)
    low = (v - high.astype(f32)).astype(bf16)
    return dot(high, pick) + dot(low, pick)


def softplus(v):
    return jnp.maximum(v, 0.0) + jnp.log1p(jnp.exp(-jnp.abs(v)))


def spread_heads(per_head, channels, head_dim):
    rows = per_head.shape[0]
    per_tile = LANES // head_dim
    lane = lax.broadcasted_iota(jnp.int32, (rows, LANES), 1)
    tiles = []
    for tile in range(channels // LANES):
        out = jnp.broadcast_to(
            per_head[:, tile * per_tile : tile * per_tile + 1], (rows, LANES)
        )
        for sub in range(1, per_tile):
            head = tile * per_tile + sub
            out = jnp.where(
                lane >= sub * head_dim,
                jnp.broadcast_to(per_head[:, head : head + 1], (rows, LANES)),
                out,
            )
        tiles.append(out)
    return jnp.concatenate(tiles, axis=1)


def conv_taps(buf, taps, offset, width):
    out = offset
    for j in range(4):
        out = out + taps[j : j + 1] * buf[pl.ds(5 + j, width), :]
    return out


def decay_matrix(mask, cum_col, cum_row):
    return jnp.exp(jnp.where(mask, cum_col - cum_row, -1e30))


def span_values(dt, head_ref):
    length = dt.shape[0]
    rows = lax.broadcasted_iota(jnp.int32, (length, length), 0)
    cols = lax.broadcasted_iota(jnp.int32, (length, length), 1)
    mask = rows >= cols
    pre = dt + head_ref[0:1, :]
    step = softplus(pre)
    rate = head_ref[1:2, :] * step
    cum = dot_exact(mask, rate)
    return mask, pre, step, rate, cum


def put_half(place_ref, span, half, mine_ref, other_ref, value):
    own = span // half == place_ref[0]

    @pl.when(own)
    def _():
        mine_ref[...] = value

    @pl.when(jnp.logical_not(own))
    def _():
        other_ref[...] = value


def place_pieces(plan, place_ref, pieces, outs):
    core, z = place_ref[0], place_ref[1]
    for piece, other, dz, start, out, per, offset, rows in plan:
        member = (1 - core if other else core) * NZ + lax.rem(z + dz, NZ)
        row = pl.multiple_of(member * per + offset, 16)
        outs[out][pl.ds(row, rows), :] = pieces[piece][start : start + rows, :]


def put_columns(place_ref, span, mine_ref, other_ref, columns):
    per = columns.shape[0] // (NC * NZ)
    rows = mine_ref.shape[0] // NZ

    def place_columns(core, ref):
        for z in range(NZ):
            at = (core * NZ + z) * per
            ref[pl.ds(pl.multiple_of(z * rows + span * per, 16), per), :] = columns[at : at + per, :]

    for core in range(NC):
        mine = place_ref[0] == core

        @pl.when(mine)
        def _(core=core):
            place_columns(core, mine_ref)

        @pl.when(jnp.logical_not(mine))
        def _(core=core):
            place_columns(core, other_ref)


def forward_kernel(plans, there_plan, head_dim, place_ref, *refs):
    last_layer = len(plans) == 2
    refs = list(refs)

    def take(count):
        taken = refs[:count]
        del refs[:count]
        return taken

    piece_refs = [take(count) for _, count in plans]
    [w_here] = take(1)
    w_there = take(len(there_plan))
    wdt_ref, cx_ref, cbc_ref, head_ref = take(4)
    w_ref, xn_ref, wbc_ref, z_ref, xp_ref, bc_ref, dt_ref, y_ref, hin_ref, mine_ref, other_ref = take(11)
    if last_layer:
        g_ref, sums_ref, gg_ref = take(3)
    w_sem, xn_all, xbuf, bbuf, hst = take(5)
    if last_layer:
        [g_all] = take(1)
    length = z_ref.shape[0]
    channels = cx_ref.shape[1]
    state = hst.shape[0]
    span = pl.program_id(0)

    @pl.when(span == 0)
    def _():
        @pl.when(place_ref[2] == 1)
        def _():
            pltpu.make_async_copy(w_here, w_ref, w_sem).start()

        @pl.when(place_ref[2] == 0)
        def _():
            for part, (start, k) in zip(w_there, there_plan):
                rows = part.shape[0]
                if k is not None:
                    start = pl.multiple_of(lax.rem(place_ref[3] + NX - k, NX) * rows, 16)
                pltpu.make_async_copy(part, w_ref.at[pl.ds(start, rows), :], w_sem).start()

        if last_layer:
            place_pieces(plans[0][0], place_ref, piece_refs[0], [xn_all])
            place_pieces(plans[1][0], place_ref, piece_refs[1], [g_all, wbc_ref])
        else:
            place_pieces(plans[0][0], place_ref, piece_refs[0], [xn_all, wbc_ref])
        xbuf[0:8, :] = jnp.zeros((8, channels), f32)
        bbuf[0:8, :] = jnp.zeros((8, 2 * state), f32)
        hst[...] = jnp.zeros_like(hst)
        pltpu.make_async_copy(w_here, w_ref, w_sem).wait()

    here = pl.ds(pl.multiple_of(span * length, length), length)
    xn = xn_all[here, :]
    xn_ref[...] = xn
    zx = dot(xn, w_ref[:, : 2 * channels])
    z = zx[:, :channels]
    z_ref[...] = z.astype(bf16)
    xp = zx[:, channels:]
    xp_ref[...] = xp.astype(bf16)
    xbuf[8:, :] = xp
    bc = dot(xn, wbc_ref[...], COLS).astype(bf16)
    bc_ref[...] = bc
    bbuf[8:, :] = bc.astype(f32)
    dt = dot(xn, wdt_ref[...], COLS)
    dt_ref[...] = dt

    pre_x = conv_taps(xbuf, cx_ref[0:4, :], cx_ref[4:5, :], length)
    xc = pre_x * sigmoid(pre_x)
    pre_bc = conv_taps(bbuf, cbc_ref[0:4, :], cbc_ref[4:5, :], length)
    bcc = (pre_bc * sigmoid(pre_bc)).astype(bf16)
    xbuf[0:8, :] = xbuf[length : length + 8, :]
    bbuf[0:8, :] = bbuf[length : length + 8, :]
    b_mat = bcc[:, :state]
    c_mat = bcc[:, state:]

    mask, _, step, _, cum = span_values(dt, head_ref)
    cum_t = jnp.transpose(cum)
    scores = dot(c_mat, b_mat, COLS)
    xs = xc * spread_heads(step, channels, head_dim)
    xs_b = xs.astype(bf16)
    lane = lax.broadcasted_iota(jnp.int32, (length, LANES), 1)
    per_tile = LANES // head_dim
    tiles = []
    for tile in range(channels // LANES):
        xs_tile = xs_b[:, tile * LANES : (tile + 1) * LANES]
        out = None
        for sub in range(per_tile):
            head = tile * per_tile + sub
            decay = decay_matrix(mask, cum[:, head : head + 1], cum_t[head : head + 1, :])
            part = dot((scores * decay).astype(bf16), xs_tile)
            out = part if out is None else jnp.where(lane >= sub * head_dim, part, out)
        tiles.append(out)
    hin = hst[...]
    hin_ref[0] = hin
    last = cum[length - 1 : length, :]
    y = jnp.concatenate(tiles, axis=1)
    y = y + dot(c_mat, hin.astype(bf16)) * spread_heads(jnp.exp(cum), channels, head_dim)
    y = y + cx_ref[6:7, :] * xc
    y_ref[...] = y.astype(bf16)
    tail = spread_heads(jnp.exp(last - cum), channels, head_dim)
    keep = spread_heads(jnp.exp(last), channels, head_dim)
    hst[...] = keep * hin + dot(b_mat, (tail * xs).astype(bf16), ROWS)

    gated = y * (z * sigmoid(z))
    scaled = gated * cx_ref[5:6, :]
    squares = jnp.sum(gated * gated, axis=1, keepdims=True)
    high = squares.astype(bf16).astype(f32)
    extra = jnp.where(lane == 0, high, jnp.where(lane == 1, squares - high, 0.0)).astype(bf16)
    mixed = dot(scaled.astype(bf16), w_ref[:, 2 * channels :], COLS).astype(bf16)
    put_half(
        place_ref,
        span,
        pl.num_programs(0) // 2,
        mine_ref,
        other_ref,
        jnp.concatenate([mixed, extra], axis=1),
    )
    if last_layer:
        g = g_all[here, :]
        g_ref[...] = g
        gg = dot(g, w_ref[:, 2 * channels :])
        gg_ref[...] = gg
        products = jnp.sum(gg * scaled, axis=1, keepdims=True)
        both = jnp.where(lane == 0, squares, jnp.where(lane == 1, products, 0.0))
        sums_ref[...] = jnp.transpose(both)[0:8, :]


def gate_part(gg, rms, coef, z, y, cx_ref):
    z, y = z.astype(f32), y.astype(f32)
    norm_gate = cx_ref[5:6, :]
    sz = sigmoid(z)
    silu_z = z * sz
    gated = y * silu_z
    rg = rms * gg
    gate_out = (gated * rms * norm_gate).astype(bf16)
    d_gated = rg * norm_gate - gated * coef
    dz = (d_gated * y * (sz * (1.0 + z * (1.0 - sz)))).astype(bf16)
    return dz, d_gated * silu_z, gate_out, jnp.sum(rg * gated, axis=0, keepdims=True)


def gate_kernel(plan, n_pieces, width, place_ref, *refs):
    pieces = refs[:n_pieces]
    z_ref, y_ref, wo_ref, cx_ref, g_ref, dz_ref, dy_ref, go_ref, acc_ref, first_all = refs[n_pieces:]
    length = z_ref.shape[0]
    span = pl.program_id(0)

    @pl.when(span == 0)
    def _():
        place_pieces(plan, place_ref, pieces, [first_all])
        acc_ref[...] = jnp.zeros_like(acc_ref)

    first = first_all[pl.ds(pl.multiple_of(span * length, length), length), :]
    g = first[:, :width]
    g_ref[...] = g
    tok = first[:, width:].astype(f32)
    rms = tok[:, 0:1] + tok[:, 1:2]
    coef = tok[:, 2:3] + tok[:, 3:4]
    gg = dot(g, wo_ref[...])
    dz, dy, gate_out, acc_norm = gate_part(gg, rms, coef, z_ref[...], y_ref[...], cx_ref)
    dz_ref[...] = dz
    dy_ref[...] = dy
    go_ref[...] = gate_out
    acc_ref[5:6, :] += acc_norm


def scan_kernel(with_gate, head_dim, inner_all, place_ref, *refs):
    if with_gate:
        (gg_ref, tok_ref, z_ref, y_ref), refs = refs[:4], refs[4:]
    else:
        (dy_ref, dz_ref), refs = refs[:2], refs[2:]
    (xn_ref, xp_ref, xhalo_ref, bc_ref, bchalo_ref, dt_ref, hin_ref,
     w_ref, wbc_ref, wdt_ref, cx_ref, cbc_ref, head_ref, pick_ref), refs = refs[:14], refs[14:]
    if with_gate:
        (dz_ref, go_ref), refs = refs[:2], refs[2:]
    (dxt_ref, bcmine_ref, bcother_ref, mine_ref, other_ref, acc_ref, acch_ref, shared_ref,
     accbc, accn, xbuf, bbuf, dubuf, dubbuf, dhst) = refs
    length = xp_ref.shape[0]
    channels = cx_ref.shape[1]
    width = xn_ref.shape[1]
    state = dhst.shape[0]
    step_id = pl.program_id(0)
    first_span = step_id == pl.num_programs(0) - 1

    @pl.when(step_id == 0)
    def _():
        dubuf[length:, :] = jnp.zeros((8, channels), f32)
        dubbuf[length:, :] = jnp.zeros((8, 2 * state), f32)
        dhst[...] = jnp.zeros_like(dhst)
        accn[...] = jnp.zeros_like(accn)
        acc_ref[...] = jnp.zeros_like(acc_ref)
        accbc[...] = jnp.zeros_like(accbc)
        acch_ref[...] = jnp.zeros_like(acch_ref)

    @pl.when(first_span)
    def _():
        xbuf[0:8, :] = jnp.zeros((8, channels), f32)
        bbuf[0:8, :] = jnp.zeros((8, 2 * state), f32)

    @pl.when(jnp.logical_not(first_span))
    def _():
        xbuf[0:8, :] = xhalo_ref[...].astype(f32)[8:16, :]
        bbuf[0:8, :] = bchalo_ref[...].astype(f32)[8:16, :]

    xbuf[8:, :] = xp_ref[...].astype(f32)
    bbuf[8:, :] = bc_ref[...].astype(f32)
    if with_gate:
        tok = jnp.transpose(tok_ref[...])
        rms = lax.rsqrt(tok[:, 0:1] / inner_all + EPS)
        coef = rms * rms * rms * tok[:, 1:2] / inner_all
        dz_b, dy, gate_out, acc_norm = gate_part(
            gg_ref[...], rms, coef, z_ref[...], y_ref[...], cx_ref
        )
        dz_ref[...] = dz_b
        go_ref[...] = gate_out
    else:
        dz_b, dy = dz_ref[...], dy_ref[...]
        acc_norm = jnp.zeros((1, channels), f32)
    skip = cx_ref[6:7, :]

    pre_x = conv_taps(xbuf, cx_ref[0:4, :], cx_ref[4:5, :], length)
    sx = sigmoid(pre_x)
    xc = pre_x * sx
    pre_bc = conv_taps(bbuf, cbc_ref[0:4, :], cbc_ref[4:5, :], length)
    sbc = sigmoid(pre_bc)
    bcc = (pre_bc * sbc).astype(bf16)
    b_mat = bcc[:, :state]
    c_mat = bcc[:, state:]
    mask, pre_dt, step, rate, cum = span_values(dt_ref[...], head_ref)
    cum_t = jnp.transpose(cum)
    last = cum[length - 1 : length, :]
    scores = dot(c_mat, b_mat, COLS)
    step_all = spread_heads(step, channels, head_dim)
    xs = xc * step_all
    xs_b = xs.astype(bf16)
    tail = spread_heads(jnp.exp(last - cum), channels, head_dim)
    keep = spread_heads(jnp.exp(last), channels, head_dim)

    hin = hin_ref[0]
    hin_b = hin.astype(bf16)
    dh = dhst[...]
    dh_b = dh.astype(bf16)
    dye = dy * spread_heads(jnp.exp(cum), channels, head_dim)
    dye_b = dye.astype(bf16)
    txs = tail * xs
    txs_b = txs.astype(bf16)
    carried = dot(c_mat, hin_b)
    pulled = dot(b_mat, dh_b)
    d_c = dot(dye_b, hin_b, COLS)
    d_b = dot(txs_b, dh_b, COLS)
    dhst[...] = keep * dh + dot(c_mat, dye_b, ROWS)
    into = txs * pulled
    across = dye * carried - into
    at_last = jnp.sum(into, axis=0, keepdims=True) + keep * jnp.sum(hin * dh, axis=0, keepdims=True)

    dy_b = dy.astype(bf16)
    dy_t = jnp.transpose(dy).astype(bf16)
    lane = lax.broadcasted_iota(jnp.int32, (length, LANES), 1)
    per_tile = LANES // head_dim
    d_scores = jnp.zeros((length, length), f32)
    row_sums = jnp.zeros((length, LANES), f32)
    col_sums = []
    dxs_parts = []
    for head in range(channels // head_dim):
        tile, sub = divmod(head, per_tile)
        dy_tile = dy_b[:, tile * LANES : (tile + 1) * LANES]
        own = (lane >= sub * head_dim) & (lane < (sub + 1) * head_dim)
        dy_head = jnp.where(own, dy_tile, jnp.zeros_like(dy_tile))
        d_m = dot(dy_head, xs_b[:, tile * LANES : (tile + 1) * LANES], COLS)
        decay = decay_matrix(mask, cum[:, head : head + 1], cum_t[head : head + 1, :])
        dxs_parts.append(
            dot(dy_t[head * head_dim : (head + 1) * head_dim, :], (scores * decay).astype(bf16))
        )
        d_m = d_m * decay
        d_scores = d_scores + d_m
        pairs = d_m * scores
        row_sums = jnp.where(lane == head, jnp.sum(pairs, axis=1, keepdims=True), row_sums)
        col_sums.append(jnp.sum(pairs, axis=0, keepdims=True))
    heads = len(col_sums)
    col_sums = jnp.concatenate(col_sums + [jnp.zeros((LANES - heads, length), f32)], axis=0)
    dxs = jnp.transpose(jnp.concatenate(dxs_parts, axis=0)) + tail * pulled
    pick = pick_ref[...].astype(bf16)
    d_cum = row_sums - jnp.transpose(col_sums) + sum_heads(across, pick)
    at_last = sum_heads(jnp.broadcast_to(at_last, (16, channels)), pick)[0:1, :]
    d_rate = dot_exact(mask, d_cum, ROWS) + at_last
    d_step = d_rate * head_ref[1:2, :] + sum_heads(dxs * xc, pick)
    d_dt = d_step * sigmoid(pre_dt)
    acch_ref[0:1, :] += jnp.sum(d_dt, axis=0, keepdims=True)
    acch_ref[1:2, :] += jnp.sum(d_rate * rate, axis=0, keepdims=True)
    dt_b = d_dt.astype(bf16)
    ds_b = d_scores.astype(bf16)
    d_c = d_c + dot(ds_b, b_mat)
    d_b = d_b + dot(ds_b, c_mat, ROWS)
    d_xc = dxs * step_all + skip * dy
    acc_skip = jnp.sum(dy * xc, axis=0, keepdims=True)

    d_u = d_xc * (sx * (1.0 + pre_x * (1.0 - sx)))
    d_ub = jnp.concatenate([d_b, d_c], axis=1) * (sbc * (1.0 + pre_bc * (1.0 - sbc)))
    dubuf[0:length, :] = d_u
    dubbuf[0:length, :] = d_ub
    d_x = jnp.zeros_like(d_u)
    d_bc = jnp.zeros_like(d_ub)
    acc_rows = []
    accbc_rows = []
    for j in range(4):
        d_x = d_x + cx_ref[j : j + 1, :] * dubuf[pl.ds(3 - j, length), :]
        d_bc = d_bc + cbc_ref[j : j + 1, :] * dubbuf[pl.ds(3 - j, length), :]
        acc_rows.append(jnp.sum(d_u * xbuf[pl.ds(5 + j, length), :], axis=0, keepdims=True))
        accbc_rows.append(jnp.sum(d_ub * bbuf[pl.ds(5 + j, length), :], axis=0, keepdims=True))
    dubuf[length:, :] = d_u[0:8, :]
    dubbuf[length:, :] = d_ub[0:8, :]
    zero = jnp.zeros((1, channels), f32)
    acc_ref[...] += jnp.concatenate(
        acc_rows + [jnp.sum(d_u, axis=0, keepdims=True), acc_norm, acc_skip, zero], axis=0
    )
    zero = jnp.zeros((3, d_ub.shape[1]), f32)
    accbc[...] += jnp.concatenate(
        accbc_rows + [jnp.sum(d_ub, axis=0, keepdims=True), zero], axis=0
    )
    dx_b = d_x.astype(bf16)
    dbc_b = d_bc.astype(bf16)
    dxt_ref[:, :channels] = dx_b
    dxt_ref[:, channels:] = dt_b
    put_columns(
        place_ref,
        pl.num_programs(0) - 1 - step_id,
        bcmine_ref,
        bcother_ref,
        jnp.transpose(d_bc).astype(bf16),
    )
    total = dot(jnp.concatenate([dz_b, dx_b], axis=1), w_ref[...], COLS)
    total = total + dot(dbc_b, wbc_ref[...]) + dot(dt_b, wdt_ref[...])
    accn[0:1, :] += jnp.sum(total * xn_ref[...].astype(f32), axis=0, keepdims=True)

    @pl.when(first_span)
    def _():
        lanes = shared_ref.shape[1]
        lines = [accn[0:1, i * lanes : (i + 1) * lanes] for i in range(width // lanes)]
        shared = jnp.concatenate(lines + [accbc[0:5, :]], axis=0)
        shared_ref[0 : shared.shape[0], :] = shared.astype(bf16)
        shared_ref[shared.shape[0] :, :] = jnp.zeros(
            (shared_ref.shape[0] - shared.shape[0], lanes), bf16
        )

    put_half(
        place_ref,
        pl.num_programs(0) - 1 - step_id,
        pl.num_programs(0) // 2,
        mine_ref,
        other_ref,
        total.astype(bf16),
    )


def whole(shape):
    zeros = (0,) * len(shape)
    return pl.BlockSpec(shape, lambda i, p: zeros)


def span_rows(columns):
    return pl.BlockSpec((SPAN, columns), lambda i, p: (i, 0))


def half_rows(columns, spans, reverse):
    half = spans // 2

    def block(i, core):
        span = spans - 1 - i if reverse else i
        return jnp.clip(span - half * core, 0, half - 1), 0

    return [
        pl.BlockSpec((SPAN, columns), lambda i, p: block(i, p[0])),
        pl.BlockSpec((SPAN, columns), lambda i, p: block(i, 1 - p[0])),
    ]


def span_call(kernel, name, spans, place, operands, in_specs, shapes, out_specs, scratch, flops):
    moved = sum(v.size * v.dtype.itemsize for v in [*operands, *shapes])
    return pl.pallas_call(
        kernel,
        grid_spec=pltpu.PrefetchScalarGridSpec(
            num_scalar_prefetch=1,
            grid=(spans,),
            in_specs=in_specs,
            out_specs=out_specs,
            scratch_shapes=scratch,
        ),
        out_shape=shapes,
        compiler_params=pltpu.CompilerParams(
            dimension_semantics=("arbitrary",), vmem_limit_bytes=VMEM_BYTES
        ),
        cost_estimate=pl.CostEstimate(flops=flops, bytes_accessed=moved, transcendentals=0),
        name=name,
    )(place, *operands)


def run_forward(place, gathered, w, wdt, small, state, head_dim):
    w_here, w_there, there_plan = w
    channels = small[0].shape[1]
    width = gathered[0][0][0].shape[1]
    anywhere = pl.BlockSpec(memory_space=pl.ANY)
    tokens = NC * NZ * gathered[0][2][0]
    spans = tokens // SPAN
    last_layer = len(gathered) == 2
    plans = [(cut_plan(*one), len(one[0])) for one in gathered]
    operands = [p for one in gathered for p in one[0]]
    in_specs = [whole(v.shape) for v in operands] + [anywhere] * (1 + len(w_there))
    operands += [w_here, *w_there, wdt, *small]
    in_specs += [whole(v.shape) for v in operands[len(in_specs) :]]
    shapes = [
        jax.ShapeDtypeStruct(w_here.shape, bf16),
        jax.ShapeDtypeStruct((tokens, width), bf16),
        jax.ShapeDtypeStruct((2 * state, width), bf16),
        jax.ShapeDtypeStruct((tokens, channels), bf16),
        jax.ShapeDtypeStruct((tokens, channels), bf16),
        jax.ShapeDtypeStruct((tokens, 2 * state), bf16),
        jax.ShapeDtypeStruct((tokens, LANES), f32),
        jax.ShapeDtypeStruct((tokens, channels), bf16),
        jax.ShapeDtypeStruct((spans, state, channels), f32),
        jax.ShapeDtypeStruct((tokens // 2, width + LANES), bf16),
        jax.ShapeDtypeStruct((tokens // 2, width + LANES), bf16),
    ]
    out_specs = [whole(w_here.shape), span_rows(width), whole((2 * state, width))]
    out_specs += [span_rows(s.shape[1]) for s in shapes[3:8]]
    out_specs.append(pl.BlockSpec((1, state, channels), lambda i, p: (i, 0, 0)))
    out_specs += half_rows(width + LANES, spans, False)
    scratch = [
        pltpu.SemaphoreType.DMA,
        pltpu.VMEM((tokens, width), bf16),
        pltpu.VMEM((SPAN + 8, channels), f32),
        pltpu.VMEM((SPAN + 8, 2 * state), f32),
        pltpu.VMEM((state, channels), f32),
    ]
    if last_layer:
        shapes += [
            jax.ShapeDtypeStruct((tokens, width), bf16),
            jax.ShapeDtypeStruct((8, tokens), f32),
            jax.ShapeDtypeStruct((tokens, channels), f32),
        ]
        out_specs += [span_rows(width), pl.BlockSpec((8, SPAN), lambda i, p: (0, i)), span_rows(channels)]
        scratch.append(pltpu.VMEM((tokens, width), bf16))
    kernel = functools.partial(forward_kernel, plans, there_plan, head_dim)
    return span_call(
        kernel, "layer_forward", spans, place, operands, in_specs, shapes, out_specs, scratch, 20 * 10**9
    )


def run_gate(place, gathered, z, y, w, cx):
    tokens, channels = z.shape
    width = w.shape[0]
    spans = tokens // SPAN
    plan, pieces = cut_plan(*gathered), list(gathered[0])
    operands = [*pieces, z, y, w, cx]
    in_specs = [whole(p.shape) for p in pieces]
    in_specs += [span_rows(channels), span_rows(channels)]
    in_specs += [pl.BlockSpec((width, channels), lambda i, p: (0, 2)), whole(cx.shape)]
    shapes = [
        jax.ShapeDtypeStruct((tokens, width), bf16),
        jax.ShapeDtypeStruct((tokens, channels), bf16),
        jax.ShapeDtypeStruct((tokens, channels), f32),
        jax.ShapeDtypeStruct((tokens, channels), bf16),
        jax.ShapeDtypeStruct((8, channels), f32),
    ]
    out_specs = [span_rows(s.shape[1]) for s in shapes[:4]] + [whole(shapes[4].shape)]
    scratch = [pltpu.VMEM((tokens, pieces[0].shape[1]), bf16)]
    kernel = functools.partial(gate_kernel, plan, len(pieces), width)
    return span_call(
        kernel, "gate_backward", spans, place, operands, in_specs, shapes, out_specs, scratch, 6 * 10**9
    )


def run_scan(place, lead, xn, xp, bc, dt, hin, weights, small, pick, head_dim, inner_all):
    tokens, channels = xp.shape
    state = hin.shape[1]
    width = xn.shape[1]
    spans = tokens // SPAN
    with_gate = len(lead) == 4

    def rev(columns):
        return pl.BlockSpec((SPAN, columns), lambda i, p: (spans - 1 - i, 0))

    def halo(columns, rows):
        per = SPAN // rows
        return pl.BlockSpec(
            (rows, columns), lambda i, p: (jnp.maximum((spans - 1 - i) * per - 1, 0), 0)
        )

    operands = [*lead, xn, xp, xp, bc, bc, dt, hin, *weights, *small, pick]
    in_specs = [rev(channels)] * 2
    if with_gate:
        tok = pl.BlockSpec((8, SPAN), lambda i, p: (0, spans - 1 - i))
        in_specs = [rev(channels), tok, rev(channels), rev(channels)]
    in_specs += [
        rev(width),
        rev(channels),
        halo(channels, 16),
        rev(2 * state),
        halo(2 * state, 16),
        rev(LANES),
        pl.BlockSpec((1, state, channels), lambda i, p: (spans - 1 - i, 0, 0)),
    ]
    in_specs.append(whole((width, 2 * channels)))
    in_specs += [whole(v.shape) for v in operands[len(in_specs) :]]
    shapes = [
        jax.ShapeDtypeStruct((tokens, channels + LANES), bf16),
        jax.ShapeDtypeStruct((state * spans, SPAN), bf16),
        jax.ShapeDtypeStruct((state * spans, SPAN), bf16),
        jax.ShapeDtypeStruct((tokens // 2, width), bf16),
        jax.ShapeDtypeStruct((tokens // 2, width), bf16),
        jax.ShapeDtypeStruct((8, channels), f32),
        jax.ShapeDtypeStruct((8, LANES), f32),
        jax.ShapeDtypeStruct((16, 2 * state), bf16),
    ]
    out_specs = [rev(channels + LANES), whole(shapes[1].shape), whole(shapes[2].shape)]
    out_specs += half_rows(width, spans, True)
    out_specs += [whole(s.shape) for s in shapes[5:]]
    if with_gate:
        shapes = [jax.ShapeDtypeStruct((tokens, channels), bf16)] * 2 + shapes
        out_specs = [rev(channels)] * 2 + out_specs
    scratch = [
        pltpu.VMEM((8, 2 * state), f32),
        pltpu.VMEM((8, width), f32),
        pltpu.VMEM((SPAN + 8, channels), f32),
        pltpu.VMEM((SPAN + 8, 2 * state), f32),
        pltpu.VMEM((SPAN + 8, channels), f32),
        pltpu.VMEM((SPAN + 8, 2 * state), f32),
        pltpu.VMEM((state, channels), f32),
    ]
    kernel = functools.partial(scan_kernel, with_gate, head_dim, inner_all)
    return span_call(
        kernel, "scan_backward", spans, place, operands, in_specs, shapes, out_specs, scratch, 28 * 10**9
    )


def weight_kernel(n_pairs, split, place_ref, *refs):
    lefts, rights, outs = refs[:n_pairs], refs[n_pairs : 2 * n_pairs], refs[2 * n_pairs :]

    def write(out_ref):
        at = 0
        for left_ref, right_ref in zip(lefts, rights):
            columns = right_ref.shape[1]
            out_ref[:, at : at + columns] = dot(left_ref[...], right_ref[...], ROWS).astype(bf16)
            at += columns

    if not split:
        write(outs[0])
        return
    for k, out_ref in enumerate(outs):
        pl.when(pl.program_id(0) == k)(functools.partial(write, out_ref))


def weight_products(place, pairs, split=True):
    tokens = pairs[0][0].shape[0]
    rows = max(left.shape[1] for left, _ in pairs)
    block = rows // 4

    def at(i, p):
        return lax.rem(p[3] + i, NX) if split else i

    lefts, rights, columns = [], [], []
    for left, right in pairs:
        quarter = left.shape[1] == block
        cut, uncut = (lambda i, p: (0, at(i, p))), (lambda i, p: (0, 0))
        lefts.append(pl.BlockSpec((tokens, block), uncut if quarter else cut))
        wide = block if quarter else right.shape[1]
        rights.append(pl.BlockSpec((tokens, wide), cut if quarter else uncut))
        columns.append(wide)
    columns = sum(columns)
    if split:
        out_specs = [whole((block, columns))] * 4
        shapes = [jax.ShapeDtypeStruct((block, columns), bf16)] * 4
    else:
        out_specs = [pl.BlockSpec((block, columns), lambda i, p: (i, 0))]
        shapes = [jax.ShapeDtypeStruct((rows, columns), bf16)]
    out = pl.pallas_call(
        functools.partial(weight_kernel, len(pairs), split),
        grid_spec=pltpu.PrefetchScalarGridSpec(
            num_scalar_prefetch=1, grid=(4,), in_specs=lefts + rights, out_specs=out_specs
        ),
        out_shape=shapes,
        compiler_params=pltpu.CompilerParams(vmem_limit_bytes=VMEM_BYTES),
        cost_estimate=pl.CostEstimate(
            flops=2 * tokens * rows * columns, bytes_accessed=8 * 10**6, transcendentals=0
        ),
        name="weight_products",
    )(place, *[left for left, _ in pairs], *[right for _, right in pairs])
    return out if split else out[0]


SIZES = (4, 2, 2, 2, 4)
NX, NYL, NC, NYH, NZ = SIZES
EVERY = [
    (x, yl, c, yh, z)
    for x in range(NX)
    for yl in range(NYL)
    for c in range(NC)
    for yh in range(NYH)
    for z in range(NZ)
]


def linear(x, yl, c, yh, z):
    return ((((x % NX) * NYL + yl % NYL) * NC + c % NC) * NYH + yh % NYH) * NZ + z % NZ


def send(v, step, only=None):
    pairs = [(linear(*d), linear(*step(*d))) for d in EVERY if only is None or only(*d)]
    return lax.ppermute(v, ("dp", "tensor"), pairs)


def send_z(v, k):
    return send(v, lambda x, yl, c, yh, z: (x, yl, c, yh, z + k))


def send_core(v):
    return send(v, lambda x, yl, c, yh, z: (x, yl, c + 1, yh, z))


def trade(v, k):
    return send(v, lambda x, yl, c, yh, z: (x, yl, yh, c, z + k))


def traded(v):
    return send(v, lambda x, yl, c, yh, z: (x, yl, yh, c, z), lambda x, yl, c, yh, z: c != yh)


def trade_places(v):
    _, _, core, yh, _ = position()
    return jnp.where(core == yh, v, traded(v))


def position():
    dp, tensor = lax.axis_index("dp"), lax.axis_index("tensor")
    return dp // (NYL * NC), dp // NC % NYL, dp % NC, tensor // NZ, tensor % NZ


def gather(v, parts, traded_own=None, later=()):
    arrays, sources = [], []
    for k in (0, 1, 3, 2):
        if traded_own is not None:
            piece = trade(v, k) if k else traded_own
        else:
            piece = send_z(v, k) if k else v
        arrays += [piece, send_core(after(piece, *later) if later else piece)]
        sources += [(False, -k % NZ, 0), (True, -k % NZ, 0)]
    return arrays, sources, parts


def cut_plan(arrays, sources, parts):
    plan = []
    for number, (piece, (other, dz, first)) in enumerate(zip(arrays, sources)):
        base = 0
        for out, per in enumerate(parts):
            begin, end = max(first, base), min(first + piece.shape[0], base + per)
            if begin < end:
                plan.append((number, other, dz, begin - first, out, per, begin - base, end - begin))
            base += per
    return plan


def fold(mine, other):
    _, _, _, _, z = position()
    rows = mine.shape[0] // NZ
    blocks = []
    for k in range(NZ):
        at = (z + k) % NZ * rows
        a = lax.dynamic_slice_in_dim(mine, at, rows, 0).astype(f32)
        blocks.append(a + lax.dynamic_slice_in_dim(other, at, rows, 0).astype(f32))
    return blocks


def fold_beside(pairs):
    folded = [fold(mine, send_core(other)) for mine, other in pairs]
    return [jnp.concatenate([blocks[k] for blocks in folded], axis=1) for k in range(NZ)]


def scatter(*pairs, meanwhile=None):
    own, one, two, three = fold_beside(pairs)
    if meanwhile is not None:
        two = after(two, meanwhile)
    return [own] + [send_z(b.astype(bf16), k) for k, b in ((1, one), (2, two), (3, three))]


def scatter_with_sum(mine, other, shared, meanwhile):
    half = mine.shape[0]
    rows = half // NZ
    got = after(send_core(jnp.concatenate([other, shared], axis=0)), *meanwhile)
    blocks = fold(mine, got[:half])
    total_shared = shared.astype(f32) + got[half:].astype(f32)
    packed = total_shared.astype(bf16)
    total = blocks[0]
    for k in range(1, NZ):
        got = send_z(jnp.concatenate([blocks[k].astype(bf16), packed], axis=0), k)
        total = total + got[:rows].astype(f32)
        total_shared = total_shared + got[rows:].astype(f32)
    return total, total_shared


def sum_members(v):
    both = v + send_core(v)
    total = both
    for k in range(1, NZ):
        total = total + send_z(both, k)
    return total


def send_far(v):
    return send(v, lambda x, yl, c, yh, z: (x, yl, c, yh + 1, z), lambda x, yl, c, yh, z: c != yh)


def sum_far(v, far=None):
    far = send_far(v) if far is None else far
    return (v.astype(f32) + far.astype(f32)).astype(bf16)


def halve(v):
    _, _, core, yh, _ = position()
    half = v.shape[0] // 2
    near = send(
        v[half:], lambda x, yl, c, yh, z: (x, yl, c + 1, yh, z), lambda x, yl, c, yh, z: c == yh
    )
    return jnp.where(core == yh, v[:half], near)


def sum_beside(part):
    beside = send(part, lambda x, yl, c, yh, z: (x, yl + 1, c, yh, z))
    return (part.astype(f32) + beside.astype(f32)).astype(bf16)


def sum_x(blocks):
    total = blocks[0].astype(f32)
    for k in range(1, NX):
        got = send(blocks[k], lambda x, yl, c, yh, z, k=k: (x + k, yl, c, yh, z))
        total = total + got.astype(f32)
    return total.astype(bf16)


def cut_x(v):
    x = position()[0]
    rows = v.shape[0] // NX
    return [lax.dynamic_slice_in_dim(v, (x + k) % NX * rows, rows, 0) for k in range(NX)]


def collect_x(part, meanwhile=()):
    parts = [part]
    for k in range(1, NX):
        got = send(part, lambda x, yl, c, yh, z, k=k: (x + k, yl, c, yh, z))
        parts.append(after(got, *meanwhile) if meanwhile else got)
    return jnp.stack(parts)


def write_kernel(plan, n_kept, place_ref, here_ref, there_ref, *refs):
    rows = here_ref.shape[1]

    def write(ref):
        for (column, kind, wide, by_half), out_ref in zip(plan, refs[n_kept:]):
            for x in range(NX):
                value = ref[lax.rem(place_ref[3] + NX - x, NX), :, column : column + wide].astype(f32)
                if kind != "blocks":
                    out_ref[0, 0 if by_half else x, x if by_half else 0] = value
                elif by_half:
                    at = x // 2 * wide
                    out_ref[0, x % 2 * rows : (x % 2 + 1) * rows, at : at + wide] = value
                else:
                    out_ref[0, :, x * wide : (x + 1) * wide] = value

    here = (pl.program_id(0) == 0) == (place_ref[2] == 1)

    @pl.when(here)
    def _():
        write(here_ref)

    @pl.when(jnp.logical_not(here))
    def _():
        write(there_ref)


def write_sums(place, halves, outputs):
    rows, columns = halves[0].shape[1:]
    total = 2 * NX * rows
    wide = total // 4
    plan, shapes, specs, finals, kept, alias = [], [], [], [], [], {}
    for column, kind, layer, array, by_half in outputs:
        lanes = LANES if kind == "flat" else wide
        layers = 1 if kind == "flat" else 2
        plan.append((column, kind, lanes, by_half))
        if kind == "blocks":
            shape = (layers, wide, total)
            if by_half:
                spec = pl.BlockSpec((1, wide, total // 2), lambda h, p, layer=layer: (layer, 0, h))
            else:
                spec = pl.BlockSpec((1, rows, total), lambda h, p, layer=layer: (layer, h, 0))
            finals.append(shape)
        elif by_half:
            shape = (layers, 2, NX, rows, lanes)
            spec = pl.BlockSpec((1, 1, NX, rows, lanes), lambda h, p, layer=layer: (layer, h, 0, 0, 0))
            finals.append((layers, total, lanes))
        else:
            shape = (layers, NX, 2, rows, lanes)
            spec = pl.BlockSpec((1, NX, 1, rows, lanes), lambda h, p, layer=layer: (layer, 0, h, 0, 0))
            finals.append((layers, total, lanes))
        shapes.append(jax.ShapeDtypeStruct(shape, f32))
        specs.append(spec)
        if array is not None:
            alias[3 + len(kept)] = len(shapes) - 1
            kept.append(array.reshape(shape))
    piece = pl.BlockSpec((NX, rows, columns), lambda h, p: (0, 0, 0))
    written = pl.pallas_call(
        functools.partial(write_kernel, plan, len(kept)),
        grid_spec=pltpu.PrefetchScalarGridSpec(
            num_scalar_prefetch=1,
            grid=(2,),
            in_specs=[piece, piece] + [pl.BlockSpec(memory_space=pl.ANY)] * len(kept),
            out_specs=specs,
        ),
        out_shape=shapes,
        input_output_aliases=alias,
        compiler_params=pltpu.CompilerParams(vmem_limit_bytes=VMEM_BYTES),
        name="write_sums",
    )(place, *halves, *kept)
    return [v.reshape(final) for v, final in zip(written, finals)]


def row_call(kernel, name, operands, shapes):
    return pl.pallas_call(
        kernel,
        grid=(1,),
        in_specs=[pl.BlockSpec((rows, v.shape[1]), lambda i: (0, 0)) for v, rows in operands],
        out_specs=[pl.BlockSpec(s.shape, lambda i, n=len(s.shape): (0,) * n) for s in shapes],
        out_shape=shapes,
        compiler_params=pltpu.CompilerParams(vmem_limit_bytes=VMEM_BYTES),
        name=name,
    )(*[v for v, _ in operands])


def inverse_rms(v):
    return lax.rsqrt(jnp.mean(v * v, axis=-1, keepdims=True) + EPS)


def first_kernel(packed_ref, gain_ref, out_ref):
    rows = 128
    v = packed_ref[0:rows, :].astype(f32)
    out_ref[0:rows, :] = (v * inverse_rms(v) * gain_ref[...]).astype(bf16)
    out_ref[rows:, :] = packed_ref[rows : out_ref.shape[0], :]


def add_terms(own_ref, a_ref, b_ref, c_ref):
    total = own_ref[...].astype(f32) + a_ref[...].astype(f32)
    return total + (b_ref[...].astype(f32) + c_ref[...].astype(f32))


def unscaled_output(inner_all, terms, width):
    total = add_terms(*terms)
    squares = total[:, width : width + 1] + total[:, width + 1 : width + 2]
    gate_rms = lax.rsqrt(squares / inner_all + EPS)
    return gate_rms, total[:, :width] * gate_rms


def middle_kernel(inner_all, own_ref, a_ref, b_ref, c_ref, res_ref, gain_ref, res1_ref, mixed_ref, rms_ref, normed_ref):
    width = res_ref.shape[1]
    gate_rms, mixed = unscaled_output(inner_all, (own_ref, a_ref, b_ref, c_ref), width)
    res = res_ref[...].astype(f32) + mixed
    res1_ref[...] = res
    mixed_ref[...] = mixed
    rms_ref[...] = jnp.broadcast_to(gate_rms, rms_ref.shape)
    normed_ref[...] = (res * inverse_rms(res) * gain_ref[...]).astype(bf16)


def input_gradient(grad_normed, res, d_res, gain):
    inv = inverse_rms(res)
    scaled = grad_normed * gain
    dots = jnp.sum(scaled * res, axis=-1, keepdims=True) / res.shape[1]
    return d_res + inv * scaled - res * (inv * inv * inv) * dots


def between_kernel(inner_all, own_ref, a_ref, b_ref, c_ref, res_ref, dres_ref, gain_ref, mixed_ref, rms_ref, out_ref, sent_ref):
    width = res_ref.shape[1]
    grad_normed = add_terms(*(ref.at[:, 0:width] for ref in (own_ref, a_ref, b_ref, c_ref)))
    d_res = input_gradient(grad_normed, res_ref[...], dres_ref[...].astype(f32), gain_ref[...])
    out_ref[...] = d_res
    g_mixed = d_res.astype(bf16)
    sent_ref[:, :width] = g_mixed
    gate_rms = rms_ref[:, 0:1]
    products = jnp.sum(g_mixed.astype(f32) * mixed_ref[...], axis=-1, keepdims=True)
    coef = gate_rms * gate_rms * products / inner_all
    lane = lax.broadcasted_iota(jnp.int32, rms_ref.shape, 1)
    rms_high = gate_rms.astype(bf16).astype(f32)
    coef_high = coef.astype(bf16).astype(f32)
    extra = jnp.where(lane == 0, rms_high, jnp.where(lane == 1, gate_rms - rms_high, 0.0))
    extra = jnp.where(lane == 2, coef_high, jnp.where(lane == 3, coef - coef_high, extra))
    sent_ref[:, width:] = extra.astype(bf16)


def end_kernel(own_ref, a_ref, b_ref, c_ref, res_ref, dres_ref, gain_ref, hidden_ref, out_ref):
    width = res_ref.shape[1]
    grad_normed = add_terms(own_ref, a_ref, b_ref, c_ref)
    grad = input_gradient(grad_normed, res_ref[...].astype(f32), dres_ref[...], gain_ref[...])
    out_ref[:, :width] = hidden_ref[...]
    out_ref[:, width:] = grad.astype(bf16)


def last_kernel(inner_all, own_ref, a_ref, b_ref, c_ref, res_ref, out_ref):
    _, mixed = unscaled_output(inner_all, (own_ref, a_ref, b_ref, c_ref), res_ref.shape[1])
    out_ref[...] = (res_ref[...] + mixed).astype(bf16)


TINY_ROWS = 56


def small_kernel(head_dim, ends, narrow0_ref, narrow1_ref, gain_ref, pick_ref, norm_ref, wbc_ref, wdt_ref, cx_ref,
                 cxb_ref, cbc_ref, cbcb_ref, dtb_ref, alog_ref, skip_ref, ng_ref):
    bc_at, tiny_at = ends
    heads = wdt_ref.shape[0]
    channels = cx_ref.shape[2]
    both = cbc_ref.shape[2]
    lanes = narrow0_ref.shape[1] - tiny_at
    for layer, ref in enumerate((narrow0_ref, narrow1_ref)):
        columns = jnp.transpose(ref[...])
        wbc_ref[layer] = columns[bc_at:tiny_at]
        wdt_ref[:, layer, :] = columns[0:heads]
    tiny = jnp.concatenate(
        [narrow0_ref[i * TINY_ROWS : (i + 1) * TINY_ROWS, tiny_at:] for i in range(channels // lanes)], axis=1
    )
    lines = norm_ref.shape[1] // both
    for layer in range(2):
        rows = tiny[8 * layer : 8 * layer + 8]
        cx_ref[layer] = rows[0:4]
        cxb_ref[layer : layer + 1, :] = rows[4:5]
        ng_ref[layer : layer + 1, :] = rows[5:6]
        skip_ref[layer : layer + 1, :] = dot(rows, pick_ref[...], PLAIN, highest)[6:7, 0:heads]
        at = 16 + 2 * layer
        dtb_ref[layer : layer + 1, :] = tiny[at : at + 1, 0:heads]
        alog_ref[layer : layer + 1, :] = tiny[at + 1 : at + 2, 0:heads]
        at = 20 + 16 * layer
        norm = jnp.concatenate([tiny[at + i : at + i + 1, 0:both] for i in range(lines)], axis=1)
        norm_ref[layer : layer + 1, :] = norm / gain_ref[layer : layer + 1, :]
        cbc_ref[layer] = tiny[at + lines : at + lines + 4, 0:both]
        cbcb_ref[layer : layer + 1, :] = tiny[at + lines + 4 : at + lines + 5, 0:both]


def after(v, *others):
    return lax.optimization_barrier((v, *others))[0]


def pad_to(v, rows, lanes):
    return jnp.pad(v, ((0, rows - v.shape[0]), (0, lanes - v.shape[1])))


def local(
    hidden_in,
    grad_out,
    norm_in,
    w_z,
    w_x,
    w_bc,
    w_dt,
    conv_x,
    conv_x_bias,
    conv_bc,
    conv_bc_bias,
    dt_bias,
    a_log,
    skip,
    norm_gate,
    w_out,
):
    layers, width, channels = w_z.shape
    heads = w_dt.shape[2]
    head_dim = channels // heads
    both = conv_bc.shape[2]
    state = both // 2
    members = NC * NZ
    inner_all = channels * members
    rows = hidden_in.shape[1]
    bc_rows = both // members
    x, _, core, yh, z = position()
    stays = core == yh
    place = jnp.stack([core, z, stays, x]).astype(jnp.int32)
    full = jax.ShapeDtypeStruct((rows, width), f32)

    def pack_weights(layer):
        return jnp.concatenate([w_z[layer], w_x[layer], w_out[layer].T], axis=1)

    bc_t = jnp.swapaxes(w_bc, 1, 2)
    dt_t = jnp.pad(jnp.swapaxes(w_dt, 1, 2), ((0, 0), (0, 8 - heads), (0, 0)))
    per_channel = jnp.concatenate(
        [conv_x, conv_x_bias[:, None], norm_gate[:, None], jnp.repeat(skip, head_dim, axis=1)[:, None]],
        axis=1,
    )
    per_channel = jnp.pad(per_channel, ((0, 0), (0, 1), (0, 0)))
    per_head = jnp.stack([dt_bias, -jnp.exp(a_log)], axis=1)
    per_head = jnp.pad(per_head, ((0, 0), (0, 6), (0, LANES - heads)))
    little = jnp.concatenate([per_channel, per_head], axis=2).reshape(layers * 8, channels + LANES)
    high = little.astype(bf16)
    low = (little - high.astype(f32)).astype(bf16)
    lines = pad_to(jnp.concatenate([high, low], axis=1), layers * 8, width)
    packed = jnp.concatenate([hidden_in[0], bc_t[0], dt_t.reshape(layers * 8, width), lines], axis=0)
    packed = trade_places(packed)
    lines = packed[packed.shape[0] - layers * 8 :].astype(f32)
    little = lines[:, : channels + LANES] + lines[:, channels + LANES : 2 * (channels + LANES)]
    little = little.reshape(layers, 8, channels + LANES)

    w0 = pack_weights(0)
    w0 = w0, [traded(after(w0, packed))], [(0, None)]
    grads = jnp.concatenate([grad_out[0], bc_t[1]], axis=0)

    [sent] = row_call(
        first_kernel,
        "first_norm",
        [(packed, packed.shape[0]), (norm_in[0:1], 1)],
        [jax.ShapeDtypeStruct((rows + bc_rows, width), bf16)],
    )
    gathered0 = gather(sent, (rows, bc_rows))
    wdt = [pad_to(packed[rows + bc_rows + 8 * l : rows + bc_rows + 8 * (l + 1)], LANES, width) for l in range(layers)]
    smalls = []
    for layer in range(layers):
        cbc = jnp.concatenate([conv_bc[layer], conv_bc_bias[layer][None], jnp.zeros((3, both), f32)], axis=0)
        smalls.append((little[layer, :, :channels], cbc, little[layer, :, channels:]))
    channel_head = jnp.arange(channels) // head_dim
    pick = (channel_head[:, None] == jnp.arange(LANES)[None, :]).astype(f32)

    out0 = run_forward(place, [gathered0], w0, wdt[0], smalls[0], state, head_dim)
    w0, xn0, wbc0, z0, xp0, bc0, dt0, y0, hin0, mine, other = out0
    grads = after(grads, sent)
    gathered_grad = gather(grads, (rows, bc_rows), jnp.where(stays, grads, after(traded(grads), mine)), (mine,))
    grad_held = gathered_grad[0][0]
    terms = scatter((mine, after(other, *gathered_grad[0][::2])))
    w1 = pack_weights(1)
    w1 = w1, [traded(after(w1, terms[0]))], [(0, None)]
    res1, mixed0, rms0, normed1 = row_call(
        functools.partial(middle_kernel, inner_all),
        "middle_norm",
        [(v, rows) for v in terms] + [(packed, rows), (norm_in[1:2], 1)],
        [full, full, jax.ShapeDtypeStruct((rows, LANES), f32), jax.ShapeDtypeStruct((rows, width), bf16)],
    )
    gathered1 = gather(normed1, (rows,))
    out1 = run_forward(
        place, [gathered1, gathered_grad], w1, wdt[1], smalls[1], state, head_dim
    )
    w1, xn1, wbc1, z1, xp1, bc1, dt1, y1, hin1, mine, other, grad_rows1, sums, gg1 = out1
    sums = sum_members(sums)

    home = fold(mine, send_core(other))
    sums = after(sums, *home)
    home = home[:1] + [send_z(home[k].astype(bf16), k) for k in range(1, NZ)]
    back1 = run_scan(
        place, (gg1, sums, z1, y1), xn1, xp1, bc1, dt1, hin1, (w1, wbc1, wdt[1]), smalls[1], pick, head_dim,
        inner_all,
    )
    dz1, go1, dxt1, *bc_halves, mine, other, acc1, acch1, shared1 = back1
    early1 = weight_products(place, [(xn1, dz1), (go1, grad_rows1)], split=False)
    terms = scatter((mine, after(other, *home)), bc_halves, meanwhile=early1)
    early1_far = send_far(early1)
    [hidden_out] = row_call(
        functools.partial(last_kernel, inner_all),
        "last_output",
        [(after(home[0], terms[1]), rows)] + [(v, rows) for v in home[1:]] + [(res1, rows)],
        [jax.ShapeDtypeStruct((rows, width), bf16)],
    )
    d_res1, sent = row_call(
        functools.partial(between_kernel, inner_all),
        "between_layers",
        [(v, rows) for v in terms]
        + [(res1, rows), (grad_held, rows), (norm_in[1:2], 1), (mixed0, rows), (rms0, rows)],
        [full, jax.ShapeDtypeStruct((rows, width + LANES), bf16)],
    )
    gathered_back = gather(sent, (rows,))

    bc_at = channels + bc_rows

    def with_bc(dxt, bc_sum):
        by_token = bc_sum.reshape(-1, bc_rows, SPAN).swapaxes(1, 2).reshape(-1, bc_rows)
        spread = jnp.pad(by_token, ((0, 0), (bc_at, dxt.shape[1] - bc_at - bc_rows)))
        return dxt + spread.astype(bf16)

    dxt1 = with_bc(dxt1, sum(v[:, width:].astype(f32) for v in terms))

    early1 = halve(sum_far(early1, after(early1_far, sent)))
    z0 = after(z0, early1)
    early1 = sum_x(cut_x(early1))
    grad_rows0, dz0, dy0, go0, acc_gate0 = run_gate(place, gathered_back, z0, y0, w0, smalls[0][0])
    dz0 = after(dz0, early1)
    early = weight_products(place, [(xn0, dz0), (go0, grad_rows0), (xn1, dxt1)])
    dy0 = after(dy0, *early)
    early = sum_x(early)
    early1 = sum_beside(after(early1, dz0))
    back0 = run_scan(
        place, (dy0, dz0), xn0, xp0, bc0, dt0, hin0, (w0, wbc0, wdt[0]), smalls[0], pick, head_dim, inner_all
    )
    dxt0, *bc_halves, mine, other, acc0, acch0, shared0 = back0
    shared = jnp.concatenate([shared0, shared1], axis=0)
    bc_sum, shared = scatter_with_sum(*bc_halves, shared, (early,))
    tiny_at = bc_at + bc_rows
    tiny_lanes = channels + LANES - tiny_at
    tiny = jnp.concatenate(
        [acc0 + acc_gate0, acc1] + [pad_to(v, v.shape[0], channels) for v in (acch0[0:2], acch1[0:2], shared)],
        axis=0,
    )
    tiny = pad_to(tiny, TINY_ROWS, channels)
    tiny = [tiny[:, i * tiny_lanes : (i + 1) * tiny_lanes] for i in range(channels // tiny_lanes)]
    tiny = pad_to(jnp.concatenate(tiny, axis=0), width, tiny_lanes)
    tiny = jnp.pad(tiny, ((0, 0), (tiny_at, 0))).astype(bf16)
    early = halve(sum_far(after(early, dxt0)))
    late = weight_products(place, [(xn0, after(with_bc(dxt0, bc_sum), early))])
    home = fold(mine, send_core(after(other, late[0])))
    early = sum_beside(early)
    tiny = after(tiny, early)
    late = [v + t for v, t in zip(late, cut_x(tiny))]
    late = sum_x(late)

    terms = home[:1] + [send_z(home[k].astype(bf16), k) for k in range(1, NZ)]
    [outputs] = row_call(
        end_kernel,
        "outputs",
        [(v, rows) for v in terms] + [(packed, rows), (d_res1, rows), (norm_in[0:1], 1), (hidden_out, rows)],
        [jax.ShapeDtypeStruct((rows, 2 * width), bf16)],
    )
    outputs_there = traded(outputs)
    outputs_home = jnp.where(stays, outputs, outputs_there).astype(f32)

    early = after(collect_x(early), outputs)
    early = early, send_core(early)
    early1 = collect_x(after(early1, early[0]))
    early1 = early1, send_core(early1)
    g_wz, g_wo, g_wx, narrow1 = write_sums(
        place,
        early,
        [
            (0, "rows", 0, None, False),
            (channels, "blocks", 0, None, False),
            (2 * channels, "rows", 1, None, False),
            (3 * channels, "flat", 0, None, False),
        ],
    )
    g_wz, g_wo = write_sums(
        place, early1, [(0, "rows", 1, g_wz, True), (channels, "blocks", 1, g_wo, True)]
    )
    late = collect_x(sum_beside(halve(sum_far(after(late, outputs_there)))), (g_wz,))
    late = late, send_core(late)
    g_wx, narrow0 = write_sums(
        place, late, [(0, "rows", 0, g_wx, False), (channels, "flat", 0, None, False)]
    )

    narrow0, narrow1 = narrow0[0], narrow1[0]
    small = row_call(
        functools.partial(small_kernel, head_dim, (bc_at - channels, tiny_at - channels)),
        "small_gradients",
        [(narrow0, width), (narrow1, width), (norm_in, layers), (pick, channels)],
        [
            jax.ShapeDtypeStruct(shape, f32)
            for shape in (
                norm_in.shape,
                (layers, bc_rows, width),
                (heads, layers, width),
                conv_x.shape,
                conv_x_bias.shape,
                conv_bc.shape,
                conv_bc_bias.shape,
                dt_bias.shape,
                a_log.shape,
                skip.shape,
                norm_gate.shape,
            )
        ],
    )
    return (
        outputs_home[None, :, :width],
        outputs_home[None, :, width:],
        small[0],
        g_wz,
        g_wx,
        jnp.transpose(small[1], (0, 2, 1)),
        jnp.transpose(small[2], (1, 2, 0)),
        *small[3:],
        g_wo,
    )


def solution(mesh):
    specs_in = (
        P("dp", "tensor", None),
        P("dp", "tensor", None),
        P(),
        P(None, None, "tensor"),
        P(None, None, "tensor"),
        P(None, None, "tensor"),
        P(None, None, "tensor"),
        P(None, None, "tensor"),
        P(None, "tensor"),
        P(),
        P(),
        P(None, "tensor"),
        P(None, "tensor"),
        P(None, "tensor"),
        P(None, "tensor"),
        P(None, "tensor", None),
    )
    specs_out = (
        P("dp", "tensor", None),
        P("dp", "tensor", None),
        P(),
        P(None, None, "tensor"),
        P(None, None, "tensor"),
        P(None, None, "tensor"),
        P(None, None, "tensor"),
        P(None, None, "tensor"),
        P(None, "tensor"),
        P(),
        P(),
        P(None, "tensor"),
        P(None, "tensor"),
        P(None, "tensor"),
        P(None, "tensor"),
        P(None, "tensor", None),
    )
    return jax.shard_map(
        local, mesh=mesh, in_specs=specs_in, out_specs=specs_out, check_vma=False
    )
```

```python
import functools

import jax
import jax.numpy as jnp
from jax import lax
from jax.experimental import pallas as pl
from jax.experimental.pallas import tpu as pltpu
from jax.sharding import PartitionSpec as P

SPAN = 256
EPS = 1e-05
LANES = 128
VMEM_BYTES = 56 * 1024 * 1024

f32 = jnp.float32
bf16 = jnp.bfloat16
highest = lax.Precision.HIGHEST

ROWS = ((0,), (0,))
COLS = ((1,), (1,))
PLAIN = ((1,), (0,))


def dot(left, right, dims=PLAIN, precision=None):
    return lax.dot_general(
        left, right, (dims, ((), ())), preferred_element_type=f32, precision=precision
    )


def sigmoid(v):
    return 0.5 + 0.5 * jnp.tanh(0.5 * v)


def dot_exact(left, right, dims=PLAIN, terms=3):
    parts = []
    for _ in range(terms):
        parts.append(right.astype(bf16))
        right = right - parts[-1].astype(f32)
    out = dot(left.astype(bf16), jnp.concatenate(parts, axis=1), dims)
    width = out.shape[1] // terms
    return sum(out[:, i * width : (i + 1) * width] for i in range(terms))


def sum_heads(v, pick):
    high = v.astype(bf16)
    low = (v - high.astype(f32)).astype(bf16)
    return dot(high, pick) + dot(low, pick)


def softplus(v):
    return jnp.maximum(v, 0.0) + jnp.log1p(jnp.exp(-jnp.abs(v)))


def spread_heads(per_head, channels, head_dim):
    rows = per_head.shape[0]
    per_tile = LANES // head_dim
    lane = lax.broadcasted_iota(jnp.int32, (rows, LANES), 1)
    tiles = []
    for tile in range(channels // LANES):
        out = jnp.broadcast_to(
            per_head[:, tile * per_tile : tile * per_tile + 1], (rows, LANES)
        )
        for sub in range(1, per_tile):
            head = tile * per_tile + sub
            out = jnp.where(
                lane >= sub * head_dim,
                jnp.broadcast_to(per_head[:, head : head + 1], (rows, LANES)),
                out,
            )
        tiles.append(out)
    return jnp.concatenate(tiles, axis=1)


def conv_taps(buf, taps, offset, width):
    out = offset
    for j in range(4):
        out = out + taps[j : j + 1] * buf[pl.ds(5 + j, width), :]
    return out


def decay_matrix(mask, cum_col, cum_row):
    return jnp.exp(jnp.where(mask, cum_col - cum_row, -1e30))


def span_values(dt, head_ref):
    length = dt.shape[0]
    rows = lax.broadcasted_iota(jnp.int32, (length, length), 0)
    cols = lax.broadcasted_iota(jnp.int32, (length, length), 1)
    mask = rows >= cols
    pre = dt + head_ref[0:1, :]
    step = softplus(pre)
    rate = head_ref[1:2, :] * step
    cum = dot_exact(mask, rate)
    return mask, pre, step, rate, cum


def put_half(place_ref, span, half, mine_ref, other_ref, value):
    own = span // half == place_ref[0]

    @pl.when(own)
    def _():
        mine_ref[...] = value

    @pl.when(jnp.logical_not(own))
    def _():
        other_ref[...] = value


def place_pieces(plan, place_ref, pieces, outs):
    core, z = place_ref[0], place_ref[1]
    for piece, other, dz, start, out, per, offset, rows in plan:
        member = (1 - core if other else core) * NZ + lax.rem(z + dz, NZ)
        row = pl.multiple_of(member * per + offset, 16)
        outs[out][pl.ds(row, rows), :] = pieces[piece][start : start + rows, :]


def put_columns(place_ref, span, mine_ref, other_ref, columns):
    per = columns.shape[0] // (NC * NZ)
    rows = mine_ref.shape[0] // NZ

    def place_columns(core, ref):
        for z in range(NZ):
            at = (core * NZ + z) * per
            ref[pl.ds(pl.multiple_of(z * rows + span * per, 16), per), :] = columns[at : at + per, :]

    for core in range(NC):
        mine = place_ref[0] == core

        @pl.when(mine)
        def _(core=core):
            place_columns(core, mine_ref)

        @pl.when(jnp.logical_not(mine))
        def _(core=core):
            place_columns(core, other_ref)


def forward_kernel(plans, there_plan, head_dim, place_ref, *refs):
    last_layer = len(plans) == 2
    refs = list(refs)

    def take(count):
        taken = refs[:count]
        del refs[:count]
        return taken

    piece_refs = [take(count) for _, count in plans]
    [w_here] = take(1)
    w_there = take(len(there_plan))
    wdt_ref, cx_ref, cbc_ref, head_ref = take(4)
    w_ref, xn_ref, wbc_ref, z_ref, xp_ref, bc_ref, dt_ref, y_ref, hin_ref, mine_ref, other_ref = take(11)
    if last_layer:
        g_ref, sums_ref, gg_ref = take(3)
    w_sem, xn_all, xbuf, bbuf, hst = take(5)
    if last_layer:
        [g_all] = take(1)
    length = z_ref.shape[0]
    channels = cx_ref.shape[1]
    state = hst.shape[0]
    span = pl.program_id(0)

    @pl.when(span == 0)
    def _():
        @pl.when(place_ref[2] == 1)
        def _():
            pltpu.make_async_copy(w_here, w_ref, w_sem).start()

        @pl.when(place_ref[2] == 0)
        def _():
            for part, (start, k) in zip(w_there, there_plan):
                rows = part.shape[0]
                if k is not None:
                    start = pl.multiple_of(lax.rem(place_ref[3] + NX - k, NX) * rows, 16)
                pltpu.make_async_copy(part, w_ref.at[pl.ds(start, rows), :], w_sem).start()

        if last_layer:
            place_pieces(plans[0][0], place_ref, piece_refs[0], [xn_all])
            place_pieces(plans[1][0], place_ref, piece_refs[1], [g_all, wbc_ref])
        else:
            place_pieces(plans[0][0], place_ref, piece_refs[0], [xn_all, wbc_ref])
        xbuf[0:8, :] = jnp.zeros((8, channels), f32)
        bbuf[0:8, :] = jnp.zeros((8, 2 * state), f32)
        hst[...] = jnp.zeros_like(hst)
        pltpu.make_async_copy(w_here, w_ref, w_sem).wait()

    here = pl.ds(pl.multiple_of(span * length, length), length)
    xn = xn_all[here, :]
    xn_ref[...] = xn
    zx = dot(xn, w_ref[:, : 2 * channels])
    z = zx[:, :channels]
    z_ref[...] = z.astype(bf16)
    xp = zx[:, channels:]
    xp_ref[...] = xp.astype(bf16)
    xbuf[8:, :] = xp
    bc = dot(xn, wbc_ref[...], COLS).astype(bf16)
    bc_ref[...] = bc
    bbuf[8:, :] = bc.astype(f32)
    dt = dot(xn, wdt_ref[...], COLS)
    dt_ref[...] = dt

    pre_x = conv_taps(xbuf, cx_ref[0:4, :], cx_ref[4:5, :], length)
    xc = pre_x * sigmoid(pre_x)
    pre_bc = conv_taps(bbuf, cbc_ref[0:4, :], cbc_ref[4:5, :], length)
    bcc = (pre_bc * sigmoid(pre_bc)).astype(bf16)
    xbuf[0:8, :] = xbuf[length : length + 8, :]
    bbuf[0:8, :] = bbuf[length : length + 8, :]
    b_mat = bcc[:, :state]
    c_mat = bcc[:, state:]

    mask, _, step, _, cum = span_values(dt, head_ref)
    cum_t = jnp.transpose(cum)
    scores = dot(c_mat, b_mat, COLS)
    xs = xc * spread_heads(step, channels, head_dim)
    xs_b = xs.astype(bf16)
    lane = lax.broadcasted_iota(jnp.int32, (length, LANES), 1)
    per_tile = LANES // head_dim
    tiles = []
    for tile in range(channels // LANES):
        xs_tile = xs_b[:, tile * LANES : (tile + 1) * LANES]
        out = None
        for sub in range(per_tile):
            head = tile * per_tile + sub
            decay = decay_matrix(mask, cum[:, head : head + 1], cum_t[head : head + 1, :])
            part = dot((scores * decay).astype(bf16), xs_tile)
            out = part if out is None else jnp.where(lane >= sub * head_dim, part, out)
        tiles.append(out)
    hin = hst[...]
    hin_ref[0] = hin
    last = cum[length - 1 : length, :]
    y = jnp.concatenate(tiles, axis=1)
    y = y + dot(c_mat, hin.astype(bf16)) * spread_heads(jnp.exp(cum), channels, head_dim)
    y = y + cx_ref[6:7, :] * xc
    y_ref[...] = y.astype(bf16)
    tail = spread_heads(jnp.exp(last - cum), channels, head_dim)
    keep = spread_heads(jnp.exp(last), channels, head_dim)
    hst[...] = keep * hin + dot(b_mat, (tail * xs).astype(bf16), ROWS)

    gated = y * (z * sigmoid(z))
    scaled = gated * cx_ref[5:6, :]
    squares = jnp.sum(gated * gated, axis=1, keepdims=True)
    high = squares.astype(bf16).astype(f32)
    extra = jnp.where(lane == 0, high, jnp.where(lane == 1, squares - high, 0.0)).astype(bf16)
    mixed = dot(scaled.astype(bf16), w_ref[:, 2 * channels :], COLS).astype(bf16)
    put_half(
        place_ref,
        span,
        pl.num_programs(0) // 2,
        mine_ref,
        other_ref,
        jnp.concatenate([mixed, extra], axis=1),
    )
    if last_layer:
        g = g_all[here, :]
        g_ref[...] = g
        gg = dot(g, w_ref[:, 2 * channels :])
        gg_ref[...] = gg
        products = jnp.sum(gg * scaled, axis=1, keepdims=True)
        both = jnp.where(lane == 0, squares, jnp.where(lane == 1, products, 0.0))
        sums_ref[...] = jnp.transpose(both)[0:8, :]


def gate_part(gg, rms, coef, z, y, cx_ref):
    z, y = z.astype(f32), y.astype(f32)
    norm_gate = cx_ref[5:6, :]
    sz = sigmoid(z)
    silu_z = z * sz
    gated = y * silu_z
    rg = rms * gg
    gate_out = (gated * rms * norm_gate).astype(bf16)
    d_gated = rg * norm_gate - gated * coef
    dz = (d_gated * y * (sz * (1.0 + z * (1.0 - sz)))).astype(bf16)
    return dz, d_gated * silu_z, gate_out, jnp.sum(rg * gated, axis=0, keepdims=True)


def gate_kernel(plan, n_pieces, width, place_ref, *refs):
    pieces = refs[:n_pieces]
    z_ref, y_ref, wo_ref, cx_ref, g_ref, dz_ref, dy_ref, go_ref, acc_ref, first_all = refs[n_pieces:]
    length = z_ref.shape[0]
    span = pl.program_id(0)

    @pl.when(span == 0)
    def _():
        place_pieces(plan, place_ref, pieces, [first_all])
        acc_ref[...] = jnp.zeros_like(acc_ref)

    first = first_all[pl.ds(pl.multiple_of(span * length, length), length), :]
    g = first[:, :width]
    g_ref[...] = g
    tok = first[:, width:].astype(f32)
    rms = tok[:, 0:1] + tok[:, 1:2]
    coef = tok[:, 2:3] + tok[:, 3:4]
    gg = dot(g, wo_ref[...])
    dz, dy, gate_out, acc_norm = gate_part(gg, rms, coef, z_ref[...], y_ref[...], cx_ref)
    dz_ref[...] = dz
    dy_ref[...] = dy
    go_ref[...] = gate_out
    acc_ref[5:6, :] += acc_norm


def scan_kernel(with_gate, head_dim, inner_all, place_ref, *refs):
    if with_gate:
        (gg_ref, tok_ref, z_ref, y_ref), refs = refs[:4], refs[4:]
    else:
        (dy_ref, dz_ref), refs = refs[:2], refs[2:]
    (xn_ref, xp_ref, xhalo_ref, bc_ref, bchalo_ref, dt_ref, hin_ref,
     w_ref, wbc_ref, wdt_ref, cx_ref, cbc_ref, head_ref, pick_ref), refs = refs[:14], refs[14:]
    if with_gate:
        (dz_ref, go_ref), refs = refs[:2], refs[2:]
    (dxt_ref, bcmine_ref, bcother_ref, mine_ref, other_ref, acc_ref, acch_ref, shared_ref,
     accbc, accn, xbuf, bbuf, dubuf, dubbuf, dhst) = refs
    length = xp_ref.shape[0]
    channels = cx_ref.shape[1]
    width = xn_ref.shape[1]
    state = dhst.shape[0]
    step_id = pl.program_id(0)
    first_span = step_id == pl.num_programs(0) - 1

    @pl.when(step_id == 0)
    def _():
        dubuf[length:, :] = jnp.zeros((8, channels), f32)
        dubbuf[length:, :] = jnp.zeros((8, 2 * state), f32)
        dhst[...] = jnp.zeros_like(dhst)
        accn[...] = jnp.zeros_like(accn)
        acc_ref[...] = jnp.zeros_like(acc_ref)
        accbc[...] = jnp.zeros_like(accbc)
        acch_ref[...] = jnp.zeros_like(acch_ref)

    @pl.when(first_span)
    def _():
        xbuf[0:8, :] = jnp.zeros((8, channels), f32)
        bbuf[0:8, :] = jnp.zeros((8, 2 * state), f32)

    @pl.when(jnp.logical_not(first_span))
    def _():
        xbuf[0:8, :] = xhalo_ref[...].astype(f32)[8:16, :]
        bbuf[0:8, :] = bchalo_ref[...].astype(f32)[8:16, :]

    xbuf[8:, :] = xp_ref[...].astype(f32)
    bbuf[8:, :] = bc_ref[...].astype(f32)
    if with_gate:
        tok = jnp.transpose(tok_ref[...])
        rms = lax.rsqrt(tok[:, 0:1] / inner_all + EPS)
        coef = rms * rms * rms * tok[:, 1:2] / inner_all
        dz_b, dy, gate_out, acc_norm = gate_part(
            gg_ref[...], rms, coef, z_ref[...], y_ref[...], cx_ref
        )
        dz_ref[...] = dz_b
        go_ref[...] = gate_out
    else:
        dz_b, dy = dz_ref[...], dy_ref[...]
        acc_norm = jnp.zeros((1, channels), f32)
    skip = cx_ref[6:7, :]

    pre_x = conv_taps(xbuf, cx_ref[0:4, :], cx_ref[4:5, :], length)
    sx = sigmoid(pre_x)
    xc = pre_x * sx
    pre_bc = conv_taps(bbuf, cbc_ref[0:4, :], cbc_ref[4:5, :], length)
    sbc = sigmoid(pre_bc)
    bcc = (pre_bc * sbc).astype(bf16)
    b_mat = bcc[:, :state]
    c_mat = bcc[:, state:]
    mask, pre_dt, step, rate, cum = span_values(dt_ref[...], head_ref)
    cum_t = jnp.transpose(cum)
    last = cum[length - 1 : length, :]
    scores = dot(c_mat, b_mat, COLS)
    step_all = spread_heads(step, channels, head_dim)
    xs = xc * step_all
    xs_b = xs.astype(bf16)
    tail = spread_heads(jnp.exp(last - cum), channels, head_dim)
    keep = spread_heads(jnp.exp(last), channels, head_dim)

    hin = hin_ref[0]
    hin_b = hin.astype(bf16)
    dh = dhst[...]
    dh_b = dh.astype(bf16)
    dye = dy * spread_heads(jnp.exp(cum), channels, head_dim)
    dye_b = dye.astype(bf16)
    txs = tail * xs
    txs_b = txs.astype(bf16)
    carried = dot(c_mat, hin_b)
    pulled = dot(b_mat, dh_b)
    d_c = dot(dye_b, hin_b, COLS)
    d_b = dot(txs_b, dh_b, COLS)
    dhst[...] = keep * dh + dot(c_mat, dye_b, ROWS)
    into = txs * pulled
    across = dye * carried - into
    at_last = jnp.sum(into, axis=0, keepdims=True) + keep * jnp.sum(hin * dh, axis=0, keepdims=True)

    dy_b = dy.astype(bf16)
    dy_t = jnp.transpose(dy).astype(bf16)
    lane = lax.broadcasted_iota(jnp.int32, (length, LANES), 1)
    per_tile = LANES // head_dim
    d_scores = jnp.zeros((length, length), f32)
    row_sums = jnp.zeros((length, LANES), f32)
    col_sums = []
    dxs_parts = []
    for head in range(channels // head_dim):
        tile, sub = divmod(head, per_tile)
        dy_tile = dy_b[:, tile * LANES : (tile + 1) * LANES]
        own = (lane >= sub * head_dim) & (lane < (sub + 1) * head_dim)
        dy_head = jnp.where(own, dy_tile, jnp.zeros_like(dy_tile))
        d_m = dot(dy_head, xs_b[:, tile * LANES : (tile + 1) * LANES], COLS)
        decay = decay_matrix(mask, cum[:, head : head + 1], cum_t[head : head + 1, :])
        dxs_parts.append(
            dot(dy_t[head * head_dim : (head + 1) * head_dim, :], (scores * decay).astype(bf16))
        )
        d_m = d_m * decay
        d_scores = d_scores + d_m
        pairs = d_m * scores
        row_sums = jnp.where(lane == head, jnp.sum(pairs, axis=1, keepdims=True), row_sums)
        col_sums.append(jnp.sum(pairs, axis=0, keepdims=True))
    heads = len(col_sums)
    col_sums = jnp.concatenate(col_sums + [jnp.zeros((LANES - heads, length), f32)], axis=0)
    dxs = jnp.transpose(jnp.concatenate(dxs_parts, axis=0)) + tail * pulled
    pick = pick_ref[...].astype(bf16)
    d_cum = row_sums - jnp.transpose(col_sums) + sum_heads(across, pick)
    at_last = sum_heads(jnp.broadcast_to(at_last, (16, channels)), pick)[0:1, :]
    d_rate = dot_exact(mask, d_cum, ROWS) + at_last
    d_step = d_rate * head_ref[1:2, :] + sum_heads(dxs * xc, pick)
    d_dt = d_step * sigmoid(pre_dt)
    acch_ref[0:1, :] += jnp.sum(d_dt, axis=0, keepdims=True)
    acch_ref[1:2, :] += jnp.sum(d_rate * rate, axis=0, keepdims=True)
    dt_b = d_dt.astype(bf16)
    ds_b = d_scores.astype(bf16)
    d_c = d_c + dot(ds_b, b_mat)
    d_b = d_b + dot(ds_b, c_mat, ROWS)
    d_xc = dxs * step_all + skip * dy
    acc_skip = jnp.sum(dy * xc, axis=0, keepdims=True)

    d_u = d_xc * (sx * (1.0 + pre_x * (1.0 - sx)))
    d_ub = jnp.concatenate([d_b, d_c], axis=1) * (sbc * (1.0 + pre_bc * (1.0 - sbc)))
    dubuf[0:length, :] = d_u
    dubbuf[0:length, :] = d_ub
    d_x = jnp.zeros_like(d_u)
    d_bc = jnp.zeros_like(d_ub)
    acc_rows = []
    accbc_rows = []
    for j in range(4):
        d_x = d_x + cx_ref[j : j + 1, :] * dubuf[pl.ds(3 - j, length), :]
        d_bc = d_bc + cbc_ref[j : j + 1, :] * dubbuf[pl.ds(3 - j, length), :]
        acc_rows.append(jnp.sum(d_u * xbuf[pl.ds(5 + j, length), :], axis=0, keepdims=True))
        accbc_rows.append(jnp.sum(d_ub * bbuf[pl.ds(5 + j, length), :], axis=0, keepdims=True))
    dubuf[length:, :] = d_u[0:8, :]
    dubbuf[length:, :] = d_ub[0:8, :]
    zero = jnp.zeros((1, channels), f32)
    acc_ref[...] += jnp.concatenate(
        acc_rows + [jnp.sum(d_u, axis=0, keepdims=True), acc_norm, acc_skip, zero], axis=0
    )
    zero = jnp.zeros((3, d_ub.shape[1]), f32)
    accbc[...] += jnp.concatenate(
        accbc_rows + [jnp.sum(d_ub, axis=0, keepdims=True), zero], axis=0
    )
    dx_b = d_x.astype(bf16)
    dbc_b = d_bc.astype(bf16)
    dxt_ref[:, :channels] = dx_b
    dxt_ref[:, channels:] = dt_b
    put_columns(
        place_ref,
        pl.num_programs(0) - 1 - step_id,
        bcmine_ref,
        bcother_ref,
        jnp.transpose(d_bc).astype(bf16),
    )
    total = dot(jnp.concatenate([dz_b, dx_b], axis=1), w_ref[...], COLS)
    total = total + dot(dbc_b, wbc_ref[...]) + dot(dt_b, wdt_ref[...])
    accn[0:1, :] += jnp.sum(total * xn_ref[...].astype(f32), axis=0, keepdims=True)

    @pl.when(first_span)
    def _():
        lanes = shared_ref.shape[1]
        lines = [accn[0:1, i * lanes : (i + 1) * lanes] for i in range(width // lanes)]
        shared = jnp.concatenate(lines + [accbc[0:5, :]], axis=0)
        shared_ref[0 : shared.shape[0], :] = shared.astype(bf16)
        shared_ref[shared.shape[0] :, :] = jnp.zeros(
            (shared_ref.shape[0] - shared.shape[0], lanes), bf16
        )

    put_half(
        place_ref,
        pl.num_programs(0) - 1 - step_id,
        pl.num_programs(0) // 2,
        mine_ref,
        other_ref,
        total.astype(bf16),
    )


def whole(shape):
    zeros = (0,) * len(shape)
    return pl.BlockSpec(shape, lambda i, p: zeros)


def span_rows(columns):
    return pl.BlockSpec((SPAN, columns), lambda i, p: (i, 0))


def half_rows(columns, spans, reverse):
    half = spans // 2

    def block(i, core):
        span = spans - 1 - i if reverse else i
        return jnp.clip(span - half * core, 0, half - 1), 0

    return [
        pl.BlockSpec((SPAN, columns), lambda i, p: block(i, p[0])),
        pl.BlockSpec((SPAN, columns), lambda i, p: block(i, 1 - p[0])),
    ]


def span_call(kernel, name, spans, place, operands, in_specs, shapes, out_specs, scratch, flops):
    moved = sum(v.size * v.dtype.itemsize for v in [*operands, *shapes])
    return pl.pallas_call(
        kernel,
        grid_spec=pltpu.PrefetchScalarGridSpec(
            num_scalar_prefetch=1,
            grid=(spans,),
            in_specs=in_specs,
            out_specs=out_specs,
            scratch_shapes=scratch,
        ),
        out_shape=shapes,
        compiler_params=pltpu.CompilerParams(
            dimension_semantics=("arbitrary",), vmem_limit_bytes=VMEM_BYTES
        ),
        cost_estimate=pl.CostEstimate(flops=flops, bytes_accessed=moved, transcendentals=0),
        name=name,
    )(place, *operands)


def run_forward(place, gathered, w, wdt, small, state, head_dim):
    w_here, w_there, there_plan = w
    channels = small[0].shape[1]
    width = gathered[0][0][0].shape[1]
    anywhere = pl.BlockSpec(memory_space=pl.ANY)
    tokens = NC * NZ * gathered[0][2][0]
    spans = tokens // SPAN
    last_layer = len(gathered) == 2
    plans = [(cut_plan(*one), len(one[0])) for one in gathered]
    operands = [p for one in gathered for p in one[0]]
    in_specs = [whole(v.shape) for v in operands] + [anywhere] * (1 + len(w_there))
    operands += [w_here, *w_there, wdt, *small]
    in_specs += [whole(v.shape) for v in operands[len(in_specs) :]]
    shapes = [
        jax.ShapeDtypeStruct(w_here.shape, bf16),
        jax.ShapeDtypeStruct((tokens, width), bf16),
        jax.ShapeDtypeStruct((2 * state, width), bf16),
        jax.ShapeDtypeStruct((tokens, channels), bf16),
        jax.ShapeDtypeStruct((tokens, channels), bf16),
        jax.ShapeDtypeStruct((tokens, 2 * state), bf16),
        jax.ShapeDtypeStruct((tokens, LANES), f32),
        jax.ShapeDtypeStruct((tokens, channels), bf16),
        jax.ShapeDtypeStruct((spans, state, channels), f32),
        jax.ShapeDtypeStruct((tokens // 2, width + LANES), bf16),
        jax.ShapeDtypeStruct((tokens // 2, width + LANES), bf16),
    ]
    out_specs = [whole(w_here.shape), span_rows(width), whole((2 * state, width))]
    out_specs += [span_rows(s.shape[1]) for s in shapes[3:8]]
    out_specs.append(pl.BlockSpec((1, state, channels), lambda i, p: (i, 0, 0)))
    out_specs += half_rows(width + LANES, spans, False)
    scratch = [
        pltpu.SemaphoreType.DMA,
        pltpu.VMEM((tokens, width), bf16),
        pltpu.VMEM((SPAN + 8, channels), f32),
        pltpu.VMEM((SPAN + 8, 2 * state), f32),
        pltpu.VMEM((state, channels), f32),
    ]
    if last_layer:
        shapes += [
            jax.ShapeDtypeStruct((tokens, width), bf16),
            jax.ShapeDtypeStruct((8, tokens), f32),
            jax.ShapeDtypeStruct((tokens, channels), f32),
        ]
        out_specs += [span_rows(width), pl.BlockSpec((8, SPAN), lambda i, p: (0, i)), span_rows(channels)]
        scratch.append(pltpu.VMEM((tokens, width), bf16))
    kernel = functools.partial(forward_kernel, plans, there_plan, head_dim)
    return span_call(
        kernel, "layer_forward", spans, place, operands, in_specs, shapes, out_specs, scratch, 20 * 10**9
    )


def run_gate(place, gathered, z, y, w, cx):
    tokens, channels = z.shape
    width = w.shape[0]
    spans = tokens // SPAN
    plan, pieces = cut_plan(*gathered), list(gathered[0])
    operands = [*pieces, z, y, w, cx]
    in_specs = [whole(p.shape) for p in pieces]
    in_specs += [span_rows(channels), span_rows(channels)]
    in_specs += [pl.BlockSpec((width, channels), lambda i, p: (0, 2)), whole(cx.shape)]
    shapes = [
        jax.ShapeDtypeStruct((tokens, width), bf16),
        jax.ShapeDtypeStruct((tokens, channels), bf16),
        jax.ShapeDtypeStruct((tokens, channels), f32),
        jax.ShapeDtypeStruct((tokens, channels), bf16),
        jax.ShapeDtypeStruct((8, channels), f32),
    ]
    out_specs = [span_rows(s.shape[1]) for s in shapes[:4]] + [whole(shapes[4].shape)]
    scratch = [pltpu.VMEM((tokens, pieces[0].shape[1]), bf16)]
    kernel = functools.partial(gate_kernel, plan, len(pieces), width)
    return span_call(
        kernel, "gate_backward", spans, place, operands, in_specs, shapes, out_specs, scratch, 6 * 10**9
    )


def run_scan(place, lead, xn, xp, bc, dt, hin, weights, small, pick, head_dim, inner_all):
    tokens, channels = xp.shape
    state = hin.shape[1]
    width = xn.shape[1]
    spans = tokens // SPAN
    with_gate = len(lead) == 4

    def rev(columns):
        return pl.BlockSpec((SPAN, columns), lambda i, p: (spans - 1 - i, 0))

    def halo(columns, rows):
        per = SPAN // rows
        return pl.BlockSpec(
            (rows, columns), lambda i, p: (jnp.maximum((spans - 1 - i) * per - 1, 0), 0)
        )

    operands = [*lead, xn, xp, xp, bc, bc, dt, hin, *weights, *small, pick]
    in_specs = [rev(channels)] * 2
    if with_gate:
        tok = pl.BlockSpec((8, SPAN), lambda i, p: (0, spans - 1 - i))
        in_specs = [rev(channels), tok, rev(channels), rev(channels)]
    in_specs += [
        rev(width),
        rev(channels),
        halo(channels, 16),
        rev(2 * state),
        halo(2 * state, 16),
        rev(LANES),
        pl.BlockSpec((1, state, channels), lambda i, p: (spans - 1 - i, 0, 0)),
    ]
    in_specs.append(whole((width, 2 * channels)))
    in_specs += [whole(v.shape) for v in operands[len(in_specs) :]]
    shapes = [
        jax.ShapeDtypeStruct((tokens, channels + LANES), bf16),
        jax.ShapeDtypeStruct((state * spans, SPAN), bf16),
        jax.ShapeDtypeStruct((state * spans, SPAN), bf16),
        jax.ShapeDtypeStruct((tokens // 2, width), bf16),
        jax.ShapeDtypeStruct((tokens // 2, width), bf16),
        jax.ShapeDtypeStruct((8, channels), f32),
        jax.ShapeDtypeStruct((8, LANES), f32),
        jax.ShapeDtypeStruct((16, 2 * state), bf16),
    ]
    out_specs = [rev(channels + LANES), whole(shapes[1].shape), whole(shapes[2].shape)]
    out_specs += half_rows(width, spans, True)
    out_specs += [whole(s.shape) for s in shapes[5:]]
    if with_gate:
        shapes = [jax.ShapeDtypeStruct((tokens, channels), bf16)] * 2 + shapes
        out_specs = [rev(channels)] * 2 + out_specs
    scratch = [
        pltpu.VMEM((8, 2 * state), f32),
        pltpu.VMEM((8, width), f32),
        pltpu.VMEM((SPAN + 8, channels), f32),
        pltpu.VMEM((SPAN + 8, 2 * state), f32),
        pltpu.VMEM((SPAN + 8, channels), f32),
        pltpu.VMEM((SPAN + 8, 2 * state), f32),
        pltpu.VMEM((state, channels), f32),
    ]
    kernel = functools.partial(scan_kernel, with_gate, head_dim, inner_all)
    return span_call(
        kernel, "scan_backward", spans, place, operands, in_specs, shapes, out_specs, scratch, 28 * 10**9
    )


def weight_kernel(n_pairs, split, place_ref, *refs):
    lefts, rights, outs = refs[:n_pairs], refs[n_pairs : 2 * n_pairs], refs[2 * n_pairs :]

    def write(out_ref):
        at = 0
        for left_ref, right_ref in zip(lefts, rights):
            columns = right_ref.shape[1]
            out_ref[:, at : at + columns] = dot(left_ref[...], right_ref[...], ROWS).astype(bf16)
            at += columns

    if not split:
        write(outs[0])
        return
    for k, out_ref in enumerate(outs):
        pl.when(pl.program_id(0) == k)(functools.partial(write, out_ref))


def weight_products(place, pairs, split=True):
    tokens = pairs[0][0].shape[0]
    rows = max(left.shape[1] for left, _ in pairs)
    block = rows // 4

    def at(i, p):
        return lax.rem(p[3] + i, NX) if split else i

    lefts, rights, columns = [], [], []
    for left, right in pairs:
        quarter = left.shape[1] == block
        cut, uncut = (lambda i, p: (0, at(i, p))), (lambda i, p: (0, 0))
        lefts.append(pl.BlockSpec((tokens, block), uncut if quarter else cut))
        wide = block if quarter else right.shape[1]
        rights.append(pl.BlockSpec((tokens, wide), cut if quarter else uncut))
        columns.append(wide)
    columns = sum(columns)
    if split:
        out_specs = [whole((block, columns))] * 4
        shapes = [jax.ShapeDtypeStruct((block, columns), bf16)] * 4
    else:
        out_specs = [pl.BlockSpec((block, columns), lambda i, p: (i, 0))]
        shapes = [jax.ShapeDtypeStruct((rows, columns), bf16)]
    out = pl.pallas_call(
        functools.partial(weight_kernel, len(pairs), split),
        grid_spec=pltpu.PrefetchScalarGridSpec(
            num_scalar_prefetch=1, grid=(4,), in_specs=lefts + rights, out_specs=out_specs
        ),
        out_shape=shapes,
        compiler_params=pltpu.CompilerParams(vmem_limit_bytes=VMEM_BYTES),
        cost_estimate=pl.CostEstimate(
            flops=2 * tokens * rows * columns, bytes_accessed=8 * 10**6, transcendentals=0
        ),
        name="weight_products",
    )(place, *[left for left, _ in pairs], *[right for _, right in pairs])
    return out if split else out[0]


SIZES = (4, 2, 2, 2, 4)
NX, NYL, NC, NYH, NZ = SIZES
EVERY = [
    (x, yl, c, yh, z)
    for x in range(NX)
    for yl in range(NYL)
    for c in range(NC)
    for yh in range(NYH)
    for z in range(NZ)
]


def linear(x, yl, c, yh, z):
    return ((((x % NX) * NYL + yl % NYL) * NC + c % NC) * NYH + yh % NYH) * NZ + z % NZ


def send(v, step, only=None):
    pairs = [(linear(*d), linear(*step(*d))) for d in EVERY if only is None or only(*d)]
    return lax.ppermute(v, ("dp", "tensor"), pairs)


def send_z(v, k):
    return send(v, lambda x, yl, c, yh, z: (x, yl, c, yh, z + k))


def send_core(v):
    return send(v, lambda x, yl, c, yh, z: (x, yl, c + 1, yh, z))


def trade(v, k):
    return send(v, lambda x, yl, c, yh, z: (x, yl, yh, c, z + k))


def traded(v):
    return send(v, lambda x, yl, c, yh, z: (x, yl, yh, c, z), lambda x, yl, c, yh, z: c != yh)


def trade_places(v):
    _, _, core, yh, _ = position()
    return jnp.where(core == yh, v, traded(v))


def position():
    dp, tensor = lax.axis_index("dp"), lax.axis_index("tensor")
    return dp // (NYL * NC), dp // NC % NYL, dp % NC, tensor // NZ, tensor % NZ


def gather(v, parts, traded_own=None, later=()):
    arrays, sources = [], []
    for k in (0, 1, 3, 2):
        if traded_own is not None:
            piece = trade(v, k) if k else traded_own
        else:
            piece = send_z(v, k) if k else v
        arrays += [piece, send_core(after(piece, *later) if later else piece)]
        sources += [(False, -k % NZ, 0), (True, -k % NZ, 0)]
    return arrays, sources, parts


def cut_plan(arrays, sources, parts):
    plan = []
    for number, (piece, (other, dz, first)) in enumerate(zip(arrays, sources)):
        base = 0
        for out, per in enumerate(parts):
            begin, end = max(first, base), min(first + piece.shape[0], base + per)
            if begin < end:
                plan.append((number, other, dz, begin - first, out, per, begin - base, end - begin))
            base += per
    return plan


def fold(mine, other):
    _, _, _, _, z = position()
    rows = mine.shape[0] // NZ
    blocks = []
    for k in range(NZ):
        at = (z + k) % NZ * rows
        a = lax.dynamic_slice_in_dim(mine, at, rows, 0).astype(f32)
        blocks.append(a + lax.dynamic_slice_in_dim(other, at, rows, 0).astype(f32))
    return blocks


def fold_beside(pairs):
    folded = [fold(mine, send_core(other)) for mine, other in pairs]
    return [jnp.concatenate([blocks[k] for blocks in folded], axis=1) for k in range(NZ)]


def scatter(*pairs, meanwhile=None):
    own, one, two, three = fold_beside(pairs)
    if meanwhile is not None:
        two = after(two, meanwhile)
    return [own] + [send_z(b.astype(bf16), k) for k, b in ((1, one), (2, two), (3, three))]


def scatter_with_sum(mine, other, shared, meanwhile):
    half = mine.shape[0]
    rows = half // NZ
    got = after(send_core(jnp.concatenate([other, shared], axis=0)), *meanwhile)
    blocks = fold(mine, got[:half])
    total_shared = shared.astype(f32) + got[half:].astype(f32)
    packed = total_shared.astype(bf16)
    total = blocks[0]
    for k in range(1, NZ):
        got = send_z(jnp.concatenate([blocks[k].astype(bf16), packed], axis=0), k)
        total = total + got[:rows].astype(f32)
        total_shared = total_shared + got[rows:].astype(f32)
    return total, total_shared


def sum_members(v):
    both = v + send_core(v)
    total = both
    for k in range(1, NZ):
        total = total + send_z(both, k)
    return total


def send_far(v):
    return send(v, lambda x, yl, c, yh, z: (x, yl, c, yh + 1, z), lambda x, yl, c, yh, z: c != yh)


def sum_far(v, far=None):
    far = send_far(v) if far is None else far
    return (v.astype(f32) + far.astype(f32)).astype(bf16)


def halve(v):
    _, _, core, yh, _ = position()
    half = v.shape[0] // 2
    near = send(
        v[half:], lambda x, yl, c, yh, z: (x, yl, c + 1, yh, z), lambda x, yl, c, yh, z: c == yh
    )
    return jnp.where(core == yh, v[:half], near)


def sum_beside(part):
    beside = send(part, lambda x, yl, c, yh, z: (x, yl + 1, c, yh, z))
    return (part.astype(f32) + beside.astype(f32)).astype(bf16)


def sum_x(blocks):
    return add_x(blocks[0], send_x(blocks))


def send_x(blocks):
    return [
        send(blocks[k], lambda x, yl, c, yh, z, k=k: (x + k, yl, c, yh, z)) for k in range(1, NX)
    ]


def add_x(own, received, meanwhile=()):
    total = own.astype(f32)
    for got in received:
        got = after(got, *meanwhile) if meanwhile else got
        total = total + got.astype(f32)
    return total.astype(bf16)


def cut_x(v):
    x = position()[0]
    rows = v.shape[0] // NX
    return [lax.dynamic_slice_in_dim(v, (x + k) % NX * rows, rows, 0) for k in range(NX)]


def collect_x(part, meanwhile=()):
    parts = [part]
    for k in range(1, NX):
        got = send(part, lambda x, yl, c, yh, z, k=k: (x + k, yl, c, yh, z))
        parts.append(after(got, *meanwhile) if meanwhile else got)
    return jnp.stack(parts)


def write_kernel(plan, n_kept, place_ref, here_ref, there_ref, *refs):
    rows = here_ref.shape[1]

    def write(ref):
        for (column, kind, wide, by_half), out_ref in zip(plan, refs[n_kept:]):
            for x in range(NX):
                value = ref[lax.rem(place_ref[3] + NX - x, NX), :, column : column + wide].astype(f32)
                if kind != "blocks":
                    out_ref[0, 0 if by_half else x, x if by_half else 0] = value
                elif by_half:
                    at = x // 2 * wide
                    out_ref[0, x % 2 * rows : (x % 2 + 1) * rows, at : at + wide] = value
                else:
                    out_ref[0, :, x * wide : (x + 1) * wide] = value

    here = (pl.program_id(0) == 0) == (place_ref[2] == 1)

    @pl.when(here)
    def _():
        write(here_ref)

    @pl.when(jnp.logical_not(here))
    def _():
        write(there_ref)


def write_sums(place, halves, outputs):
    rows, columns = halves[0].shape[1:]
    total = 2 * NX * rows
    wide = total // 4
    plan, shapes, specs, finals, kept, alias = [], [], [], [], [], {}
    for column, kind, layer, array, by_half in outputs:
        lanes = LANES if kind == "flat" else wide
        layers = 1 if kind == "flat" else 2
        plan.append((column, kind, lanes, by_half))
        if kind == "blocks":
            shape = (layers, wide, total)
            if by_half:
                spec = pl.BlockSpec((1, wide, total // 2), lambda h, p, layer=layer: (layer, 0, h))
            else:
                spec = pl.BlockSpec((1, rows, total), lambda h, p, layer=layer: (layer, h, 0))
            finals.append(shape)
        elif by_half:
            shape = (layers, 2, NX, rows, lanes)
            spec = pl.BlockSpec((1, 1, NX, rows, lanes), lambda h, p, layer=layer: (layer, h, 0, 0, 0))
            finals.append((layers, total, lanes))
        else:
            shape = (layers, NX, 2, rows, lanes)
            spec = pl.BlockSpec((1, NX, 1, rows, lanes), lambda h, p, layer=layer: (layer, 0, h, 0, 0))
            finals.append((layers, total, lanes))
        shapes.append(jax.ShapeDtypeStruct(shape, f32))
        specs.append(spec)
        if array is not None:
            alias[3 + len(kept)] = len(shapes) - 1
            kept.append(array.reshape(shape))
    piece = pl.BlockSpec((NX, rows, columns), lambda h, p: (0, 0, 0))
    written = pl.pallas_call(
        functools.partial(write_kernel, plan, len(kept)),
        grid_spec=pltpu.PrefetchScalarGridSpec(
            num_scalar_prefetch=1,
            grid=(2,),
            in_specs=[piece, piece] + [pl.BlockSpec(memory_space=pl.ANY)] * len(kept),
            out_specs=specs,
        ),
        out_shape=shapes,
        input_output_aliases=alias,
        compiler_params=pltpu.CompilerParams(vmem_limit_bytes=VMEM_BYTES),
        name="write_sums",
    )(place, *halves, *kept)
    return [v.reshape(final) for v, final in zip(written, finals)]


def row_call(kernel, name, operands, shapes):
    return pl.pallas_call(
        kernel,
        grid=(1,),
        in_specs=[pl.BlockSpec((rows, v.shape[1]), lambda i: (0, 0)) for v, rows in operands],
        out_specs=[pl.BlockSpec(s.shape, lambda i, n=len(s.shape): (0,) * n) for s in shapes],
        out_shape=shapes,
        compiler_params=pltpu.CompilerParams(vmem_limit_bytes=VMEM_BYTES),
        name=name,
    )(*[v for v, _ in operands])


def inverse_rms(v):
    return lax.rsqrt(jnp.mean(v * v, axis=-1, keepdims=True) + EPS)


def first_kernel(packed_ref, gain_ref, out_ref):
    rows = 128
    v = packed_ref[0:rows, :].astype(f32)
    out_ref[0:rows, :] = (v * inverse_rms(v) * gain_ref[...]).astype(bf16)
    out_ref[rows:, :] = packed_ref[rows : out_ref.shape[0], :]


def add_terms(own_ref, a_ref, b_ref, c_ref):
    total = own_ref[...].astype(f32) + a_ref[...].astype(f32)
    return total + (b_ref[...].astype(f32) + c_ref[...].astype(f32))


def unscaled_output(inner_all, terms, width):
    total = add_terms(*terms)
    squares = total[:, width : width + 1] + total[:, width + 1 : width + 2]
    gate_rms = lax.rsqrt(squares / inner_all + EPS)
    return gate_rms, total[:, :width] * gate_rms


def middle_kernel(inner_all, own_ref, a_ref, b_ref, c_ref, res_ref, gain_ref, res1_ref, mixed_ref, rms_ref, normed_ref):
    width = res_ref.shape[1]
    gate_rms, mixed = unscaled_output(inner_all, (own_ref, a_ref, b_ref, c_ref), width)
    res = res_ref[...].astype(f32) + mixed
    res1_ref[...] = res
    mixed_ref[...] = mixed
    rms_ref[...] = jnp.broadcast_to(gate_rms, rms_ref.shape)
    normed_ref[...] = (res * inverse_rms(res) * gain_ref[...]).astype(bf16)


def input_gradient(grad_normed, res, d_res, gain):
    inv = inverse_rms(res)
    scaled = grad_normed * gain
    dots = jnp.sum(scaled * res, axis=-1, keepdims=True) / res.shape[1]
    return d_res + inv * scaled - res * (inv * inv * inv) * dots


def between_kernel(inner_all, own_ref, a_ref, b_ref, c_ref, res_ref, dres_ref, gain_ref, mixed_ref, rms_ref, out_ref, sent_ref):
    width = res_ref.shape[1]
    grad_normed = add_terms(*(ref.at[:, 0:width] for ref in (own_ref, a_ref, b_ref, c_ref)))
    d_res = input_gradient(grad_normed, res_ref[...], dres_ref[...].astype(f32), gain_ref[...])
    out_ref[...] = d_res
    g_mixed = d_res.astype(bf16)
    sent_ref[:, :width] = g_mixed
    gate_rms = rms_ref[:, 0:1]
    products = jnp.sum(g_mixed.astype(f32) * mixed_ref[...], axis=-1, keepdims=True)
    coef = gate_rms * gate_rms * products / inner_all
    lane = lax.broadcasted_iota(jnp.int32, rms_ref.shape, 1)
    rms_high = gate_rms.astype(bf16).astype(f32)
    coef_high = coef.astype(bf16).astype(f32)
    extra = jnp.where(lane == 0, rms_high, jnp.where(lane == 1, gate_rms - rms_high, 0.0))
    extra = jnp.where(lane == 2, coef_high, jnp.where(lane == 3, coef - coef_high, extra))
    sent_ref[:, width:] = extra.astype(bf16)


def end_kernel(own_ref, a_ref, b_ref, c_ref, res_ref, dres_ref, gain_ref, hidden_ref, out_ref):
    width = res_ref.shape[1]
    grad_normed = add_terms(own_ref, a_ref, b_ref, c_ref)
    grad = input_gradient(grad_normed, res_ref[...].astype(f32), dres_ref[...], gain_ref[...])
    out_ref[:, :width] = hidden_ref[...]
    out_ref[:, width:] = grad.astype(bf16)


def last_kernel(inner_all, own_ref, a_ref, b_ref, c_ref, res_ref, out_ref):
    _, mixed = unscaled_output(inner_all, (own_ref, a_ref, b_ref, c_ref), res_ref.shape[1])
    out_ref[...] = (res_ref[...] + mixed).astype(bf16)


TINY_ROWS = 56


def small_kernel(head_dim, ends, narrow0_ref, narrow1_ref, gain_ref, pick_ref, norm_ref, wbc_ref, wdt_ref, cx_ref,
                 cxb_ref, cbc_ref, cbcb_ref, dtb_ref, alog_ref, skip_ref, ng_ref):
    bc_at, tiny_at = ends
    heads = wdt_ref.shape[0]
    channels = cx_ref.shape[2]
    both = cbc_ref.shape[2]
    lanes = narrow0_ref.shape[1] - tiny_at
    for layer, ref in enumerate((narrow0_ref, narrow1_ref)):
        columns = jnp.transpose(ref[...])
        wbc_ref[layer] = columns[bc_at:tiny_at]
        wdt_ref[:, layer, :] = columns[0:heads]
    tiny = jnp.concatenate(
        [narrow0_ref[i * TINY_ROWS : (i + 1) * TINY_ROWS, tiny_at:] for i in range(channels // lanes)], axis=1
    )
    lines = norm_ref.shape[1] // both
    for layer in range(2):
        rows = tiny[8 * layer : 8 * layer + 8]
        cx_ref[layer] = rows[0:4]
        cxb_ref[layer : layer + 1, :] = rows[4:5]
        ng_ref[layer : layer + 1, :] = rows[5:6]
        skip_ref[layer : layer + 1, :] = dot(rows, pick_ref[...], PLAIN, highest)[6:7, 0:heads]
        at = 16 + 2 * layer
        dtb_ref[layer : layer + 1, :] = tiny[at : at + 1, 0:heads]
        alog_ref[layer : layer + 1, :] = tiny[at + 1 : at + 2, 0:heads]
        at = 20 + 16 * layer
        norm = jnp.concatenate([tiny[at + i : at + i + 1, 0:both] for i in range(lines)], axis=1)
        norm_ref[layer : layer + 1, :] = norm / gain_ref[layer : layer + 1, :]
        cbc_ref[layer] = tiny[at + lines : at + lines + 4, 0:both]
        cbcb_ref[layer : layer + 1, :] = tiny[at + lines + 4 : at + lines + 5, 0:both]


def after(v, *others):
    return lax.optimization_barrier((v, *others))[0]


def pad_to(v, rows, lanes):
    return jnp.pad(v, ((0, rows - v.shape[0]), (0, lanes - v.shape[1])))


def local(
    hidden_in,
    grad_out,
    norm_in,
    w_z,
    w_x,
    w_bc,
    w_dt,
    conv_x,
    conv_x_bias,
    conv_bc,
    conv_bc_bias,
    dt_bias,
    a_log,
    skip,
    norm_gate,
    w_out,
):
    layers, width, channels = w_z.shape
    heads = w_dt.shape[2]
    head_dim = channels // heads
    both = conv_bc.shape[2]
    state = both // 2
    members = NC * NZ
    inner_all = channels * members
    rows = hidden_in.shape[1]
    bc_rows = both // members
    x, _, core, yh, z = position()
    stays = core == yh
    place = jnp.stack([core, z, stays, x]).astype(jnp.int32)
    full = jax.ShapeDtypeStruct((rows, width), f32)

    def pack_weights(layer):
        return jnp.concatenate([w_z[layer], w_x[layer], w_out[layer].T], axis=1)

    bc_t = jnp.swapaxes(w_bc, 1, 2)
    dt_t = jnp.pad(jnp.swapaxes(w_dt, 1, 2), ((0, 0), (0, 8 - heads), (0, 0)))
    per_channel = jnp.concatenate(
        [conv_x, conv_x_bias[:, None], norm_gate[:, None], jnp.repeat(skip, head_dim, axis=1)[:, None]],
        axis=1,
    )
    per_channel = jnp.pad(per_channel, ((0, 0), (0, 1), (0, 0)))
    per_head = jnp.stack([dt_bias, -jnp.exp(a_log)], axis=1)
    per_head = jnp.pad(per_head, ((0, 0), (0, 6), (0, LANES - heads)))
    little = jnp.concatenate([per_channel, per_head], axis=2).reshape(layers * 8, channels + LANES)
    high = little.astype(bf16)
    low = (little - high.astype(f32)).astype(bf16)
    lines = pad_to(jnp.concatenate([high, low], axis=1), layers * 8, width)
    packed = jnp.concatenate([hidden_in[0], bc_t[0], dt_t.reshape(layers * 8, width), lines], axis=0)
    packed = trade_places(packed)
    lines = packed[packed.shape[0] - layers * 8 :].astype(f32)
    little = lines[:, : channels + LANES] + lines[:, channels + LANES : 2 * (channels + LANES)]
    little = little.reshape(layers, 8, channels + LANES)

    w0 = pack_weights(0)
    w0 = w0, [traded(after(w0, packed))], [(0, None)]
    grads = jnp.concatenate([grad_out[0], bc_t[1]], axis=0)

    [sent] = row_call(
        first_kernel,
        "first_norm",
        [(packed, packed.shape[0]), (norm_in[0:1], 1)],
        [jax.ShapeDtypeStruct((rows + bc_rows, width), bf16)],
    )
    gathered0 = gather(sent, (rows, bc_rows))
    wdt = [pad_to(packed[rows + bc_rows + 8 * l : rows + bc_rows + 8 * (l + 1)], LANES, width) for l in range(layers)]
    smalls = []
    for layer in range(layers):
        cbc = jnp.concatenate([conv_bc[layer], conv_bc_bias[layer][None], jnp.zeros((3, both), f32)], axis=0)
        smalls.append((little[layer, :, :channels], cbc, little[layer, :, channels:]))
    channel_head = jnp.arange(channels) // head_dim
    pick = (channel_head[:, None] == jnp.arange(LANES)[None, :]).astype(f32)

    out0 = run_forward(place, [gathered0], w0, wdt[0], smalls[0], state, head_dim)
    w0, xn0, wbc0, z0, xp0, bc0, dt0, y0, hin0, mine, other = out0
    grads = after(grads, sent)
    gathered_grad = gather(grads, (rows, bc_rows), jnp.where(stays, grads, after(traded(grads), mine)), (mine,))
    grad_held = gathered_grad[0][0]
    terms = scatter((mine, after(other, *gathered_grad[0][::2])))
    w1 = pack_weights(1)
    w1 = w1, [traded(after(w1, terms[0]))], [(0, None)]
    res1, mixed0, rms0, normed1 = row_call(
        functools.partial(middle_kernel, inner_all),
        "middle_norm",
        [(v, rows) for v in terms] + [(packed, rows), (norm_in[1:2], 1)],
        [full, full, jax.ShapeDtypeStruct((rows, LANES), f32), jax.ShapeDtypeStruct((rows, width), bf16)],
    )
    gathered1 = gather(normed1, (rows,))
    out1 = run_forward(
        place, [gathered1, gathered_grad], w1, wdt[1], smalls[1], state, head_dim
    )
    w1, xn1, wbc1, z1, xp1, bc1, dt1, y1, hin1, mine, other, grad_rows1, sums, gg1 = out1
    sums = sum_members(sums)

    home = fold(mine, send_core(other))
    sums = after(sums, *home)
    home = home[:1] + [send_z(home[k].astype(bf16), k) for k in range(1, NZ)]
    back1 = run_scan(
        place, (gg1, sums, z1, y1), xn1, xp1, bc1, dt1, hin1, (w1, wbc1, wdt[1]), smalls[1], pick, head_dim,
        inner_all,
    )
    dz1, go1, dxt1, *bc_halves, mine, other, acc1, acch1, shared1 = back1
    early1 = weight_products(place, [(xn1, dz1), (go1, grad_rows1)], split=False)
    terms = scatter((mine, after(other, *home)), bc_halves, meanwhile=early1)
    early1_far = send_far(early1)
    [hidden_out] = row_call(
        functools.partial(last_kernel, inner_all),
        "last_output",
        [(after(home[0], terms[1]), rows)] + [(v, rows) for v in home[1:]] + [(res1, rows)],
        [jax.ShapeDtypeStruct((rows, width), bf16)],
    )
    d_res1, sent = row_call(
        functools.partial(between_kernel, inner_all),
        "between_layers",
        [(v, rows) for v in terms]
        + [(res1, rows), (grad_held, rows), (norm_in[1:2], 1), (mixed0, rows), (rms0, rows)],
        [full, jax.ShapeDtypeStruct((rows, width + LANES), bf16)],
    )
    gathered_back = gather(sent, (rows,))

    bc_at = channels + bc_rows

    def with_bc(dxt, bc_sum):
        by_token = bc_sum.reshape(-1, bc_rows, SPAN).swapaxes(1, 2).reshape(-1, bc_rows)
        spread = jnp.pad(by_token, ((0, 0), (bc_at, dxt.shape[1] - bc_at - bc_rows)))
        return dxt + spread.astype(bf16)

    dxt1 = with_bc(dxt1, sum(v[:, width:].astype(f32) for v in terms))

    early1 = halve(sum_far(early1, after(early1_far, sent)))
    z0 = after(z0, early1, hidden_out)
    early1 = sum_x(cut_x(early1))
    grad_rows0, dz0, dy0, go0, acc_gate0 = run_gate(place, gathered_back, z0, y0, w0, smalls[0][0])
    dz0 = after(dz0, early1)
    early = weight_products(place, [(xn0, dz0), (go0, grad_rows0), (xn1, dxt1)])
    dy0 = after(dy0, *early)
    early = sum_x(early)
    early1 = sum_beside(after(early1, dz0))
    back0 = run_scan(
        place, (dy0, dz0), xn0, xp0, bc0, dt0, hin0, (w0, wbc0, wdt[0]), smalls[0], pick, head_dim, inner_all
    )
    dxt0, *bc_halves, mine, other, acc0, acch0, shared0 = back0
    shared = jnp.concatenate([shared0, shared1], axis=0)
    bc_sum, shared = scatter_with_sum(*bc_halves, shared, (early,))
    tiny_at = bc_at + bc_rows
    tiny_lanes = channels + LANES - tiny_at
    tiny = jnp.concatenate(
        [acc0 + acc_gate0, acc1] + [pad_to(v, v.shape[0], channels) for v in (acch0[0:2], acch1[0:2], shared)],
        axis=0,
    )
    tiny = pad_to(tiny, TINY_ROWS, channels)
    tiny = [tiny[:, i * tiny_lanes : (i + 1) * tiny_lanes] for i in range(channels // tiny_lanes)]
    tiny = pad_to(jnp.concatenate(tiny, axis=0), width, tiny_lanes)
    tiny = jnp.pad(tiny, ((0, 0), (tiny_at, 0))).astype(bf16)
    early = halve(sum_far(after(early, dxt0)))
    late = weight_products(place, [(xn0, after(with_bc(dxt0, bc_sum), early))])
    home = fold(mine, send_core(after(other, late[0])))
    early = sum_beside(early)
    tiny = after(tiny, early)
    late = [v + t for v, t in zip(late, cut_x(tiny))]
    late_own, late = late[0], send_x(late)

    terms = home[:1] + [send_z(home[k].astype(bf16), k) for k in range(1, NZ)]
    [outputs] = row_call(
        end_kernel,
        "outputs",
        [(v, rows) for v in terms] + [(packed, rows), (d_res1, rows), (norm_in[0:1], 1), (hidden_out, rows)],
        [jax.ShapeDtypeStruct((rows, 2 * width), bf16)],
    )
    outputs_there = traded(outputs)
    outputs_home = jnp.where(stays, outputs, outputs_there).astype(f32)

    early = after(collect_x(early), outputs)
    early = early, send_core(early)
    early1 = collect_x(after(early1, early[0]))
    early1 = early1, send_core(early1)
    g_wz, g_wo, g_wx, narrow1 = write_sums(
        place,
        early,
        [
            (0, "rows", 0, None, False),
            (channels, "blocks", 0, None, False),
            (2 * channels, "rows", 1, None, False),
            (3 * channels, "flat", 0, None, False),
        ],
    )
    late = add_x(late_own, late, (g_wz,))
    g_wz, g_wo = write_sums(
        place, early1, [(0, "rows", 1, g_wz, True), (channels, "blocks", 1, g_wo, True)]
    )
    late = collect_x(sum_beside(halve(sum_far(after(late, outputs_there)))), (g_wz,))
    late = late, send_core(late)
    g_wx, narrow0 = write_sums(
        place, late, [(0, "rows", 0, g_wx, False), (channels, "flat", 0, None, False)]
    )

    narrow0, narrow1 = narrow0[0], narrow1[0]
    small = row_call(
        functools.partial(small_kernel, head_dim, (bc_at - channels, tiny_at - channels)),
        "small_gradients",
        [(narrow0, width), (narrow1, width), (norm_in, layers), (pick, channels)],
        [
            jax.ShapeDtypeStruct(shape, f32)
            for shape in (
                norm_in.shape,
                (layers, bc_rows, width),
                (heads, layers, width),
                conv_x.shape,
                conv_x_bias.shape,
                conv_bc.shape,
                conv_bc_bias.shape,
                dt_bias.shape,
                a_log.shape,
                skip.shape,
                norm_gate.shape,
            )
        ],
    )
    return (
        outputs_home[None, :, :width],
        outputs_home[None, :, width:],
        small[0],
        g_wz,
        g_wx,
        jnp.transpose(small[1], (0, 2, 1)),
        jnp.transpose(small[2], (1, 2, 0)),
        *small[3:],
        g_wo,
    )


def solution(mesh):
    specs_in = (
        P("dp", "tensor", None),
        P("dp", "tensor", None),
        P(),
        P(None, None, "tensor"),
        P(None, None, "tensor"),
        P(None, None, "tensor"),
        P(None, None, "tensor"),
        P(None, None, "tensor"),
        P(None, "tensor"),
        P(),
        P(),
        P(None, "tensor"),
        P(None, "tensor"),
        P(None, "tensor"),
        P(None, "tensor"),
        P(None, "tensor", None),
    )
    specs_out = (
        P("dp", "tensor", None),
        P("dp", "tensor", None),
        P(),
        P(None, None, "tensor"),
        P(None, None, "tensor"),
        P(None, None, "tensor"),
        P(None, None, "tensor"),
        P(None, None, "tensor"),
        P(None, "tensor"),
        P(),
        P(),
        P(None, "tensor"),
        P(None, "tensor"),
        P(None, "tensor"),
        P(None, "tensor"),
        P(None, "tensor", None),
    )
    return jax.shard_map(
        local, mesh=mesh, in_specs=specs_in, out_specs=specs_out, check_vma=False
    )
```

```python
import functools

import jax
import jax.numpy as jnp
from jax import lax
from jax.experimental import pallas as pl
from jax.experimental.pallas import tpu as pltpu
from jax.sharding import PartitionSpec as P

SPAN = 256
EPS = 1e-05
LANES = 128
VMEM_BYTES = 56 * 1024 * 1024

f32 = jnp.float32
bf16 = jnp.bfloat16
highest = lax.Precision.HIGHEST

ROWS = ((0,), (0,))
COLS = ((1,), (1,))
PLAIN = ((1,), (0,))


def dot(left, right, dims=PLAIN, precision=None):
    return lax.dot_general(
        left, right, (dims, ((), ())), preferred_element_type=f32, precision=precision
    )


def sigmoid(v):
    return 0.5 + 0.5 * jnp.tanh(0.5 * v)


def dot_exact(left, right, dims=PLAIN, terms=3):
    parts = []
    for _ in range(terms):
        parts.append(right.astype(bf16))
        right = right - parts[-1].astype(f32)
    out = dot(left.astype(bf16), jnp.concatenate(parts, axis=1), dims)
    width = out.shape[1] // terms
    return sum(out[:, i * width : (i + 1) * width] for i in range(terms))


def sum_heads(v, pick):
    high = v.astype(bf16)
    low = (v - high.astype(f32)).astype(bf16)
    return dot(high, pick) + dot(low, pick)


def softplus(v):
    return jnp.maximum(v, 0.0) + jnp.log1p(jnp.exp(-jnp.abs(v)))


def spread_heads(per_head, channels, head_dim):
    rows = per_head.shape[0]
    per_tile = LANES // head_dim
    lane = lax.broadcasted_iota(jnp.int32, (rows, LANES), 1)
    tiles = []
    for tile in range(channels // LANES):
        out = jnp.broadcast_to(
            per_head[:, tile * per_tile : tile * per_tile + 1], (rows, LANES)
        )
        for sub in range(1, per_tile):
            head = tile * per_tile + sub
            out = jnp.where(
                lane >= sub * head_dim,
                jnp.broadcast_to(per_head[:, head : head + 1], (rows, LANES)),
                out,
            )
        tiles.append(out)
    return jnp.concatenate(tiles, axis=1)


def conv_taps(buf, taps, offset, width):
    out = offset
    for j in range(4):
        out = out + taps[j : j + 1] * buf[pl.ds(5 + j, width), :]
    return out


def decay_matrix(mask, cum_col, cum_row):
    return jnp.exp(jnp.where(mask, cum_col - cum_row, -1e30))


def span_values(dt, head_ref):
    length = dt.shape[0]
    rows = lax.broadcasted_iota(jnp.int32, (length, length), 0)
    cols = lax.broadcasted_iota(jnp.int32, (length, length), 1)
    mask = rows >= cols
    pre = dt + head_ref[0:1, :]
    step = softplus(pre)
    rate = head_ref[1:2, :] * step
    cum = dot_exact(mask, rate)
    return mask, pre, step, rate, cum


def put_half(place_ref, span, half, mine_ref, other_ref, value):
    own = span // half == place_ref[0]

    @pl.when(own)
    def _():
        mine_ref[...] = value

    @pl.when(jnp.logical_not(own))
    def _():
        other_ref[...] = value


def place_pieces(plan, place_ref, pieces, outs):
    core, z = place_ref[0], place_ref[1]
    for piece, other, dz, start, out, per, offset, rows in plan:
        member = (1 - core if other else core) * NZ + lax.rem(z + dz, NZ)
        row = pl.multiple_of(member * per + offset, 16)
        outs[out][pl.ds(row, rows), :] = pieces[piece][start : start + rows, :]


def put_columns(place_ref, span, mine_ref, other_ref, columns):
    per = columns.shape[0] // (NC * NZ)
    rows = mine_ref.shape[0] // NZ

    def place_columns(core, ref):
        for z in range(NZ):
            at = (core * NZ + z) * per
            ref[pl.ds(pl.multiple_of(z * rows + span * per, 16), per), :] = columns[at : at + per, :]

    for core in range(NC):
        mine = place_ref[0] == core

        @pl.when(mine)
        def _(core=core):
            place_columns(core, mine_ref)

        @pl.when(jnp.logical_not(mine))
        def _(core=core):
            place_columns(core, other_ref)


def forward_kernel(plans, there_plan, head_dim, place_ref, *refs):
    last_layer = len(plans) == 2
    refs = list(refs)

    def take(count):
        taken = refs[:count]
        del refs[:count]
        return taken

    piece_refs = [take(count) for _, count in plans]
    [w_here] = take(1)
    w_there = take(len(there_plan))
    wdt_ref, cx_ref, cbc_ref, head_ref = take(4)
    w_ref, xn_ref, wbc_ref, z_ref, xp_ref, bc_ref, dt_ref, y_ref, hin_ref, mine_ref, other_ref = take(11)
    if last_layer:
        g_ref, sums_ref, gg_ref = take(3)
    w_sem, xn_all, xbuf, bbuf, hst = take(5)
    if last_layer:
        [g_all] = take(1)
    length = z_ref.shape[0]
    channels = cx_ref.shape[1]
    state = hst.shape[0]
    span = pl.program_id(0)

    @pl.when(span == 0)
    def _():
        @pl.when(place_ref[2] == 1)
        def _():
            pltpu.make_async_copy(w_here, w_ref, w_sem).start()

        @pl.when(place_ref[2] == 0)
        def _():
            for part, (start, k) in zip(w_there, there_plan):
                rows = part.shape[0]
                if k is not None:
                    start = pl.multiple_of(lax.rem(place_ref[3] + NX - k, NX) * rows, 16)
                pltpu.make_async_copy(part, w_ref.at[pl.ds(start, rows), :], w_sem).start()

        if last_layer:
            place_pieces(plans[0][0], place_ref, piece_refs[0], [xn_all])
            place_pieces(plans[1][0], place_ref, piece_refs[1], [g_all, wbc_ref])
        else:
            place_pieces(plans[0][0], place_ref, piece_refs[0], [xn_all, wbc_ref])
        xbuf[0:8, :] = jnp.zeros((8, channels), f32)
        bbuf[0:8, :] = jnp.zeros((8, 2 * state), f32)
        hst[...] = jnp.zeros_like(hst)
        pltpu.make_async_copy(w_here, w_ref, w_sem).wait()

    here = pl.ds(pl.multiple_of(span * length, length), length)
    xn = xn_all[here, :]
    xn_ref[...] = xn
    zx = dot(xn, w_ref[:, : 2 * channels])
    z = zx[:, :channels]
    z_ref[...] = z.astype(bf16)
    xp = zx[:, channels:]
    xp_ref[...] = xp.astype(bf16)
    xbuf[8:, :] = xp
    bc = dot(xn, wbc_ref[...], COLS).astype(bf16)
    bc_ref[...] = bc
    bbuf[8:, :] = bc.astype(f32)
    dt = dot(xn, wdt_ref[...], COLS)
    dt_ref[...] = dt

    pre_x = conv_taps(xbuf, cx_ref[0:4, :], cx_ref[4:5, :], length)
    xc = pre_x * sigmoid(pre_x)
    pre_bc = conv_taps(bbuf, cbc_ref[0:4, :], cbc_ref[4:5, :], length)
    bcc = (pre_bc * sigmoid(pre_bc)).astype(bf16)
    xbuf[0:8, :] = xbuf[length : length + 8, :]
    bbuf[0:8, :] = bbuf[length : length + 8, :]
    b_mat = bcc[:, :state]
    c_mat = bcc[:, state:]

    mask, _, step, _, cum = span_values(dt, head_ref)
    cum_t = jnp.transpose(cum)
    scores = dot(c_mat, b_mat, COLS)
    xs = xc * spread_heads(step, channels, head_dim)
    xs_b = xs.astype(bf16)
    lane = lax.broadcasted_iota(jnp.int32, (length, LANES), 1)
    per_tile = LANES // head_dim
    tiles = []
    for tile in range(channels // LANES):
        xs_tile = xs_b[:, tile * LANES : (tile + 1) * LANES]
        out = None
        for sub in range(per_tile):
            head = tile * per_tile + sub
            decay = decay_matrix(mask, cum[:, head : head + 1], cum_t[head : head + 1, :])
            part = dot((scores * decay).astype(bf16), xs_tile)
            out = part if out is None else jnp.where(lane >= sub * head_dim, part, out)
        tiles.append(out)
    hin = hst[...]
    hin_ref[0] = hin
    last = cum[length - 1 : length, :]
    y = jnp.concatenate(tiles, axis=1)
    y = y + dot(c_mat, hin.astype(bf16)) * spread_heads(jnp.exp(cum), channels, head_dim)
    y = y + cx_ref[6:7, :] * xc
    y_ref[...] = y.astype(bf16)
    tail = spread_heads(jnp.exp(last - cum), channels, head_dim)
    keep = spread_heads(jnp.exp(last), channels, head_dim)
    hst[...] = keep * hin + dot(b_mat, (tail * xs).astype(bf16), ROWS)

    gated = y * (z * sigmoid(z))
    scaled = gated * cx_ref[5:6, :]
    squares = jnp.sum(gated * gated, axis=1, keepdims=True)
    high = squares.astype(bf16).astype(f32)
    extra = jnp.where(lane == 0, high, jnp.where(lane == 1, squares - high, 0.0)).astype(bf16)
    mixed = dot(scaled.astype(bf16), w_ref[:, 2 * channels :], COLS).astype(bf16)
    put_half(
        place_ref,
        span,
        pl.num_programs(0) // 2,
        mine_ref,
        other_ref,
        jnp.concatenate([mixed, extra], axis=1),
    )
    if last_layer:
        g = g_all[here, :]
        g_ref[...] = g
        gg = dot(g, w_ref[:, 2 * channels :])
        gg_ref[...] = gg
        products = jnp.sum(gg * scaled, axis=1, keepdims=True)
        both = jnp.where(lane == 0, squares, jnp.where(lane == 1, products, 0.0))
        sums_ref[...] = jnp.transpose(both)[0:8, :]


def gate_part(gg, rms, coef, z, y, cx_ref):
    z, y = z.astype(f32), y.astype(f32)
    norm_gate = cx_ref[5:6, :]
    sz = sigmoid(z)
    silu_z = z * sz
    gated = y * silu_z
    rg = rms * gg
    gate_out = (gated * rms * norm_gate).astype(bf16)
    d_gated = rg * norm_gate - gated * coef
    dz = (d_gated * y * (sz * (1.0 + z * (1.0 - sz)))).astype(bf16)
    return dz, d_gated * silu_z, gate_out, jnp.sum(rg * gated, axis=0, keepdims=True)


def gate_kernel(plan, n_pieces, width, place_ref, *refs):
    pieces = refs[:n_pieces]
    z_ref, y_ref, wo_ref, cx_ref, g_ref, dz_ref, dy_ref, go_ref, acc_ref, first_all = refs[n_pieces:]
    length = z_ref.shape[0]
    span = pl.program_id(0)

    @pl.when(span == 0)
    def _():
        place_pieces(plan, place_ref, pieces, [first_all])
        acc_ref[...] = jnp.zeros_like(acc_ref)

    first = first_all[pl.ds(pl.multiple_of(span * length, length), length), :]
    g = first[:, :width]
    g_ref[...] = g
    tok = first[:, width:].astype(f32)
    rms = tok[:, 0:1] + tok[:, 1:2]
    coef = tok[:, 2:3] + tok[:, 3:4]
    gg = dot(g, wo_ref[...])
    dz, dy, gate_out, acc_norm = gate_part(gg, rms, coef, z_ref[...], y_ref[...], cx_ref)
    dz_ref[...] = dz
    dy_ref[...] = dy
    go_ref[...] = gate_out
    acc_ref[5:6, :] += acc_norm


def scan_kernel(with_gate, head_dim, inner_all, place_ref, *refs):
    if with_gate:
        (gg_ref, tok_ref, z_ref, y_ref), refs = refs[:4], refs[4:]
    else:
        (dy_ref, dz_ref), refs = refs[:2], refs[2:]
    (xn_ref, xp_ref, xhalo_ref, bc_ref, bchalo_ref, dt_ref, hin_ref,
     w_ref, wbc_ref, wdt_ref, cx_ref, cbc_ref, head_ref, pick_ref), refs = refs[:14], refs[14:]
    if with_gate:
        (dz_ref, go_ref), refs = refs[:2], refs[2:]
    (dxt_ref, bcmine_ref, bcother_ref, mine_ref, other_ref, acc_ref, acch_ref, shared_ref,
     accbc, accn, xbuf, bbuf, dubuf, dubbuf, dhst) = refs
    length = xp_ref.shape[0]
    channels = cx_ref.shape[1]
    width = xn_ref.shape[1]
    state = dhst.shape[0]
    step_id = pl.program_id(0)
    first_span = step_id == pl.num_programs(0) - 1

    @pl.when(step_id == 0)
    def _():
        dubuf[length:, :] = jnp.zeros((8, channels), f32)
        dubbuf[length:, :] = jnp.zeros((8, 2 * state), f32)
        dhst[...] = jnp.zeros_like(dhst)
        accn[...] = jnp.zeros_like(accn)
        acc_ref[...] = jnp.zeros_like(acc_ref)
        accbc[...] = jnp.zeros_like(accbc)
        acch_ref[...] = jnp.zeros_like(acch_ref)

    @pl.when(first_span)
    def _():
        xbuf[0:8, :] = jnp.zeros((8, channels), f32)
        bbuf[0:8, :] = jnp.zeros((8, 2 * state), f32)

    @pl.when(jnp.logical_not(first_span))
    def _():
        xbuf[0:8, :] = xhalo_ref[...].astype(f32)[8:16, :]
        bbuf[0:8, :] = bchalo_ref[...].astype(f32)[8:16, :]

    xbuf[8:, :] = xp_ref[...].astype(f32)
    bbuf[8:, :] = bc_ref[...].astype(f32)
    if with_gate:
        tok = jnp.transpose(tok_ref[...])
        rms = lax.rsqrt(tok[:, 0:1] / inner_all + EPS)
        coef = rms * rms * rms * tok[:, 1:2] / inner_all
        dz_b, dy, gate_out, acc_norm = gate_part(
            gg_ref[...], rms, coef, z_ref[...], y_ref[...], cx_ref
        )
        dz_ref[...] = dz_b
        go_ref[...] = gate_out
    else:
        dz_b, dy = dz_ref[...], dy_ref[...]
        acc_norm = jnp.zeros((1, channels), f32)
    skip = cx_ref[6:7, :]

    pre_x = conv_taps(xbuf, cx_ref[0:4, :], cx_ref[4:5, :], length)
    sx = sigmoid(pre_x)
    xc = pre_x * sx
    pre_bc = conv_taps(bbuf, cbc_ref[0:4, :], cbc_ref[4:5, :], length)
    sbc = sigmoid(pre_bc)
    bcc = (pre_bc * sbc).astype(bf16)
    b_mat = bcc[:, :state]
    c_mat = bcc[:, state:]
    mask, pre_dt, step, rate, cum = span_values(dt_ref[...], head_ref)
    cum_t = jnp.transpose(cum)
    last = cum[length - 1 : length, :]
    scores = dot(c_mat, b_mat, COLS)
    step_all = spread_heads(step, channels, head_dim)
    xs = xc * step_all
    xs_b = xs.astype(bf16)
    tail = spread_heads(jnp.exp(last - cum), channels, head_dim)
    keep = spread_heads(jnp.exp(last), channels, head_dim)

    hin = hin_ref[0]
    hin_b = hin.astype(bf16)
    dh = dhst[...]
    dh_b = dh.astype(bf16)
    dye = dy * spread_heads(jnp.exp(cum), channels, head_dim)
    dye_b = dye.astype(bf16)
    txs = tail * xs
    txs_b = txs.astype(bf16)
    carried = dot(c_mat, hin_b)
    pulled = dot(b_mat, dh_b)
    d_c = dot(dye_b, hin_b, COLS)
    d_b = dot(txs_b, dh_b, COLS)
    dhst[...] = keep * dh + dot(c_mat, dye_b, ROWS)
    into = txs * pulled
    across = dye * carried - into
    at_last = jnp.sum(into, axis=0, keepdims=True) + keep * jnp.sum(hin * dh, axis=0, keepdims=True)

    dy_b = dy.astype(bf16)
    dy_t = jnp.transpose(dy).astype(bf16)
    lane = lax.broadcasted_iota(jnp.int32, (length, LANES), 1)
    per_tile = LANES // head_dim
    d_scores = jnp.zeros((length, length), f32)
    row_sums = jnp.zeros((length, LANES), f32)
    col_sums = []
    dxs_parts = []
    for head in range(channels // head_dim):
        tile, sub = divmod(head, per_tile)
        dy_tile = dy_b[:, tile * LANES : (tile + 1) * LANES]
        own = (lane >= sub * head_dim) & (lane < (sub + 1) * head_dim)
        dy_head = jnp.where(own, dy_tile, jnp.zeros_like(dy_tile))
        d_m = dot(dy_head, xs_b[:, tile * LANES : (tile + 1) * LANES], COLS)
        decay = decay_matrix(mask, cum[:, head : head + 1], cum_t[head : head + 1, :])
        dxs_parts.append(
            dot(dy_t[head * head_dim : (head + 1) * head_dim, :], (scores * decay).astype(bf16))
        )
        d_m = d_m * decay
        d_scores = d_scores + d_m
        pairs = d_m * scores
        row_sums = jnp.where(lane == head, jnp.sum(pairs, axis=1, keepdims=True), row_sums)
        col_sums.append(jnp.sum(pairs, axis=0, keepdims=True))
    heads = len(col_sums)
    col_sums = jnp.concatenate(col_sums + [jnp.zeros((LANES - heads, length), f32)], axis=0)
    dxs = jnp.transpose(jnp.concatenate(dxs_parts, axis=0)) + tail * pulled
    pick = pick_ref[...].astype(bf16)
    d_cum = row_sums - jnp.transpose(col_sums) + sum_heads(across, pick)
    at_last = sum_heads(jnp.broadcast_to(at_last, (16, channels)), pick)[0:1, :]
    d_rate = dot_exact(mask, d_cum, ROWS) + at_last
    d_step = d_rate * head_ref[1:2, :] + sum_heads(dxs * xc, pick)
    d_dt = d_step * sigmoid(pre_dt)
    acch_ref[0:1, :] += jnp.sum(d_dt, axis=0, keepdims=True)
    acch_ref[1:2, :] += jnp.sum(d_rate * rate, axis=0, keepdims=True)
    dt_b = d_dt.astype(bf16)
    ds_b = d_scores.astype(bf16)
    d_c = d_c + dot(ds_b, b_mat)
    d_b = d_b + dot(ds_b, c_mat, ROWS)
    d_xc = dxs * step_all + skip * dy
    acc_skip = jnp.sum(dy * xc, axis=0, keepdims=True)

    d_u = d_xc * (sx * (1.0 + pre_x * (1.0 - sx)))
    d_ub = jnp.concatenate([d_b, d_c], axis=1) * (sbc * (1.0 + pre_bc * (1.0 - sbc)))
    dubuf[0:length, :] = d_u
    dubbuf[0:length, :] = d_ub
    d_x = jnp.zeros_like(d_u)
    d_bc = jnp.zeros_like(d_ub)
    acc_rows = []
    accbc_rows = []
    for j in range(4):
        d_x = d_x + cx_ref[j : j + 1, :] * dubuf[pl.ds(3 - j, length), :]
        d_bc = d_bc + cbc_ref[j : j + 1, :] * dubbuf[pl.ds(3 - j, length), :]
        acc_rows.append(jnp.sum(d_u * xbuf[pl.ds(5 + j, length), :], axis=0, keepdims=True))
        accbc_rows.append(jnp.sum(d_ub * bbuf[pl.ds(5 + j, length), :], axis=0, keepdims=True))
    dubuf[length:, :] = d_u[0:8, :]
    dubbuf[length:, :] = d_ub[0:8, :]
    zero = jnp.zeros((1, channels), f32)
    acc_ref[...] += jnp.concatenate(
        acc_rows + [jnp.sum(d_u, axis=0, keepdims=True), acc_norm, acc_skip, zero], axis=0
    )
    zero = jnp.zeros((3, d_ub.shape[1]), f32)
    accbc[...] += jnp.concatenate(
        accbc_rows + [jnp.sum(d_ub, axis=0, keepdims=True), zero], axis=0
    )
    dx_b = d_x.astype(bf16)
    dbc_b = d_bc.astype(bf16)
    dxt_ref[:, :channels] = dx_b
    dxt_ref[:, channels:] = dt_b
    put_columns(
        place_ref,
        pl.num_programs(0) - 1 - step_id,
        bcmine_ref,
        bcother_ref,
        jnp.transpose(d_bc).astype(bf16),
    )
    total = dot(jnp.concatenate([dz_b, dx_b], axis=1), w_ref[...], COLS)
    total = total + dot(dbc_b, wbc_ref[...]) + dot(dt_b, wdt_ref[...])
    accn[0:1, :] += jnp.sum(total * xn_ref[...].astype(f32), axis=0, keepdims=True)

    @pl.when(first_span)
    def _():
        lanes = shared_ref.shape[1]
        lines = [accn[0:1, i * lanes : (i + 1) * lanes] for i in range(width // lanes)]
        shared = jnp.concatenate(lines + [accbc[0:5, :]], axis=0)
        shared_ref[0 : shared.shape[0], :] = shared.astype(bf16)
        shared_ref[shared.shape[0] :, :] = jnp.zeros(
            (shared_ref.shape[0] - shared.shape[0], lanes), bf16
        )

    put_half(
        place_ref,
        pl.num_programs(0) - 1 - step_id,
        pl.num_programs(0) // 2,
        mine_ref,
        other_ref,
        total.astype(bf16),
    )


def whole(shape):
    zeros = (0,) * len(shape)
    return pl.BlockSpec(shape, lambda i, p: zeros)


def span_rows(columns):
    return pl.BlockSpec((SPAN, columns), lambda i, p: (i, 0))


def half_rows(columns, spans, reverse):
    half = spans // 2

    def block(i, core):
        span = spans - 1 - i if reverse else i
        return jnp.clip(span - half * core, 0, half - 1), 0

    return [
        pl.BlockSpec((SPAN, columns), lambda i, p: block(i, p[0])),
        pl.BlockSpec((SPAN, columns), lambda i, p: block(i, 1 - p[0])),
    ]


def span_call(kernel, name, spans, place, operands, in_specs, shapes, out_specs, scratch, flops):
    moved = sum(v.size * v.dtype.itemsize for v in [*operands, *shapes])
    return pl.pallas_call(
        kernel,
        grid_spec=pltpu.PrefetchScalarGridSpec(
            num_scalar_prefetch=1,
            grid=(spans,),
            in_specs=in_specs,
            out_specs=out_specs,
            scratch_shapes=scratch,
        ),
        out_shape=shapes,
        compiler_params=pltpu.CompilerParams(
            dimension_semantics=("arbitrary",), vmem_limit_bytes=VMEM_BYTES
        ),
        cost_estimate=pl.CostEstimate(flops=flops, bytes_accessed=moved, transcendentals=0),
        name=name,
    )(place, *operands)


def run_forward(place, gathered, w, wdt, small, state, head_dim):
    w_here, w_there, there_plan = w
    channels = small[0].shape[1]
    width = gathered[0][0][0].shape[1]
    anywhere = pl.BlockSpec(memory_space=pl.ANY)
    tokens = NC * NZ * gathered[0][2][0]
    spans = tokens // SPAN
    last_layer = len(gathered) == 2
    plans = [(cut_plan(*one), len(one[0])) for one in gathered]
    operands = [p for one in gathered for p in one[0]]
    in_specs = [whole(v.shape) for v in operands] + [anywhere] * (1 + len(w_there))
    operands += [w_here, *w_there, wdt, *small]
    in_specs += [whole(v.shape) for v in operands[len(in_specs) :]]
    shapes = [
        jax.ShapeDtypeStruct(w_here.shape, bf16),
        jax.ShapeDtypeStruct((tokens, width), bf16),
        jax.ShapeDtypeStruct((2 * state, width), bf16),
        jax.ShapeDtypeStruct((tokens, channels), bf16),
        jax.ShapeDtypeStruct((tokens, channels), bf16),
        jax.ShapeDtypeStruct((tokens, 2 * state), bf16),
        jax.ShapeDtypeStruct((tokens, LANES), f32),
        jax.ShapeDtypeStruct((tokens, channels), bf16),
        jax.ShapeDtypeStruct((spans, state, channels), f32),
        jax.ShapeDtypeStruct((tokens // 2, width + LANES), bf16),
        jax.ShapeDtypeStruct((tokens // 2, width + LANES), bf16),
    ]
    out_specs = [whole(w_here.shape), span_rows(width), whole((2 * state, width))]
    out_specs += [span_rows(s.shape[1]) for s in shapes[3:8]]
    out_specs.append(pl.BlockSpec((1, state, channels), lambda i, p: (i, 0, 0)))
    out_specs += half_rows(width + LANES, spans, False)
    scratch = [
        pltpu.SemaphoreType.DMA,
        pltpu.VMEM((tokens, width), bf16),
        pltpu.VMEM((SPAN + 8, channels), f32),
        pltpu.VMEM((SPAN + 8, 2 * state), f32),
        pltpu.VMEM((state, channels), f32),
    ]
    if last_layer:
        shapes += [
            jax.ShapeDtypeStruct((tokens, width), bf16),
            jax.ShapeDtypeStruct((8, tokens), f32),
            jax.ShapeDtypeStruct((tokens, channels), f32),
        ]
        out_specs += [span_rows(width), pl.BlockSpec((8, SPAN), lambda i, p: (0, i)), span_rows(channels)]
        scratch.append(pltpu.VMEM((tokens, width), bf16))
    kernel = functools.partial(forward_kernel, plans, there_plan, head_dim)
    return span_call(
        kernel, "layer_forward", spans, place, operands, in_specs, shapes, out_specs, scratch, 20 * 10**9
    )


def run_gate(place, gathered, z, y, w, cx):
    tokens, channels = z.shape
    width = w.shape[0]
    spans = tokens // SPAN
    plan, pieces = cut_plan(*gathered), list(gathered[0])
    operands = [*pieces, z, y, w, cx]
    in_specs = [whole(p.shape) for p in pieces]
    in_specs += [span_rows(channels), span_rows(channels)]
    in_specs += [pl.BlockSpec((width, channels), lambda i, p: (0, 2)), whole(cx.shape)]
    shapes = [
        jax.ShapeDtypeStruct((tokens, width), bf16),
        jax.ShapeDtypeStruct((tokens, channels), bf16),
        jax.ShapeDtypeStruct((tokens, channels), f32),
        jax.ShapeDtypeStruct((tokens, channels), bf16),
        jax.ShapeDtypeStruct((8, channels), f32),
    ]
    out_specs = [span_rows(s.shape[1]) for s in shapes[:4]] + [whole(shapes[4].shape)]
    scratch = [pltpu.VMEM((tokens, pieces[0].shape[1]), bf16)]
    kernel = functools.partial(gate_kernel, plan, len(pieces), width)
    return span_call(
        kernel, "gate_backward", spans, place, operands, in_specs, shapes, out_specs, scratch, 6 * 10**9
    )


def run_scan(place, lead, xn, xp, bc, dt, hin, weights, small, pick, head_dim, inner_all):
    tokens, channels = xp.shape
    state = hin.shape[1]
    width = xn.shape[1]
    spans = tokens // SPAN
    with_gate = len(lead) == 4

    def rev(columns):
        return pl.BlockSpec((SPAN, columns), lambda i, p: (spans - 1 - i, 0))

    def halo(columns, rows):
        per = SPAN // rows
        return pl.BlockSpec(
            (rows, columns), lambda i, p: (jnp.maximum((spans - 1 - i) * per - 1, 0), 0)
        )

    operands = [*lead, xn, xp, xp, bc, bc, dt, hin, *weights, *small, pick]
    in_specs = [rev(channels)] * 2
    if with_gate:
        tok = pl.BlockSpec((8, SPAN), lambda i, p: (0, spans - 1 - i))
        in_specs = [rev(channels), tok, rev(channels), rev(channels)]
    in_specs += [
        rev(width),
        rev(channels),
        halo(channels, 16),
        rev(2 * state),
        halo(2 * state, 16),
        rev(LANES),
        pl.BlockSpec((1, state, channels), lambda i, p: (spans - 1 - i, 0, 0)),
    ]
    in_specs.append(whole((width, 2 * channels)))
    in_specs += [whole(v.shape) for v in operands[len(in_specs) :]]
    shapes = [
        jax.ShapeDtypeStruct((tokens, channels + LANES), bf16),
        jax.ShapeDtypeStruct((state * spans, SPAN), bf16),
        jax.ShapeDtypeStruct((state * spans, SPAN), bf16),
        jax.ShapeDtypeStruct((tokens // 2, width), bf16),
        jax.ShapeDtypeStruct((tokens // 2, width), bf16),
        jax.ShapeDtypeStruct((8, channels), f32),
        jax.ShapeDtypeStruct((8, LANES), f32),
        jax.ShapeDtypeStruct((16, 2 * state), bf16),
    ]
    out_specs = [rev(channels + LANES), whole(shapes[1].shape), whole(shapes[2].shape)]
    out_specs += half_rows(width, spans, True)
    out_specs += [whole(s.shape) for s in shapes[5:]]
    if with_gate:
        shapes = [jax.ShapeDtypeStruct((tokens, channels), bf16)] * 2 + shapes
        out_specs = [rev(channels)] * 2 + out_specs
    scratch = [
        pltpu.VMEM((8, 2 * state), f32),
        pltpu.VMEM((8, width), f32),
        pltpu.VMEM((SPAN + 8, channels), f32),
        pltpu.VMEM((SPAN + 8, 2 * state), f32),
        pltpu.VMEM((SPAN + 8, channels), f32),
        pltpu.VMEM((SPAN + 8, 2 * state), f32),
        pltpu.VMEM((state, channels), f32),
    ]
    kernel = functools.partial(scan_kernel, with_gate, head_dim, inner_all)
    return span_call(
        kernel, "scan_backward", spans, place, operands, in_specs, shapes, out_specs, scratch, 28 * 10**9
    )


def weight_kernel(n_pairs, split, place_ref, *refs):
    lefts, rights, outs = refs[:n_pairs], refs[n_pairs : 2 * n_pairs], refs[2 * n_pairs :]

    def write(out_ref):
        at = 0
        for left_ref, right_ref in zip(lefts, rights):
            columns = right_ref.shape[1]
            out_ref[:, at : at + columns] = dot(left_ref[...], right_ref[...], ROWS).astype(bf16)
            at += columns

    if not split:
        write(outs[0])
        return
    for k, out_ref in enumerate(outs):
        pl.when(pl.program_id(0) == k)(functools.partial(write, out_ref))


def weight_products(place, pairs, split=True):
    tokens = pairs[0][0].shape[0]
    rows = max(left.shape[1] for left, _ in pairs)
    block = rows // 4

    def at(i, p):
        return lax.rem(p[3] + i, NX) if split else i

    lefts, rights, columns = [], [], []
    for left, right in pairs:
        quarter = left.shape[1] == block
        cut, uncut = (lambda i, p: (0, at(i, p))), (lambda i, p: (0, 0))
        lefts.append(pl.BlockSpec((tokens, block), uncut if quarter else cut))
        wide = block if quarter else right.shape[1]
        rights.append(pl.BlockSpec((tokens, wide), cut if quarter else uncut))
        columns.append(wide)
    columns = sum(columns)
    if split:
        out_specs = [whole((block, columns))] * 4
        shapes = [jax.ShapeDtypeStruct((block, columns), bf16)] * 4
    else:
        out_specs = [pl.BlockSpec((block, columns), lambda i, p: (i, 0))]
        shapes = [jax.ShapeDtypeStruct((rows, columns), bf16)]
    out = pl.pallas_call(
        functools.partial(weight_kernel, len(pairs), split),
        grid_spec=pltpu.PrefetchScalarGridSpec(
            num_scalar_prefetch=1, grid=(4,), in_specs=lefts + rights, out_specs=out_specs
        ),
        out_shape=shapes,
        compiler_params=pltpu.CompilerParams(vmem_limit_bytes=VMEM_BYTES),
        cost_estimate=pl.CostEstimate(
            flops=2 * tokens * rows * columns, bytes_accessed=8 * 10**6, transcendentals=0
        ),
        name="weight_products",
    )(place, *[left for left, _ in pairs], *[right for _, right in pairs])
    return out if split else out[0]


SIZES = (4, 2, 2, 2, 4)
NX, NYL, NC, NYH, NZ = SIZES
EVERY = [
    (x, yl, c, yh, z)
    for x in range(NX)
    for yl in range(NYL)
    for c in range(NC)
    for yh in range(NYH)
    for z in range(NZ)
]


def linear(x, yl, c, yh, z):
    return ((((x % NX) * NYL + yl % NYL) * NC + c % NC) * NYH + yh % NYH) * NZ + z % NZ


def send(v, step, only=None):
    pairs = [(linear(*d), linear(*step(*d))) for d in EVERY if only is None or only(*d)]
    return lax.ppermute(v, ("dp", "tensor"), pairs)


def send_z(v, k):
    return send(v, lambda x, yl, c, yh, z: (x, yl, c, yh, z + k))


def send_core(v):
    return send(v, lambda x, yl, c, yh, z: (x, yl, c + 1, yh, z))


def trade(v, k):
    return send(v, lambda x, yl, c, yh, z: (x, yl, yh, c, z + k))


def traded(v):
    return send(v, lambda x, yl, c, yh, z: (x, yl, yh, c, z), lambda x, yl, c, yh, z: c != yh)


def trade_places(v):
    _, _, core, yh, _ = position()
    return jnp.where(core == yh, v, traded(v))


def position():
    dp, tensor = lax.axis_index("dp"), lax.axis_index("tensor")
    return dp // (NYL * NC), dp // NC % NYL, dp % NC, tensor // NZ, tensor % NZ


def gather(v, parts, traded_own=None, later=()):
    arrays, sources = [], []
    for k in (0, 1, 3, 2):
        if traded_own is not None:
            piece = trade(v, k) if k else traded_own
        else:
            piece = send_z(v, k) if k else v
        arrays += [piece, send_core(after(piece, *later) if later else piece)]
        sources += [(False, -k % NZ, 0), (True, -k % NZ, 0)]
    return arrays, sources, parts


def cut_plan(arrays, sources, parts):
    plan = []
    for number, (piece, (other, dz, first)) in enumerate(zip(arrays, sources)):
        base = 0
        for out, per in enumerate(parts):
            begin, end = max(first, base), min(first + piece.shape[0], base + per)
            if begin < end:
                plan.append((number, other, dz, begin - first, out, per, begin - base, end - begin))
            base += per
    return plan


def fold(mine, other):
    _, _, _, _, z = position()
    rows = mine.shape[0] // NZ
    blocks = []
    for k in range(NZ):
        at = (z + k) % NZ * rows
        a = lax.dynamic_slice_in_dim(mine, at, rows, 0).astype(f32)
        blocks.append(a + lax.dynamic_slice_in_dim(other, at, rows, 0).astype(f32))
    return blocks


def fold_beside(pairs):
    folded = [fold(mine, send_core(other)) for mine, other in pairs]
    return [jnp.concatenate([blocks[k] for blocks in folded], axis=1) for k in range(NZ)]


def scatter(*pairs, meanwhile=None):
    own, one, two, three = fold_beside(pairs)
    if meanwhile is not None:
        two = after(two, meanwhile)
    return [own] + [send_z(b.astype(bf16), k) for k, b in ((1, one), (2, two), (3, three))]


def scatter_with_sum(mine, other, shared, meanwhile):
    half = mine.shape[0]
    rows = half // NZ
    got = after(send_core(jnp.concatenate([other, shared], axis=0)), *meanwhile)
    blocks = fold(mine, got[:half])
    total_shared = shared.astype(f32) + got[half:].astype(f32)
    packed = total_shared.astype(bf16)
    total = blocks[0]
    for k in range(1, NZ):
        got = send_z(jnp.concatenate([blocks[k].astype(bf16), packed], axis=0), k)
        total = total + got[:rows].astype(f32)
        total_shared = total_shared + got[rows:].astype(f32)
    return total, total_shared


def sum_members(v):
    both = v + send_core(v)
    total = both
    for k in range(1, NZ):
        total = total + send_z(both, k)
    return total


def send_far(v):
    return send(v, lambda x, yl, c, yh, z: (x, yl, c, yh + 1, z), lambda x, yl, c, yh, z: c != yh)


def sum_far(v, far=None):
    far = send_far(v) if far is None else far
    return (v.astype(f32) + far.astype(f32)).astype(bf16)


def halve(v):
    _, _, core, yh, _ = position()
    half = v.shape[0] // 2
    near = send(
        v[half:], lambda x, yl, c, yh, z: (x, yl, c + 1, yh, z), lambda x, yl, c, yh, z: c == yh
    )
    return jnp.where(core == yh, v[:half], near)


def sum_beside(part):
    beside = send(part, lambda x, yl, c, yh, z: (x, yl + 1, c, yh, z))
    return (part.astype(f32) + beside.astype(f32)).astype(bf16)


def sum_x(blocks):
    total = blocks[0].astype(f32)
    for k in range(1, NX):
        got = send(blocks[k], lambda x, yl, c, yh, z, k=k: (x + k, yl, c, yh, z))
        total = total + got.astype(f32)
    return total.astype(bf16)


def cut_x(v):
    x = position()[0]
    rows = v.shape[0] // NX
    return [lax.dynamic_slice_in_dim(v, (x + k) % NX * rows, rows, 0) for k in range(NX)]


def collect_x(part, meanwhile=()):
    parts = [part]
    for k in range(1, NX):
        got = send(part, lambda x, yl, c, yh, z, k=k: (x + k, yl, c, yh, z))
        parts.append(after(got, *meanwhile) if meanwhile else got)
    return jnp.stack(parts)


def write_kernel(plan, n_kept, place_ref, here_ref, there_ref, *refs):
    rows = here_ref.shape[1]

    def write(ref):
        for (column, kind, wide, by_half), out_ref in zip(plan, refs[n_kept:]):
            for x in range(NX):
                value = ref[lax.rem(place_ref[3] + NX - x, NX), :, column : column + wide].astype(f32)
                if kind != "blocks":
                    out_ref[0, 0 if by_half else x, x if by_half else 0] = value
                elif by_half:
                    at = x // 2 * wide
                    out_ref[0, x % 2 * rows : (x % 2 + 1) * rows, at : at + wide] = value
                else:
                    out_ref[0, :, x * wide : (x + 1) * wide] = value

    here = (pl.program_id(0) == 0) == (place_ref[2] == 1)

    @pl.when(here)
    def _():
        write(here_ref)

    @pl.when(jnp.logical_not(here))
    def _():
        write(there_ref)


def write_sums(place, halves, outputs):
    rows, columns = halves[0].shape[1:]
    total = 2 * NX * rows
    wide = total // 4
    plan, shapes, specs, finals, kept, alias = [], [], [], [], [], {}
    for column, kind, layer, array, by_half in outputs:
        lanes = LANES if kind == "flat" else wide
        layers = 1 if kind == "flat" else 2
        plan.append((column, kind, lanes, by_half))
        if kind == "blocks":
            shape = (layers, wide, total)
            if by_half:
                spec = pl.BlockSpec((1, wide, total // 2), lambda h, p, layer=layer: (layer, 0, h))
            else:
                spec = pl.BlockSpec((1, rows, total), lambda h, p, layer=layer: (layer, h, 0))
            finals.append(shape)
        elif by_half:
            shape = (layers, 2, NX, rows, lanes)
            spec = pl.BlockSpec((1, 1, NX, rows, lanes), lambda h, p, layer=layer: (layer, h, 0, 0, 0))
            finals.append((layers, total, lanes))
        else:
            shape = (layers, NX, 2, rows, lanes)
            spec = pl.BlockSpec((1, NX, 1, rows, lanes), lambda h, p, layer=layer: (layer, 0, h, 0, 0))
            finals.append((layers, total, lanes))
        shapes.append(jax.ShapeDtypeStruct(shape, f32))
        specs.append(spec)
        if array is not None:
            alias[3 + len(kept)] = len(shapes) - 1
            kept.append(array.reshape(shape))
    piece = pl.BlockSpec((NX, rows, columns), lambda h, p: (0, 0, 0))
    written = pl.pallas_call(
        functools.partial(write_kernel, plan, len(kept)),
        grid_spec=pltpu.PrefetchScalarGridSpec(
            num_scalar_prefetch=1,
            grid=(2,),
            in_specs=[piece, piece] + [pl.BlockSpec(memory_space=pl.ANY)] * len(kept),
            out_specs=specs,
        ),
        out_shape=shapes,
        input_output_aliases=alias,
        compiler_params=pltpu.CompilerParams(vmem_limit_bytes=VMEM_BYTES),
        name="write_sums",
    )(place, *halves, *kept)
    return [v.reshape(final) for v, final in zip(written, finals)]


def row_call(kernel, name, operands, shapes):
    return pl.pallas_call(
        kernel,
        grid=(1,),
        in_specs=[pl.BlockSpec((rows, v.shape[1]), lambda i: (0, 0)) for v, rows in operands],
        out_specs=[pl.BlockSpec(s.shape, lambda i, n=len(s.shape): (0,) * n) for s in shapes],
        out_shape=shapes,
        compiler_params=pltpu.CompilerParams(vmem_limit_bytes=VMEM_BYTES),
        name=name,
    )(*[v for v, _ in operands])


def inverse_rms(v):
    return lax.rsqrt(jnp.mean(v * v, axis=-1, keepdims=True) + EPS)


def first_kernel(packed_ref, gain_ref, out_ref):
    rows = 128
    v = packed_ref[0:rows, :].astype(f32)
    out_ref[0:rows, :] = (v * inverse_rms(v) * gain_ref[...]).astype(bf16)
    out_ref[rows:, :] = packed_ref[rows : out_ref.shape[0], :]


def add_terms(own_ref, a_ref, b_ref, c_ref):
    total = own_ref[...].astype(f32) + a_ref[...].astype(f32)
    return total + (b_ref[...].astype(f32) + c_ref[...].astype(f32))


def unscaled_output(inner_all, terms, width):
    total = add_terms(*terms)
    squares = total[:, width : width + 1] + total[:, width + 1 : width + 2]
    gate_rms = lax.rsqrt(squares / inner_all + EPS)
    return gate_rms, total[:, :width] * gate_rms


def middle_kernel(inner_all, own_ref, a_ref, b_ref, c_ref, res_ref, gain_ref, res1_ref, mixed_ref, rms_ref, normed_ref):
    width = res_ref.shape[1]
    gate_rms, mixed = unscaled_output(inner_all, (own_ref, a_ref, b_ref, c_ref), width)
    res = res_ref[...].astype(f32) + mixed
    res1_ref[...] = res
    mixed_ref[...] = mixed
    rms_ref[...] = jnp.broadcast_to(gate_rms, rms_ref.shape)
    normed_ref[...] = (res * inverse_rms(res) * gain_ref[...]).astype(bf16)


def input_gradient(grad_normed, res, d_res, gain):
    inv = inverse_rms(res)
    scaled = grad_normed * gain
    dots = jnp.sum(scaled * res, axis=-1, keepdims=True) / res.shape[1]
    return d_res + inv * scaled - res * (inv * inv * inv) * dots


def between_kernel(inner_all, own_ref, a_ref, b_ref, c_ref, res_ref, dres_ref, gain_ref, mixed_ref, rms_ref, out_ref, sent_ref):
    width = res_ref.shape[1]
    grad_normed = add_terms(*(ref.at[:, 0:width] for ref in (own_ref, a_ref, b_ref, c_ref)))
    d_res = input_gradient(grad_normed, res_ref[...], dres_ref[...].astype(f32), gain_ref[...])
    out_ref[...] = d_res
    g_mixed = d_res.astype(bf16)
    sent_ref[:, :width] = g_mixed
    gate_rms = rms_ref[:, 0:1]
    products = jnp.sum(g_mixed.astype(f32) * mixed_ref[...], axis=-1, keepdims=True)
    coef = gate_rms * gate_rms * products / inner_all
    lane = lax.broadcasted_iota(jnp.int32, rms_ref.shape, 1)
    rms_high = gate_rms.astype(bf16).astype(f32)
    coef_high = coef.astype(bf16).astype(f32)
    extra = jnp.where(lane == 0, rms_high, jnp.where(lane == 1, gate_rms - rms_high, 0.0))
    extra = jnp.where(lane == 2, coef_high, jnp.where(lane == 3, coef - coef_high, extra))
    sent_ref[:, width:] = extra.astype(bf16)


def end_kernel(own_ref, a_ref, b_ref, c_ref, res_ref, dres_ref, gain_ref, hidden_ref, out_ref):
    width = res_ref.shape[1]
    grad_normed = add_terms(own_ref, a_ref, b_ref, c_ref)
    grad = input_gradient(grad_normed, res_ref[...].astype(f32), dres_ref[...], gain_ref[...])
    out_ref[:, :width] = hidden_ref[...]
    out_ref[:, width:] = grad.astype(bf16)


def last_kernel(inner_all, own_ref, a_ref, b_ref, c_ref, res_ref, out_ref):
    _, mixed = unscaled_output(inner_all, (own_ref, a_ref, b_ref, c_ref), res_ref.shape[1])
    out_ref[...] = (res_ref[...] + mixed).astype(bf16)


TINY_ROWS = 56


def small_kernel(head_dim, ends, narrow0_ref, narrow1_ref, gain_ref, pick_ref, norm_ref, wbc_ref, wdt_ref, cx_ref,
                 cxb_ref, cbc_ref, cbcb_ref, dtb_ref, alog_ref, skip_ref, ng_ref):
    bc_at, tiny_at = ends
    heads = wdt_ref.shape[0]
    channels = cx_ref.shape[2]
    both = cbc_ref.shape[2]
    lanes = narrow0_ref.shape[1] - tiny_at
    for layer, ref in enumerate((narrow0_ref, narrow1_ref)):
        columns = jnp.transpose(ref[...])
        wbc_ref[layer] = columns[bc_at:tiny_at]
        wdt_ref[:, layer, :] = columns[0:heads]
    tiny = jnp.concatenate(
        [narrow0_ref[i * TINY_ROWS : (i + 1) * TINY_ROWS, tiny_at:] for i in range(channels // lanes)], axis=1
    )
    lines = norm_ref.shape[1] // both
    for layer in range(2):
        rows = tiny[8 * layer : 8 * layer + 8]
        cx_ref[layer] = rows[0:4]
        cxb_ref[layer : layer + 1, :] = rows[4:5]
        ng_ref[layer : layer + 1, :] = rows[5:6]
        skip_ref[layer : layer + 1, :] = dot(rows, pick_ref[...], PLAIN, highest)[6:7, 0:heads]
        at = 16 + 2 * layer
        dtb_ref[layer : layer + 1, :] = tiny[at : at + 1, 0:heads]
        alog_ref[layer : layer + 1, :] = tiny[at + 1 : at + 2, 0:heads]
        at = 20 + 16 * layer
        norm = jnp.concatenate([tiny[at + i : at + i + 1, 0:both] for i in range(lines)], axis=1)
        norm_ref[layer : layer + 1, :] = norm / gain_ref[layer : layer + 1, :]
        cbc_ref[layer] = tiny[at + lines : at + lines + 4, 0:both]
        cbcb_ref[layer : layer + 1, :] = tiny[at + lines + 4 : at + lines + 5, 0:both]


def after(v, *others):
    return lax.optimization_barrier((v, *others))[0]


def pad_to(v, rows, lanes):
    return jnp.pad(v, ((0, rows - v.shape[0]), (0, lanes - v.shape[1])))


def local(
    hidden_in,
    grad_out,
    norm_in,
    w_z,
    w_x,
    w_bc,
    w_dt,
    conv_x,
    conv_x_bias,
    conv_bc,
    conv_bc_bias,
    dt_bias,
    a_log,
    skip,
    norm_gate,
    w_out,
):
    layers, width, channels = w_z.shape
    heads = w_dt.shape[2]
    head_dim = channels // heads
    both = conv_bc.shape[2]
    state = both // 2
    members = NC * NZ
    inner_all = channels * members
    rows = hidden_in.shape[1]
    bc_rows = both // members
    x, _, core, yh, z = position()
    stays = core == yh
    place = jnp.stack([core, z, stays, x]).astype(jnp.int32)
    full = jax.ShapeDtypeStruct((rows, width), f32)

    def pack_weights(layer):
        return jnp.concatenate([w_z[layer], w_x[layer], w_out[layer].T], axis=1)

    bc_t = jnp.swapaxes(w_bc, 1, 2)
    dt_t = jnp.pad(jnp.swapaxes(w_dt, 1, 2), ((0, 0), (0, 8 - heads), (0, 0)))
    per_channel = jnp.concatenate(
        [conv_x, conv_x_bias[:, None], norm_gate[:, None], jnp.repeat(skip, head_dim, axis=1)[:, None]],
        axis=1,
    )
    per_channel = jnp.pad(per_channel, ((0, 0), (0, 1), (0, 0)))
    per_head = jnp.stack([dt_bias, -jnp.exp(a_log)], axis=1)
    per_head = jnp.pad(per_head, ((0, 0), (0, 6), (0, LANES - heads)))
    little = jnp.concatenate([per_channel, per_head], axis=2).reshape(layers * 8, channels + LANES)
    high = little.astype(bf16)
    low = (little - high.astype(f32)).astype(bf16)
    lines = pad_to(jnp.concatenate([high, low], axis=1), layers * 8, width)
    packed = jnp.concatenate([hidden_in[0], bc_t[0], dt_t.reshape(layers * 8, width), lines], axis=0)
    packed = trade_places(packed)
    lines = packed[packed.shape[0] - layers * 8 :].astype(f32)
    little = lines[:, : channels + LANES] + lines[:, channels + LANES : 2 * (channels + LANES)]
    little = little.reshape(layers, 8, channels + LANES)

    w0 = pack_weights(0)
    w0 = w0, [traded(after(w0, packed))], [(0, None)]
    grads = jnp.concatenate([grad_out[0], bc_t[1]], axis=0)

    [sent] = row_call(
        first_kernel,
        "first_norm",
        [(packed, packed.shape[0]), (norm_in[0:1], 1)],
        [jax.ShapeDtypeStruct((rows + bc_rows, width), bf16)],
    )
    gathered0 = gather(sent, (rows, bc_rows))
    wdt = [pad_to(packed[rows + bc_rows + 8 * l : rows + bc_rows + 8 * (l + 1)], LANES, width) for l in range(layers)]
    smalls = []
    for layer in range(layers):
        cbc = jnp.concatenate([conv_bc[layer], conv_bc_bias[layer][None], jnp.zeros((3, both), f32)], axis=0)
        smalls.append((little[layer, :, :channels], cbc, little[layer, :, channels:]))
    channel_head = jnp.arange(channels) // head_dim
    pick = (channel_head[:, None] == jnp.arange(LANES)[None, :]).astype(f32)

    out0 = run_forward(place, [gathered0], w0, wdt[0], smalls[0], state, head_dim)
    w0, xn0, wbc0, z0, xp0, bc0, dt0, y0, hin0, mine, other = out0
    grads = after(grads, sent)
    gathered_grad = gather(grads, (rows, bc_rows), jnp.where(stays, grads, after(traded(grads), mine)), (mine,))
    grad_held = gathered_grad[0][0]
    terms = scatter((mine, after(other, *gathered_grad[0][::2])))
    w1 = pack_weights(1)
    w1 = w1, [traded(after(w1, terms[0]))], [(0, None)]
    res1, mixed0, rms0, normed1 = row_call(
        functools.partial(middle_kernel, inner_all),
        "middle_norm",
        [(v, rows) for v in terms] + [(packed, rows), (norm_in[1:2], 1)],
        [full, full, jax.ShapeDtypeStruct((rows, LANES), f32), jax.ShapeDtypeStruct((rows, width), bf16)],
    )
    gathered1 = gather(normed1, (rows,))
    out1 = run_forward(
        place, [gathered1, gathered_grad], w1, wdt[1], smalls[1], state, head_dim
    )
    w1, xn1, wbc1, z1, xp1, bc1, dt1, y1, hin1, mine, other, grad_rows1, sums, gg1 = out1
    sums = sum_members(sums)

    home = fold(mine, send_core(other))
    sums = after(sums, *home)
    home = home[:1] + [send_z(home[k].astype(bf16), k) for k in range(1, NZ)]
    back1 = run_scan(
        place, (gg1, sums, z1, y1), xn1, xp1, bc1, dt1, hin1, (w1, wbc1, wdt[1]), smalls[1], pick, head_dim,
        inner_all,
    )
    dz1, go1, dxt1, *bc_halves, mine, other, acc1, acch1, shared1 = back1
    terms = scatter((mine, after(other, *home)), bc_halves)
    [hidden_out] = row_call(
        functools.partial(last_kernel, inner_all),
        "last_output",
        [(after(home[0], terms[1]), rows)] + [(v, rows) for v in home[1:]] + [(res1, rows)],
        [jax.ShapeDtypeStruct((rows, width), bf16)],
    )
    d_res1, sent = row_call(
        functools.partial(between_kernel, inner_all),
        "between_layers",
        [(v, rows) for v in terms]
        + [(res1, rows), (grad_held, rows), (norm_in[1:2], 1), (mixed0, rows), (rms0, rows)],
        [full, jax.ShapeDtypeStruct((rows, width + LANES), bf16)],
    )
    gathered_back = gather(sent, (rows,))
    early1 = weight_products(place, [(xn1, after(dz1, sent)), (go1, grad_rows1)], split=False)
    early1_far = send_far(early1)

    bc_at = channels + bc_rows

    def with_bc(dxt, bc_sum):
        by_token = bc_sum.reshape(-1, bc_rows, SPAN).swapaxes(1, 2).reshape(-1, bc_rows)
        spread = jnp.pad(by_token, ((0, 0), (bc_at, dxt.shape[1] - bc_at - bc_rows)))
        return dxt + spread.astype(bf16)

    dxt1 = with_bc(dxt1, sum(v[:, width:].astype(f32) for v in terms))

    z0 = after(z0, early1)
    grad_rows0, dz0, dy0, go0, acc_gate0 = run_gate(place, gathered_back, z0, y0, w0, smalls[0][0])
    early = weight_products(place, [(xn0, dz0), (go0, grad_rows0), (xn1, dxt1)])
    dy0 = after(dy0, *early)
    early = sum_x(early)
    back0 = run_scan(
        place, (dy0, dz0), xn0, xp0, bc0, dt0, hin0, (w0, wbc0, wdt[0]), smalls[0], pick, head_dim, inner_all
    )
    dxt0, *bc_halves, mine, other, acc0, acch0, shared0 = back0
    early1 = sum_x(cut_x(halve(sum_far(early1, after(early1_far, early)))))
    early1 = sum_beside(early1)
    shared = jnp.concatenate([shared0, shared1], axis=0)
    bc_sum, shared = scatter_with_sum(*bc_halves, shared, (early,))
    tiny_at = bc_at + bc_rows
    tiny_lanes = channels + LANES - tiny_at
    tiny = jnp.concatenate(
        [acc0 + acc_gate0, acc1] + [pad_to(v, v.shape[0], channels) for v in (acch0[0:2], acch1[0:2], shared)],
        axis=0,
    )
    tiny = pad_to(tiny, TINY_ROWS, channels)
    tiny = [tiny[:, i * tiny_lanes : (i + 1) * tiny_lanes] for i in range(channels // tiny_lanes)]
    tiny = pad_to(jnp.concatenate(tiny, axis=0), width, tiny_lanes)
    tiny = jnp.pad(tiny, ((0, 0), (tiny_at, 0))).astype(bf16)
    early = halve(sum_far(after(early, dxt0)))
    late = weight_products(place, [(xn0, after(with_bc(dxt0, bc_sum), early))])
    home = fold(mine, send_core(after(other, late[0])))
    early = sum_beside(early)
    tiny = after(tiny, early)
    late = [v + t for v, t in zip(late, cut_x(tiny))]
    late = sum_x(late)

    terms = home[:1] + [send_z(home[k].astype(bf16), k) for k in range(1, NZ)]
    [outputs] = row_call(
        end_kernel,
        "outputs",
        [(v, rows) for v in terms] + [(packed, rows), (d_res1, rows), (norm_in[0:1], 1), (hidden_out, rows)],
        [jax.ShapeDtypeStruct((rows, 2 * width), bf16)],
    )
    outputs_there = traded(outputs)
    outputs_home = jnp.where(stays, outputs, outputs_there).astype(f32)

    early = after(collect_x(early), outputs)
    early = early, send_core(early)
    early1 = collect_x(after(early1, early[0]))
    early1 = early1, send_core(early1)
    g_wz, g_wo, g_wx, narrow1 = write_sums(
        place,
        early,
        [
            (0, "rows", 0, None, False),
            (channels, "blocks", 0, None, False),
            (2 * channels, "rows", 1, None, False),
            (3 * channels, "flat", 0, None, False),
        ],
    )
    g_wz, g_wo = write_sums(
        place, early1, [(0, "rows", 1, g_wz, True), (channels, "blocks", 1, g_wo, True)]
    )
    late = collect_x(sum_beside(halve(sum_far(after(late, outputs_there)))), (g_wz,))
    late = late, send_core(late)
    g_wx, narrow0 = write_sums(
        place, late, [(0, "rows", 0, g_wx, False), (channels, "flat", 0, None, False)]
    )

    narrow0, narrow1 = narrow0[0], narrow1[0]
    small = row_call(
        functools.partial(small_kernel, head_dim, (bc_at - channels, tiny_at - channels)),
        "small_gradients",
        [(narrow0, width), (narrow1, width), (norm_in, layers), (pick, channels)],
        [
            jax.ShapeDtypeStruct(shape, f32)
            for shape in (
                norm_in.shape,
                (layers, bc_rows, width),
                (heads, layers, width),
                conv_x.shape,
                conv_x_bias.shape,
                conv_bc.shape,
                conv_bc_bias.shape,
                dt_bias.shape,
                a_log.shape,
                skip.shape,
                norm_gate.shape,
            )
        ],
    )
    return (
        outputs_home[None, :, :width],
        outputs_home[None, :, width:],
        small[0],
        g_wz,
        g_wx,
        jnp.transpose(small[1], (0, 2, 1)),
        jnp.transpose(small[2], (1, 2, 0)),
        *small[3:],
        g_wo,
    )


def solution(mesh):
    specs_in = (
        P("dp", "tensor", None),
        P("dp", "tensor", None),
        P(),
        P(None, None, "tensor"),
        P(None, None, "tensor"),
        P(None, None, "tensor"),
        P(None, None, "tensor"),
        P(None, None, "tensor"),
        P(None, "tensor"),
        P(),
        P(),
        P(None, "tensor"),
        P(None, "tensor"),
        P(None, "tensor"),
        P(None, "tensor"),
        P(None, "tensor", None),
    )
    specs_out = (
        P("dp", "tensor", None),
        P("dp", "tensor", None),
        P(),
        P(None, None, "tensor"),
        P(None, None, "tensor"),
        P(None, None, "tensor"),
        P(None, None, "tensor"),
        P(None, None, "tensor"),
        P(None, "tensor"),
        P(),
        P(),
        P(None, "tensor"),
        P(None, "tensor"),
        P(None, "tensor"),
        P(None, "tensor"),
        P(None, "tensor", None),
    )
    return jax.shard_map(
        local, mesh=mesh, in_specs=specs_in, out_specs=specs_out, check_vma=False
    )
```
